32 devices in a mesh: image: 2 (over y), brick: 4 (over z), probe: 2 (over x), chan: 2 (over core).
Axes of the slice: x: 2, y: 2, z: 4, core: 2. Of those that a mesh axis runs over, the one named last changes fastest.
Arguments:
- atom_s: bfloat16 [2048, 128], P(('image', 'brick', 'probe'), 'chan'), parts along dimension 0, may hold values from -6 to 6
- atom_pos: float32 [3, 2048], P(None, ('image', 'brick', 'probe')), parts along dimension 1, may hold values from 0 to 4
- edge_vec: float32 [3, 32768], P(None, ('image', 'brick', 'probe')), parts along dimension 1, may hold values from -5 to 5, as said below
- edge_nbr: int32 [32768], P(('image', 'brick', 'probe')), parts along dimension 0, may hold values from 0 to 191
- border_index: int32 [1024], P(('image', 'brick', 'probe')), parts along dimension 0, may hold values from 0 to 127
- send_index: int32 [16, 32], P(('image', 'brick', 'probe')), parts along dimension 0, may hold values from 0 to 127
- probe_list: int32 [64, 128], P(('image', 'brick', 'probe')), parts along dimension 0, may hold values from 0 to 31
- probe_count: int32 [64], P(('image', 'brick', 'probe')), parts along dimension 0, may hold values from 64 to 128, as said below
- w_in: bfloat16 [2, 128, 128], replicated, may hold values from -0.5 to 0.5
- b_in: float32 [2, 128], replicated, may hold values from -3 to 3
- w_msg: bfloat16 [2, 128, 3, 128], P(None, None, None, 'chan'), may hold values from -0.5 to 0.5
- w_rad: bfloat16 [2, 16, 3, 128], P(None, None, None, 'chan'), may hold values from -1.5 to 1.5
- w_probe: bfloat16 [16, 2, 128], P(None, None, 'chan'), may hold values from -0.5 to 0.5
- w_mix: bfloat16 [128, 128], replicated, may hold values from -0.5 to 0.5
- b_mix: float32 [128], replicated, may hold values from -3 to 3
- w_out: float32 [128], replicated, may hold values from -0.5 to 0.5
Outputs:
- density: float32 [8192], P(('image', 'brick', 'probe')), parts along dimension 0
The draws below stay inside these ranges and needn't reach their ends.
There are 2 independent parts, one for each index of `image`. The reference program is written for one: setup_inputs(seed, part) draws one part's arguments, and reference() takes and returns one part's arrays. A program takes and returns all parts, laid end to end along the dimension named above; an argument that names none is the same for every part. Nothing has to cross between parts.
Inputs may be any that keep to these rules, and one draw needn't show every extreme that they name: `edge_vec`: edge displacements have lengths between 1 and 5. `probe_count`: in every group some block has all 128 entries live.
All inputs are finite; a program needn't handle non-finite values.
Results may differ from the reference program's by a relative error of at most 0.012.
Values may be sent and summed in bfloat16 or wider, within the bound.
No kernel may reach another device: no remote copies, remote signals or barrier semaphores. Data moves between devices by JAX's collectives and lax.ppermute only.
A program may use at most 64 MiB of HBM per device.

```python
import math
import jax
import jax.numpy as jnp
from jax import lax

C = 128
R = 16
K = 16
LAYERS = 2
AD = 128
P_DEV = 512
PB = 128
MB = 128
GH = 32
CAP = 4
NPB = 4
GROUPS = 8
ATOMS = 1024


def draw_edge_vec(key, part):
    key = jax.random.fold_in(key, 11)
    key_len, key_cos, key_ang = jax.random.split(key, 3)
    count = ATOMS * K
    length = jax.random.uniform(key_len, (count,), jnp.float32, 1.0, 5.0)
    cosine = jax.random.uniform(key_cos, (count,), jnp.float32, -1.0, 1.0)
    angle = jax.random.uniform(key_ang, (count,), jnp.float32, -math.pi, math.pi)
    sine = jnp.sqrt(jnp.maximum(1.0 - cosine * cosine, 0.0))
    return jnp.stack([length * sine * jnp.cos(angle), length * sine * jnp.sin(angle), length * cosine]).astype(jnp.float32)


def draw_probe_count(key, part):
    key = jax.random.fold_in(key, 17)
    key_base, key_full = jax.random.split(key, 2)
    base = jax.random.randint(key_base, (GROUPS, NPB), MB // 2, MB + 1)
    full_block = jax.random.randint(key_full, (GROUPS,), 0, NPB)
    blocks = jnp.arange(NPB, dtype=jnp.int32)[None, :]
    base = jnp.where(blocks == full_block[:, None], MB, base)
    return base.reshape(GROUPS * NPB).astype(jnp.int32)


def set_ends(result, key, smallest, top_value):
    place = [jax.random.randint(jax.random.fold_in(key, axis), (), 0, length) for axis, length in enumerate(result.shape)]
    main_axis = result.shape.index(max(result.shape))
    next_to = place[:main_axis] + [(place[main_axis] + 1) % result.shape[main_axis]] + place[main_axis + 1:]
    return result.at[tuple(place)].set(smallest).at[tuple(next_to)].set(top_value)


def level_of(key, dims, cuts, least, largest):
    gain = 1.0
    for dim, blocks in cuts:
        steps = jax.random.uniform(jax.random.fold_in(jax.random.fold_in(key, 6), dim), (blocks,), jnp.float32, least / len(cuts), largest / len(cuts))
        gain = gain * jnp.repeat(jnp.exp(steps), dims[dim] // blocks).reshape((-1,) + (1,) * (len(dims) - 1 - dim))
    return gain


def bell_draw(rng, extent, spread, reach, shards=(), held_as=jnp.bfloat16):
    result = spread * jax.random.normal(rng, extent, jnp.float32)
    if shards:
        result = result * level_of(rng, extent, shards, -0.22, 0.18)
    return jnp.clip(result, -reach, reach).astype(held_as)


def setup_inputs(seed: int = 0, part: int = 0) -> dict:
    key_list = jax.random.split(jax.random.key(seed), 17)
    part_splits = jax.random.split(jax.random.fold_in(key_list[16], part), 17)
    return {
        "atom_s": bell_draw(part_splits[0], (ATOMS, C), 1.0, 6.0, ((0, 8), (1, 2))),
        "atom_pos": jnp.clip(4.0 * jax.random.uniform(part_splits[1], (3, ATOMS), jnp.float32) ** level_of(part_splits[1], (3, ATOMS), ((1, 8),), -0.2, 0.2), 0.0, 4.0),
        "edge_vec": draw_edge_vec(jax.random.fold_in(jax.random.fold_in(key_list[16], part), 71), part),
        "edge_nbr": set_ends(jax.random.randint(part_splits[3], (ATOMS * K,), 0, AD + 2 * GH), jax.random.fold_in(part_splits[3], 1), 0, (AD + 2 * GH) - 1).astype(jnp.int32),
        "border_index": set_ends(jax.random.randint(part_splits[4], (2 * GH * GROUPS,), 0, AD), jax.random.fold_in(part_splits[4], 1), 0, AD - 1).astype(jnp.int32),
        "send_index": set_ends(jax.random.randint(part_splits[5], (GROUPS, GROUPS * CAP), 0, AD), jax.random.fold_in(part_splits[5], 1), 0, AD - 1).astype(jnp.int32),
        "probe_list": set_ends(jax.random.randint(part_splits[6], (GROUPS * NPB, MB), 0, GROUPS * CAP), jax.random.fold_in(part_splits[6], 1), 0, (GROUPS * CAP) - 1).astype(jnp.int32),
        "probe_count": draw_probe_count(jax.random.fold_in(jax.random.fold_in(key_list[16], part), 71), part),
        "w_in": bell_draw(key_list[8], (LAYERS, C, C), C ** -0.5, 0.5),
        "b_in": bell_draw(key_list[9], (LAYERS, C), 0.5, 3.0, (), jnp.float32),
        "w_msg": bell_draw(key_list[10], (LAYERS, C, 3, C), C ** -0.5, 0.5, ((3, 2),)),
        "w_rad": bell_draw(key_list[11], (LAYERS, R, 3, C), R ** -0.5, 1.5, ((3, 2),)),
        "w_probe": bell_draw(key_list[12], (R, 2, C), MB ** -0.5, 0.5, ((2, 2),)),
        "w_mix": bell_draw(key_list[13], (C, C), C ** -0.5, 0.5),
        "b_mix": bell_draw(key_list[14], (C,), 0.5, 3.0, (), jnp.float32),
        "w_out": bell_draw(key_list[15], (C,), C ** -0.5, 0.5, (), jnp.float32),
    }


def radial(distance, count, top):
    centers = jnp.arange(count).astype(jnp.float32) * (top / (count - 1))
    return jnp.exp(-2.0 * (distance[..., None] - centers) ** 2)

def reference(atom_s, atom_pos, edge_vec, edge_nbr, border_index, send_index, probe_list, probe_count, w_in, b_in, w_msg, w_rad, w_probe, w_mix, b_mix, w_out):
    root_fan = K ** 0.5
    length = jnp.sqrt(lax.optimization_barrier(jnp.sum(edge_vec * edge_vec, axis=0)))
    edge_env = (1.0 - length * length / 36.0) ** 2
    edge_basis = (radial(length, R, 6.0) * edge_env[:, None]).astype(jnp.bfloat16)
    scalars = atom_s
    vectors = jnp.zeros((ATOMS, 3, C), jnp.bfloat16)
    neighbours = edge_nbr.reshape(GROUPS, AD * K)
    border_rows = border_index.reshape(GROUPS, 2 * GH)
    edge_group = jnp.transpose(edge_vec.reshape(3, GROUPS, AD * K), (1, 2, 0))
    basis_group = edge_basis.reshape(GROUPS, AD * K, R)
    for layer_no in range(LAYERS):
        hidden_act = jax.nn.silu(jnp.dot(scalars, w_in[layer_no], preferred_element_type=jnp.float32) + b_in[layer_no]).astype(jnp.bfloat16)
        messages = jnp.dot(hidden_act, w_msg[layer_no].reshape(C, 3 * C), preferred_element_type=jnp.float32).astype(jnp.bfloat16)
        own_rows = jnp.concatenate([messages, vectors.reshape(ATOMS, 3 * C)], axis=1).reshape(GROUPS, AD, 6 * C)
        face_rows = jax.vmap(lambda tab_in, idx_in: tab_in[idx_in])(own_rows, border_rows)
        lower_rim = jnp.roll(face_rows[:, GH:], 1, axis=0)
        upper_rim = jnp.roll(face_rows[:, :GH], -1, axis=0)
        lookup = jnp.concatenate([own_rows, lower_rim, upper_rim], axis=1)
        rad_weight = w_rad[layer_no].reshape(R, 3 * C)

        def update_group(item_in):
            tab_in, idx_in, vec_in, bas_in = item_in
            rows_in = tab_in[idx_in]
            filters = jnp.dot(bas_in, rad_weight, preferred_element_type=jnp.float32)
            weighted = rows_in[:, :3 * C].astype(jnp.float32) * filters
            neighbour_vec = rows_in[:, 3 * C:].astype(jnp.float32).reshape(AD * K, 3, C)
            delta_vec = neighbour_vec * weighted[:, None, C:2 * C] + weighted[:, None, 2 * C:] * vec_in[:, :, None]
            delta_scalar = weighted[:, :C].reshape(AD, K, C).sum(axis=1) / root_fan
            delta_vec = delta_vec.reshape(AD, K, 3, C).sum(axis=1) / root_fan
            return (delta_scalar, delta_vec)
        delta_scalar, delta_vec = lax.map(update_group, (lookup, neighbours, edge_group, basis_group))
        scalars = (scalars + delta_scalar.reshape(ATOMS, C)).astype(jnp.bfloat16)
        vectors = (vectors + delta_vec.reshape(ATOMS, 3, C)).astype(jnp.bfloat16)
    feat_scalar = scalars.reshape(GROUPS, AD, C)
    feat_vector = vectors.reshape(GROUPS, AD, 3, C)
    pos_bf16 = atom_pos.astype(jnp.bfloat16).reshape(3, GROUPS, AD)
    sends = send_index.reshape(GROUPS, GROUPS, CAP)
    source = jnp.arange(GROUPS, dtype=jnp.int32)[:, None]
    w_scalar = w_probe[:, 0, :].astype(jnp.float32)
    w_vector = w_probe[:, 1, :].astype(jnp.float32)

    def probe_group(item_in):
        group_no, lists_in, counts_in = item_in
        picked = sends[:, group_no, :]
        recv_scalar = feat_scalar[source, picked].reshape(GROUPS * CAP, C)
        recv_vector = feat_vector[source, picked].reshape(GROUPS * CAP, 3, C)
        recv_pos = lax.optimization_barrier(pos_bf16[:, source, picked].reshape(3, GROUPS * CAP)).astype(jnp.float32)

        def probe_block(block_in):
            block_no, listed, live_count = block_in
            index_row = (group_no * NPB + block_no) * PB + jnp.arange(PB, dtype=jnp.int32)
            grid_xyz = jnp.stack([index_row % 16, index_row // 16 % 16, index_row // 256 % 16], axis=1).astype(jnp.float32) * 0.25
            atom_xyz = recv_pos[:, listed]
            disp = grid_xyz[:, :, None] - atom_xyz[None]
            dist_sq = lax.optimization_barrier(jnp.sum(disp * disp, axis=1))
            live = (jnp.arange(MB, dtype=jnp.int32) < live_count).astype(jnp.float32)
            envelope = (1.0 - dist_sq / 64.0) ** 2 * live[None, :]
            basis = radial(jnp.sqrt(dist_sq), R, 7.0) * envelope[:, :, None]
            scalar_w = basis.astype(jnp.bfloat16).reshape(PB, MB * R)
            vector_w = (disp[:, :, :, None] * basis[:, None]).astype(jnp.bfloat16).reshape(PB, 3 * MB * R)
            atom_terms = (recv_scalar[listed].astype(jnp.float32)[:, None, :] * w_scalar[None]).astype(jnp.bfloat16).reshape(MB * R, C)
            vec_rows = jnp.transpose(recv_vector[listed], (1, 0, 2)).astype(jnp.float32)
            vector_terms = (vec_rows[:, :, None, :] * w_vector[None, None]).astype(jnp.bfloat16).reshape(3 * MB * R, C)
            charge = jnp.dot(scalar_w, atom_terms, preferred_element_type=jnp.float32) + jnp.dot(vector_w, vector_terms, preferred_element_type=jnp.float32)
            return charge.astype(jnp.bfloat16)
        charges = lax.map(probe_block, (jnp.arange(NPB, dtype=jnp.int32), lists_in, counts_in)).reshape(P_DEV, C)
        mixed = jnp.dot(charges, w_mix, preferred_element_type=jnp.float32) + b_mix
        return lax.optimization_barrier(jnp.sum(jax.nn.silu(mixed) * w_out, axis=1))
    density = lax.map(probe_group, (jnp.arange(GROUPS, dtype=jnp.int32), probe_list.reshape(GROUPS, NPB, MB), probe_count.reshape(GROUPS, NPB)))
    return density.reshape(GROUPS * P_DEV)
```

```python
import functools

import jax
import jax.numpy as jnp
from jax import lax
from jax.experimental import pallas as pl
from jax.experimental.pallas import tpu as pltpu
from jax.sharding import PartitionSpec as P

PB = 128
LANES = 128
FEW_GROUPS = 8
F32 = jnp.float32
BF16 = jnp.bfloat16


def iota(shape, dim):
    return lax.broadcasted_iota(jnp.int32, shape, dim)


def dot(a, b):
    return jnp.dot(a, b, preferred_element_type=F32)


def dot_tn(a, b):
    return lax.dot_general(a, b, (((0,), (0,)), ((), ())), preferred_element_type=F32)


def one_hot(mask):
    return jnp.where(mask, 1.0, 0.0).astype(BF16)


def silu(x):
    return x / (1.0 + jnp.exp(-x))


def lane_atom(lane, fan, tiles):
    return (lane % tiles) * (LANES // fan) + lane // tiles


def split_rows(value):
    high = value.astype(BF16)
    return high, (value - high.astype(F32)).astype(BF16)


def pack_kernel(
    fan,
    atom_s,
    atom_pos,
    edge_vec,
    edge_nbr,
    border,
    send,
    w_msg,
    w_rad,
    w_probe,
    data_out,
    weight_out,
    natural,
):
    atoms, half = atom_s.shape
    tiles = atoms * fan // LANES
    per_tile = LANES // fan
    part = lax.axis_index("chan")
    perm = one_hot(lane_atom(iota((atoms, LANES), 1), fan, tiles) == iota((atoms, LANES), 0))
    data_out[0:half, :] = dot_tn(atom_s[...], perm).astype(BF16)
    for comp in range(3):
        for tile in range(tiles):
            natural[comp * tiles + tile : comp * tiles + tile + 1, :] = edge_vec[
                comp : comp + 1, tile * LANES : (tile + 1) * LANES
            ]
    natural[3 * tiles : 4 * tiles, :] = edge_nbr[...].astype(F32)
    natural[4 * tiles :, :] = jnp.zeros((LANES - 4 * tiles, LANES), F32)
    turned = natural[...].T
    lane = iota((fan, LANES), 1)
    sorted_rows = []
    for comp in range(4):
        rows = jnp.zeros((fan, LANES), F32)
        for a in range(per_tile):
            piece = turned[a * fan : (a + 1) * fan, :]
            shift = (a * tiles - comp * tiles) % LANES
            piece = pltpu.roll(piece, shift, 1) if shift else piece
            rows = jnp.where(lane // tiles == a, piece, rows)
        mine = jnp.where(part == 0, rows[: fan // 2], rows[fan // 2 :])
        sorted_rows.append(mine)
    highs, lows = [], []
    for comp in range(3):
        high = sorted_rows[comp].astype(BF16).astype(F32)
        highs.append(high)
        lows.append(sorted_rows[comp] - high)
    edge_rows = jnp.concatenate(highs + lows + [sorted_rows[3]], axis=0)
    n_edge = edge_rows.shape[0]
    pos = dot(atom_pos[...].astype(BF16), perm)
    blank = jnp.zeros((1, LANES), F32)
    border_row = jnp.concatenate(
        [border[...].astype(F32), jnp.zeros((1, LANES - border.shape[1]), F32)], axis=1
    )
    send_row = jnp.concatenate(
        [send[...].astype(F32), jnp.zeros((1, LANES - send.shape[1]), F32)], axis=1
    )
    rest = jnp.concatenate([pos, border_row, send_row, blank, blank, blank], axis=0)
    data_out[half:, :] = jnp.concatenate([edge_rows, rest], axis=0).astype(BF16)
    layers = w_msg.shape[0]
    for layer in range(layers):
        weight_out[layer * 3 * half : (layer + 1) * 3 * half, :] = w_msg[layer].astype(F32).T.astype(BF16)
    radial_rows = [
        w_rad[layer][:, p * half : (p + 1) * half].astype(F32) for layer in range(layers) for p in range(3)
    ]
    radial_rows += [w_probe[:, p * half : (p + 1) * half].astype(F32) for p in range(2)]
    weight_out[layers * 3 * half :, :] = jnp.concatenate(radial_rows, axis=0).T.astype(BF16)


def pack(atom_s, atom_pos, edge_vec, edge_nbr, border_index, send_index, w_msg, w_rad, w_probe):
    atoms, half = atom_s.shape
    fan = edge_nbr.shape[0] // atoms
    layers, width = w_msg.shape[:2]
    n_basis = w_rad.shape[1]
    return pl.pallas_call(
        functools.partial(pack_kernel, fan),
        out_shape=(
            jax.ShapeDtypeStruct((half + 7 * fan // 2 + 8, LANES), BF16),
            jax.ShapeDtypeStruct((layers * 3 * half + half, width), BF16),
        ),
        scratch_shapes=[pltpu.VMEM((LANES, LANES), F32)],
        name="pack",
    )(
        atom_s,
        atom_pos,
        edge_vec,
        edge_nbr.reshape(-1, LANES),
        border_index.reshape(1, -1),
        send_index,
        w_msg.reshape(layers, width, 3 * half),
        w_rad.reshape(layers, n_basis, 3 * half),
        w_probe.reshape(n_basis, 2 * half),
    )


def density_kernel(
    sizes,
    data,
    weights,
    w_in,
    b_in,
    probe_list,
    probe_count,
    w_mix,
    b_mix,
    w_out,
    density,
    state0,
    own0,
    faces0,
    state1,
    table1,
):
    groups, fan, rim, half, n_basis, cap = sizes
    width = 2 * half
    tiles = LANES * fan // LANES
    root_fan = fan**0.5
    me = lax.axis_index("brick") * lax.axis_size("probe") + lax.axis_index("probe")
    every = groups * LANES
    edge_at = half
    n_edge = 7 * fan // 2
    rest_at = half + n_edge

    columns = jnp.concatenate(
        [b_in[...], b_mix[...], w_out[...], jnp.zeros((4, width), F32)], axis=0
    ).T

    def weight(layer, p):
        at = (layer * 3 + p) * half
        return jnp.concatenate([weights[c, at : at + half, :] for c in range(2)], axis=0)

    radial_at = weights.shape[1] - half
    radial_all = jnp.concatenate([weights[c, radial_at:, :] for c in range(2)], axis=0)

    def radial_weight(layer, p):
        at = (layer * 3 + p) * n_basis
        return radial_all[:, at : at + n_basis]

    def edge_rows(group):
        return [data[2 * group + c, edge_at:rest_at, :].astype(F32) for c in range(2)]

    def basis_of(dist_row, env_row):
        centers = iota((n_basis, 1), 0).astype(F32) * (6.0 / (n_basis - 1))
        return (jnp.exp(-2.0 * (dist_row - centers) ** 2) * env_row).astype(BF16)

    for group in range(groups):
        for c in range(2):
            state0[c * half : (c + 1) * half, group * LANES : (group + 1) * LANES] = data[
                2 * group + c, 0:half, :
            ]
    hidden = silu(dot_tn(w_in[0], state0[...]) + columns[:, 0:1]).astype(BF16)
    weight_ac = jnp.concatenate([weight(0, 0), weight(0, 2)], axis=0)
    messages = dot(weight_ac, hidden).astype(BF16)
    atom_col = lane_atom(iota((LANES, 2 * rim), 0), fan, tiles).astype(F32)
    for group in range(groups):
        own = messages[:, group * LANES : (group + 1) * LANES]
        own0[group] = own
        border_row = data[2 * group, rest_at + 3 : rest_at + 4, 0 : 2 * rim].astype(F32)
        faces0[group, :, 0 : 2 * rim] = dot(own, one_hot(atom_col == border_row)).astype(BF16)

    row = iota((LANES + 2 * rim, 1), 0)
    names = jnp.where(
        row < LANES,
        lane_atom(row, fan, tiles),
        jnp.where(row < LANES + rim, row + rim, row - rim),
    ).astype(F32)
    upper_lane = iota((2 * width, 2 * rim), 1) < rim
    radial_ac = jnp.concatenate([radial_weight(0, 0), radial_weight(0, 2)], axis=0)

    def update(group, carry):
        up = lax.rem(group + 1, groups)
        low = lax.rem(group + groups - 1, groups)
        ghosts = jnp.where(
            upper_lane,
            faces0[up, :, 0 : 2 * rim].astype(F32),
            faces0[low, :, 0 : 2 * rim].astype(F32),
        ).astype(BF16)
        table = jnp.concatenate([own0[group], ghosts], axis=1)
        halves = edge_rows(group)
        step = fan // 2
        acc = jnp.zeros((width, LANES), F32)
        acc_vec = [jnp.zeros((width, LANES), F32) for _ in range(3)]
        for c in range(2):
            rows = halves[c]
            vec = [rows[x * step : (x + 1) * step] + rows[(3 + x) * step : (4 + x) * step] for x in range(3)]
            nbr = rows[6 * step : 7 * step]
            length_sq = vec[0] * vec[0] + vec[1] * vec[1] + vec[2] * vec[2]
            length = jnp.sqrt(length_sq)
            env = (1.0 - length * length / 36.0) ** 2
            for pair in range(step // 2):
                ks = (2 * pair, 2 * pair + 1)
                picked = jnp.concatenate([one_hot(names == nbr[k : k + 1]) for k in ks], axis=1)
                basis = jnp.concatenate(
                    [basis_of(length[k : k + 1], env[k : k + 1]) for k in ks], axis=1
                )
                prod = dot(table, picked) * dot(radial_ac, basis)
                for i, k in enumerate(ks):
                    block = prod[:, i * LANES : (i + 1) * LANES]
                    acc = acc + block[:width]
                    for x in range(3):
                        acc_vec[x] = acc_vec[x] + block[width:] * vec[x][k : k + 1]
        lanes = pl.ds(pl.multiple_of(group * LANES, LANES), LANES)
        state1[0:width, lanes] = (state0[:, lanes].astype(F32) + acc / root_fan).astype(BF16)
        for x in range(3):
            state1[(x + 1) * width : (x + 2) * width, lanes] = (acc_vec[x] / root_fan).astype(BF16)
        return carry

    lax.fori_loop(0, groups, update, 0)

    hidden = silu(dot_tn(w_in[1], state1[0:width, :]) + columns[:, 1:2]).astype(BF16)
    for p in range(3):
        table1[p * width : (p + 1) * width, :] = dot(weight(1, p), hidden).astype(BF16)
    table1[3 * width :, :] = state1[width:, :]

    received = groups * cap
    edges = received * fan
    send_rows = jnp.concatenate(
        [data[2 * g, rest_at + 4 : rest_at + 5, :].astype(F32) for g in range(groups)], axis=0
    )

    def picks(lane_count, per_group):
        lane = iota((LANES, lane_count), 1)
        wanted = me * cap + lane % cap
        spread = dot(send_rows.astype(BF16), one_hot(iota((LANES, lane_count), 0) == wanted))
        lane = iota((groups, lane_count), 1)
        spread = jnp.where(lane // per_group == iota((groups, lane_count), 0), spread, 0.0)
        return jnp.sum(spread, axis=0, keepdims=True)

    per_group = fan * cap
    pick_edges = picks(edges, per_group)
    pick_atoms = picks(received, cap)
    atom_rows = lane_atom(iota((LANES, per_group), 0), fan, tiles).astype(F32)
    chosen = []
    for group in range(groups):
        rows = jnp.concatenate([data[2 * group + c, edge_at:rest_at, :] for c in range(2)], axis=0)
        want = pick_edges[:, group * per_group : (group + 1) * per_group]
        chosen.append(dot(rows, one_hot(atom_rows == want)))
    chosen = jnp.concatenate(chosen, axis=1)
    step = fan // 2
    row = iota((2 * n_edge, edges), 0)
    slot_k = (row // n_edge) * step + row % step
    lane_k = (iota((2 * n_edge, edges), 1) % per_group) // cap
    chosen = jnp.where(slot_k == lane_k, chosen, 0.0)
    chosen = jnp.sum(chosen.reshape(2 * 7, step, edges), axis=1)
    chosen = chosen[0:7] + chosen[7:14]
    vec = [chosen[x : x + 1] + chosen[3 + x : 4 + x] for x in range(3)]
    nbr = chosen[6:7]
    length = jnp.sqrt(vec[0] * vec[0] + vec[1] * vec[1] + vec[2] * vec[2])
    basis = basis_of(length, (1.0 - length * length / 36.0) ** 2)

    nbr = nbr.astype(jnp.int32)
    home = iota((1, edges), 1) // per_group
    is_low = (nbr >= LANES) & (nbr < LANES + rim)
    is_up = nbr >= LANES + rim
    owner = jnp.where(
        is_low, (home + groups - 1) % groups, jnp.where(is_up, (home + 1) % groups, home)
    )
    entry = owner * 2 * rim + jnp.where(is_low, nbr - (LANES - rim), nbr - (LANES + rim))
    entry = jnp.where(is_low | is_up, entry, -1)
    border_all = jnp.concatenate(
        [data[2 * g, rest_at + 3 : rest_at + 4, 0 : 2 * rim].astype(F32) for g in range(groups)], axis=1
    )
    border_all = jnp.broadcast_to(border_all, (16, groups * 2 * rim)).astype(BF16)
    seen = dot(border_all, one_hot(iota((groups * 2 * rim, edges), 0) == entry))[0:1]
    target = owner * LANES + jnp.where(entry < 0, nbr, seen.astype(jnp.int32))
    column = iota((every, 1), 0)
    column_name = (column // LANES) * LANES + lane_atom(column % LANES, fan, tiles)
    rows = dot(table1[...], one_hot(column_name == target))
    radial_abc = jnp.concatenate([radial_weight(1, p) for p in range(3)], axis=0)
    filters = dot(radial_abc, basis)
    gate = rows[width : 2 * width] * filters[width : 2 * width]
    along = rows[2 * width : 3 * width] * filters[2 * width :]
    parts = [rows[:width] * filters[:width]]
    for x in range(3):
        parts.append(rows[(3 + x) * width : (4 + x) * width] * gate + along * vec[x])
    parts = jnp.concatenate(parts, axis=0).astype(BF16)
    edge = iota((edges, received), 0)
    slot = (edge // per_group) * cap + edge % cap
    delta = dot(parts, one_hot(slot == iota((edges, received), 1)))
    wanted = (iota((1, received), 1) // cap) * LANES + pick_atoms.astype(jnp.int32)
    chosen_atoms = one_hot(column_name == wanted)
    final = (dot(state1[...], chosen_atoms) + delta / root_fan).astype(BF16).astype(F32)

    pos_rows = jnp.concatenate(
        [data[2 * g, rest_at : rest_at + 8, :] for g in range(groups)], axis=1
    )
    pos = dot(pos_rows, chosen_atoms) - 1.875
    pos_cols = jnp.concatenate(
        [
            jnp.concatenate([pos, jnp.zeros((8, LANES - received), F32)], axis=1),
            jnp.zeros((LANES - 8, LANES), F32),
        ],
        axis=0,
    ).T
    n_blocks, list_len = probe_list.shape
    counts = []
    for block in range(n_blocks):
        live = iota((1, list_len), 1) < probe_count[block]
        named = jnp.where(live, probe_list[block : block + 1, :], -1)
        hits = jnp.where(iota((received, list_len), 0) == named, 1.0, 0.0)
        counts.append(
            jnp.broadcast_to(jnp.sum(hits, axis=1, keepdims=True), (received, PB))
        )
    counts = jnp.concatenate(counts, axis=1)
    probes = n_blocks * PB
    number = me * probes + iota((1, probes), 1)
    grid = [
        (n % 16).astype(F32) * 0.25 - 1.875 for n in (number, number // 16, number // 256)
    ]
    dist_sq = jnp.zeros((received, probes), F32)
    for x in range(3):
        dist_sq = dist_sq + (grid[x] - pos_cols[0:received, x : x + 1]) ** 2
    dist = jnp.sqrt(dist_sq)
    envelope = (1.0 - dist_sq / 64.0) ** 2 * counts
    basis = jnp.concatenate(
        [
            (jnp.exp(-2.0 * (dist - r * (7.0 / (n_basis - 1))) ** 2) * envelope).astype(BF16)
            for r in range(n_basis)
        ],
        axis=0,
    )
    spread = one_hot(
        iota((n_basis, n_basis * received), 1) // received
        == iota((n_basis, n_basis * received), 0)
    )
    probe_at = 6 * n_basis
    w_scalar = dot(radial_all[:, probe_at : probe_at + n_basis], spread)
    w_vector = dot(radial_all[:, probe_at + n_basis :], spread)
    along = final[width : 2 * width] * pos[0:1]
    for x in range(1, 3):
        along = along + final[(x + 1) * width : (x + 2) * width] * pos[x : x + 1]
    def repeat(value):
        return jnp.concatenate([value] * n_basis, axis=1)
    terms = [w_scalar * repeat(final[:width]) - w_vector * repeat(along)]
    for x in range(3):
        terms.append(w_vector * repeat(final[(x + 1) * width : (x + 2) * width]))
    sums = dot(jnp.concatenate(terms, axis=0).astype(BF16), basis)
    charges = sums[:width]
    for x in range(3):
        charges = charges + grid[x] * sums[(x + 1) * width : (x + 2) * width]
    mixed = dot_tn(w_mix[...], charges.astype(BF16)) + columns[:, 2:3]
    density[...] = jnp.sum(silu(mixed) * columns[:, 3:4], axis=0, keepdims=True)


def few_groups(
    atom_s, atom_pos, edge_vec, edge_nbr, border_index, send_index, probe_list, probe_count,
    w_in, b_in, w_msg, w_rad, w_probe, w_mix, b_mix, w_out,
):
    atoms, half = atom_s.shape
    groups = lax.axis_size("brick") * lax.axis_size("probe")
    fan = edge_nbr.shape[0] // atoms
    rim = border_index.shape[0] // 2
    n_basis = w_rad.shape[1]
    cap = send_index.shape[1] // groups
    width = 2 * half
    every = groups * LANES
    data, weights = pack(
        atom_s, atom_pos, edge_vec, edge_nbr, border_index, send_index, w_msg, w_rad, w_probe
    )
    weights = lax.all_gather(weights, "chan")
    data = lax.all_gather(data, ("brick", "probe", "chan"))
    n_probes = probe_list.shape[0] * PB
    vmem = pl.BlockSpec(memory_space=pltpu.VMEM)
    smem = pl.BlockSpec(memory_space=pltpu.SMEM)
    density = pl.pallas_call(
        functools.partial(density_kernel, (groups, fan, rim, half, n_basis, cap)),
        out_shape=jax.ShapeDtypeStruct((1, n_probes), F32),
        in_specs=[vmem] * 5 + [smem] + [vmem] * 3,
        scratch_shapes=[
            pltpu.VMEM((width, every), BF16),
            pltpu.VMEM((groups, 2 * width, LANES), BF16),
            pltpu.VMEM((groups, 2 * width, LANES), BF16),
            pltpu.VMEM((4 * width, every), BF16),
            pltpu.VMEM((6 * width, every), BF16),
        ],
        compiler_params=pltpu.CompilerParams(vmem_limit_bytes=40 * 1024 * 1024),
        name="density",
    )(
        data, weights, w_in, b_in, probe_list, probe_count, w_mix,
        b_mix.reshape(1, -1), w_out.reshape(1, -1),
    )
    return density.reshape(n_probes)


def per_device(*args):
    if lax.axis_size("brick") * lax.axis_size("probe") <= FEW_GROUPS:
        return few_groups(*args)
    return many_groups(*args)


def extended(block, sides, width):
    for axis, dim in sides:
        count = lax.axis_size(axis)
        forward = [(i, i + 1) for i in range(count - 1)]
        forward.append((count - 1, 0))
        backward = [(target, source) for source, target in forward]
        low = lax.ppermute(
            lax.slice_in_dim(block, block.shape[dim] - width, None, axis=dim), axis, forward
        )
        high = lax.ppermute(lax.slice_in_dim(block, 0, width, axis=dim), axis, backward)
        block = jnp.concatenate([low, block, high], axis=dim)
    return block


def radial(distance, count, top):
    centers = jnp.arange(count).astype(jnp.float32) * (top / (count - 1))
    return jnp.exp(-2.0 * (distance[..., None] - centers) ** 2)


def make_block(
    recv_rows, recv_pos, w_scalar, w_vector, feat_width, group_no, n_blocks, list_len, n_basis
):

    def probe_block(block_in):
        block_no, listed, live_count = block_in
        index_row = (group_no * n_blocks + block_no) * PB + jnp.arange(PB, dtype=jnp.int32)
        grid_xyz = (
            jnp.stack([index_row % 16, index_row // 16 % 16, index_row // 256 % 16], axis=1).astype(
                jnp.float32
            )
            * 0.25
        )
        atom_xyz = recv_pos[:, listed]
        disp = grid_xyz[:, :, None] - atom_xyz[None]
        dist_sq = jnp.sum(disp * disp, axis=1)
        live = (jnp.arange(list_len, dtype=jnp.int32) < live_count).astype(jnp.float32)
        envelope = (1.0 - dist_sq / 64.0) ** 2 * live[None, :]
        basis = radial(jnp.sqrt(dist_sq), n_basis, 7.0) * envelope[:, :, None]
        scalar_w = basis.astype(jnp.bfloat16).reshape(PB, list_len * n_basis)
        vector_w = (
            (disp[:, :, :, None] * basis[:, None])
            .astype(jnp.bfloat16)
            .reshape(PB, 3 * list_len * n_basis)
        )
        atom_rows = recv_rows[listed]
        atom_terms = (atom_rows[:, None, :feat_width] * w_scalar[None]).reshape(
            list_len * n_basis, feat_width
        )
        vec_rows = jnp.transpose(
            atom_rows[:, feat_width:].reshape(list_len, 3, feat_width), (1, 0, 2)
        )
        vector_terms = (vec_rows[:, :, None, :] * w_vector[None, None]).reshape(
            3 * list_len * n_basis, feat_width
        )
        charge = jnp.dot(scalar_w, atom_terms, preferred_element_type=jnp.float32) + jnp.dot(
            vector_w, vector_terms, preferred_element_type=jnp.float32
        )
        return charge.astype(jnp.bfloat16)

    return probe_block


def many_groups(
    atom_s,
    atom_pos,
    edge_vec,
    edge_nbr,
    border_index,
    send_index,
    probe_list,
    probe_count,
    w_in,
    b_in,
    w_msg,
    w_rad,
    w_probe,
    w_mix,
    b_mix,
    w_out,
):
    atom_count, half_width = atom_s.shape
    n_layers = w_in.shape[0]
    width = w_in.shape[1]
    n_basis = w_rad.shape[1]
    fan_out = edge_nbr.shape[0] // atom_count
    root_fan = fan_out**0.5
    rim_rows = border_index.shape[0] // 2
    length = jnp.sqrt(jnp.sum(edge_vec * edge_vec, axis=0))
    edge_env = (1.0 - length * length / 36.0) ** 2
    edge_basis = (radial(length, n_basis, 6.0) * edge_env[:, None]).astype(jnp.bfloat16)
    edge_cols = jnp.transpose(edge_vec)
    scalars = atom_s
    vectors = jnp.zeros((atom_count, 3 * half_width), jnp.bfloat16)
    for layer_no in range(n_layers):
        full_rows = lax.all_gather(scalars, "chan", axis=1, tiled=True)
        in_weight = w_in[layer_no]
        in_bias = b_in[layer_no]
        msg_weight = w_msg[layer_no].reshape(width, 3 * half_width)
        rad_weight = w_rad[layer_no].reshape(n_basis, 3 * half_width)
        hidden_act = jax.nn.silu(
            jnp.dot(full_rows, in_weight, preferred_element_type=jnp.float32) + in_bias
        ).astype(jnp.bfloat16)
        inner_tab = jnp.concatenate(
            [
                jnp.dot(hidden_act, msg_weight, preferred_element_type=jnp.float32).astype(
                    jnp.bfloat16
                ),
                vectors,
            ],
            axis=1,
        )
        padded = extended(inner_tab[border_index], ((("brick", "probe"), 0),), rim_rows)
        lookup = jnp.concatenate([inner_tab, padded[:rim_rows], padded[3 * rim_rows :]], axis=0)
        neighbour_rows = lookup[edge_nbr]
        filters = jnp.dot(edge_basis, rad_weight, preferred_element_type=jnp.float32)
        weighted = neighbour_rows[:, : 3 * half_width] * filters
        neighbour_vec = neighbour_rows[:, 3 * half_width :].reshape(-1, 3, half_width)
        vector_gate = weighted[:, None, half_width : 2 * half_width]
        along_edge = weighted[:, None, 2 * half_width :]
        delta_vec = neighbour_vec * vector_gate + along_edge * edge_cols[:, :, None]
        delta_scalar = (
            weighted[:, :half_width].reshape(atom_count, fan_out, half_width).sum(axis=1) / root_fan
        )
        delta_vec = delta_vec.reshape(atom_count, fan_out, 3 * half_width).sum(axis=1) / root_fan
        scalars = (scalars + delta_scalar).astype(jnp.bfloat16)
        vectors = (vectors + delta_vec).astype(jnp.bfloat16)
    features = jnp.concatenate([scalars, vectors], axis=1)
    picks = send_index[0]
    n_brick = lax.axis_size("brick")
    n_probe = lax.axis_size("probe")
    n_groups = n_brick * n_probe
    slot_cap = picks.shape[0] // n_groups
    out_rows = features[picks]
    out_pos = jnp.transpose(atom_pos)[picks].astype(jnp.bfloat16)
    received = (
        lax.all_to_all(
            out_rows.reshape(n_groups, slot_cap, 4 * half_width),
            ("brick", "probe"),
            split_axis=0,
            concat_axis=0,
            tiled=True,
        ),
        lax.all_to_all(
            out_pos.reshape(n_groups, slot_cap, 3),
            ("brick", "probe"),
            split_axis=0,
            concat_axis=0,
            tiled=True,
        ),
    )
    recv_count = n_groups * slot_cap
    recv_rows = received[0].reshape(recv_count, 4 * half_width)
    recv_pos = jnp.transpose(received[1].reshape(recv_count, 3)).astype(jnp.float32)
    group_no = lax.axis_index("brick") * n_probe + lax.axis_index("probe")
    n_blocks, list_len = probe_list.shape
    probe_block = make_block(
        recv_rows,
        recv_pos,
        w_probe[:, 0, :],
        w_probe[:, 1, :],
        half_width,
        group_no,
        n_blocks,
        list_len,
        n_basis,
    )
    charges = lax.map(
        probe_block, (jnp.arange(n_blocks, dtype=jnp.int32), probe_list, probe_count)
    ).reshape(n_blocks * PB, half_width)
    mix_rows = lax.dynamic_slice_in_dim(w_mix, lax.axis_index("chan") * half_width, half_width, 0)
    mixed = lax.psum(jnp.dot(charges, mix_rows, preferred_element_type=jnp.float32), "chan")
    return jnp.sum(jax.nn.silu(mixed + b_mix) * w_out, axis=1)


def solution(mesh):
    in_specs = (
        P(("image", "brick", "probe"), "chan"),
        P(None, ("image", "brick", "probe")),
        P(None, ("image", "brick", "probe")),
        P(("image", "brick", "probe")),
        P(("image", "brick", "probe")),
        P(("image", "brick", "probe"), None),
        P(("image", "brick", "probe"), None),
        P(("image", "brick", "probe")),
        P(),
        P(),
        P(None, None, None, "chan"),
        P(None, None, None, "chan"),
        P(None, None, "chan"),
        P(),
        P(),
        P(),
    )
    out_specs = P(("image", "brick", "probe"))
    return jax.shard_map(
        per_device, mesh=mesh, in_specs=in_specs, out_specs=out_specs, check_vma=False
    )
```

```python
import functools

import jax
import jax.numpy as jnp
from jax import lax
from jax.experimental import pallas as pl
from jax.experimental.pallas import tpu as pltpu
from jax.sharding import PartitionSpec as P

PB = 128
LANES = 128
FEW_GROUPS = 8
F32 = jnp.float32
BF16 = jnp.bfloat16


def iota(shape, dim):
    return lax.broadcasted_iota(jnp.int32, shape, dim)


def dot(a, b):
    return jnp.dot(a, b, preferred_element_type=F32)


def dot_tn(a, b):
    return lax.dot_general(a, b, (((0,), (0,)), ((), ())), preferred_element_type=F32)


def one_hot(mask):
    return jnp.where(mask, 1.0, 0.0).astype(BF16)


def silu(x):
    return x / (1.0 + jnp.exp(-x))


def lane_atom(lane, fan, tiles):
    return (lane % tiles) * (LANES // fan) + lane // tiles


def pack_kernel(
    fan, atom_s, atom_pos, edge_vec, edge_nbr, border, send, w_msg, w_rad, w_probe, data_out, weight_out, natural
):
    half, atoms = atom_s.shape
    tiles = atoms * fan // LANES
    per_tile = LANES // fan
    part = lax.axis_index("chan")
    perm = one_hot(lane_atom(iota((atoms, LANES), 1), fan, tiles) == iota((atoms, LANES), 0))
    data_out[0:half, :] = dot(atom_s[...], perm).astype(BF16)
    vec = edge_vec[...]
    vec_high = vec.astype(BF16).astype(F32)
    length = jnp.sqrt(jnp.sum(vec * vec, axis=0, keepdims=True))
    short = length - jnp.sqrt(jnp.sum(vec_high * vec_high, axis=0, keepdims=True))
    rows = jnp.concatenate([vec_high, short], axis=0)
    for tile in range(tiles):
        for comp in range(4):
            natural[comp * tiles + tile : comp * tiles + tile + 1, :] = rows[
                comp : comp + 1, tile * LANES : (tile + 1) * LANES
            ]
    natural[4 * tiles : 5 * tiles, :] = edge_nbr[...].astype(F32)
    natural[5 * tiles :, :] = jnp.zeros((LANES - 5 * tiles, LANES), F32)
    turned = natural[...].T
    lane = iota((fan, LANES), 1)
    sorted_rows = []
    for comp in range(5):
        rows = jnp.zeros((fan, LANES), F32)
        for a in range(per_tile):
            piece = turned[a * fan : (a + 1) * fan, :]
            shift = (a * tiles - comp * tiles) % LANES
            piece = pltpu.roll(piece, shift, 1) if shift else piece
            rows = jnp.where(lane // tiles == a, piece, rows)
        sorted_rows.append(jnp.where(part == 0, rows[: fan // 2], rows[fan // 2 :]))
    pos = dot(atom_pos[...].astype(BF16), perm)
    blank = jnp.zeros((1, LANES), F32)
    border_row = jnp.concatenate(
        [border[...].astype(F32), jnp.zeros((1, LANES - border.shape[1]), F32)], axis=1
    )
    send_row = jnp.concatenate(
        [send[...].astype(F32), jnp.zeros((1, LANES - send.shape[1]), F32)], axis=1
    )
    rest = jnp.concatenate([pos, border_row, send_row, blank, blank, blank], axis=0)
    data_out[half:, :] = jnp.concatenate(sorted_rows + [rest], axis=0).astype(BF16)
    probe_rows = [w_probe[r].astype(F32) for r in range(w_probe.shape[0])]
    radial = jnp.concatenate([w_rad[...].astype(F32)] + probe_rows, axis=0).T.astype(BF16)
    weight_out[: w_msg.shape[0], :] = w_msg[...]
    weight_out[w_msg.shape[0] :, :] = radial


def pack(atom_s, atom_pos, edge_vec, edge_nbr, border_index, send_index, w_msg, w_rad, w_probe):
    atoms, half = atom_s.shape
    fan = edge_nbr.shape[0] // atoms
    return pl.pallas_call(
        functools.partial(pack_kernel, fan),
        out_shape=(
            jax.ShapeDtypeStruct((half + 5 * fan // 2 + 8, LANES), BF16),
            jax.ShapeDtypeStruct((w_msg.size // LANES + half, LANES), BF16),
        ),
        scratch_shapes=[pltpu.VMEM((LANES, LANES), F32)],
        name="pack",
    )(
        atom_s.T,
        atom_pos,
        edge_vec,
        edge_nbr.reshape(-1, LANES),
        border_index.reshape(1, -1),
        send_index,
        jnp.transpose(w_msg, (0, 2, 3, 1)).reshape(-1, LANES),
        jnp.transpose(w_rad, (0, 2, 1, 3)).reshape(-1, half),
        w_probe,
    )


def density_kernel(
    sizes,
    data_all,
    weights,
    w_in,
    b_in,
    probe_list,
    probe_count,
    w_mix,
    b_mix,
    w_out,
    density,
    state0,
    own0,
    faces0,
    state1,
    table1,
):
    groups, fan, rim, half, n_basis, cap = sizes
    width = 2 * half
    tiles = LANES * fan // LANES
    root_fan = fan**0.5
    me = lax.axis_index("brick") * lax.axis_size("probe") + lax.axis_index("probe")
    every = groups * LANES
    edge_at = half
    n_edge = 5 * fan // 2
    rest_at = half + n_edge
    n_probe = data_all.shape[1]

    def data(group, c, rows):
        return data_all[c, lax.rem(group, n_probe), group // n_probe, rows, :]

    columns = jnp.concatenate(
        [b_in[...], b_mix[...], w_out[...], jnp.zeros((4, width), F32)], axis=0
    ).T

    def weight(layer, p):
        at = (layer * 3 + p) * half
        return jnp.concatenate([weights[c, at : at + half, :] for c in range(2)], axis=0)

    radial_at = weights.shape[1] - half
    radial_all = jnp.concatenate([weights[c, radial_at:, :] for c in range(2)], axis=0)

    def radial_weight(layer, p):
        at = (layer * 3 + p) * n_basis
        return radial_all[:, at : at + n_basis]

    def edge_rows(group):
        return [data(group, c, slice(edge_at, rest_at)).astype(F32) for c in range(2)]

    def border_of(group):
        return data(group, 0, slice(rest_at, rest_at + 8)).astype(F32)[3:4, 0 : 2 * rim]

    def basis_of(dist_row, env_row):
        centers = iota((n_basis, 1), 0).astype(F32) * (6.0 / (n_basis - 1))
        return (jnp.exp(-2.0 * (dist_row - centers) ** 2) * env_row).astype(BF16)

    for group in range(groups):
        for c in range(2):
            state0[c * half : (c + 1) * half, group * LANES : (group + 1) * LANES] = data(
                group, c, slice(0, half)
            )
    hidden = silu(dot_tn(w_in[0], state0[...]) + columns[:, 0:1]).astype(BF16)
    weight_ac = jnp.concatenate([weight(0, 0), weight(0, 2)], axis=0)
    messages = dot(weight_ac, hidden).astype(BF16)
    atom_col = lane_atom(iota((LANES, 2 * rim), 0), fan, tiles).astype(F32)
    for group in range(groups):
        own = messages[:, group * LANES : (group + 1) * LANES]
        own0[group] = own
        border_row = border_of(group)
        faces0[group, :, 0 : 2 * rim] = dot(own, one_hot(atom_col == border_row)).astype(BF16)

    row = iota((LANES + 2 * rim, 1), 0)
    names = jnp.where(
        row < LANES,
        lane_atom(row, fan, tiles),
        jnp.where(row < LANES + rim, row + rim, row - rim),
    ).astype(F32)
    upper_lane = iota((2 * width, 2 * rim), 1) < rim
    radial_ac = jnp.concatenate([radial_weight(0, 0), radial_weight(0, 2)], axis=0)

    def update(group, carry):
        up = lax.rem(group + 1, groups)
        low = lax.rem(group + groups - 1, groups)
        ghosts = jnp.where(
            upper_lane,
            faces0[up, :, 0 : 2 * rim].astype(F32),
            faces0[low, :, 0 : 2 * rim].astype(F32),
        ).astype(BF16)
        table = jnp.concatenate([own0[group], ghosts], axis=1)
        halves = edge_rows(group)
        step = fan // 2
        acc = jnp.zeros((width, LANES), F32)
        acc_vec = [jnp.zeros((width, LANES), F32) for _ in range(3)]
        for c in range(2):
            rows = halves[c]
            vec = [rows[x * step : (x + 1) * step] for x in range(3)]
            nbr = rows[4 * step : 5 * step]
            length_sq = vec[0] * vec[0] + vec[1] * vec[1] + vec[2] * vec[2]
            length = jnp.sqrt(length_sq) + rows[3 * step : 4 * step]
            env = (1.0 - length * length / 36.0) ** 2
            for pair in range(step // 2):
                ks = (2 * pair, 2 * pair + 1)
                picked = jnp.concatenate([one_hot(names == nbr[k : k + 1]) for k in ks], axis=1)
                basis = jnp.concatenate(
                    [basis_of(length[k : k + 1], env[k : k + 1]) for k in ks], axis=1
                )
                prod = dot(table, picked) * dot(radial_ac, basis)
                for i, k in enumerate(ks):
                    block = prod[:, i * LANES : (i + 1) * LANES]
                    acc = acc + block[:width]
                    for x in range(3):
                        acc_vec[x] = acc_vec[x] + block[width:] * vec[x][k : k + 1]
        lanes = pl.ds(pl.multiple_of(group * LANES, LANES), LANES)
        state1[0:width, lanes] = (state0[:, lanes].astype(F32) + acc / root_fan).astype(BF16)
        for x in range(3):
            state1[(x + 1) * width : (x + 2) * width, lanes] = (acc_vec[x] / root_fan).astype(BF16)
        return carry

    lax.fori_loop(0, groups, update, 0)

    hidden = silu(dot_tn(w_in[1], state1[0:width, :]) + columns[:, 1:2]).astype(BF16)
    for p in range(3):
        table1[p * width : (p + 1) * width, :] = dot(weight(1, p), hidden).astype(BF16)
    table1[3 * width :, :] = state1[width:, :]

    received = groups * cap
    edges = received * fan
    send_rows = jnp.concatenate(
        [data(g, 0, slice(rest_at, rest_at + 8)).astype(F32)[4:5] for g in range(groups)], axis=0
    )

    def picks(lane_count, per_group):
        lane = iota((LANES, lane_count), 1)
        wanted = me * cap + lane % cap
        spread = dot(send_rows.astype(BF16), one_hot(iota((LANES, lane_count), 0) == wanted))
        lane = iota((groups, lane_count), 1)
        spread = jnp.where(lane // per_group == iota((groups, lane_count), 0), spread, 0.0)
        return jnp.sum(spread, axis=0, keepdims=True)

    per_group = fan * cap
    pick_edges = picks(edges, per_group)
    pick_atoms = picks(received, cap)
    atom_rows = lane_atom(iota((LANES, per_group), 0), fan, tiles).astype(F32)
    chosen = []
    for group in range(groups):
        rows = jnp.concatenate([data(group, c, slice(edge_at, rest_at)) for c in range(2)], axis=0)
        want = pick_edges[:, group * per_group : (group + 1) * per_group]
        chosen.append(dot(rows, one_hot(atom_rows == want)))
    chosen = jnp.concatenate(chosen, axis=1)
    step = fan // 2
    row = iota((2 * n_edge, edges), 0)
    slot_k = (row // n_edge) * step + row % step
    lane_k = (iota((2 * n_edge, edges), 1) % per_group) // cap
    chosen = jnp.where(slot_k == lane_k, chosen, 0.0)
    chosen = jnp.sum(chosen.reshape(2 * 5, step, edges), axis=1)
    chosen = chosen[0:5] + chosen[5:10]
    vec = [chosen[x : x + 1] for x in range(3)]
    nbr = chosen[4:5]
    length = jnp.sqrt(vec[0] * vec[0] + vec[1] * vec[1] + vec[2] * vec[2]) + chosen[3:4]
    basis = basis_of(length, (1.0 - length * length / 36.0) ** 2)

    nbr = nbr.astype(jnp.int32)
    home = iota((1, edges), 1) // per_group
    is_low = (nbr >= LANES) & (nbr < LANES + rim)
    is_up = nbr >= LANES + rim
    owner = jnp.where(
        is_low, (home + groups - 1) % groups, jnp.where(is_up, (home + 1) % groups, home)
    )
    entry = owner * 2 * rim + jnp.where(is_low, nbr - (LANES - rim), nbr - (LANES + rim))
    entry = jnp.where(is_low | is_up, entry, -1)
    border_all = jnp.concatenate(
        [border_of(g) for g in range(groups)], axis=1
    )
    border_all = jnp.broadcast_to(border_all, (16, groups * 2 * rim)).astype(BF16)
    seen = dot(border_all, one_hot(iota((groups * 2 * rim, edges), 0) == entry))[0:1]
    target = owner * LANES + jnp.where(entry < 0, nbr, seen.astype(jnp.int32))
    column = iota((every, 1), 0)
    column_name = (column // LANES) * LANES + lane_atom(column % LANES, fan, tiles)
    rows = dot(table1[...], one_hot(column_name == target))
    radial_abc = jnp.concatenate([radial_weight(1, p) for p in range(3)], axis=0)
    filters = dot(radial_abc, basis)
    gate = rows[width : 2 * width] * filters[width : 2 * width]
    along = rows[2 * width : 3 * width] * filters[2 * width :]
    parts = [rows[:width] * filters[:width]]
    for x in range(3):
        parts.append(rows[(3 + x) * width : (4 + x) * width] * gate + along * vec[x])
    parts = jnp.concatenate(parts, axis=0).astype(BF16)
    edge = iota((edges, received), 0)
    slot = (edge // per_group) * cap + edge % cap
    delta = dot(parts, one_hot(slot == iota((edges, received), 1)))
    wanted = (iota((1, received), 1) // cap) * LANES + pick_atoms.astype(jnp.int32)
    chosen_atoms = one_hot(column_name == wanted)
    final = (dot(state1[...], chosen_atoms) + delta / root_fan).astype(BF16).astype(F32)

    pos_rows = jnp.concatenate(
        [data(g, 0, slice(rest_at, rest_at + 8)) for g in range(groups)], axis=1
    )
    pos = dot(pos_rows, chosen_atoms) - 1.875
    pos_cols = jnp.concatenate(
        [
            jnp.concatenate([pos, jnp.zeros((8, LANES - received), F32)], axis=1),
            jnp.zeros((LANES - 8, LANES), F32),
        ],
        axis=0,
    ).T
    n_blocks, list_len = probe_list.shape
    counts = []
    for block in range(n_blocks):
        live = iota((1, list_len), 1) < probe_count[block]
        named = jnp.where(live, probe_list[block : block + 1, :], -1)
        hits = jnp.where(iota((received, list_len), 0) == named, 1.0, 0.0)
        counts.append(
            jnp.broadcast_to(jnp.sum(hits, axis=1, keepdims=True), (received, PB))
        )
    counts = jnp.concatenate(counts, axis=1)
    probes = n_blocks * PB
    number = me * probes + iota((1, probes), 1)
    grid = [
        (n % 16).astype(F32) * 0.25 - 1.875 for n in (number, number // 16, number // 256)
    ]
    dist_sq = jnp.zeros((received, probes), F32)
    for x in range(3):
        dist_sq = dist_sq + (grid[x] - pos_cols[0:received, x : x + 1]) ** 2
    dist = jnp.sqrt(dist_sq)
    envelope = (1.0 - dist_sq / 64.0) ** 2 * counts
    basis = jnp.concatenate(
        [
            (jnp.exp(-2.0 * (dist - r * (7.0 / (n_basis - 1))) ** 2) * envelope).astype(BF16)
            for r in range(n_basis)
        ],
        axis=0,
    )
    terms_shape = (2 * n_basis, n_basis * received)
    probe_weight = radial_all[:, 3 * b_in.shape[0] * n_basis :]
    w_scalar, w_vector = (
        dot(probe_weight, one_hot(iota(terms_shape, 1) // received * 2 + p == iota(terms_shape, 0)))
        for p in range(2)
    )
    along = final[width : 2 * width] * pos[0:1]
    for x in range(1, 3):
        along = along + final[(x + 1) * width : (x + 2) * width] * pos[x : x + 1]
    def repeat(value):
        return jnp.concatenate([value] * n_basis, axis=1)
    terms = [w_scalar * repeat(final[:width]) - w_vector * repeat(along)]
    for x in range(3):
        terms.append(w_vector * repeat(final[(x + 1) * width : (x + 2) * width]))
    sums = dot(jnp.concatenate(terms, axis=0).astype(BF16), basis)
    charges = sums[:width]
    for x in range(3):
        charges = charges + grid[x] * sums[(x + 1) * width : (x + 2) * width]
    mixed = dot_tn(w_mix[...], charges.astype(BF16)) + columns[:, 2:3]
    density[...] = jnp.sum(silu(mixed) * columns[:, 3:4], axis=0, keepdims=True)


def few_groups(
    atom_s, atom_pos, edge_vec, edge_nbr, border_index, send_index, probe_list, probe_count,
    w_in, b_in, w_msg, w_rad, w_probe, w_mix, b_mix, w_out,
):
    atoms, half = atom_s.shape
    groups = lax.axis_size("brick") * lax.axis_size("probe")
    fan = edge_nbr.shape[0] // atoms
    rim = border_index.shape[0] // 2
    n_basis = w_rad.shape[1]
    cap = send_index.shape[1] // groups
    width = 2 * half
    every = groups * LANES
    data, weights = pack(
        atom_s, atom_pos, edge_vec, edge_nbr, border_index, send_index, w_msg, w_rad, w_probe
    )
    data = lax.all_gather(lax.all_gather(data, "brick"), "probe")
    data, weights = lax.all_gather(data, "chan"), lax.all_gather(weights, "chan")
    n_probes = probe_list.shape[0] * PB
    vmem = pl.BlockSpec(memory_space=pltpu.VMEM)
    smem = pl.BlockSpec(memory_space=pltpu.SMEM)
    density = pl.pallas_call(
        functools.partial(density_kernel, (groups, fan, rim, half, n_basis, cap)),
        out_shape=jax.ShapeDtypeStruct((1, n_probes), F32),
        in_specs=[vmem] * 5 + [smem] + [vmem] * 3,
        scratch_shapes=[
            pltpu.VMEM((width, every), BF16),
            pltpu.VMEM((groups, 2 * width, LANES), BF16),
            pltpu.VMEM((groups, 2 * width, LANES), BF16),
            pltpu.VMEM((4 * width, every), BF16),
            pltpu.VMEM((6 * width, every), BF16),
        ],
        compiler_params=pltpu.CompilerParams(vmem_limit_bytes=40 * 1024 * 1024),
        name="density",
    )(
        data, weights, w_in, b_in, probe_list, probe_count, w_mix,
        b_mix.reshape(1, -1), w_out.reshape(1, -1),
    )
    return density.reshape(n_probes)


def per_device(*args):
    if lax.axis_size("brick") * lax.axis_size("probe") <= FEW_GROUPS:
        return few_groups(*args)
    return many_groups(*args)


def extended(block, sides, width):
    for axis, dim in sides:
        count = lax.axis_size(axis)
        forward = [(i, i + 1) for i in range(count - 1)]
        forward.append((count - 1, 0))
        backward = [(target, source) for source, target in forward]
        low = lax.ppermute(
            lax.slice_in_dim(block, block.shape[dim] - width, None, axis=dim), axis, forward
        )
        high = lax.ppermute(lax.slice_in_dim(block, 0, width, axis=dim), axis, backward)
        block = jnp.concatenate([low, block, high], axis=dim)
    return block


def radial(distance, count, top):
    centers = jnp.arange(count).astype(jnp.float32) * (top / (count - 1))
    return jnp.exp(-2.0 * (distance[..., None] - centers) ** 2)


def make_block(
    recv_rows, recv_pos, w_scalar, w_vector, feat_width, group_no, n_blocks, list_len, n_basis
):

    def probe_block(block_in):
        block_no, listed, live_count = block_in
        index_row = (group_no * n_blocks + block_no) * PB + jnp.arange(PB, dtype=jnp.int32)
        grid_xyz = (
            jnp.stack([index_row % 16, index_row // 16 % 16, index_row // 256 % 16], axis=1).astype(
                jnp.float32
            )
            * 0.25
        )
        atom_xyz = recv_pos[:, listed]
        disp = grid_xyz[:, :, None] - atom_xyz[None]
        dist_sq = jnp.sum(disp * disp, axis=1)
        live = (jnp.arange(list_len, dtype=jnp.int32) < live_count).astype(jnp.float32)
        envelope = (1.0 - dist_sq / 64.0) ** 2 * live[None, :]
        basis = radial(jnp.sqrt(dist_sq), n_basis, 7.0) * envelope[:, :, None]
        scalar_w = basis.astype(jnp.bfloat16).reshape(PB, list_len * n_basis)
        vector_w = (
            (disp[:, :, :, None] * basis[:, None])
            .astype(jnp.bfloat16)
            .reshape(PB, 3 * list_len * n_basis)
        )
        atom_rows = recv_rows[listed]
        atom_terms = (atom_rows[:, None, :feat_width] * w_scalar[None]).reshape(
            list_len * n_basis, feat_width
        )
        vec_rows = jnp.transpose(
            atom_rows[:, feat_width:].reshape(list_len, 3, feat_width), (1, 0, 2)
        )
        vector_terms = (vec_rows[:, :, None, :] * w_vector[None, None]).reshape(
            3 * list_len * n_basis, feat_width
        )
        charge = jnp.dot(scalar_w, atom_terms, preferred_element_type=jnp.float32) + jnp.dot(
            vector_w, vector_terms, preferred_element_type=jnp.float32
        )
        return charge.astype(jnp.bfloat16)

    return probe_block


def many_groups(
    atom_s,
    atom_pos,
    edge_vec,
    edge_nbr,
    border_index,
    send_index,
    probe_list,
    probe_count,
    w_in,
    b_in,
    w_msg,
    w_rad,
    w_probe,
    w_mix,
    b_mix,
    w_out,
):
    atom_count, half_width = atom_s.shape
    n_layers = w_in.shape[0]
    width = w_in.shape[1]
    n_basis = w_rad.shape[1]
    fan_out = edge_nbr.shape[0] // atom_count
    root_fan = fan_out**0.5
    rim_rows = border_index.shape[0] // 2
    length = jnp.sqrt(jnp.sum(edge_vec * edge_vec, axis=0))
    edge_env = (1.0 - length * length / 36.0) ** 2
    edge_basis = (radial(length, n_basis, 6.0) * edge_env[:, None]).astype(jnp.bfloat16)
    edge_cols = jnp.transpose(edge_vec)
    scalars = atom_s
    vectors = jnp.zeros((atom_count, 3 * half_width), jnp.bfloat16)
    for layer_no in range(n_layers):
        full_rows = lax.all_gather(scalars, "chan", axis=1, tiled=True)
        in_weight = w_in[layer_no]
        in_bias = b_in[layer_no]
        msg_weight = w_msg[layer_no].reshape(width, 3 * half_width)
        rad_weight = w_rad[layer_no].reshape(n_basis, 3 * half_width)
        hidden_act = jax.nn.silu(
            jnp.dot(full_rows, in_weight, preferred_element_type=jnp.float32) + in_bias
        ).astype(jnp.bfloat16)
        inner_tab = jnp.concatenate(
            [
                jnp.dot(hidden_act, msg_weight, preferred_element_type=jnp.float32).astype(
                    jnp.bfloat16
                ),
                vectors,
            ],
            axis=1,
        )
        padded = extended(inner_tab[border_index], ((("brick", "probe"), 0),), rim_rows)
        lookup = jnp.concatenate([inner_tab, padded[:rim_rows], padded[3 * rim_rows :]], axis=0)
        neighbour_rows = lookup[edge_nbr]
        filters = jnp.dot(edge_basis, rad_weight, preferred_element_type=jnp.float32)
        weighted = neighbour_rows[:, : 3 * half_width] * filters
        neighbour_vec = neighbour_rows[:, 3 * half_width :].reshape(-1, 3, half_width)
        vector_gate = weighted[:, None, half_width : 2 * half_width]
        along_edge = weighted[:, None, 2 * half_width :]
        delta_vec = neighbour_vec * vector_gate + along_edge * edge_cols[:, :, None]
        delta_scalar = (
            weighted[:, :half_width].reshape(atom_count, fan_out, half_width).sum(axis=1) / root_fan
        )
        delta_vec = delta_vec.reshape(atom_count, fan_out, 3 * half_width).sum(axis=1) / root_fan
        scalars = (scalars + delta_scalar).astype(jnp.bfloat16)
        vectors = (vectors + delta_vec).astype(jnp.bfloat16)
    features = jnp.concatenate([scalars, vectors], axis=1)
    picks = send_index[0]
    n_brick = lax.axis_size("brick")
    n_probe = lax.axis_size("probe")
    n_groups = n_brick * n_probe
    slot_cap = picks.shape[0] // n_groups
    out_rows = features[picks]
    out_pos = jnp.transpose(atom_pos)[picks].astype(jnp.bfloat16)
    received = (
        lax.all_to_all(
            out_rows.reshape(n_groups, slot_cap, 4 * half_width),
            ("brick", "probe"),
            split_axis=0,
            concat_axis=0,
            tiled=True,
        ),
        lax.all_to_all(
            out_pos.reshape(n_groups, slot_cap, 3),
            ("brick", "probe"),
            split_axis=0,
            concat_axis=0,
            tiled=True,
        ),
    )
    recv_count = n_groups * slot_cap
    recv_rows = received[0].reshape(recv_count, 4 * half_width)
    recv_pos = jnp.transpose(received[1].reshape(recv_count, 3)).astype(jnp.float32)
    group_no = lax.axis_index("brick") * n_probe + lax.axis_index("probe")
    n_blocks, list_len = probe_list.shape
    probe_block = make_block(
        recv_rows,
        recv_pos,
        w_probe[:, 0, :],
        w_probe[:, 1, :],
        half_width,
        group_no,
        n_blocks,
        list_len,
        n_basis,
    )
    charges = lax.map(
        probe_block, (jnp.arange(n_blocks, dtype=jnp.int32), probe_list, probe_count)
    ).reshape(n_blocks * PB, half_width)
    mix_rows = lax.dynamic_slice_in_dim(w_mix, lax.axis_index("chan") * half_width, half_width, 0)
    mixed = lax.psum(jnp.dot(charges, mix_rows, preferred_element_type=jnp.float32), "chan")
    return jnp.sum(jax.nn.silu(mixed + b_mix) * w_out, axis=1)


def solution(mesh):
    in_specs = (
        P(("image", "brick", "probe"), "chan"),
        P(None, ("image", "brick", "probe")),
        P(None, ("image", "brick", "probe")),
        P(("image", "brick", "probe")),
        P(("image", "brick", "probe")),
        P(("image", "brick", "probe"), None),
        P(("image", "brick", "probe"), None),
        P(("image", "brick", "probe")),
        P(),
        P(),
        P(None, None, None, "chan"),
        P(None, None, None, "chan"),
        P(None, None, "chan"),
        P(),
        P(),
        P(),
    )
    out_specs = P(("image", "brick", "probe"))
    return jax.shard_map(
        per_device, mesh=mesh, in_specs=in_specs, out_specs=out_specs, check_vma=False
    )
```

```python
import functools

import jax
import jax.numpy as jnp
from jax import lax
from jax.experimental import pallas as pl
from jax.experimental.pallas import tpu as pltpu
from jax.sharding import PartitionSpec as P

PB = 128
LANES = 128
FEW_GROUPS = 8
SMALL = 16
F32 = jnp.float32
BF16 = jnp.bfloat16


def iota(shape, dim):
    return lax.broadcasted_iota(jnp.int32, shape, dim)


def dot(a, b):
    return jnp.dot(a, b, preferred_element_type=F32)


def dot_tn(a, b):
    return lax.dot_general(a, b, (((0,), (0,)), ((), ())), preferred_element_type=F32)


def one_hot(mask):
    return jnp.where(mask, 1.0, 0.0).astype(BF16)


def silu(x):
    return x / (1.0 + jnp.exp(-x))


def lane_atom(lane, fan, tiles):
    return (lane % tiles) * (LANES // fan) + lane // tiles


def pack_kernel(
    fan, atom_s, atom_pos, edge_vec, edge_nbr, border, send, w_msg, w_rad, w_probe,
    b_in, b_mix, w_out, probe_list, probe_count, data_out, weight_out, small_out, natural,
):
    half, atoms = atom_s.shape
    tiles = atoms * fan // LANES
    per_tile = LANES // fan
    part = lax.axis_index("chan")
    perm = one_hot(lane_atom(iota((atoms, LANES), 1), fan, tiles) == iota((atoms, LANES), 0))
    scalars = dot(atom_s[...], perm).astype(BF16)
    vec = edge_vec[...]
    vec_high = vec.astype(BF16).astype(F32)
    length = jnp.sqrt(jnp.sum(vec * vec, axis=0, keepdims=True))
    short = length - jnp.sqrt(jnp.sum(vec_high * vec_high, axis=0, keepdims=True))
    rows = jnp.concatenate([vec_high, short], axis=0)
    for tile in range(tiles):
        for comp in range(4):
            natural[comp * tiles + tile : comp * tiles + tile + 1, :] = rows[
                comp : comp + 1, tile * LANES : (tile + 1) * LANES
            ]
    natural[4 * tiles : 5 * tiles, :] = edge_nbr[...].astype(F32)
    natural[5 * tiles :, :] = jnp.zeros((LANES - 5 * tiles, LANES), F32)
    turned = natural[...].T
    lane = iota((fan, LANES), 1)
    sorted_rows = []
    for comp in range(5):
        rows = jnp.zeros((fan, LANES), F32)
        for a in range(per_tile):
            piece = turned[a * fan : (a + 1) * fan, :]
            shift = (a * tiles - comp * tiles) % LANES
            piece = pltpu.roll(piece, shift, 1) if shift else piece
            rows = jnp.where(lane // tiles == a, piece, rows)
        sorted_rows.append(jnp.where(part == 0, rows[: fan // 2], rows[fan // 2 :]))
    pos = dot(atom_pos[...].astype(BF16), perm)
    blank = jnp.zeros((1, LANES), F32)
    border_row = jnp.concatenate(
        [border[...].astype(F32), jnp.zeros((1, LANES - border.shape[1]), F32)], axis=1
    )
    send_row = jnp.concatenate(
        [send[...].astype(F32), jnp.zeros((1, LANES - send.shape[1]), F32)], axis=1
    )
    rest = jnp.concatenate([pos, border_row, send_row, blank, blank, blank], axis=0)
    others = jnp.concatenate(sorted_rows + [rest], axis=0).astype(BF16)
    for group in range(data_out.shape[0]):
        data_out[group, 0:half, :] = scalars
        data_out[group, half:, :] = others
    at = 0
    for piece in (b_in, b_mix, w_out, probe_list, probe_count):
        rows, cols = piece.shape
        small_out[at : at + rows, 0:cols] = piece[...].astype(F32)
        at += rows
    probe_rows = [w_probe[r].astype(F32) for r in range(w_probe.shape[0])]
    radial = jnp.concatenate([w_rad[...].astype(F32)] + probe_rows, axis=0).T.astype(BF16)
    weight_out[: w_msg.shape[0], :] = w_msg[...]
    weight_out[w_msg.shape[0] :, :] = radial


def pack(
    groups, atom_s, atom_pos, edge_vec, edge_nbr, border_index, send_index, w_msg, w_rad, w_probe,
    b_in, b_mix, w_out, probe_list, probe_count,
):
    atoms, half = atom_s.shape
    fan = edge_nbr.shape[0] // atoms
    return pl.pallas_call(
        functools.partial(pack_kernel, fan),
        out_shape=(
            jax.ShapeDtypeStruct((groups, half + 5 * fan // 2 + 8, LANES), BF16),
            jax.ShapeDtypeStruct((w_msg.size // LANES + half, LANES), BF16),
            jax.ShapeDtypeStruct((SMALL, LANES), F32),
        ),
        scratch_shapes=[pltpu.VMEM((LANES, LANES), F32)],
        name="pack",
    )(
        atom_s.T,
        atom_pos,
        edge_vec,
        edge_nbr.reshape(-1, LANES),
        border_index.reshape(1, -1),
        send_index,
        jnp.transpose(w_msg, (0, 2, 3, 1)).reshape(-1, LANES),
        jnp.transpose(w_rad, (0, 2, 1, 3)).reshape(-1, half),
        w_probe,
        b_in,
        b_mix.reshape(1, -1),
        w_out.reshape(1, -1),
        probe_list,
        probe_count.reshape(1, -1),
    )


def density_kernel(
    sizes,
    data_all,
    weights_mine,
    weights_other,
    small,
    w_in,
    w_mix,
    density,
    state0,
    own0,
    faces0,
    state1,
    table1,
    weights,
):
    groups, fan, rim, half, n_basis, cap, n_blocks = sizes
    layers = w_in.shape[0]
    width = 2 * half
    tiles = LANES * fan // LANES
    root_fan = fan**0.5
    me = lax.axis_index("brick") * lax.axis_size("probe") + lax.axis_index("probe")
    part = lax.axis_index("chan")
    weights[part] = weights_mine[...]
    weights[1 - part] = weights_other[...]
    every = groups * LANES
    edge_at = half
    n_edge = 5 * fan // 2
    rest_at = half + n_edge

    def data(group, c, rows):
        return data_all[c, group, rows, :]

    small_rows = small[...]
    columns = small_rows.T

    def weight(layer, p):
        at = (layer * 3 + p) * half
        return jnp.concatenate([weights[c, at : at + half, :] for c in range(2)], axis=0)

    radial_at = weights.shape[1] - half
    radial_all = jnp.concatenate([weights[c, radial_at:, :] for c in range(2)], axis=0)

    def radial_weight(layer, p):
        at = (layer * 3 + p) * n_basis
        return radial_all[:, at : at + n_basis]

    def edge_rows(group):
        return [data(group, c, slice(edge_at, rest_at)).astype(F32) for c in range(2)]

    def border_of(group):
        return data(group, 0, slice(rest_at, rest_at + 8)).astype(F32)[3:4, 0 : 2 * rim]

    def basis_of(dist_row, env_row):
        centers = iota((n_basis, 1), 0).astype(F32) * (6.0 / (n_basis - 1))
        return (jnp.exp(-2.0 * (dist_row - centers) ** 2) * env_row).astype(BF16)

    for group in range(groups):
        for c in range(2):
            state0[c * half : (c + 1) * half, group * LANES : (group + 1) * LANES] = data(
                group, c, slice(0, half)
            )
    hidden = silu(dot_tn(w_in[0], state0[...]) + columns[:, 0:1]).astype(BF16)
    weight_ac = jnp.concatenate([weight(0, 0), weight(0, 2)], axis=0)
    messages = dot(weight_ac, hidden).astype(BF16)
    atom_col = lane_atom(iota((LANES, 2 * rim), 0), fan, tiles).astype(F32)
    for group in range(groups):
        own = messages[:, group * LANES : (group + 1) * LANES]
        own0[group] = own
        border_row = border_of(group)
        faces0[group, :, 0 : 2 * rim] = dot(own, one_hot(atom_col == border_row)).astype(BF16)

    row = iota((LANES + 2 * rim, 1), 0)
    names = jnp.where(
        row < LANES,
        lane_atom(row, fan, tiles),
        jnp.where(row < LANES + rim, row + rim, row - rim),
    ).astype(F32)
    upper_lane = iota((2 * width, 2 * rim), 1) < rim
    radial_ac = jnp.concatenate([radial_weight(0, 0), radial_weight(0, 2)], axis=0)

    def update(group, carry):
        up = lax.rem(group + 1, groups)
        low = lax.rem(group + groups - 1, groups)
        ghosts = jnp.where(
            upper_lane,
            faces0[up, :, 0 : 2 * rim].astype(F32),
            faces0[low, :, 0 : 2 * rim].astype(F32),
        ).astype(BF16)
        table = jnp.concatenate([own0[group], ghosts], axis=1)
        halves = edge_rows(group)
        step = fan // 2
        acc = jnp.zeros((width, LANES), F32)
        acc_vec = [jnp.zeros((width, LANES), F32) for _ in range(3)]
        for c in range(2):
            rows = halves[c]
            vec = [rows[x * step : (x + 1) * step] for x in range(3)]
            nbr = rows[4 * step : 5 * step]
            length_sq = vec[0] * vec[0] + vec[1] * vec[1] + vec[2] * vec[2]
            length = jnp.sqrt(length_sq) + rows[3 * step : 4 * step]
            env = (1.0 - length * length / 36.0) ** 2
            for pair in range(step // 2):
                ks = (2 * pair, 2 * pair + 1)
                picked = jnp.concatenate([one_hot(names == nbr[k : k + 1]) for k in ks], axis=1)
                basis = jnp.concatenate(
                    [basis_of(length[k : k + 1], env[k : k + 1]) for k in ks], axis=1
                )
                prod = dot(table, picked) * dot(radial_ac, basis)
                for i, k in enumerate(ks):
                    block = prod[:, i * LANES : (i + 1) * LANES]
                    acc = acc + block[:width]
                    for x in range(3):
                        acc_vec[x] = acc_vec[x] + block[width:] * vec[x][k : k + 1]
        lanes = pl.ds(pl.multiple_of(group * LANES, LANES), LANES)
        state1[0:width, lanes] = (state0[:, lanes].astype(F32) + acc / root_fan).astype(BF16)
        for x in range(3):
            state1[(x + 1) * width : (x + 2) * width, lanes] = (acc_vec[x] / root_fan).astype(BF16)
        return carry

    lax.fori_loop(0, groups, update, 0)

    hidden = silu(dot_tn(w_in[1], state1[0:width, :]) + columns[:, 1:2]).astype(BF16)
    for p in range(3):
        table1[p * width : (p + 1) * width, :] = dot(weight(1, p), hidden).astype(BF16)
    table1[3 * width :, :] = state1[width:, :]

    received = groups * cap
    edges = received * fan
    send_rows = jnp.concatenate(
        [data(g, 0, slice(rest_at, rest_at + 8)).astype(F32)[4:5] for g in range(groups)], axis=0
    )

    def picks(lane_count, per_group):
        lane = iota((LANES, lane_count), 1)
        wanted = me * cap + lane % cap
        spread = dot(send_rows.astype(BF16), one_hot(iota((LANES, lane_count), 0) == wanted))
        lane = iota((groups, lane_count), 1)
        spread = jnp.where(lane // per_group == iota((groups, lane_count), 0), spread, 0.0)
        return jnp.sum(spread, axis=0, keepdims=True)

    per_group = fan * cap
    pick_edges = picks(edges, per_group)
    pick_atoms = picks(received, cap)
    atom_rows = lane_atom(iota((LANES, per_group), 0), fan, tiles).astype(F32)
    chosen = []
    for group in range(groups):
        rows = jnp.concatenate([data(group, c, slice(edge_at, rest_at)) for c in range(2)], axis=0)
        want = pick_edges[:, group * per_group : (group + 1) * per_group]
        chosen.append(dot(rows, one_hot(atom_rows == want)))
    chosen = jnp.concatenate(chosen, axis=1)
    step = fan // 2
    row = iota((2 * n_edge, edges), 0)
    slot_k = (row // n_edge) * step + row % step
    lane_k = (iota((2 * n_edge, edges), 1) % per_group) // cap
    chosen = jnp.where(slot_k == lane_k, chosen, 0.0)
    chosen = jnp.sum(chosen.reshape(2 * 5, step, edges), axis=1)
    chosen = chosen[0:5] + chosen[5:10]
    vec = [chosen[x : x + 1] for x in range(3)]
    nbr = chosen[4:5]
    length = jnp.sqrt(vec[0] * vec[0] + vec[1] * vec[1] + vec[2] * vec[2]) + chosen[3:4]
    basis = basis_of(length, (1.0 - length * length / 36.0) ** 2)

    nbr = nbr.astype(jnp.int32)
    home = iota((1, edges), 1) // per_group
    is_low = (nbr >= LANES) & (nbr < LANES + rim)
    is_up = nbr >= LANES + rim
    owner = jnp.where(
        is_low, (home + groups - 1) % groups, jnp.where(is_up, (home + 1) % groups, home)
    )
    entry = owner * 2 * rim + jnp.where(is_low, nbr - (LANES - rim), nbr - (LANES + rim))
    entry = jnp.where(is_low | is_up, entry, -1)
    border_all = jnp.concatenate(
        [border_of(g) for g in range(groups)], axis=1
    )
    border_all = jnp.broadcast_to(border_all, (16, groups * 2 * rim)).astype(BF16)
    seen = dot(border_all, one_hot(iota((groups * 2 * rim, edges), 0) == entry))[0:1]
    target = owner * LANES + jnp.where(entry < 0, nbr, seen.astype(jnp.int32))
    column = iota((every, 1), 0)
    column_name = (column // LANES) * LANES + lane_atom(column % LANES, fan, tiles)
    rows = dot(table1[...], one_hot(column_name == target))
    radial_abc = jnp.concatenate([radial_weight(1, p) for p in range(3)], axis=0)
    filters = dot(radial_abc, basis)
    gate = rows[width : 2 * width] * filters[width : 2 * width]
    along = rows[2 * width : 3 * width] * filters[2 * width :]
    parts = [rows[:width] * filters[:width]]
    for x in range(3):
        parts.append(rows[(3 + x) * width : (4 + x) * width] * gate + along * vec[x])
    parts = jnp.concatenate(parts, axis=0).astype(BF16)
    edge = iota((edges, received), 0)
    slot = (edge // per_group) * cap + edge % cap
    delta = dot(parts, one_hot(slot == iota((edges, received), 1)))
    wanted = (iota((1, received), 1) // cap) * LANES + pick_atoms.astype(jnp.int32)
    chosen_atoms = one_hot(column_name == wanted)
    final = (dot(state1[...], chosen_atoms) + delta / root_fan).astype(BF16).astype(F32)

    pos_rows = jnp.concatenate(
        [data(g, 0, slice(rest_at, rest_at + 8)) for g in range(groups)], axis=1
    )
    pos = dot(pos_rows, chosen_atoms) - 1.875
    pos_cols = jnp.concatenate(
        [
            jnp.concatenate([pos, jnp.zeros((8, LANES - received), F32)], axis=1),
            jnp.zeros((LANES - 8, LANES), F32),
        ],
        axis=0,
    ).T
    list_len = width
    list_at = layers + 2
    counts = []
    for block in range(n_blocks):
        live = iota((1, list_len), 1).astype(F32) < small_rows[list_at + n_blocks : list_at + n_blocks + 1, block : block + 1]
        named = jnp.where(live, small_rows[list_at + block : list_at + block + 1], -1.0)
        hits = jnp.where(iota((received, list_len), 0).astype(F32) == named, 1.0, 0.0)
        counts.append(
            jnp.broadcast_to(jnp.sum(hits, axis=1, keepdims=True), (received, PB))
        )
    counts = jnp.concatenate(counts, axis=1)
    probes = n_blocks * PB
    number = me * probes + iota((1, probes), 1)
    grid = [
        (n % 16).astype(F32) * 0.25 - 1.875 for n in (number, number // 16, number // 256)
    ]
    dist_sq = jnp.zeros((received, probes), F32)
    for x in range(3):
        dist_sq = dist_sq + (grid[x] - pos_cols[0:received, x : x + 1]) ** 2
    dist = jnp.sqrt(dist_sq)
    envelope = (1.0 - dist_sq / 64.0) ** 2 * counts
    basis = jnp.concatenate(
        [
            (jnp.exp(-2.0 * (dist - r * (7.0 / (n_basis - 1))) ** 2) * envelope).astype(BF16)
            for r in range(n_basis)
        ],
        axis=0,
    )
    terms_shape = (2 * n_basis, n_basis * received)
    probe_weight = radial_all[:, 3 * layers * n_basis :]
    w_scalar, w_vector = (
        dot(probe_weight, one_hot(iota(terms_shape, 1) // received * 2 + p == iota(terms_shape, 0)))
        for p in range(2)
    )
    along = final[width : 2 * width] * pos[0:1]
    for x in range(1, 3):
        along = along + final[(x + 1) * width : (x + 2) * width] * pos[x : x + 1]
    def repeat(value):
        return jnp.concatenate([value] * n_basis, axis=1)
    terms = [w_scalar * repeat(final[:width]) - w_vector * repeat(along)]
    for x in range(3):
        terms.append(w_vector * repeat(final[(x + 1) * width : (x + 2) * width]))
    sums = dot(jnp.concatenate(terms, axis=0).astype(BF16), basis)
    charges = sums[:width]
    for x in range(3):
        charges = charges + grid[x] * sums[(x + 1) * width : (x + 2) * width]
    mixed = dot_tn(w_mix[...], charges.astype(BF16)) + columns[:, layers : layers + 1]
    density[...] = jnp.sum(silu(mixed) * columns[:, layers + 1 : layers + 2], axis=0, keepdims=True)


def few_groups(
    atom_s, atom_pos, edge_vec, edge_nbr, border_index, send_index, probe_list, probe_count,
    w_in, b_in, w_msg, w_rad, w_probe, w_mix, b_mix, w_out,
):
    atoms, half = atom_s.shape
    groups = lax.axis_size("brick") * lax.axis_size("probe")
    fan = edge_nbr.shape[0] // atoms
    rim = border_index.shape[0] // 2
    n_basis = w_rad.shape[1]
    cap = send_index.shape[1] // groups
    width = 2 * half
    every = groups * LANES
    data, weights, small = pack(
        groups, atom_s, atom_pos, edge_vec, edge_nbr, border_index, send_index, w_msg, w_rad, w_probe,
        b_in, b_mix, w_out, probe_list, probe_count,
    )
    data = lax.all_to_all(data, ("brick", "probe"), split_axis=0, concat_axis=0, tiled=True)
    other = lax.ppermute(weights, "chan", [(0, 1), (1, 0)])
    data = lax.all_gather(data, "chan")
    n_probes = probe_list.shape[0] * PB
    density = pl.pallas_call(
        functools.partial(density_kernel, (groups, fan, rim, half, n_basis, cap, probe_list.shape[0])),
        out_shape=jax.ShapeDtypeStruct((1, n_probes), F32),
                scratch_shapes=[
            pltpu.VMEM((width, every), BF16),
            pltpu.VMEM((groups, 2 * width, LANES), BF16),
            pltpu.VMEM((groups, 2 * width, LANES), BF16),
            pltpu.VMEM((4 * width, every), BF16),
            pltpu.VMEM((6 * width, every), BF16),
            pltpu.VMEM((2,) + weights.shape, BF16),
        ],
        compiler_params=pltpu.CompilerParams(vmem_limit_bytes=40 * 1024 * 1024),
        name="density",
    )(data, weights, other, small, w_in, w_mix)
    return density.reshape(n_probes)


def per_device(*args):
    if lax.axis_size("brick") * lax.axis_size("probe") <= FEW_GROUPS:
        return few_groups(*args)
    return many_groups(*args)


def extended(block, sides, width):
    for axis, dim in sides:
        count = lax.axis_size(axis)
        forward = [(i, i + 1) for i in range(count - 1)]
        forward.append((count - 1, 0))
        backward = [(target, source) for source, target in forward]
        low = lax.ppermute(
            lax.slice_in_dim(block, block.shape[dim] - width, None, axis=dim), axis, forward
        )
        high = lax.ppermute(lax.slice_in_dim(block, 0, width, axis=dim), axis, backward)
        block = jnp.concatenate([low, block, high], axis=dim)
    return block


def radial(distance, count, top):
    centers = jnp.arange(count).astype(jnp.float32) * (top / (count - 1))
    return jnp.exp(-2.0 * (distance[..., None] - centers) ** 2)


def make_block(
    recv_rows, recv_pos, w_scalar, w_vector, feat_width, group_no, n_blocks, list_len, n_basis
):

    def probe_block(block_in):
        block_no, listed, live_count = block_in
        index_row = (group_no * n_blocks + block_no) * PB + jnp.arange(PB, dtype=jnp.int32)
        grid_xyz = (
            jnp.stack([index_row % 16, index_row // 16 % 16, index_row // 256 % 16], axis=1).astype(
                jnp.float32
            )
            * 0.25
        )
        atom_xyz = recv_pos[:, listed]
        disp = grid_xyz[:, :, None] - atom_xyz[None]
        dist_sq = jnp.sum(disp * disp, axis=1)
        live = (jnp.arange(list_len, dtype=jnp.int32) < live_count).astype(jnp.float32)
        envelope = (1.0 - dist_sq / 64.0) ** 2 * live[None, :]
        basis = radial(jnp.sqrt(dist_sq), n_basis, 7.0) * envelope[:, :, None]
        scalar_w = basis.astype(jnp.bfloat16).reshape(PB, list_len * n_basis)
        vector_w = (
            (disp[:, :, :, None] * basis[:, None])
            .astype(jnp.bfloat16)
            .reshape(PB, 3 * list_len * n_basis)
        )
        atom_rows = recv_rows[listed]
        atom_terms = (atom_rows[:, None, :feat_width] * w_scalar[None]).reshape(
            list_len * n_basis, feat_width
        )
        vec_rows = jnp.transpose(
            atom_rows[:, feat_width:].reshape(list_len, 3, feat_width), (1, 0, 2)
        )
        vector_terms = (vec_rows[:, :, None, :] * w_vector[None, None]).reshape(
            3 * list_len * n_basis, feat_width
        )
        charge = jnp.dot(scalar_w, atom_terms, preferred_element_type=jnp.float32) + jnp.dot(
            vector_w, vector_terms, preferred_element_type=jnp.float32
        )
        return charge.astype(jnp.bfloat16)

    return probe_block


def many_groups(
    atom_s,
    atom_pos,
    edge_vec,
    edge_nbr,
    border_index,
    send_index,
    probe_list,
    probe_count,
    w_in,
    b_in,
    w_msg,
    w_rad,
    w_probe,
    w_mix,
    b_mix,
    w_out,
):
    atom_count, half_width = atom_s.shape
    n_layers = w_in.shape[0]
    width = w_in.shape[1]
    n_basis = w_rad.shape[1]
    fan_out = edge_nbr.shape[0] // atom_count
    root_fan = fan_out**0.5
    rim_rows = border_index.shape[0] // 2
    length = jnp.sqrt(jnp.sum(edge_vec * edge_vec, axis=0))
    edge_env = (1.0 - length * length / 36.0) ** 2
    edge_basis = (radial(length, n_basis, 6.0) * edge_env[:, None]).astype(jnp.bfloat16)
    edge_cols = jnp.transpose(edge_vec)
    scalars = atom_s
    vectors = jnp.zeros((atom_count, 3 * half_width), jnp.bfloat16)
    for layer_no in range(n_layers):
        full_rows = lax.all_gather(scalars, "chan", axis=1, tiled=True)
        in_weight = w_in[layer_no]
        in_bias = b_in[layer_no]
        msg_weight = w_msg[layer_no].reshape(width, 3 * half_width)
        rad_weight = w_rad[layer_no].reshape(n_basis, 3 * half_width)
        hidden_act = jax.nn.silu(
            jnp.dot(full_rows, in_weight, preferred_element_type=jnp.float32) + in_bias
        ).astype(jnp.bfloat16)
        inner_tab = jnp.concatenate(
            [
                jnp.dot(hidden_act, msg_weight, preferred_element_type=jnp.float32).astype(
                    jnp.bfloat16
                ),
                vectors,
            ],
            axis=1,
        )
        padded = extended(inner_tab[border_index], ((("brick", "probe"), 0),), rim_rows)
        lookup = jnp.concatenate([inner_tab, padded[:rim_rows], padded[3 * rim_rows :]], axis=0)
        neighbour_rows = lookup[edge_nbr]
        filters = jnp.dot(edge_basis, rad_weight, preferred_element_type=jnp.float32)
        weighted = neighbour_rows[:, : 3 * half_width] * filters
        neighbour_vec = neighbour_rows[:, 3 * half_width :].reshape(-1, 3, half_width)
        vector_gate = weighted[:, None, half_width : 2 * half_width]
        along_edge = weighted[:, None, 2 * half_width :]
        delta_vec = neighbour_vec * vector_gate + along_edge * edge_cols[:, :, None]
        delta_scalar = (
            weighted[:, :half_width].reshape(atom_count, fan_out, half_width).sum(axis=1) / root_fan
        )
        delta_vec = delta_vec.reshape(atom_count, fan_out, 3 * half_width).sum(axis=1) / root_fan
        scalars = (scalars + delta_scalar).astype(jnp.bfloat16)
        vectors = (vectors + delta_vec).astype(jnp.bfloat16)
    features = jnp.concatenate([scalars, vectors], axis=1)
    picks = send_index[0]
    n_brick = lax.axis_size("brick")
    n_probe = lax.axis_size("probe")
    n_groups = n_brick * n_probe
    slot_cap = picks.shape[0] // n_groups
    out_rows = features[picks]
    out_pos = jnp.transpose(atom_pos)[picks].astype(jnp.bfloat16)
    received = (
        lax.all_to_all(
            out_rows.reshape(n_groups, slot_cap, 4 * half_width),
            ("brick", "probe"),
            split_axis=0,
            concat_axis=0,
            tiled=True,
        ),
        lax.all_to_all(
            out_pos.reshape(n_groups, slot_cap, 3),
            ("brick", "probe"),
            split_axis=0,
            concat_axis=0,
            tiled=True,
        ),
    )
    recv_count = n_groups * slot_cap
    recv_rows = received[0].reshape(recv_count, 4 * half_width)
    recv_pos = jnp.transpose(received[1].reshape(recv_count, 3)).astype(jnp.float32)
    group_no = lax.axis_index("brick") * n_probe + lax.axis_index("probe")
    n_blocks, list_len = probe_list.shape
    probe_block = make_block(
        recv_rows,
        recv_pos,
        w_probe[:, 0, :],
        w_probe[:, 1, :],
        half_width,
        group_no,
        n_blocks,
        list_len,
        n_basis,
    )
    charges = lax.map(
        probe_block, (jnp.arange(n_blocks, dtype=jnp.int32), probe_list, probe_count)
    ).reshape(n_blocks * PB, half_width)
    mix_rows = lax.dynamic_slice_in_dim(w_mix, lax.axis_index("chan") * half_width, half_width, 0)
    mixed = lax.psum(jnp.dot(charges, mix_rows, preferred_element_type=jnp.float32), "chan")
    return jnp.sum(jax.nn.silu(mixed + b_mix) * w_out, axis=1)


def solution(mesh):
    in_specs = (
        P(("image", "brick", "probe"), "chan"),
        P(None, ("image", "brick", "probe")),
        P(None, ("image", "brick", "probe")),
        P(("image", "brick", "probe")),
        P(("image", "brick", "probe")),
        P(("image", "brick", "probe"), None),
        P(("image", "brick", "probe"), None),
        P(("image", "brick", "probe")),
        P(),
        P(),
        P(None, None, None, "chan"),
        P(None, None, None, "chan"),
        P(None, None, "chan"),
        P(),
        P(),
        P(),
    )
    out_specs = P(("image", "brick", "probe"))
    return jax.shard_map(
        per_device, mesh=mesh, in_specs=in_specs, out_specs=out_specs, check_vma=False
    )
```

```python
import functools

import jax
import jax.numpy as jnp
from jax import lax
from jax.experimental import pallas as pl
from jax.experimental.pallas import tpu as pltpu
from jax.sharding import PartitionSpec as P

PB = 128
LANES = 128
FEW_GROUPS = 8
SMALL = 16
F32 = jnp.float32
BF16 = jnp.bfloat16


def iota(shape, dim):
    return lax.broadcasted_iota(jnp.int32, shape, dim)


def dot(a, b):
    return jnp.dot(a, b, preferred_element_type=F32)


def dot_tn(a, b):
    return lax.dot_general(a, b, (((0,), (0,)), ((), ())), preferred_element_type=F32)


def one_hot(mask):
    return jnp.where(mask, 1.0, 0.0).astype(BF16)


def silu(x):
    return x / (1.0 + jnp.exp(-x))


def lane_atom(lane, fan, tiles):
    return (lane % tiles) * (LANES // fan) + lane // tiles


def pack_kernel(
    fan, atom_s, atom_pos, edge_vec, edge_nbr, border, send, w_msg, w_rad, w_probe,
    b_in, b_mix, w_out, probe_list, probe_count, data_out, weight_out, small_out, natural,
):
    half, atoms = atom_s.shape
    tiles = atoms * fan // LANES
    per_tile = LANES // fan
    part = lax.axis_index("chan")
    perm = one_hot(lane_atom(iota((atoms, LANES), 1), fan, tiles) == iota((atoms, LANES), 0))
    scalars = dot(atom_s[...], perm).astype(BF16)
    vec = edge_vec[...]
    vec_high = vec.astype(BF16).astype(F32)
    length = jnp.sqrt(jnp.sum(vec * vec, axis=0, keepdims=True))
    short = length - jnp.sqrt(jnp.sum(vec_high * vec_high, axis=0, keepdims=True))
    rows = jnp.concatenate([vec_high, short], axis=0)
    for tile in range(tiles):
        for comp in range(4):
            natural[comp * tiles + tile : comp * tiles + tile + 1, :] = rows[
                comp : comp + 1, tile * LANES : (tile + 1) * LANES
            ]
    natural[4 * tiles : 5 * tiles, :] = edge_nbr[...].astype(F32)
    natural[5 * tiles :, :] = jnp.zeros((LANES - 5 * tiles, LANES), F32)
    turned = natural[...].T
    lane = iota((fan, LANES), 1)
    sorted_rows = []
    for comp in range(5):
        rows = jnp.zeros((fan, LANES), F32)
        for a in range(per_tile):
            piece = turned[a * fan : (a + 1) * fan, :]
            shift = (a * tiles - comp * tiles) % LANES
            piece = pltpu.roll(piece, shift, 1) if shift else piece
            rows = jnp.where(lane // tiles == a, piece, rows)
        sorted_rows.append(jnp.where(part == 0, rows[: fan // 2], rows[fan // 2 :]))
    pos = dot(atom_pos[...].astype(BF16), perm)
    blank = jnp.zeros((1, LANES), F32)
    border_row = jnp.concatenate(
        [border[...].astype(F32), jnp.zeros((1, LANES - border.shape[1]), F32)], axis=1
    )
    send_row = jnp.concatenate(
        [send[...].astype(F32), jnp.zeros((1, LANES - send.shape[1]), F32)], axis=1
    )
    rest = jnp.concatenate([pos, border_row, send_row, blank, blank, blank], axis=0)
    others = jnp.concatenate(sorted_rows + [rest], axis=0).astype(BF16)
    for copy in range(data_out.shape[0]):
        data_out[copy, 0:half, :] = scalars
        data_out[copy, half:, :] = others
    at = 0
    for piece in (b_in, b_mix, w_out, probe_list, probe_count):
        rows, cols = piece.shape
        small_out[at : at + rows, 0:cols] = piece[...].astype(F32)
        at += rows
    probe_rows = [w_probe[r].astype(F32) for r in range(w_probe.shape[0])]
    radial = jnp.concatenate([w_rad[...].astype(F32)] + probe_rows, axis=0).T.astype(BF16)
    weight_out[: w_msg.shape[0], :] = w_msg[...]
    weight_out[w_msg.shape[0] :, :] = radial


def pack(
    copies, atom_s, atom_pos, edge_vec, edge_nbr, border_index, send_index, w_msg, w_rad, w_probe,
    b_in, b_mix, w_out, probe_list, probe_count,
):
    atoms, half = atom_s.shape
    fan = edge_nbr.shape[0] // atoms
    return pl.pallas_call(
        functools.partial(pack_kernel, fan),
        out_shape=(
            jax.ShapeDtypeStruct((copies, half + 5 * fan // 2 + 8, LANES), BF16),
            jax.ShapeDtypeStruct((w_msg.size // LANES + half, LANES), BF16),
            jax.ShapeDtypeStruct((SMALL, LANES), F32),
        ),
        scratch_shapes=[pltpu.VMEM((LANES, LANES), F32)],
        name="pack",
    )(
        atom_s.T,
        atom_pos,
        edge_vec,
        edge_nbr.reshape(-1, LANES),
        border_index.reshape(1, -1),
        send_index,
        jnp.transpose(w_msg, (0, 2, 3, 1)).reshape(-1, LANES),
        jnp.transpose(w_rad, (0, 2, 1, 3)).reshape(-1, half),
        w_probe,
        b_in,
        b_mix.reshape(1, -1),
        w_out.reshape(1, -1),
        probe_list,
        probe_count.reshape(1, -1),
    )


def density_kernel(
    sizes,
    data_mine,
    data_beside,
    data_other,
    data_across,
    weights_mine,
    weights_other,
    small,
    w_in,
    w_mix,
    density,
    state0,
    own0,
    faces0,
    state1,
    table1,
    weights,
    data_all,
):
    groups, fan, rim, half, n_basis, cap, n_blocks = sizes
    layers = w_in.shape[0]
    width = 2 * half
    tiles = LANES * fan // LANES
    root_fan = fan**0.5
    me = lax.axis_index("brick") * lax.axis_size("probe") + lax.axis_index("probe")
    part = lax.axis_index("chan")
    weights[part] = weights_mine[...]
    weights[1 - part] = weights_other[...]
    column = lax.axis_index("probe")
    data_all[part, column] = data_mine[...]
    data_all[part, 1 - column] = data_beside[...]
    data_all[1 - part, column] = data_other[...]
    data_all[1 - part, 1 - column] = data_across[...]
    every = groups * LANES
    edge_at = half
    n_edge = 5 * fan // 2
    rest_at = half + n_edge

    def data(group, c, rows):
        return data_all[c, lax.rem(group, 2), group // 2, rows, :]

    small_rows = small[...]
    columns = small_rows.T

    def weight(layer, p):
        at = (layer * 3 + p) * half
        return jnp.concatenate([weights[c, at : at + half, :] for c in range(2)], axis=0)

    radial_at = weights.shape[1] - half
    radial_all = jnp.concatenate([weights[c, radial_at:, :] for c in range(2)], axis=0)

    def radial_weight(layer, p):
        at = (layer * 3 + p) * n_basis
        return radial_all[:, at : at + n_basis]

    def edge_rows(group):
        return [data(group, c, slice(edge_at, rest_at)).astype(F32) for c in range(2)]

    def border_of(group):
        return data(group, 0, slice(rest_at, rest_at + 8)).astype(F32)[3:4, 0 : 2 * rim]

    def basis_of(dist_row, env_row):
        centers = iota((n_basis, 1), 0).astype(F32) * (6.0 / (n_basis - 1))
        return (jnp.exp(-2.0 * (dist_row - centers) ** 2) * env_row).astype(BF16)

    for group in range(groups):
        for c in range(2):
            state0[c * half : (c + 1) * half, group * LANES : (group + 1) * LANES] = data(
                group, c, slice(0, half)
            )
    hidden = silu(dot_tn(w_in[0], state0[...]) + columns[:, 0:1]).astype(BF16)
    weight_ac = jnp.concatenate([weight(0, 0), weight(0, 2)], axis=0)
    messages = dot(weight_ac, hidden).astype(BF16)
    atom_col = lane_atom(iota((LANES, 2 * rim), 0), fan, tiles).astype(F32)
    for group in range(groups):
        own = messages[:, group * LANES : (group + 1) * LANES]
        own0[group] = own
        border_row = border_of(group)
        faces0[group, :, 0 : 2 * rim] = dot(own, one_hot(atom_col == border_row)).astype(BF16)

    row = iota((LANES + 2 * rim, 1), 0)
    names = jnp.where(
        row < LANES,
        lane_atom(row, fan, tiles),
        jnp.where(row < LANES + rim, row + rim, row - rim),
    ).astype(F32)
    upper_lane = iota((2 * width, 2 * rim), 1) < rim
    radial_ac = jnp.concatenate([radial_weight(0, 0), radial_weight(0, 2)], axis=0)

    def update(group, carry):
        up = lax.rem(group + 1, groups)
        low = lax.rem(group + groups - 1, groups)
        ghosts = jnp.where(
            upper_lane,
            faces0[up, :, 0 : 2 * rim].astype(F32),
            faces0[low, :, 0 : 2 * rim].astype(F32),
        ).astype(BF16)
        table = jnp.concatenate([own0[group], ghosts], axis=1)
        halves = edge_rows(group)
        step = fan // 2
        acc = jnp.zeros((width, LANES), F32)
        acc_vec = [jnp.zeros((width, LANES), F32) for _ in range(3)]
        for c in range(2):
            rows = halves[c]
            vec = [rows[x * step : (x + 1) * step] for x in range(3)]
            nbr = rows[4 * step : 5 * step]
            length_sq = vec[0] * vec[0] + vec[1] * vec[1] + vec[2] * vec[2]
            length = jnp.sqrt(length_sq) + rows[3 * step : 4 * step]
            env = (1.0 - length * length / 36.0) ** 2
            for pair in range(step // 2):
                ks = (2 * pair, 2 * pair + 1)
                picked = jnp.concatenate([one_hot(names == nbr[k : k + 1]) for k in ks], axis=1)
                basis = jnp.concatenate(
                    [basis_of(length[k : k + 1], env[k : k + 1]) for k in ks], axis=1
                )
                prod = dot(table, picked) * dot(radial_ac, basis)
                for i, k in enumerate(ks):
                    block = prod[:, i * LANES : (i + 1) * LANES]
                    acc = acc + block[:width]
                    for x in range(3):
                        acc_vec[x] = acc_vec[x] + block[width:] * vec[x][k : k + 1]
        lanes = pl.ds(pl.multiple_of(group * LANES, LANES), LANES)
        state1[0:width, lanes] = (state0[:, lanes].astype(F32) + acc / root_fan).astype(BF16)
        for x in range(3):
            state1[(x + 1) * width : (x + 2) * width, lanes] = (acc_vec[x] / root_fan).astype(BF16)
        return carry

    lax.fori_loop(0, groups, update, 0)

    hidden = silu(dot_tn(w_in[1], state1[0:width, :]) + columns[:, 1:2]).astype(BF16)
    for p in range(3):
        table1[p * width : (p + 1) * width, :] = dot(weight(1, p), hidden).astype(BF16)
    table1[3 * width :, :] = state1[width:, :]

    received = groups * cap
    edges = received * fan
    send_rows = jnp.concatenate(
        [data(g, 0, slice(rest_at, rest_at + 8)).astype(F32)[4:5] for g in range(groups)], axis=0
    )

    def picks(lane_count, per_group):
        lane = iota((LANES, lane_count), 1)
        wanted = me * cap + lane % cap
        spread = dot(send_rows.astype(BF16), one_hot(iota((LANES, lane_count), 0) == wanted))
        lane = iota((groups, lane_count), 1)
        spread = jnp.where(lane // per_group == iota((groups, lane_count), 0), spread, 0.0)
        return jnp.sum(spread, axis=0, keepdims=True)

    per_group = fan * cap
    pick_edges = picks(edges, per_group)
    pick_atoms = picks(received, cap)
    atom_rows = lane_atom(iota((LANES, per_group), 0), fan, tiles).astype(F32)
    chosen = []
    for group in range(groups):
        rows = jnp.concatenate([data(group, c, slice(edge_at, rest_at)) for c in range(2)], axis=0)
        want = pick_edges[:, group * per_group : (group + 1) * per_group]
        chosen.append(dot(rows, one_hot(atom_rows == want)))
    chosen = jnp.concatenate(chosen, axis=1)
    step = fan // 2
    row = iota((2 * n_edge, edges), 0)
    slot_k = (row // n_edge) * step + row % step
    lane_k = (iota((2 * n_edge, edges), 1) % per_group) // cap
    chosen = jnp.where(slot_k == lane_k, chosen, 0.0)
    chosen = jnp.sum(chosen.reshape(2 * 5, step, edges), axis=1)
    chosen = chosen[0:5] + chosen[5:10]
    vec = [chosen[x : x + 1] for x in range(3)]
    nbr = chosen[4:5]
    length = jnp.sqrt(vec[0] * vec[0] + vec[1] * vec[1] + vec[2] * vec[2]) + chosen[3:4]
    basis = basis_of(length, (1.0 - length * length / 36.0) ** 2)

    nbr = nbr.astype(jnp.int32)
    home = iota((1, edges), 1) // per_group
    is_low = (nbr >= LANES) & (nbr < LANES + rim)
    is_up = nbr >= LANES + rim
    owner = jnp.where(
        is_low, (home + groups - 1) % groups, jnp.where(is_up, (home + 1) % groups, home)
    )
    entry = owner * 2 * rim + jnp.where(is_low, nbr - (LANES - rim), nbr - (LANES + rim))
    entry = jnp.where(is_low | is_up, entry, -1)
    border_all = jnp.concatenate(
        [border_of(g) for g in range(groups)], axis=1
    )
    border_all = jnp.broadcast_to(border_all, (16, groups * 2 * rim)).astype(BF16)
    seen = dot(border_all, one_hot(iota((groups * 2 * rim, edges), 0) == entry))[0:1]
    target = owner * LANES + jnp.where(entry < 0, nbr, seen.astype(jnp.int32))
    row = iota((every, 1), 0)
    column_name = (row // LANES) * LANES + lane_atom(row % LANES, fan, tiles)
    rows = dot(table1[...], one_hot(column_name == target))
    radial_abc = jnp.concatenate([radial_weight(1, p) for p in range(3)], axis=0)
    filters = dot(radial_abc, basis)
    gate = rows[width : 2 * width] * filters[width : 2 * width]
    along = rows[2 * width : 3 * width] * filters[2 * width :]
    parts = [rows[:width] * filters[:width]]
    for x in range(3):
        parts.append(rows[(3 + x) * width : (4 + x) * width] * gate + along * vec[x])
    parts = jnp.concatenate(parts, axis=0).astype(BF16)
    edge = iota((edges, received), 0)
    slot = (edge // per_group) * cap + edge % cap
    delta = dot(parts, one_hot(slot == iota((edges, received), 1)))
    wanted = (iota((1, received), 1) // cap) * LANES + pick_atoms.astype(jnp.int32)
    chosen_atoms = one_hot(column_name == wanted)
    final = (dot(state1[...], chosen_atoms) + delta / root_fan).astype(BF16).astype(F32)

    pos_rows = jnp.concatenate(
        [data(g, 0, slice(rest_at, rest_at + 8)) for g in range(groups)], axis=1
    )
    pos = dot(pos_rows, chosen_atoms) - 1.875
    pos_cols = jnp.concatenate(
        [
            jnp.concatenate([pos, jnp.zeros((8, LANES - received), F32)], axis=1),
            jnp.zeros((LANES - 8, LANES), F32),
        ],
        axis=0,
    ).T
    list_len = width
    list_at = layers + 2
    counts = []
    for block in range(n_blocks):
        live = iota((1, list_len), 1).astype(F32) < small_rows[list_at + n_blocks : list_at + n_blocks + 1, block : block + 1]
        named = jnp.where(live, small_rows[list_at + block : list_at + block + 1], -1.0)
        hits = jnp.where(iota((received, list_len), 0).astype(F32) == named, 1.0, 0.0)
        counts.append(
            jnp.broadcast_to(jnp.sum(hits, axis=1, keepdims=True), (received, PB))
        )
    counts = jnp.concatenate(counts, axis=1)
    probes = n_blocks * PB
    number = me * probes + iota((1, probes), 1)
    grid = [
        (n % 16).astype(F32) * 0.25 - 1.875 for n in (number, number // 16, number // 256)
    ]
    dist_sq = jnp.zeros((received, probes), F32)
    for x in range(3):
        dist_sq = dist_sq + (grid[x] - pos_cols[0:received, x : x + 1]) ** 2
    dist = jnp.sqrt(dist_sq)
    envelope = (1.0 - dist_sq / 64.0) ** 2 * counts
    basis = jnp.concatenate(
        [
            (jnp.exp(-2.0 * (dist - r * (7.0 / (n_basis - 1))) ** 2) * envelope).astype(BF16)
            for r in range(n_basis)
        ],
        axis=0,
    )
    terms_shape = (2 * n_basis, n_basis * received)
    probe_weight = radial_all[:, 3 * layers * n_basis :]
    w_scalar, w_vector = (
        dot(probe_weight, one_hot(iota(terms_shape, 1) // received * 2 + p == iota(terms_shape, 0)))
        for p in range(2)
    )
    along = final[width : 2 * width] * pos[0:1]
    for x in range(1, 3):
        along = along + final[(x + 1) * width : (x + 2) * width] * pos[x : x + 1]
    def repeat(value):
        return jnp.concatenate([value] * n_basis, axis=1)
    terms = [w_scalar * repeat(final[:width]) - w_vector * repeat(along)]
    for x in range(3):
        terms.append(w_vector * repeat(final[(x + 1) * width : (x + 2) * width]))
    sums = dot(jnp.concatenate(terms, axis=0).astype(BF16), basis)
    charges = sums[:width]
    for x in range(3):
        charges = charges + grid[x] * sums[(x + 1) * width : (x + 2) * width]
    mixed = dot_tn(w_mix[...], charges.astype(BF16)) + columns[:, layers : layers + 1]
    density[...] = jnp.sum(silu(mixed) * columns[:, layers + 1 : layers + 2], axis=0, keepdims=True)


def few_groups(
    atom_s, atom_pos, edge_vec, edge_nbr, border_index, send_index, probe_list, probe_count,
    w_in, b_in, w_msg, w_rad, w_probe, w_mix, b_mix, w_out,
):
    atoms, half = atom_s.shape
    groups = lax.axis_size("brick") * lax.axis_size("probe")
    fan = edge_nbr.shape[0] // atoms
    rim = border_index.shape[0] // 2
    n_basis = w_rad.shape[1]
    cap = send_index.shape[1] // groups
    width = 2 * half
    every = groups * LANES
    bricks = lax.axis_size("brick")
    data, weights, small = pack(
        bricks, atom_s, atom_pos, edge_vec, edge_nbr, border_index, send_index, w_msg, w_rad, w_probe,
        b_in, b_mix, w_out, probe_list, probe_count,
    )
    swap = [(0, 1), (1, 0)]
    mine = lax.all_to_all(data, "brick", split_axis=0, concat_axis=0, tiled=True)
    beside = lax.ppermute(mine, "probe", swap)
    other = lax.ppermute(mine, "chan", swap)
    across = lax.ppermute(beside, "chan", swap)
    weights_other = lax.ppermute(weights, "chan", swap)
    n_probes = probe_list.shape[0] * PB
    density = pl.pallas_call(
        functools.partial(density_kernel, (groups, fan, rim, half, n_basis, cap, probe_list.shape[0])),
        out_shape=jax.ShapeDtypeStruct((1, n_probes), F32),
                scratch_shapes=[
            pltpu.VMEM((width, every), BF16),
            pltpu.VMEM((groups, 2 * width, LANES), BF16),
            pltpu.VMEM((groups, 2 * width, LANES), BF16),
            pltpu.VMEM((4 * width, every), BF16),
            pltpu.VMEM((6 * width, every), BF16),
            pltpu.VMEM((2,) + weights.shape, BF16),
            pltpu.VMEM((2, 2) + data.shape, BF16),
        ],
        compiler_params=pltpu.CompilerParams(vmem_limit_bytes=40 * 1024 * 1024),
        name="density",
    )(mine, beside, other, across, weights, weights_other, small, w_in, w_mix)
    return density.reshape(n_probes)


def per_device(*args):
    columns = lax.axis_size("probe")
    if columns == 2 and lax.axis_size("brick") * columns <= FEW_GROUPS:
        return few_groups(*args)
    return many_groups(*args)


def extended(block, sides, width):
    for axis, dim in sides:
        count = lax.axis_size(axis)
        forward = [(i, i + 1) for i in range(count - 1)]
        forward.append((count - 1, 0))
        backward = [(target, source) for source, target in forward]
        low = lax.ppermute(
            lax.slice_in_dim(block, block.shape[dim] - width, None, axis=dim), axis, forward
        )
        high = lax.ppermute(lax.slice_in_dim(block, 0, width, axis=dim), axis, backward)
        block = jnp.concatenate([low, block, high], axis=dim)
    return block


def radial(distance, count, top):
    centers = jnp.arange(count).astype(jnp.float32) * (top / (count - 1))
    return jnp.exp(-2.0 * (distance[..., None] - centers) ** 2)


def make_block(
    recv_rows, recv_pos, w_scalar, w_vector, feat_width, group_no, n_blocks, list_len, n_basis
):

    def probe_block(block_in):
        block_no, listed, live_count = block_in
        index_row = (group_no * n_blocks + block_no) * PB + jnp.arange(PB, dtype=jnp.int32)
        grid_xyz = (
            jnp.stack([index_row % 16, index_row // 16 % 16, index_row // 256 % 16], axis=1).astype(
                jnp.float32
            )
            * 0.25
        )
        atom_xyz = recv_pos[:, listed]
        disp = grid_xyz[:, :, None] - atom_xyz[None]
        dist_sq = jnp.sum(disp * disp, axis=1)
        live = (jnp.arange(list_len, dtype=jnp.int32) < live_count).astype(jnp.float32)
        envelope = (1.0 - dist_sq / 64.0) ** 2 * live[None, :]
        basis = radial(jnp.sqrt(dist_sq), n_basis, 7.0) * envelope[:, :, None]
        scalar_w = basis.astype(jnp.bfloat16).reshape(PB, list_len * n_basis)
        vector_w = (
            (disp[:, :, :, None] * basis[:, None])
            .astype(jnp.bfloat16)
            .reshape(PB, 3 * list_len * n_basis)
        )
        atom_rows = recv_rows[listed]
        atom_terms = (atom_rows[:, None, :feat_width] * w_scalar[None]).reshape(
            list_len * n_basis, feat_width
        )
        vec_rows = jnp.transpose(
            atom_rows[:, feat_width:].reshape(list_len, 3, feat_width), (1, 0, 2)
        )
        vector_terms = (vec_rows[:, :, None, :] * w_vector[None, None]).reshape(
            3 * list_len * n_basis, feat_width
        )
        charge = jnp.dot(scalar_w, atom_terms, preferred_element_type=jnp.float32) + jnp.dot(
            vector_w, vector_terms, preferred_element_type=jnp.float32
        )
        return charge.astype(jnp.bfloat16)

    return probe_block


def many_groups(
    atom_s,
    atom_pos,
    edge_vec,
    edge_nbr,
    border_index,
    send_index,
    probe_list,
    probe_count,
    w_in,
    b_in,
    w_msg,
    w_rad,
    w_probe,
    w_mix,
    b_mix,
    w_out,
):
    atom_count, half_width = atom_s.shape
    n_layers = w_in.shape[0]
    width = w_in.shape[1]
    n_basis = w_rad.shape[1]
    fan_out = edge_nbr.shape[0] // atom_count
    root_fan = fan_out**0.5
    rim_rows = border_index.shape[0] // 2
    length = jnp.sqrt(jnp.sum(edge_vec * edge_vec, axis=0))
    edge_env = (1.0 - length * length / 36.0) ** 2
    edge_basis = (radial(length, n_basis, 6.0) * edge_env[:, None]).astype(jnp.bfloat16)
    edge_cols = jnp.transpose(edge_vec)
    scalars = atom_s
    vectors = jnp.zeros((atom_count, 3 * half_width), jnp.bfloat16)
    for layer_no in range(n_layers):
        full_rows = lax.all_gather(scalars, "chan", axis=1, tiled=True)
        in_weight = w_in[layer_no]
        in_bias = b_in[layer_no]
        msg_weight = w_msg[layer_no].reshape(width, 3 * half_width)
        rad_weight = w_rad[layer_no].reshape(n_basis, 3 * half_width)
        hidden_act = jax.nn.silu(
            jnp.dot(full_rows, in_weight, preferred_element_type=jnp.float32) + in_bias
        ).astype(jnp.bfloat16)
        inner_tab = jnp.concatenate(
            [
                jnp.dot(hidden_act, msg_weight, preferred_element_type=jnp.float32).astype(
                    jnp.bfloat16
                ),
                vectors,
            ],
            axis=1,
        )
        padded = extended(inner_tab[border_index], ((("brick", "probe"), 0),), rim_rows)
        lookup = jnp.concatenate([inner_tab, padded[:rim_rows], padded[3 * rim_rows :]], axis=0)
        neighbour_rows = lookup[edge_nbr]
        filters = jnp.dot(edge_basis, rad_weight, preferred_element_type=jnp.float32)
        weighted = neighbour_rows[:, : 3 * half_width] * filters
        neighbour_vec = neighbour_rows[:, 3 * half_width :].reshape(-1, 3, half_width)
        vector_gate = weighted[:, None, half_width : 2 * half_width]
        along_edge = weighted[:, None, 2 * half_width :]
        delta_vec = neighbour_vec * vector_gate + along_edge * edge_cols[:, :, None]
        delta_scalar = (
            weighted[:, :half_width].reshape(atom_count, fan_out, half_width).sum(axis=1) / root_fan
        )
        delta_vec = delta_vec.reshape(atom_count, fan_out, 3 * half_width).sum(axis=1) / root_fan
        scalars = (scalars + delta_scalar).astype(jnp.bfloat16)
        vectors = (vectors + delta_vec).astype(jnp.bfloat16)
    features = jnp.concatenate([scalars, vectors], axis=1)
    picks = send_index[0]
    n_brick = lax.axis_size("brick")
    n_probe = lax.axis_size("probe")
    n_groups = n_brick * n_probe
    slot_cap = picks.shape[0] // n_groups
    out_rows = features[picks]
    out_pos = jnp.transpose(atom_pos)[picks].astype(jnp.bfloat16)
    received = (
        lax.all_to_all(
            out_rows.reshape(n_groups, slot_cap, 4 * half_width),
            ("brick", "probe"),
            split_axis=0,
            concat_axis=0,
            tiled=True,
        ),
        lax.all_to_all(
            out_pos.reshape(n_groups, slot_cap, 3),
            ("brick", "probe"),
            split_axis=0,
            concat_axis=0,
            tiled=True,
        ),
    )
    recv_count = n_groups * slot_cap
    recv_rows = received[0].reshape(recv_count, 4 * half_width)
    recv_pos = jnp.transpose(received[1].reshape(recv_count, 3)).astype(jnp.float32)
    group_no = lax.axis_index("brick") * n_probe + lax.axis_index("probe")
    n_blocks, list_len = probe_list.shape
    probe_block = make_block(
        recv_rows,
        recv_pos,
        w_probe[:, 0, :],
        w_probe[:, 1, :],
        half_width,
        group_no,
        n_blocks,
        list_len,
        n_basis,
    )
    charges = lax.map(
        probe_block, (jnp.arange(n_blocks, dtype=jnp.int32), probe_list, probe_count)
    ).reshape(n_blocks * PB, half_width)
    mix_rows = lax.dynamic_slice_in_dim(w_mix, lax.axis_index("chan") * half_width, half_width, 0)
    mixed = lax.psum(jnp.dot(charges, mix_rows, preferred_element_type=jnp.float32), "chan")
    return jnp.sum(jax.nn.silu(mixed + b_mix) * w_out, axis=1)


def solution(mesh):
    in_specs = (
        P(("image", "brick", "probe"), "chan"),
        P(None, ("image", "brick", "probe")),
        P(None, ("image", "brick", "probe")),
        P(("image", "brick", "probe")),
        P(("image", "brick", "probe")),
        P(("image", "brick", "probe"), None),
        P(("image", "brick", "probe"), None),
        P(("image", "brick", "probe")),
        P(),
        P(),
        P(None, None, None, "chan"),
        P(None, None, None, "chan"),
        P(None, None, "chan"),
        P(),
        P(),
        P(),
    )
    out_specs = P(("image", "brick", "probe"))
    return jax.shard_map(
        per_device, mesh=mesh, in_specs=in_specs, out_specs=out_specs, check_vma=False
    )
```

```python
import functools

import jax
import jax.numpy as jnp
from jax import lax
from jax.experimental import pallas as pl
from jax.experimental.pallas import tpu as pltpu
from jax.sharding import PartitionSpec as P

PB = 128
LANES = 128
FEW_GROUPS = 8
SMALL = 16
F32 = jnp.float32
BF16 = jnp.bfloat16


def iota(shape, dim):
    return lax.broadcasted_iota(jnp.int32, shape, dim)


def dot(a, b):
    return jnp.dot(a, b, preferred_element_type=F32)


def dot_tn(a, b):
    return lax.dot_general(a, b, (((0,), (0,)), ((), ())), preferred_element_type=F32)


def one_hot(mask):
    return jnp.where(mask, 1.0, 0.0).astype(BF16)


def silu(x):
    return x / (1.0 + jnp.exp(-x))


def lane_atom(lane, fan, tiles):
    return (lane % tiles) * (LANES // fan) + lane // tiles


def pack_kernel(
    fan, atom_s, atom_pos, edge_vec, edge_nbr, border, send, w_msg, w_rad, w_probe,
    b_in, b_mix, w_out, probe_list, probe_count, data_out, weight_out, small_out, natural,
):
    half, atoms = atom_s.shape
    tiles = atoms * fan // LANES
    per_tile = LANES // fan
    part = lax.axis_index("chan")
    perm = one_hot(lane_atom(iota((atoms, LANES), 1), fan, tiles) == iota((atoms, LANES), 0))
    scalars = dot(atom_s[...], perm).astype(BF16)
    vec = edge_vec[...]
    vec_high = vec.astype(BF16).astype(F32)
    length = jnp.sqrt(jnp.sum(vec * vec, axis=0, keepdims=True))
    short = length - jnp.sqrt(jnp.sum(vec_high * vec_high, axis=0, keepdims=True))
    rows = jnp.concatenate([vec_high, short], axis=0)
    for tile in range(tiles):
        for comp in range(4):
            natural[comp * tiles + tile : comp * tiles + tile + 1, :] = rows[
                comp : comp + 1, tile * LANES : (tile + 1) * LANES
            ]
    natural[4 * tiles : 5 * tiles, :] = edge_nbr[...].astype(F32)
    natural[5 * tiles :, :] = jnp.zeros((LANES - 5 * tiles, LANES), F32)
    turned = natural[...].T
    lane = iota((fan, LANES), 1)
    sorted_rows = []
    for comp in range(5):
        rows = jnp.zeros((fan, LANES), F32)
        for a in range(per_tile):
            piece = turned[a * fan : (a + 1) * fan, :]
            shift = (a * tiles - comp * tiles) % LANES
            piece = pltpu.roll(piece, shift, 1) if shift else piece
            rows = jnp.where(lane // tiles == a, piece, rows)
        sorted_rows.append(jnp.where(part == 0, rows[: fan // 2], rows[fan // 2 :]))
    pos = dot(atom_pos[...].astype(BF16), perm)
    blank = jnp.zeros((1, LANES), F32)
    border_row = jnp.concatenate(
        [border[...].astype(F32), jnp.zeros((1, LANES - border.shape[1]), F32)], axis=1
    )
    send_row = jnp.concatenate(
        [send[...].astype(F32), jnp.zeros((1, LANES - send.shape[1]), F32)], axis=1
    )
    rest = jnp.concatenate([pos, border_row, send_row, blank, blank, blank], axis=0)
    others = jnp.concatenate(sorted_rows + [rest], axis=0).astype(BF16)
    data_out[0:half, :] = scalars
    data_out[half:, :] = others
    at = 0
    for piece in (b_in, b_mix, w_out, probe_list, probe_count):
        rows, cols = piece.shape
        small_out[at : at + rows, 0:cols] = piece[...].astype(F32)
        at += rows
    probe_rows = [w_probe[r].astype(F32) for r in range(w_probe.shape[0])]
    radial = jnp.concatenate([w_rad[...].astype(F32)] + probe_rows, axis=0).T.astype(BF16)
    weight_out[: w_msg.shape[0], :] = w_msg[...]
    weight_out[w_msg.shape[0] :, :] = radial


def pack(
    atom_s, atom_pos, edge_vec, edge_nbr, border_index, send_index, w_msg, w_rad, w_probe,
    b_in, b_mix, w_out, probe_list, probe_count,
):
    atoms, half = atom_s.shape
    fan = edge_nbr.shape[0] // atoms
    return pl.pallas_call(
        functools.partial(pack_kernel, fan),
        out_shape=(
            jax.ShapeDtypeStruct((half + 5 * fan // 2 + 8, LANES), BF16),
            jax.ShapeDtypeStruct((w_msg.size // LANES + half, LANES), BF16),
            jax.ShapeDtypeStruct((SMALL, LANES), F32),
        ),
        scratch_shapes=[pltpu.VMEM((LANES, LANES), F32)],
        name="pack",
    )(
        atom_s.T,
        atom_pos,
        edge_vec,
        edge_nbr.reshape(-1, LANES),
        border_index.reshape(1, -1),
        send_index,
        jnp.transpose(w_msg, (0, 2, 3, 1)).reshape(-1, LANES),
        jnp.transpose(w_rad, (0, 2, 1, 3)).reshape(-1, half),
        w_probe,
        b_in,
        b_mix.reshape(1, -1),
        w_out.reshape(1, -1),
        probe_list,
        probe_count.reshape(1, -1),
    )


def density_kernel(
    sizes,
    *refs,
):
    (weights_mine, weights_other, small, w_in, w_mix, density) = refs[-13:-7]
    (state0, own0, faces0, state1, table1, weights, data_all) = refs[-7:]
    blocks = refs[:-13]
    groups, fan, rim, half, n_basis, cap, n_blocks = sizes
    layers = w_in.shape[0]
    width = 2 * half
    tiles = LANES * fan // LANES
    root_fan = fan**0.5
    me = lax.axis_index("brick") * lax.axis_size("probe") + lax.axis_index("probe")
    part = lax.axis_index("chan")
    weights[part] = weights_mine[...]
    weights[1 - part] = weights_other[...]
    column = lax.axis_index("probe")
    brick = lax.axis_index("brick")
    bricks = data_all.shape[2]
    for far, core in enumerate((part, 1 - part)):
        for side, place in enumerate((column, 1 - column)):
            for shift in range(bricks):
                source = lax.rem(brick + bricks - shift, bricks)
                data_all[core, place, source] = blocks[(far * 2 + side) * bricks + shift][...]
    every = groups * LANES
    edge_at = half
    n_edge = 5 * fan // 2
    rest_at = half + n_edge

    def data(group, c, rows):
        return data_all[c, lax.rem(group, 2), group // 2, rows, :]

    small_rows = small[...]
    columns = small_rows.T

    def weight(layer, p):
        at = (layer * 3 + p) * half
        return jnp.concatenate([weights[c, at : at + half, :] for c in range(2)], axis=0)

    radial_at = weights.shape[1] - half
    radial_all = jnp.concatenate([weights[c, radial_at:, :] for c in range(2)], axis=0)

    def radial_weight(layer, p):
        at = (layer * 3 + p) * n_basis
        return radial_all[:, at : at + n_basis]

    def edge_rows(group):
        return [data(group, c, slice(edge_at, rest_at)).astype(F32) for c in range(2)]

    def border_of(group):
        return data(group, 0, slice(rest_at, rest_at + 8)).astype(F32)[3:4, 0 : 2 * rim]

    def basis_of(dist_row, env_row):
        centers = iota((n_basis, 1), 0).astype(F32) * (6.0 / (n_basis - 1))
        return (jnp.exp(-2.0 * (dist_row - centers) ** 2) * env_row).astype(BF16)

    for group in range(groups):
        for c in range(2):
            state0[c * half : (c + 1) * half, group * LANES : (group + 1) * LANES] = data(
                group, c, slice(0, half)
            )
    hidden = silu(dot_tn(w_in[0], state0[...]) + columns[:, 0:1]).astype(BF16)
    weight_ac = jnp.concatenate([weight(0, 0), weight(0, 2)], axis=0)
    messages = dot(weight_ac, hidden).astype(BF16)
    atom_col = lane_atom(iota((LANES, 2 * rim), 0), fan, tiles).astype(F32)
    for group in range(groups):
        own = messages[:, group * LANES : (group + 1) * LANES]
        own0[group] = own
        border_row = border_of(group)
        faces0[group, :, 0 : 2 * rim] = dot(own, one_hot(atom_col == border_row)).astype(BF16)

    row = iota((LANES + 2 * rim, 1), 0)
    names = jnp.where(
        row < LANES,
        lane_atom(row, fan, tiles),
        jnp.where(row < LANES + rim, row + rim, row - rim),
    ).astype(F32)
    upper_lane = iota((2 * width, 2 * rim), 1) < rim
    radial_ac = jnp.concatenate([radial_weight(0, 0), radial_weight(0, 2)], axis=0)

    def update(group, carry):
        up = lax.rem(group + 1, groups)
        low = lax.rem(group + groups - 1, groups)
        ghosts = jnp.where(
            upper_lane,
            faces0[up, :, 0 : 2 * rim].astype(F32),
            faces0[low, :, 0 : 2 * rim].astype(F32),
        ).astype(BF16)
        table = jnp.concatenate([own0[group], ghosts], axis=1)
        halves = edge_rows(group)
        step = fan // 2
        acc = jnp.zeros((width, LANES), F32)
        acc_vec = [jnp.zeros((width, LANES), F32) for _ in range(3)]
        for c in range(2):
            rows = halves[c]
            vec = [rows[x * step : (x + 1) * step] for x in range(3)]
            nbr = rows[4 * step : 5 * step]
            length_sq = vec[0] * vec[0] + vec[1] * vec[1] + vec[2] * vec[2]
            length = jnp.sqrt(length_sq) + rows[3 * step : 4 * step]
            env = (1.0 - length * length / 36.0) ** 2
            for pair in range(step // 2):
                ks = (2 * pair, 2 * pair + 1)
                picked = jnp.concatenate([one_hot(names == nbr[k : k + 1]) for k in ks], axis=1)
                basis = jnp.concatenate(
                    [basis_of(length[k : k + 1], env[k : k + 1]) for k in ks], axis=1
                )
                prod = dot(table, picked) * dot(radial_ac, basis)
                for i, k in enumerate(ks):
                    block = prod[:, i * LANES : (i + 1) * LANES]
                    acc = acc + block[:width]
                    for x in range(3):
                        acc_vec[x] = acc_vec[x] + block[width:] * vec[x][k : k + 1]
        lanes = pl.ds(pl.multiple_of(group * LANES, LANES), LANES)
        state1[0:width, lanes] = (state0[:, lanes].astype(F32) + acc / root_fan).astype(BF16)
        for x in range(3):
            state1[(x + 1) * width : (x + 2) * width, lanes] = (acc_vec[x] / root_fan).astype(BF16)
        return carry

    lax.fori_loop(0, groups, update, 0)

    hidden = silu(dot_tn(w_in[1], state1[0:width, :]) + columns[:, 1:2]).astype(BF16)
    for p in range(3):
        table1[p * width : (p + 1) * width, :] = dot(weight(1, p), hidden).astype(BF16)
    table1[3 * width :, :] = state1[width:, :]

    received = groups * cap
    edges = received * fan
    send_rows = jnp.concatenate(
        [data(g, 0, slice(rest_at, rest_at + 8)).astype(F32)[4:5] for g in range(groups)], axis=0
    )

    def picks(lane_count, per_group):
        lane = iota((LANES, lane_count), 1)
        wanted = me * cap + lane % cap
        spread = dot(send_rows.astype(BF16), one_hot(iota((LANES, lane_count), 0) == wanted))
        lane = iota((groups, lane_count), 1)
        spread = jnp.where(lane // per_group == iota((groups, lane_count), 0), spread, 0.0)
        return jnp.sum(spread, axis=0, keepdims=True)

    per_group = fan * cap
    pick_edges = picks(edges, per_group)
    pick_atoms = picks(received, cap)
    atom_rows = lane_atom(iota((LANES, per_group), 0), fan, tiles).astype(F32)
    chosen = []
    for group in range(groups):
        rows = jnp.concatenate([data(group, c, slice(edge_at, rest_at)) for c in range(2)], axis=0)
        want = pick_edges[:, group * per_group : (group + 1) * per_group]
        chosen.append(dot(rows, one_hot(atom_rows == want)))
    chosen = jnp.concatenate(chosen, axis=1)
    step = fan // 2
    row = iota((2 * n_edge, edges), 0)
    slot_k = (row // n_edge) * step + row % step
    lane_k = (iota((2 * n_edge, edges), 1) % per_group) // cap
    chosen = jnp.where(slot_k == lane_k, chosen, 0.0)
    chosen = jnp.sum(chosen.reshape(2 * 5, step, edges), axis=1)
    chosen = chosen[0:5] + chosen[5:10]
    vec = [chosen[x : x + 1] for x in range(3)]
    nbr = chosen[4:5]
    length = jnp.sqrt(vec[0] * vec[0] + vec[1] * vec[1] + vec[2] * vec[2]) + chosen[3:4]
    basis = basis_of(length, (1.0 - length * length / 36.0) ** 2)

    nbr = nbr.astype(jnp.int32)
    home = iota((1, edges), 1) // per_group
    is_low = (nbr >= LANES) & (nbr < LANES + rim)
    is_up = nbr >= LANES + rim
    owner = jnp.where(
        is_low, (home + groups - 1) % groups, jnp.where(is_up, (home + 1) % groups, home)
    )
    entry = owner * 2 * rim + jnp.where(is_low, nbr - (LANES - rim), nbr - (LANES + rim))
    entry = jnp.where(is_low | is_up, entry, -1)
    border_all = jnp.concatenate(
        [border_of(g) for g in range(groups)], axis=1
    )
    border_all = jnp.broadcast_to(border_all, (16, groups * 2 * rim)).astype(BF16)
    seen = dot(border_all, one_hot(iota((groups * 2 * rim, edges), 0) == entry))[0:1]
    target = owner * LANES + jnp.where(entry < 0, nbr, seen.astype(jnp.int32))
    row = iota((every, 1), 0)
    column_name = (row // LANES) * LANES + lane_atom(row % LANES, fan, tiles)
    rows = dot(table1[...], one_hot(column_name == target))
    radial_abc = jnp.concatenate([radial_weight(1, p) for p in range(3)], axis=0)
    filters = dot(radial_abc, basis)
    gate = rows[width : 2 * width] * filters[width : 2 * width]
    along = rows[2 * width : 3 * width] * filters[2 * width :]
    parts = [rows[:width] * filters[:width]]
    for x in range(3):
        parts.append(rows[(3 + x) * width : (4 + x) * width] * gate + along * vec[x])
    parts = jnp.concatenate(parts, axis=0).astype(BF16)
    edge = iota((edges, received), 0)
    slot = (edge // per_group) * cap + edge % cap
    delta = dot(parts, one_hot(slot == iota((edges, received), 1)))
    wanted = (iota((1, received), 1) // cap) * LANES + pick_atoms.astype(jnp.int32)
    chosen_atoms = one_hot(column_name == wanted)
    final = (dot(state1[...], chosen_atoms) + delta / root_fan).astype(BF16).astype(F32)

    pos_rows = jnp.concatenate(
        [data(g, 0, slice(rest_at, rest_at + 8)) for g in range(groups)], axis=1
    )
    pos = dot(pos_rows, chosen_atoms) - 1.875
    pos_cols = jnp.concatenate(
        [
            jnp.concatenate([pos, jnp.zeros((8, LANES - received), F32)], axis=1),
            jnp.zeros((LANES - 8, LANES), F32),
        ],
        axis=0,
    ).T
    list_len = width
    list_at = layers + 2
    counts = []
    for block in range(n_blocks):
        live = iota((1, list_len), 1).astype(F32) < small_rows[list_at + n_blocks : list_at + n_blocks + 1, block : block + 1]
        named = jnp.where(live, small_rows[list_at + block : list_at + block + 1], -1.0)
        hits = jnp.where(iota((received, list_len), 0).astype(F32) == named, 1.0, 0.0)
        counts.append(
            jnp.broadcast_to(jnp.sum(hits, axis=1, keepdims=True), (received, PB))
        )
    counts = jnp.concatenate(counts, axis=1)
    probes = n_blocks * PB
    number = me * probes + iota((1, probes), 1)
    grid = [
        (n % 16).astype(F32) * 0.25 - 1.875 for n in (number, number // 16, number // 256)
    ]
    dist_sq = jnp.zeros((received, probes), F32)
    for x in range(3):
        dist_sq = dist_sq + (grid[x] - pos_cols[0:received, x : x + 1]) ** 2
    dist = jnp.sqrt(dist_sq)
    envelope = (1.0 - dist_sq / 64.0) ** 2 * counts
    basis = jnp.concatenate(
        [
            (jnp.exp(-2.0 * (dist - r * (7.0 / (n_basis - 1))) ** 2) * envelope).astype(BF16)
            for r in range(n_basis)
        ],
        axis=0,
    )
    terms_shape = (2 * n_basis, n_basis * received)
    probe_weight = radial_all[:, 3 * layers * n_basis :]
    w_scalar, w_vector = (
        dot(probe_weight, one_hot(iota(terms_shape, 1) // received * 2 + p == iota(terms_shape, 0)))
        for p in range(2)
    )
    along = final[width : 2 * width] * pos[0:1]
    for x in range(1, 3):
        along = along + final[(x + 1) * width : (x + 2) * width] * pos[x : x + 1]
    def repeat(value):
        return jnp.concatenate([value] * n_basis, axis=1)
    terms = [w_scalar * repeat(final[:width]) - w_vector * repeat(along)]
    for x in range(3):
        terms.append(w_vector * repeat(final[(x + 1) * width : (x + 2) * width]))
    sums = dot(jnp.concatenate(terms, axis=0).astype(BF16), basis)
    charges = sums[:width]
    for x in range(3):
        charges = charges + grid[x] * sums[(x + 1) * width : (x + 2) * width]
    mixed = dot_tn(w_mix[...], charges.astype(BF16)) + columns[:, layers : layers + 1]
    density[...] = jnp.sum(silu(mixed) * columns[:, layers + 1 : layers + 2], axis=0, keepdims=True)


def few_groups(
    atom_s, atom_pos, edge_vec, edge_nbr, border_index, send_index, probe_list, probe_count,
    w_in, b_in, w_msg, w_rad, w_probe, w_mix, b_mix, w_out,
):
    atoms, half = atom_s.shape
    groups = lax.axis_size("brick") * lax.axis_size("probe")
    fan = edge_nbr.shape[0] // atoms
    rim = border_index.shape[0] // 2
    n_basis = w_rad.shape[1]
    cap = send_index.shape[1] // groups
    width = 2 * half
    every = groups * LANES
    bricks = lax.axis_size("brick")
    data, weights, small = pack(
        atom_s, atom_pos, edge_vec, edge_nbr, border_index, send_index, w_msg, w_rad, w_probe,
        b_in, b_mix, w_out, probe_list, probe_count,
    )
    swap = [(0, 1), (1, 0)]
    weights_other = lax.ppermute(weights, "chan", swap)
    column = [data]
    for shift in range(1, bricks):
        column.append(lax.ppermute(data, "brick", [(i, (i + shift) % bricks) for i in range(bricks)]))
    blocks = column + [lax.ppermute(x, "probe", swap) for x in column]
    blocks += [lax.ppermute(x, "chan", swap) for x in blocks]
    n_probes = probe_list.shape[0] * PB
    density = pl.pallas_call(
        functools.partial(density_kernel, (groups, fan, rim, half, n_basis, cap, probe_list.shape[0])),
        out_shape=jax.ShapeDtypeStruct((1, n_probes), F32),
                scratch_shapes=[
            pltpu.VMEM((width, every), BF16),
            pltpu.VMEM((groups, 2 * width, LANES), BF16),
            pltpu.VMEM((groups, 2 * width, LANES), BF16),
            pltpu.VMEM((4 * width, every), BF16),
            pltpu.VMEM((6 * width, every), BF16),
            pltpu.VMEM((2,) + weights.shape, BF16),
            pltpu.VMEM((2, 2, bricks) + data.shape, BF16),
        ],
        compiler_params=pltpu.CompilerParams(vmem_limit_bytes=40 * 1024 * 1024),
        name="density",
    )(*blocks, weights, weights_other, small, w_in, w_mix)
    return density.reshape(n_probes)


def per_device(*args):
    columns = lax.axis_size("probe")
    if columns == 2 and lax.axis_size("brick") * columns <= FEW_GROUPS:
        return few_groups(*args)
    return many_groups(*args)


def extended(block, sides, width):
    for axis, dim in sides:
        count = lax.axis_size(axis)
        forward = [(i, i + 1) for i in range(count - 1)]
        forward.append((count - 1, 0))
        backward = [(target, source) for source, target in forward]
        low = lax.ppermute(
            lax.slice_in_dim(block, block.shape[dim] - width, None, axis=dim), axis, forward
        )
        high = lax.ppermute(lax.slice_in_dim(block, 0, width, axis=dim), axis, backward)
        block = jnp.concatenate([low, block, high], axis=dim)
    return block


def radial(distance, count, top):
    centers = jnp.arange(count).astype(jnp.float32) * (top / (count - 1))
    return jnp.exp(-2.0 * (distance[..., None] - centers) ** 2)


def make_block(
    recv_rows, recv_pos, w_scalar, w_vector, feat_width, group_no, n_blocks, list_len, n_basis
):

    def probe_block(block_in):
        block_no, listed, live_count = block_in
        index_row = (group_no * n_blocks + block_no) * PB + jnp.arange(PB, dtype=jnp.int32)
        grid_xyz = (
            jnp.stack([index_row % 16, index_row // 16 % 16, index_row // 256 % 16], axis=1).astype(
                jnp.float32
            )
            * 0.25
        )
        atom_xyz = recv_pos[:, listed]
        disp = grid_xyz[:, :, None] - atom_xyz[None]
        dist_sq = jnp.sum(disp * disp, axis=1)
        live = (jnp.arange(list_len, dtype=jnp.int32) < live_count).astype(jnp.float32)
        envelope = (1.0 - dist_sq / 64.0) ** 2 * live[None, :]
        basis = radial(jnp.sqrt(dist_sq), n_basis, 7.0) * envelope[:, :, None]
        scalar_w = basis.astype(jnp.bfloat16).reshape(PB, list_len * n_basis)
        vector_w = (
            (disp[:, :, :, None] * basis[:, None])
            .astype(jnp.bfloat16)
            .reshape(PB, 3 * list_len * n_basis)
        )
        atom_rows = recv_rows[listed]
        atom_terms = (atom_rows[:, None, :feat_width] * w_scalar[None]).reshape(
            list_len * n_basis, feat_width
        )
        vec_rows = jnp.transpose(
            atom_rows[:, feat_width:].reshape(list_len, 3, feat_width), (1, 0, 2)
        )
        vector_terms = (vec_rows[:, :, None, :] * w_vector[None, None]).reshape(
            3 * list_len * n_basis, feat_width
        )
        charge = jnp.dot(scalar_w, atom_terms, preferred_element_type=jnp.float32) + jnp.dot(
            vector_w, vector_terms, preferred_element_type=jnp.float32
        )
        return charge.astype(jnp.bfloat16)

    return probe_block


def many_groups(
    atom_s,
    atom_pos,
    edge_vec,
    edge_nbr,
    border_index,
    send_index,
    probe_list,
    probe_count,
    w_in,
    b_in,
    w_msg,
    w_rad,
    w_probe,
    w_mix,
    b_mix,
    w_out,
):
    atom_count, half_width = atom_s.shape
    n_layers = w_in.shape[0]
    width = w_in.shape[1]
    n_basis = w_rad.shape[1]
    fan_out = edge_nbr.shape[0] // atom_count
    root_fan = fan_out**0.5
    rim_rows = border_index.shape[0] // 2
    length = jnp.sqrt(jnp.sum(edge_vec * edge_vec, axis=0))
    edge_env = (1.0 - length * length / 36.0) ** 2
    edge_basis = (radial(length, n_basis, 6.0) * edge_env[:, None]).astype(jnp.bfloat16)
    edge_cols = jnp.transpose(edge_vec)
    scalars = atom_s
    vectors = jnp.zeros((atom_count, 3 * half_width), jnp.bfloat16)
    for layer_no in range(n_layers):
        full_rows = lax.all_gather(scalars, "chan", axis=1, tiled=True)
        in_weight = w_in[layer_no]
        in_bias = b_in[layer_no]
        msg_weight = w_msg[layer_no].reshape(width, 3 * half_width)
        rad_weight = w_rad[layer_no].reshape(n_basis, 3 * half_width)
        hidden_act = jax.nn.silu(
            jnp.dot(full_rows, in_weight, preferred_element_type=jnp.float32) + in_bias
        ).astype(jnp.bfloat16)
        inner_tab = jnp.concatenate(
            [
                jnp.dot(hidden_act, msg_weight, preferred_element_type=jnp.float32).astype(
                    jnp.bfloat16
                ),
                vectors,
            ],
            axis=1,
        )
        padded = extended(inner_tab[border_index], ((("brick", "probe"), 0),), rim_rows)
        lookup = jnp.concatenate([inner_tab, padded[:rim_rows], padded[3 * rim_rows :]], axis=0)
        neighbour_rows = lookup[edge_nbr]
        filters = jnp.dot(edge_basis, rad_weight, preferred_element_type=jnp.float32)
        weighted = neighbour_rows[:, : 3 * half_width] * filters
        neighbour_vec = neighbour_rows[:, 3 * half_width :].reshape(-1, 3, half_width)
        vector_gate = weighted[:, None, half_width : 2 * half_width]
        along_edge = weighted[:, None, 2 * half_width :]
        delta_vec = neighbour_vec * vector_gate + along_edge * edge_cols[:, :, None]
        delta_scalar = (
            weighted[:, :half_width].reshape(atom_count, fan_out, half_width).sum(axis=1) / root_fan
        )
        delta_vec = delta_vec.reshape(atom_count, fan_out, 3 * half_width).sum(axis=1) / root_fan
        scalars = (scalars + delta_scalar).astype(jnp.bfloat16)
        vectors = (vectors + delta_vec).astype(jnp.bfloat16)
    features = jnp.concatenate([scalars, vectors], axis=1)
    picks = send_index[0]
    n_brick = lax.axis_size("brick")
    n_probe = lax.axis_size("probe")
    n_groups = n_brick * n_probe
    slot_cap = picks.shape[0] // n_groups
    out_rows = features[picks]
    out_pos = jnp.transpose(atom_pos)[picks].astype(jnp.bfloat16)
    received = (
        lax.all_to_all(
            out_rows.reshape(n_groups, slot_cap, 4 * half_width),
            ("brick", "probe"),
            split_axis=0,
            concat_axis=0,
            tiled=True,
        ),
        lax.all_to_all(
            out_pos.reshape(n_groups, slot_cap, 3),
            ("brick", "probe"),
            split_axis=0,
            concat_axis=0,
            tiled=True,
        ),
    )
    recv_count = n_groups * slot_cap
    recv_rows = received[0].reshape(recv_count, 4 * half_width)
    recv_pos = jnp.transpose(received[1].reshape(recv_count, 3)).astype(jnp.float32)
    group_no = lax.axis_index("brick") * n_probe + lax.axis_index("probe")
    n_blocks, list_len = probe_list.shape
    probe_block = make_block(
        recv_rows,
        recv_pos,
        w_probe[:, 0, :],
        w_probe[:, 1, :],
        half_width,
        group_no,
        n_blocks,
        list_len,
        n_basis,
    )
    charges = lax.map(
        probe_block, (jnp.arange(n_blocks, dtype=jnp.int32), probe_list, probe_count)
    ).reshape(n_blocks * PB, half_width)
    mix_rows = lax.dynamic_slice_in_dim(w_mix, lax.axis_index("chan") * half_width, half_width, 0)
    mixed = lax.psum(jnp.dot(charges, mix_rows, preferred_element_type=jnp.float32), "chan")
    return jnp.sum(jax.nn.silu(mixed + b_mix) * w_out, axis=1)


def solution(mesh):
    in_specs = (
        P(("image", "brick", "probe"), "chan"),
        P(None, ("image", "brick", "probe")),
        P(None, ("image", "brick", "probe")),
        P(("image", "brick", "probe")),
        P(("image", "brick", "probe")),
        P(("image", "brick", "probe"), None),
        P(("image", "brick", "probe"), None),
        P(("image", "brick", "probe")),
        P(),
        P(),
        P(None, None, None, "chan"),
        P(None, None, None, "chan"),
        P(None, None, "chan"),
        P(),
        P(),
        P(),
    )
    out_specs = P(("image", "brick", "probe"))
    return jax.shard_map(
        per_device, mesh=mesh, in_specs=in_specs, out_specs=out_specs, check_vma=False
    )
```

```python
import functools
import math

import jax
import jax.numpy as jnp
from jax import lax
from jax.experimental import pallas as pl
from jax.experimental.pallas import tpu as pltpu
from jax.sharding import PartitionSpec as P

PB = 128
LANES = 128
FEW_GROUPS = 8
SMALL = 16
ROOT = (2.0 * math.log2(math.e)) ** 0.5
F32 = jnp.float32
BF16 = jnp.bfloat16


def iota(shape, dim):
    return lax.broadcasted_iota(jnp.int32, shape, dim)


def dot(a, b):
    return jnp.dot(a, b, preferred_element_type=F32)


def dot_tn(a, b):
    return lax.dot_general(a, b, (((0,), (0,)), ((), ())), preferred_element_type=F32)


def one_hot(mask):
    return jnp.where(mask, 1.0, 0.0).astype(BF16)


def same(names, row):
    return jnp.where(names == row, jnp.ones_like(names), jnp.zeros_like(names))


def silu(x):
    half_x = 0.5 * x
    return half_x * jnp.tanh(half_x) + half_x


def bell(scaled, center):
    away = scaled - center
    return jnp.exp2(-(away * away))


def lane_atom(lane, fan, tiles):
    return (lane % tiles) * (LANES // fan) + lane // tiles


def pack_kernel(
    fan, atom_s, atom_pos, edge_vec, edge_nbr, border, send, w_msg, w_rad, w_probe,
    b_in, b_mix, w_out, probe_list, probe_count, data_out, weight_out, small_out, natural,
):
    half, atoms = atom_s.shape
    tiles = atoms * fan // LANES
    per_tile = LANES // fan
    part = lax.axis_index("chan")
    perm = one_hot(lane_atom(iota((atoms, LANES), 1), fan, tiles) == iota((atoms, LANES), 0))
    scalars = dot(atom_s[...], perm).astype(BF16)
    vec = edge_vec[...]
    vec_high = vec.astype(BF16).astype(F32)
    length = jnp.sqrt(jnp.sum(vec * vec, axis=0, keepdims=True))
    short = length - jnp.sqrt(jnp.sum(vec_high * vec_high, axis=0, keepdims=True))
    rows = jnp.concatenate([vec_high, short], axis=0)
    for tile in range(tiles):
        for comp in range(4):
            natural[comp * tiles + tile : comp * tiles + tile + 1, :] = rows[
                comp : comp + 1, tile * LANES : (tile + 1) * LANES
            ]
    natural[4 * tiles : 5 * tiles, :] = edge_nbr[...].astype(F32)
    natural[5 * tiles :, :] = jnp.zeros((LANES - 5 * tiles, LANES), F32)
    turned = natural[...].T
    lane = iota((fan, LANES), 1)
    sorted_rows = []
    for comp in range(5):
        rows = jnp.zeros((fan, LANES), F32)
        for a in range(per_tile):
            piece = turned[a * fan : (a + 1) * fan, :]
            shift = (a * tiles - comp * tiles) % LANES
            piece = pltpu.roll(piece, shift, 1) if shift else piece
            rows = jnp.where(lane // tiles == a, piece, rows)
        sorted_rows.append(jnp.where(part == 0, rows[: fan // 2], rows[fan // 2 :]))
    pos = dot(atom_pos[...].astype(BF16), perm)
    blank = jnp.zeros((1, LANES), F32)
    border_row = jnp.concatenate(
        [border[...].astype(F32), jnp.zeros((1, LANES - border.shape[1]), F32)], axis=1
    )
    send_row = jnp.concatenate(
        [send[...].astype(F32), jnp.zeros((1, LANES - send.shape[1]), F32)], axis=1
    )
    rest = jnp.concatenate([pos, border_row, send_row, blank, blank, blank], axis=0)
    others = jnp.concatenate(sorted_rows + [rest], axis=0).astype(BF16)
    for group in range(data_out.shape[0]):
        data_out[group, 0:half, :] = scalars
        data_out[group, half:, :] = others
    at = 0
    for piece in (b_in, b_mix, w_out, probe_list, probe_count):
        rows, cols = piece.shape
        small_out[at : at + rows, 0:cols] = piece[...].astype(F32)
        at += rows
    probe_rows = [w_probe[r].astype(F32) for r in range(w_probe.shape[0])]
    radial = jnp.concatenate([w_rad[...].astype(F32)] + probe_rows, axis=0).T.astype(BF16)
    weight_out[: w_msg.shape[0], :] = w_msg[...]
    weight_out[w_msg.shape[0] :, :] = radial


def pack(
    groups, atom_s, atom_pos, edge_vec, edge_nbr, border_index, send_index, w_msg, w_rad, w_probe,
    b_in, b_mix, w_out, probe_list, probe_count,
):
    atoms, half = atom_s.shape
    fan = edge_nbr.shape[0] // atoms
    return pl.pallas_call(
        functools.partial(pack_kernel, fan),
        out_shape=(
            jax.ShapeDtypeStruct((groups, half + 5 * fan // 2 + 8, LANES), BF16),
            jax.ShapeDtypeStruct((w_msg.size // LANES + half, LANES), BF16),
            jax.ShapeDtypeStruct((SMALL, LANES), F32),
        ),
        scratch_shapes=[pltpu.VMEM((LANES, LANES), F32)],
        name="pack",
    )(
        atom_s.T,
        atom_pos,
        edge_vec,
        edge_nbr.reshape(-1, LANES),
        border_index.reshape(1, -1),
        send_index,
        jnp.transpose(w_msg, (0, 2, 3, 1)).reshape(-1, LANES),
        jnp.transpose(w_rad, (0, 2, 1, 3)).reshape(-1, half),
        w_probe,
        b_in,
        b_mix.reshape(1, -1),
        w_out.reshape(1, -1),
        probe_list,
        probe_count.reshape(1, -1),
    )


def density_kernel(
    sizes,
    data_all,
    weights_mine,
    weights_other,
    small,
    w_in,
    w_mix,
    density,
    state0,
    own0,
    faces0,
    state1,
    table1,
    weights,
):
    groups, fan, rim, half, n_basis, cap, n_blocks = sizes
    layers = w_in.shape[0]
    width = 2 * half
    tiles = LANES * fan // LANES
    root_fan = fan**0.5
    me = lax.axis_index("brick") * lax.axis_size("probe") + lax.axis_index("probe")
    part = lax.axis_index("chan")
    weights[part] = weights_mine[...]
    weights[1 - part] = weights_other[...]
    every = groups * LANES
    edge_at = half
    n_edge = 5 * fan // 2
    rest_at = half + n_edge

    def data(group, c, rows):
        return data_all[c, group, rows, :]

    small_rows = small[...]
    columns = small_rows.T

    def weight(layer, p):
        at = (layer * 3 + p) * half
        return jnp.concatenate([weights[c, at : at + half, :] for c in range(2)], axis=0)

    radial_at = weights.shape[1] - half
    radial_all = jnp.concatenate([weights[c, radial_at:, :] for c in range(2)], axis=0)

    def radial_weight(layer, p):
        at = (layer * 3 + p) * n_basis
        return radial_all[:, at : at + n_basis]

    def edge_rows(group):
        return [data(group, c, slice(edge_at, rest_at)).astype(F32) for c in range(2)]

    def border_of(group):
        return data(group, 0, slice(rest_at, rest_at + 8)).astype(F32)[3:4, 0 : 2 * rim]

    centers = iota((n_basis, 1), 0).astype(F32) * (ROOT * 6.0 / (n_basis - 1))

    def basis_of(length, env):
        return (bell(length * ROOT, centers) * env).astype(BF16)

    received = groups * cap
    edges = received * fan
    send_rows = jnp.concatenate(
        [data(g, 0, slice(rest_at, rest_at + 8)).astype(F32)[4:5] for g in range(groups)], axis=0
    )

    def picks(lane_count, per_group):
        lane = iota((LANES, lane_count), 1)
        wanted = me * cap + lane % cap
        spread = dot(send_rows.astype(BF16), one_hot(iota((LANES, lane_count), 0) == wanted))
        lane = iota((groups, lane_count), 1)
        spread = jnp.where(lane // per_group == iota((groups, lane_count), 0), spread, 0.0)
        return jnp.sum(spread, axis=0, keepdims=True)

    per_group = fan * cap
    pick_edges = picks(edges, per_group)
    pick_atoms = picks(received, cap)
    atom_rows = lane_atom(iota((LANES, per_group), 0), fan, tiles).astype(F32)
    chosen = []
    for group in range(groups):
        rows = jnp.concatenate([data(group, c, slice(edge_at, rest_at)) for c in range(2)], axis=0)
        want = pick_edges[:, group * per_group : (group + 1) * per_group]
        chosen.append(dot(rows, one_hot(atom_rows == want)))
    chosen = jnp.concatenate(chosen, axis=1)
    step = fan // 2
    row = iota((2 * n_edge, edges), 0)
    slot_k = (row // n_edge) * step + row % step
    lane_k = (iota((2 * n_edge, edges), 1) % per_group) // cap
    chosen = jnp.where(slot_k == lane_k, chosen, 0.0)
    chosen = jnp.sum(chosen.reshape(2 * 5, step, edges), axis=1)
    chosen = chosen[0:5] + chosen[5:10]
    pick_vec = [chosen[x : x + 1] for x in range(3)]
    nbr = chosen[4:5]
    length = jnp.sqrt(sum(x * x for x in pick_vec)) + chosen[3:4]
    basis1 = basis_of(length, (1.0 - length * length / 36.0) ** 2)

    nbr = nbr.astype(jnp.int32)
    home = iota((1, edges), 1) // per_group
    is_low = (nbr >= LANES) & (nbr < LANES + rim)
    is_up = nbr >= LANES + rim
    owner = jnp.where(
        is_low, (home + groups - 1) % groups, jnp.where(is_up, (home + 1) % groups, home)
    )
    entry = owner * 2 * rim + jnp.where(is_low, nbr - (LANES - rim), nbr - (LANES + rim))
    entry = jnp.where(is_low | is_up, entry, -1)
    border_all = jnp.concatenate(
        [border_of(g) for g in range(groups)], axis=1
    )
    border_all = jnp.broadcast_to(border_all, (16, groups * 2 * rim)).astype(BF16)
    seen = dot(border_all, one_hot(iota((groups * 2 * rim, edges), 0) == entry))[0:1]
    target_atom = jnp.where(entry < 0, nbr, seen.astype(jnp.int32))
    column = iota((every, 1), 0)
    column_name = (column // LANES) * LANES + lane_atom(column % LANES, fan, tiles)
    quad = groups // 2
    window = [[(h * quad + groups - 1 + i) % groups for i in range(quad + 2)] for h in range(2)]
    window_pick = []
    for h in range(2):
        lanes = slice(h * edges // 2, (h + 1) * edges // 2)
        near = lax.rem(owner[:, lanes] + 2 * groups - (h * quad + groups - 1), groups)
        name = near * LANES + target_atom[:, lanes]
        window_pick.append(one_hot(column_name[: (quad + 2) * LANES] == name))
    wanted = (iota((1, received), 1) // cap) * LANES + pick_atoms.astype(jnp.int32)
    chosen_atoms = one_hot(column_name == wanted)

    pos_rows = jnp.concatenate(
        [data(g, 0, slice(rest_at, rest_at + 8)) for g in range(groups)], axis=1
    )
    pos = dot(pos_rows, chosen_atoms) - 1.875
    pos_cols = jnp.concatenate(
        [
            jnp.concatenate([pos, jnp.zeros((8, LANES - received), F32)], axis=1),
            jnp.zeros((LANES - 8, LANES), F32),
        ],
        axis=0,
    ).T
    list_len = width
    list_at = layers + 2
    counts = []
    for block in range(n_blocks):
        live = iota((1, list_len), 1).astype(F32) < small_rows[list_at + n_blocks : list_at + n_blocks + 1, block : block + 1]
        named = jnp.where(live, small_rows[list_at + block : list_at + block + 1], -1.0)
        hits = jnp.where(iota((received, list_len), 0).astype(F32) == named, 1.0, 0.0)
        counts.append(
            jnp.broadcast_to(jnp.sum(hits, axis=1, keepdims=True), (received, PB))
        )
    counts = jnp.concatenate(counts, axis=1)
    probes = n_blocks * PB
    number = me * probes + iota((1, probes), 1)
    grid = [
        (n % 16).astype(F32) * 0.25 - 1.875 for n in (number, number // 16, number // 256)
    ]
    dist_sq = jnp.zeros((received, probes), F32)
    for x in range(3):
        dist_sq = dist_sq + (grid[x] - pos_cols[0:received, x : x + 1]) ** 2
    dist = jnp.sqrt(dist_sq) * ROOT
    envelope = (1.0 - dist_sq / 64.0) ** 2 * counts
    probe_basis = jnp.concatenate(
        [
            (bell(dist, r * (ROOT * 7.0 / (n_basis - 1))) * envelope).astype(BF16)
            for r in range(n_basis)
        ],
        axis=0,
    )
    terms_shape = (2 * n_basis, n_basis * received)
    probe_weight = radial_all[:, 3 * layers * n_basis :]
    w_scalar, w_vector = (
        dot(probe_weight, one_hot(iota(terms_shape, 1) // received * 2 + p == iota(terms_shape, 0)))
        for p in range(2)
    )

    for group in range(groups):
        for c in range(2):
            state0[c * half : (c + 1) * half, group * LANES : (group + 1) * LANES] = data(
                group, c, slice(0, half)
            )
    hidden = silu(dot_tn(w_in[0], state0[...]) + columns[:, 0:1]).astype(BF16)
    weight_ac = jnp.concatenate([weight(0, 0), weight(0, 2)], axis=0)
    messages = dot(weight_ac, hidden).astype(BF16)
    atom_col = lane_atom(iota((LANES, 2 * rim), 0), fan, tiles).astype(F32)
    for group in range(groups):
        own = messages[:, group * LANES : (group + 1) * LANES]
        own0[group] = own
        border_row = border_of(group)
        faces0[group, :, 0 : 2 * rim] = dot(own, one_hot(atom_col == border_row)).astype(BF16)

    row = iota((LANES + 2 * rim, 1), 0)
    names = jnp.where(
        row < LANES,
        lane_atom(row, fan, tiles),
        jnp.where(row < LANES + rim, row + rim, row - rim),
    ).astype(F32)
    names = jnp.broadcast_to(names, (LANES + 2 * rim, LANES)).astype(BF16)
    upper_lane = iota((2 * width, 2 * rim), 1) < rim
    radial_ac = jnp.concatenate([radial_weight(0, 0), radial_weight(0, 2)], axis=0)

    for group in range(groups):
        up = (group + 1) % groups
        low = (group + groups - 1) % groups
        ghosts = jnp.where(
            upper_lane,
            faces0[up, :, 0 : 2 * rim].astype(F32),
            faces0[low, :, 0 : 2 * rim].astype(F32),
        ).astype(BF16)
        table = jnp.concatenate([own0[group], ghosts], axis=1)
        halves = edge_rows(group)
        step = fan // 2
        acc = jnp.zeros((width, LANES), F32)
        acc_vec = [jnp.zeros((width, LANES), F32) for _ in range(3)]
        for c in range(2):
            rows = halves[c]
            vec = [rows[x * step : (x + 1) * step] for x in range(3)]
            nbr = rows[4 * step : 5 * step]
            length_sq = vec[0] * vec[0] + vec[1] * vec[1] + vec[2] * vec[2]
            length = jnp.sqrt(length_sq) + rows[3 * step : 4 * step]
            env = (1.0 - length * length / 36.0) ** 2
            for pair in range(step // 2):
                ks = (2 * pair, 2 * pair + 1)
                picked = jnp.concatenate([same(names, nbr[k : k + 1].astype(BF16)) for k in ks], axis=1)
                basis = jnp.concatenate(
                    [basis_of(length[k : k + 1], env[k : k + 1]) for k in ks], axis=1
                )
                prod = dot(table, picked) * dot(radial_ac, basis)
                for i, k in enumerate(ks):
                    block = prod[:, i * LANES : (i + 1) * LANES]
                    acc = acc + block[:width]
                    for x in range(3):
                        acc_vec[x] = acc_vec[x] + block[width:] * vec[x][k : k + 1]
        lanes = slice(group * LANES, (group + 1) * LANES)
        state1[0:width, lanes] = (state0[:, lanes].astype(F32) + acc / root_fan).astype(BF16)
        for x in range(3):
            state1[(x + 1) * width : (x + 2) * width, lanes] = (acc_vec[x] / root_fan).astype(BF16)

    hidden = silu(dot_tn(w_in[1], state1[0:width, :]) + columns[:, 1:2]).astype(BF16)
    for p in range(3):
        table1[p * width : (p + 1) * width, :] = dot(weight(1, p), hidden).astype(BF16)
    table1[3 * width :, :] = state1[width:, :]

    rows = []
    for h in range(2):
        near_table = jnp.concatenate(
            [table1[:, g * LANES : (g + 1) * LANES] for g in window[h]], axis=1
        )
        rows.append(dot(near_table, window_pick[h]))
    rows = jnp.concatenate(rows, axis=1)
    radial_abc = jnp.concatenate([radial_weight(1, p) for p in range(3)], axis=0)
    filters = dot(radial_abc, basis1)
    gate = rows[width : 2 * width] * filters[width : 2 * width]
    along = rows[2 * width : 3 * width] * filters[2 * width :]
    parts = [rows[:width] * filters[:width]]
    for x in range(3):
        parts.append(rows[(3 + x) * width : (4 + x) * width] * gate + along * pick_vec[x])
    parts = jnp.concatenate(parts, axis=0).astype(BF16)
    edge = iota((edges, received), 0)
    slot = (edge // per_group) * cap + edge % cap
    delta = dot(parts, one_hot(slot == iota((edges, received), 1)))
    final = (dot(state1[...], chosen_atoms) + delta / root_fan).astype(BF16).astype(F32)

    along = final[width : 2 * width] * pos[0:1]
    for x in range(1, 3):
        along = along + final[(x + 1) * width : (x + 2) * width] * pos[x : x + 1]
    def repeat(value):
        return jnp.concatenate([value] * n_basis, axis=1)
    terms = [w_scalar * repeat(final[:width]) - w_vector * repeat(along)]
    for x in range(3):
        terms.append(w_vector * repeat(final[(x + 1) * width : (x + 2) * width]))
    sums = dot(jnp.concatenate(terms, axis=0).astype(BF16), probe_basis)
    charges = sums[:width]
    for x in range(3):
        charges = charges + grid[x] * sums[(x + 1) * width : (x + 2) * width]
    mixed = dot_tn(w_mix[...], charges.astype(BF16)) + columns[:, layers : layers + 1]
    density[...] = jnp.sum(silu(mixed) * columns[:, layers + 1 : layers + 2], axis=0, keepdims=True)


def few_groups(
    atom_s, atom_pos, edge_vec, edge_nbr, border_index, send_index, probe_list, probe_count,
    w_in, b_in, w_msg, w_rad, w_probe, w_mix, b_mix, w_out,
):
    atoms, half = atom_s.shape
    groups = lax.axis_size("brick") * lax.axis_size("probe")
    fan = edge_nbr.shape[0] // atoms
    rim = border_index.shape[0] // 2
    n_basis = w_rad.shape[1]
    cap = send_index.shape[1] // groups
    width = 2 * half
    every = groups * LANES
    data, weights, small = pack(
        groups, atom_s, atom_pos, edge_vec, edge_nbr, border_index, send_index, w_msg, w_rad, w_probe,
        b_in, b_mix, w_out, probe_list, probe_count,
    )
    data = lax.all_to_all(data, ("brick", "probe"), split_axis=0, concat_axis=0, tiled=True)
    other = lax.ppermute(weights, "chan", [(0, 1), (1, 0)])
    data = lax.all_gather(data, "chan")
    n_probes = probe_list.shape[0] * PB
    density = pl.pallas_call(
        functools.partial(density_kernel, (groups, fan, rim, half, n_basis, cap, probe_list.shape[0])),
        out_shape=jax.ShapeDtypeStruct((1, n_probes), F32),
                scratch_shapes=[
            pltpu.VMEM((width, every), BF16),
            pltpu.VMEM((groups, 2 * width, LANES), BF16),
            pltpu.VMEM((groups, 2 * width, LANES), BF16),
            pltpu.VMEM((4 * width, every), BF16),
            pltpu.VMEM((6 * width, every), BF16),
            pltpu.VMEM((2,) + weights.shape, BF16),
        ],
        compiler_params=pltpu.CompilerParams(vmem_limit_bytes=40 * 1024 * 1024),
        name="density",
    )(data, weights, other, small, w_in, w_mix)
    return density.reshape(n_probes)


def per_device(*args):
    if lax.axis_size("brick") * lax.axis_size("probe") == FEW_GROUPS:
        return few_groups(*args)
    return many_groups(*args)


def extended(block, sides, width):
    for axis, dim in sides:
        count = lax.axis_size(axis)
        forward = [(i, i + 1) for i in range(count - 1)]
        forward.append((count - 1, 0))
        backward = [(target, source) for source, target in forward]
        low = lax.ppermute(
            lax.slice_in_dim(block, block.shape[dim] - width, None, axis=dim), axis, forward
        )
        high = lax.ppermute(lax.slice_in_dim(block, 0, width, axis=dim), axis, backward)
        block = jnp.concatenate([low, block, high], axis=dim)
    return block


def radial(distance, count, top):
    centers = jnp.arange(count).astype(jnp.float32) * (top / (count - 1))
    return jnp.exp(-2.0 * (distance[..., None] - centers) ** 2)


def make_block(
    recv_rows, recv_pos, w_scalar, w_vector, feat_width, group_no, n_blocks, list_len, n_basis
):

    def probe_block(block_in):
        block_no, listed, live_count = block_in
        index_row = (group_no * n_blocks + block_no) * PB + jnp.arange(PB, dtype=jnp.int32)
        grid_xyz = (
            jnp.stack([index_row % 16, index_row // 16 % 16, index_row // 256 % 16], axis=1).astype(
                jnp.float32
            )
            * 0.25
        )
        atom_xyz = recv_pos[:, listed]
        disp = grid_xyz[:, :, None] - atom_xyz[None]
        dist_sq = jnp.sum(disp * disp, axis=1)
        live = (jnp.arange(list_len, dtype=jnp.int32) < live_count).astype(jnp.float32)
        envelope = (1.0 - dist_sq / 64.0) ** 2 * live[None, :]
        basis = radial(jnp.sqrt(dist_sq), n_basis, 7.0) * envelope[:, :, None]
        scalar_w = basis.astype(jnp.bfloat16).reshape(PB, list_len * n_basis)
        vector_w = (
            (disp[:, :, :, None] * basis[:, None])
            .astype(jnp.bfloat16)
            .reshape(PB, 3 * list_len * n_basis)
        )
        atom_rows = recv_rows[listed]
        atom_terms = (atom_rows[:, None, :feat_width] * w_scalar[None]).reshape(
            list_len * n_basis, feat_width
        )
        vec_rows = jnp.transpose(
            atom_rows[:, feat_width:].reshape(list_len, 3, feat_width), (1, 0, 2)
        )
        vector_terms = (vec_rows[:, :, None, :] * w_vector[None, None]).reshape(
            3 * list_len * n_basis, feat_width
        )
        charge = jnp.dot(scalar_w, atom_terms, preferred_element_type=jnp.float32) + jnp.dot(
            vector_w, vector_terms, preferred_element_type=jnp.float32
        )
        return charge.astype(jnp.bfloat16)

    return probe_block


def many_groups(
    atom_s,
    atom_pos,
    edge_vec,
    edge_nbr,
    border_index,
    send_index,
    probe_list,
    probe_count,
    w_in,
    b_in,
    w_msg,
    w_rad,
    w_probe,
    w_mix,
    b_mix,
    w_out,
):
    atom_count, half_width = atom_s.shape
    n_layers = w_in.shape[0]
    width = w_in.shape[1]
    n_basis = w_rad.shape[1]
    fan_out = edge_nbr.shape[0] // atom_count
    root_fan = fan_out**0.5
    rim_rows = border_index.shape[0] // 2
    length = jnp.sqrt(jnp.sum(edge_vec * edge_vec, axis=0))
    edge_env = (1.0 - length * length / 36.0) ** 2
    edge_basis = (radial(length, n_basis, 6.0) * edge_env[:, None]).astype(jnp.bfloat16)
    edge_cols = jnp.transpose(edge_vec)
    scalars = atom_s
    vectors = jnp.zeros((atom_count, 3 * half_width), jnp.bfloat16)
    for layer_no in range(n_layers):
        full_rows = lax.all_gather(scalars, "chan", axis=1, tiled=True)
        in_weight = w_in[layer_no]
        in_bias = b_in[layer_no]
        msg_weight = w_msg[layer_no].reshape(width, 3 * half_width)
        rad_weight = w_rad[layer_no].reshape(n_basis, 3 * half_width)
        hidden_act = jax.nn.silu(
            jnp.dot(full_rows, in_weight, preferred_element_type=jnp.float32) + in_bias
        ).astype(jnp.bfloat16)
        inner_tab = jnp.concatenate(
            [
                jnp.dot(hidden_act, msg_weight, preferred_element_type=jnp.float32).astype(
                    jnp.bfloat16
                ),
                vectors,
            ],
            axis=1,
        )
        padded = extended(inner_tab[border_index], ((("brick", "probe"), 0),), rim_rows)
        lookup = jnp.concatenate([inner_tab, padded[:rim_rows], padded[3 * rim_rows :]], axis=0)
        neighbour_rows = lookup[edge_nbr]
        filters = jnp.dot(edge_basis, rad_weight, preferred_element_type=jnp.float32)
        weighted = neighbour_rows[:, : 3 * half_width] * filters
        neighbour_vec = neighbour_rows[:, 3 * half_width :].reshape(-1, 3, half_width)
        vector_gate = weighted[:, None, half_width : 2 * half_width]
        along_edge = weighted[:, None, 2 * half_width :]
        delta_vec = neighbour_vec * vector_gate + along_edge * edge_cols[:, :, None]
        delta_scalar = (
            weighted[:, :half_width].reshape(atom_count, fan_out, half_width).sum(axis=1) / root_fan
        )
        delta_vec = delta_vec.reshape(atom_count, fan_out, 3 * half_width).sum(axis=1) / root_fan
        scalars = (scalars + delta_scalar).astype(jnp.bfloat16)
        vectors = (vectors + delta_vec).astype(jnp.bfloat16)
    features = jnp.concatenate([scalars, vectors], axis=1)
    picks = send_index[0]
    n_brick = lax.axis_size("brick")
    n_probe = lax.axis_size("probe")
    n_groups = n_brick * n_probe
    slot_cap = picks.shape[0] // n_groups
    out_rows = features[picks]
    out_pos = jnp.transpose(atom_pos)[picks].astype(jnp.bfloat16)
    received = (
        lax.all_to_all(
            out_rows.reshape(n_groups, slot_cap, 4 * half_width),
            ("brick", "probe"),
            split_axis=0,
            concat_axis=0,
            tiled=True,
        ),
        lax.all_to_all(
            out_pos.reshape(n_groups, slot_cap, 3),
            ("brick", "probe"),
            split_axis=0,
            concat_axis=0,
            tiled=True,
        ),
    )
    recv_count = n_groups * slot_cap
    recv_rows = received[0].reshape(recv_count, 4 * half_width)
    recv_pos = jnp.transpose(received[1].reshape(recv_count, 3)).astype(jnp.float32)
    group_no = lax.axis_index("brick") * n_probe + lax.axis_index("probe")
    n_blocks, list_len = probe_list.shape
    probe_block = make_block(
        recv_rows,
        recv_pos,
        w_probe[:, 0, :],
        w_probe[:, 1, :],
        half_width,
        group_no,
        n_blocks,
        list_len,
        n_basis,
    )
    charges = lax.map(
        probe_block, (jnp.arange(n_blocks, dtype=jnp.int32), probe_list, probe_count)
    ).reshape(n_blocks * PB, half_width)
    mix_rows = lax.dynamic_slice_in_dim(w_mix, lax.axis_index("chan") * half_width, half_width, 0)
    mixed = lax.psum(jnp.dot(charges, mix_rows, preferred_element_type=jnp.float32), "chan")
    return jnp.sum(jax.nn.silu(mixed + b_mix) * w_out, axis=1)


def solution(mesh):
    in_specs = (
        P(("image", "brick", "probe"), "chan"),
        P(None, ("image", "brick", "probe")),
        P(None, ("image", "brick", "probe")),
        P(("image", "brick", "probe")),
        P(("image", "brick", "probe")),
        P(("image", "brick", "probe"), None),
        P(("image", "brick", "probe"), None),
        P(("image", "brick", "probe")),
        P(),
        P(),
        P(None, None, None, "chan"),
        P(None, None, None, "chan"),
        P(None, None, "chan"),
        P(),
        P(),
        P(),
    )
    out_specs = P(("image", "brick", "probe"))
    return jax.shard_map(
        per_device, mesh=mesh, in_specs=in_specs, out_specs=out_specs, check_vma=False
    )
```

```python
import functools
import math

import jax
import jax.numpy as jnp
from jax import lax
from jax.experimental import pallas as pl
from jax.experimental.pallas import tpu as pltpu
from jax.sharding import PartitionSpec as P

PB = 128
LANES = 128
FEW_GROUPS = 8
SMALL = 16
ROOT = (2.0 * math.log2(math.e)) ** 0.5
F32 = jnp.float32
BF16 = jnp.bfloat16


def iota(shape, dim):
    return lax.broadcasted_iota(jnp.int32, shape, dim)


def dot(a, b):
    return jnp.dot(a, b, preferred_element_type=F32)


def dot_tn(a, b):
    return lax.dot_general(a, b, (((0,), (0,)), ((), ())), preferred_element_type=F32)


def one_hot(mask):
    return jnp.where(mask, 1.0, 0.0).astype(BF16)


def same(names, row):
    return jnp.where(names == row, jnp.ones_like(names), jnp.zeros_like(names))


def silu(x):
    half_x = 0.5 * x
    return half_x * jnp.tanh(half_x) + half_x


def bell(scaled, center):
    away = scaled - center
    return jnp.exp2(-(away * away))


def lane_atom(lane, fan, tiles):
    return (lane % tiles) * (LANES // fan) + lane // tiles


def pack_kernel(
    fan, atom_s, atom_pos, edge_vec, edge_nbr, border, send, data_out, natural
):
    half, atoms = atom_s.shape
    tiles = atoms * fan // LANES
    per_tile = LANES // fan
    part = lax.axis_index("chan")
    perm = one_hot(lane_atom(iota((atoms, LANES), 1), fan, tiles) == iota((atoms, LANES), 0))
    scalars = dot(atom_s[...], perm).astype(BF16)
    vec = edge_vec[...]
    vec_high = vec.astype(BF16).astype(F32)
    length = jnp.sqrt(jnp.sum(vec * vec, axis=0, keepdims=True))
    short = length - jnp.sqrt(jnp.sum(vec_high * vec_high, axis=0, keepdims=True))
    rows = jnp.concatenate([vec_high, short], axis=0)
    for tile in range(tiles):
        for comp in range(4):
            natural[comp * tiles + tile : comp * tiles + tile + 1, :] = rows[
                comp : comp + 1, tile * LANES : (tile + 1) * LANES
            ]
    natural[4 * tiles : 5 * tiles, :] = edge_nbr[...].astype(F32)
    natural[5 * tiles :, :] = jnp.zeros((LANES - 5 * tiles, LANES), F32)
    turned = natural[...].T
    lane = iota((fan, LANES), 1)
    sorted_rows = []
    for comp in range(5):
        rows = jnp.zeros((fan, LANES), F32)
        for a in range(per_tile):
            piece = turned[a * fan : (a + 1) * fan, :]
            shift = (a * tiles - comp * tiles) % LANES
            piece = pltpu.roll(piece, shift, 1) if shift else piece
            rows = jnp.where(lane // tiles == a, piece, rows)
        sorted_rows.append(jnp.where(part == 0, rows[: fan // 2], rows[fan // 2 :]))
    pos = dot(atom_pos[...].astype(BF16), perm)
    blank = jnp.zeros((1, LANES), F32)
    border_row = jnp.concatenate(
        [border[...].astype(F32), jnp.zeros((1, LANES - border.shape[1]), F32)], axis=1
    )
    send_row = jnp.concatenate(
        [send[...].astype(F32), jnp.zeros((1, LANES - send.shape[1]), F32)], axis=1
    )
    rest = jnp.concatenate([pos, border_row, send_row, blank, blank, blank], axis=0)
    others = jnp.concatenate(sorted_rows + [rest], axis=0).astype(BF16)
    for group in range(data_out.shape[0]):
        data_out[group, 0:half, :] = scalars
        data_out[group, half:, :] = others


def weight_kernel(
    w_msg, w_rad, w_probe, b_in, b_mix, w_out, probe_list, probe_count, weight_out, small_out
):
    at = 0
    for piece in (b_in, b_mix, w_out, probe_list, probe_count):
        rows, cols = piece.shape
        small_out[at : at + rows, 0:cols] = piece[...].astype(F32)
        at += rows
    probe_rows = [w_probe[r].astype(F32) for r in range(w_probe.shape[0])]
    radial = jnp.concatenate([w_rad[...].astype(F32)] + probe_rows, axis=0).T.astype(BF16)
    weight_out[: w_msg.shape[0], :] = w_msg[...]
    weight_out[w_msg.shape[0] :, :] = radial


def pack(copies, atom_s, atom_pos, edge_vec, edge_nbr, border_index, send_index):
    atoms, half = atom_s.shape
    fan = edge_nbr.shape[0] // atoms
    return pl.pallas_call(
        functools.partial(pack_kernel, fan),
        out_shape=jax.ShapeDtypeStruct((copies, half + 5 * fan // 2 + 8, LANES), BF16),
        scratch_shapes=[pltpu.VMEM((LANES, LANES), F32)],
        name="pack",
    )(
        atom_s.T,
        atom_pos,
        edge_vec,
        edge_nbr.reshape(-1, LANES),
        border_index.reshape(1, -1),
        send_index,
    )


def pack_weights(half, w_msg, w_rad, w_probe, b_in, b_mix, w_out, probe_list, probe_count):
    return pl.pallas_call(
        weight_kernel,
        out_shape=(
            jax.ShapeDtypeStruct((w_msg.size // LANES + half, LANES), BF16),
            jax.ShapeDtypeStruct((SMALL, LANES), F32),
        ),
        name="pack_weights",
    )(
        jnp.transpose(w_msg, (0, 2, 3, 1)).reshape(-1, LANES),
        jnp.transpose(w_rad, (0, 2, 1, 3)).reshape(-1, half),
        w_probe,
        b_in,
        b_mix.reshape(1, -1),
        w_out.reshape(1, -1),
        probe_list,
        probe_count.reshape(1, -1),
    )


def density_kernel(
    sizes,
    data_mine,
    data_other,
    weights_mine,
    weights_other,
    small,
    w_in,
    w_mix,
    density,
    state0,
    own0,
    faces0,
    state1,
    table1,
    weights,
):
    groups, fan, rim, half, n_basis, cap, n_blocks = sizes
    layers = w_in.shape[0]
    width = 2 * half
    tiles = LANES * fan // LANES
    root_fan = fan**0.5
    me = lax.axis_index("brick") * lax.axis_size("probe") + lax.axis_index("probe")
    part = lax.axis_index("chan")
    weights[part] = weights_mine[...]
    weights[1 - part] = weights_other[...]
    every = groups * LANES
    edge_at = half
    n_edge = 5 * fan // 2
    rest_at = half + n_edge

    def data(group, c, rows):
        return (data_mine, data_other)[c][group, rows, :]

    small_rows = small[...]
    columns = small_rows.T

    def weight(layer, p):
        at = (layer * 3 + p) * half
        return jnp.concatenate([weights[c, at : at + half, :] for c in range(2)], axis=0)

    radial_at = weights.shape[1] - half
    radial_all = jnp.concatenate([weights[c, radial_at:, :] for c in range(2)], axis=0)

    def radial_weight(layer, p):
        at = (layer * 3 + p) * n_basis
        return radial_all[:, at : at + n_basis]

    def edge_rows(group):
        return [data(group, c, slice(edge_at, rest_at)).astype(F32) for c in range(2)]

    def border_of(group):
        return data(group, 0, slice(rest_at, rest_at + 8)).astype(F32)[3:4, 0 : 2 * rim]

    centers = iota((n_basis, 1), 0).astype(F32) * (ROOT * 6.0 / (n_basis - 1))

    def basis_of(length, env):
        return (bell(length * ROOT, centers) * env).astype(BF16)

    received = groups * cap
    edges = received * fan
    send_rows = jnp.concatenate(
        [data(g, 0, slice(rest_at, rest_at + 8)).astype(F32)[4:5] for g in range(groups)], axis=0
    )

    def picks(lane_count, per_group):
        lane = iota((LANES, lane_count), 1)
        wanted = me * cap + lane % cap
        spread = dot(send_rows.astype(BF16), one_hot(iota((LANES, lane_count), 0) == wanted))
        lane = iota((groups, lane_count), 1)
        spread = jnp.where(lane // per_group == iota((groups, lane_count), 0), spread, 0.0)
        return jnp.sum(spread, axis=0, keepdims=True)

    per_group = fan * cap
    pick_edges = picks(edges, per_group)
    pick_atoms = picks(received, cap)
    atom_rows = lane_atom(iota((LANES, per_group), 0), fan, tiles).astype(F32)
    chosen = []
    for group in range(groups):
        rows = jnp.concatenate([data(group, c, slice(edge_at, rest_at)) for c in range(2)], axis=0)
        want = pick_edges[:, group * per_group : (group + 1) * per_group]
        chosen.append(dot(rows, one_hot(atom_rows == want)))
    chosen = jnp.concatenate(chosen, axis=1)
    step = fan // 2
    row = iota((2 * n_edge, edges), 0)
    slot_k = (row // n_edge) * step + row % step
    lane_k = (iota((2 * n_edge, edges), 1) % per_group) // cap
    chosen = jnp.where(slot_k == lane_k, chosen, 0.0)
    chosen = jnp.sum(chosen.reshape(2 * 5, step, edges), axis=1)
    chosen = chosen[0:5] + chosen[5:10]
    pick_vec = [chosen[x : x + 1] for x in range(3)]
    nbr = chosen[4:5]
    length = jnp.sqrt(sum(x * x for x in pick_vec)) + chosen[3:4]
    basis1 = basis_of(length, (1.0 - length * length / 36.0) ** 2)

    nbr = nbr.astype(jnp.int32)
    home = iota((1, edges), 1) // per_group
    is_low = (nbr >= LANES) & (nbr < LANES + rim)
    is_up = nbr >= LANES + rim
    owner = jnp.where(
        is_low, (home + groups - 1) % groups, jnp.where(is_up, (home + 1) % groups, home)
    )
    entry = owner * 2 * rim + jnp.where(is_low, nbr - (LANES - rim), nbr - (LANES + rim))
    entry = jnp.where(is_low | is_up, entry, -1)
    border_all = jnp.concatenate(
        [border_of(g) for g in range(groups)], axis=1
    )
    border_all = jnp.broadcast_to(border_all, (16, groups * 2 * rim)).astype(BF16)
    seen = dot(border_all, one_hot(iota((groups * 2 * rim, edges), 0) == entry))[0:1]
    target_atom = jnp.where(entry < 0, nbr, seen.astype(jnp.int32))
    column = iota((every, 1), 0)
    column_name = (column // LANES) * LANES + lane_atom(column % LANES, fan, tiles)
    quad = groups // 2
    window = [[(h * quad + groups - 1 + i) % groups for i in range(quad + 2)] for h in range(2)]
    window_pick = []
    for h in range(2):
        lanes = slice(h * edges // 2, (h + 1) * edges // 2)
        near = lax.rem(owner[:, lanes] + 2 * groups - (h * quad + groups - 1), groups)
        name = near * LANES + target_atom[:, lanes]
        window_pick.append(one_hot(column_name[: (quad + 2) * LANES] == name))
    wanted = (iota((1, received), 1) // cap) * LANES + pick_atoms.astype(jnp.int32)
    chosen_atoms = one_hot(column_name == wanted)

    pos_rows = jnp.concatenate(
        [data(g, 0, slice(rest_at, rest_at + 8)) for g in range(groups)], axis=1
    )
    pos = dot(pos_rows, chosen_atoms) - 1.875
    pos_cols = jnp.concatenate(
        [
            jnp.concatenate([pos, jnp.zeros((8, LANES - received), F32)], axis=1),
            jnp.zeros((LANES - 8, LANES), F32),
        ],
        axis=0,
    ).T
    list_len = width
    list_at = layers + 2
    counts = []
    for block in range(n_blocks):
        live = iota((1, list_len), 1).astype(F32) < small_rows[list_at + n_blocks : list_at + n_blocks + 1, block : block + 1]
        named = jnp.where(live, small_rows[list_at + block : list_at + block + 1], -1.0)
        hits = jnp.where(iota((received, list_len), 0).astype(F32) == named, 1.0, 0.0)
        counts.append(
            jnp.broadcast_to(jnp.sum(hits, axis=1, keepdims=True), (received, PB))
        )
    counts = jnp.concatenate(counts, axis=1)
    probes = n_blocks * PB
    number = me * probes + iota((1, probes), 1)
    grid = [
        (n % 16).astype(F32) * 0.25 - 1.875 for n in (number, number // 16, number // 256)
    ]
    dist_sq = jnp.zeros((received, probes), F32)
    for x in range(3):
        dist_sq = dist_sq + (grid[x] - pos_cols[0:received, x : x + 1]) ** 2
    dist = jnp.sqrt(dist_sq) * ROOT
    envelope = (1.0 - dist_sq / 64.0) ** 2 * counts
    probe_basis = jnp.concatenate(
        [
            (bell(dist, r * (ROOT * 7.0 / (n_basis - 1))) * envelope).astype(BF16)
            for r in range(n_basis)
        ],
        axis=0,
    )
    terms_shape = (2 * n_basis, n_basis * received)
    probe_weight = radial_all[:, 3 * layers * n_basis :]
    w_scalar, w_vector = (
        dot(probe_weight, one_hot(iota(terms_shape, 1) // received * 2 + p == iota(terms_shape, 0)))
        for p in range(2)
    )

    for group in range(groups):
        for c in range(2):
            place = part if c == 0 else 1 - part
            rows = pl.ds(pl.multiple_of(place * half, half), half)
            state0[rows, group * LANES : (group + 1) * LANES] = data(group, c, slice(0, half))
    hidden = silu(dot_tn(w_in[0], state0[...]) + columns[:, 0:1]).astype(BF16)
    weight_ac = jnp.concatenate([weight(0, 0), weight(0, 2)], axis=0)
    messages = dot(weight_ac, hidden).astype(BF16)
    atom_col = lane_atom(iota((LANES, 2 * rim), 0), fan, tiles).astype(F32)
    for group in range(groups):
        own = messages[:, group * LANES : (group + 1) * LANES]
        own0[group] = own
        border_row = border_of(group)
        faces0[group, :, 0 : 2 * rim] = dot(own, one_hot(atom_col == border_row)).astype(BF16)

    row = iota((LANES + 2 * rim, 1), 0)
    names = jnp.where(
        row < LANES,
        lane_atom(row, fan, tiles),
        jnp.where(row < LANES + rim, row + rim, row - rim),
    ).astype(F32)
    names = jnp.broadcast_to(names, (LANES + 2 * rim, LANES)).astype(BF16)
    upper_lane = iota((2 * width, 2 * rim), 1) < rim
    radial_ac = jnp.concatenate([radial_weight(0, 0), radial_weight(0, 2)], axis=0)

    for group in range(groups):
        up = (group + 1) % groups
        low = (group + groups - 1) % groups
        ghosts = jnp.where(
            upper_lane,
            faces0[up, :, 0 : 2 * rim].astype(F32),
            faces0[low, :, 0 : 2 * rim].astype(F32),
        ).astype(BF16)
        table = jnp.concatenate([own0[group], ghosts], axis=1)
        halves = edge_rows(group)
        step = fan // 2
        acc = jnp.zeros((width, LANES), F32)
        acc_vec = [jnp.zeros((width, LANES), F32) for _ in range(3)]
        for c in range(2):
            rows = halves[c]
            vec = [rows[x * step : (x + 1) * step] for x in range(3)]
            nbr = rows[4 * step : 5 * step]
            length_sq = vec[0] * vec[0] + vec[1] * vec[1] + vec[2] * vec[2]
            length = jnp.sqrt(length_sq) + rows[3 * step : 4 * step]
            env = (1.0 - length * length / 36.0) ** 2
            for pair in range(step // 2):
                ks = (2 * pair, 2 * pair + 1)
                picked = jnp.concatenate([same(names, nbr[k : k + 1].astype(BF16)) for k in ks], axis=1)
                basis = jnp.concatenate(
                    [basis_of(length[k : k + 1], env[k : k + 1]) for k in ks], axis=1
                )
                prod = dot(table, picked) * dot(radial_ac, basis)
                for i, k in enumerate(ks):
                    block = prod[:, i * LANES : (i + 1) * LANES]
                    acc = acc + block[:width]
                    for x in range(3):
                        acc_vec[x] = acc_vec[x] + block[width:] * vec[x][k : k + 1]
        lanes = slice(group * LANES, (group + 1) * LANES)
        state1[0:width, lanes] = (state0[:, lanes].astype(F32) + acc / root_fan).astype(BF16)
        for x in range(3):
            state1[(x + 1) * width : (x + 2) * width, lanes] = (acc_vec[x] / root_fan).astype(BF16)

    hidden = silu(dot_tn(w_in[1], state1[0:width, :]) + columns[:, 1:2]).astype(BF16)
    for p in range(3):
        table1[p * width : (p + 1) * width, :] = dot(weight(1, p), hidden).astype(BF16)
    table1[3 * width :, :] = state1[width:, :]

    rows = []
    for h in range(2):
        near_table = jnp.concatenate(
            [table1[:, g * LANES : (g + 1) * LANES] for g in window[h]], axis=1
        )
        rows.append(dot(near_table, window_pick[h]))
    rows = jnp.concatenate(rows, axis=1)
    radial_abc = jnp.concatenate([radial_weight(1, p) for p in range(3)], axis=0)
    filters = dot(radial_abc, basis1)
    gate = rows[width : 2 * width] * filters[width : 2 * width]
    along = rows[2 * width : 3 * width] * filters[2 * width :]
    parts = [rows[:width] * filters[:width]]
    for x in range(3):
        parts.append(rows[(3 + x) * width : (4 + x) * width] * gate + along * pick_vec[x])
    parts = jnp.concatenate(parts, axis=0).astype(BF16)
    edge = iota((edges, received), 0)
    slot = (edge // per_group) * cap + edge % cap
    delta = dot(parts, one_hot(slot == iota((edges, received), 1)))
    final = (dot(state1[...], chosen_atoms) + delta / root_fan).astype(BF16).astype(F32)

    along = final[width : 2 * width] * pos[0:1]
    for x in range(1, 3):
        along = along + final[(x + 1) * width : (x + 2) * width] * pos[x : x + 1]
    def repeat(value):
        return jnp.concatenate([value] * n_basis, axis=1)
    terms = [w_scalar * repeat(final[:width]) - w_vector * repeat(along)]
    for x in range(3):
        terms.append(w_vector * repeat(final[(x + 1) * width : (x + 2) * width]))
    sums = dot(jnp.concatenate(terms, axis=0).astype(BF16), probe_basis)
    charges = sums[:width]
    for x in range(3):
        charges = charges + grid[x] * sums[(x + 1) * width : (x + 2) * width]
    mixed = dot_tn(w_mix[...], charges.astype(BF16)) + columns[:, layers : layers + 1]
    density[...] = jnp.sum(silu(mixed) * columns[:, layers + 1 : layers + 2], axis=0, keepdims=True)


def few_groups(
    atom_s, atom_pos, edge_vec, edge_nbr, border_index, send_index, probe_list, probe_count,
    w_in, b_in, w_msg, w_rad, w_probe, w_mix, b_mix, w_out,
):
    atoms, half = atom_s.shape
    groups = lax.axis_size("brick") * lax.axis_size("probe")
    fan = edge_nbr.shape[0] // atoms
    rim = border_index.shape[0] // 2
    n_basis = w_rad.shape[1]
    cap = send_index.shape[1] // groups
    width = 2 * half
    every = groups * LANES
    swap = [(0, 1), (1, 0)]
    data = pack(groups, atom_s, atom_pos, edge_vec, edge_nbr, border_index, send_index)
    weights, small = pack_weights(
        half, w_msg, w_rad, w_probe, b_in, b_mix, w_out, probe_list, probe_count
    )
    weights_other = lax.ppermute(weights, "chan", swap)
    mine = lax.all_to_all(data, ("brick", "probe"), split_axis=0, concat_axis=0, tiled=True)
    other = lax.ppermute(mine, "chan", swap)
    n_probes = probe_list.shape[0] * PB
    density = pl.pallas_call(
        functools.partial(density_kernel, (groups, fan, rim, half, n_basis, cap, probe_list.shape[0])),
        out_shape=jax.ShapeDtypeStruct((1, n_probes), F32),
                scratch_shapes=[
            pltpu.VMEM((width, every), BF16),
            pltpu.VMEM((groups, 2 * width, LANES), BF16),
            pltpu.VMEM((groups, 2 * width, LANES), BF16),
            pltpu.VMEM((4 * width, every), BF16),
            pltpu.VMEM((6 * width, every), BF16),
            pltpu.VMEM((2,) + weights.shape, BF16),
        ],
        compiler_params=pltpu.CompilerParams(vmem_limit_bytes=40 * 1024 * 1024),
        name="density",
    )(mine, other, weights, weights_other, small, w_in, w_mix)
    return density.reshape(n_probes)


def per_device(*args):
    if lax.axis_size("brick") * lax.axis_size("probe") == FEW_GROUPS:
        return few_groups(*args)
    return many_groups(*args)


def extended(block, sides, width):
    for axis, dim in sides:
        count = lax.axis_size(axis)
        forward = [(i, i + 1) for i in range(count - 1)]
        forward.append((count - 1, 0))
        backward = [(target, source) for source, target in forward]
        low = lax.ppermute(
            lax.slice_in_dim(block, block.shape[dim] - width, None, axis=dim), axis, forward
        )
        high = lax.ppermute(lax.slice_in_dim(block, 0, width, axis=dim), axis, backward)
        block = jnp.concatenate([low, block, high], axis=dim)
    return block


def radial(distance, count, top):
    centers = jnp.arange(count).astype(jnp.float32) * (top / (count - 1))
    return jnp.exp(-2.0 * (distance[..., None] - centers) ** 2)


def make_block(
    recv_rows, recv_pos, w_scalar, w_vector, feat_width, group_no, n_blocks, list_len, n_basis
):

    def probe_block(block_in):
        block_no, listed, live_count = block_in
        index_row = (group_no * n_blocks + block_no) * PB + jnp.arange(PB, dtype=jnp.int32)
        grid_xyz = (
            jnp.stack([index_row % 16, index_row // 16 % 16, index_row // 256 % 16], axis=1).astype(
                jnp.float32
            )
            * 0.25
        )
        atom_xyz = recv_pos[:, listed]
        disp = grid_xyz[:, :, None] - atom_xyz[None]
        dist_sq = jnp.sum(disp * disp, axis=1)
        live = (jnp.arange(list_len, dtype=jnp.int32) < live_count).astype(jnp.float32)
        envelope = (1.0 - dist_sq / 64.0) ** 2 * live[None, :]
        basis = radial(jnp.sqrt(dist_sq), n_basis, 7.0) * envelope[:, :, None]
        scalar_w = basis.astype(jnp.bfloat16).reshape(PB, list_len * n_basis)
        vector_w = (
            (disp[:, :, :, None] * basis[:, None])
            .astype(jnp.bfloat16)
            .reshape(PB, 3 * list_len * n_basis)
        )
        atom_rows = recv_rows[listed]
        atom_terms = (atom_rows[:, None, :feat_width] * w_scalar[None]).reshape(
            list_len * n_basis, feat_width
        )
        vec_rows = jnp.transpose(
            atom_rows[:, feat_width:].reshape(list_len, 3, feat_width), (1, 0, 2)
        )
        vector_terms = (vec_rows[:, :, None, :] * w_vector[None, None]).reshape(
            3 * list_len * n_basis, feat_width
        )
        charge = jnp.dot(scalar_w, atom_terms, preferred_element_type=jnp.float32) + jnp.dot(
            vector_w, vector_terms, preferred_element_type=jnp.float32
        )
        return charge.astype(jnp.bfloat16)

    return probe_block


def many_groups(
    atom_s,
    atom_pos,
    edge_vec,
    edge_nbr,
    border_index,
    send_index,
    probe_list,
    probe_count,
    w_in,
    b_in,
    w_msg,
    w_rad,
    w_probe,
    w_mix,
    b_mix,
    w_out,
):
    atom_count, half_width = atom_s.shape
    n_layers = w_in.shape[0]
    width = w_in.shape[1]
    n_basis = w_rad.shape[1]
    fan_out = edge_nbr.shape[0] // atom_count
    root_fan = fan_out**0.5
    rim_rows = border_index.shape[0] // 2
    length = jnp.sqrt(jnp.sum(edge_vec * edge_vec, axis=0))
    edge_env = (1.0 - length * length / 36.0) ** 2
    edge_basis = (radial(length, n_basis, 6.0) * edge_env[:, None]).astype(jnp.bfloat16)
    edge_cols = jnp.transpose(edge_vec)
    scalars = atom_s
    vectors = jnp.zeros((atom_count, 3 * half_width), jnp.bfloat16)
    for layer_no in range(n_layers):
        full_rows = lax.all_gather(scalars, "chan", axis=1, tiled=True)
        in_weight = w_in[layer_no]
        in_bias = b_in[layer_no]
        msg_weight = w_msg[layer_no].reshape(width, 3 * half_width)
        rad_weight = w_rad[layer_no].reshape(n_basis, 3 * half_width)
        hidden_act = jax.nn.silu(
            jnp.dot(full_rows, in_weight, preferred_element_type=jnp.float32) + in_bias
        ).astype(jnp.bfloat16)
        inner_tab = jnp.concatenate(
            [
                jnp.dot(hidden_act, msg_weight, preferred_element_type=jnp.float32).astype(
                    jnp.bfloat16
                ),
                vectors,
            ],
            axis=1,
        )
        padded = extended(inner_tab[border_index], ((("brick", "probe"), 0),), rim_rows)
        lookup = jnp.concatenate([inner_tab, padded[:rim_rows], padded[3 * rim_rows :]], axis=0)
        neighbour_rows = lookup[edge_nbr]
        filters = jnp.dot(edge_basis, rad_weight, preferred_element_type=jnp.float32)
        weighted = neighbour_rows[:, : 3 * half_width] * filters
        neighbour_vec = neighbour_rows[:, 3 * half_width :].reshape(-1, 3, half_width)
        vector_gate = weighted[:, None, half_width : 2 * half_width]
        along_edge = weighted[:, None, 2 * half_width :]
        delta_vec = neighbour_vec * vector_gate + along_edge * edge_cols[:, :, None]
        delta_scalar = (
            weighted[:, :half_width].reshape(atom_count, fan_out, half_width).sum(axis=1) / root_fan
        )
        delta_vec = delta_vec.reshape(atom_count, fan_out, 3 * half_width).sum(axis=1) / root_fan
        scalars = (scalars + delta_scalar).astype(jnp.bfloat16)
        vectors = (vectors + delta_vec).astype(jnp.bfloat16)
    features = jnp.concatenate([scalars, vectors], axis=1)
    picks = send_index[0]
    n_brick = lax.axis_size("brick")
    n_probe = lax.axis_size("probe")
    n_groups = n_brick * n_probe
    slot_cap = picks.shape[0] // n_groups
    out_rows = features[picks]
    out_pos = jnp.transpose(atom_pos)[picks].astype(jnp.bfloat16)
    received = (
        lax.all_to_all(
            out_rows.reshape(n_groups, slot_cap, 4 * half_width),
            ("brick", "probe"),
            split_axis=0,
            concat_axis=0,
            tiled=True,
        ),
        lax.all_to_all(
            out_pos.reshape(n_groups, slot_cap, 3),
            ("brick", "probe"),
            split_axis=0,
            concat_axis=0,
            tiled=True,
        ),
    )
    recv_count = n_groups * slot_cap
    recv_rows = received[0].reshape(recv_count, 4 * half_width)
    recv_pos = jnp.transpose(received[1].reshape(recv_count, 3)).astype(jnp.float32)
    group_no = lax.axis_index("brick") * n_probe + lax.axis_index("probe")
    n_blocks, list_len = probe_list.shape
    probe_block = make_block(
        recv_rows,
        recv_pos,
        w_probe[:, 0, :],
        w_probe[:, 1, :],
        half_width,
        group_no,
        n_blocks,
        list_len,
        n_basis,
    )
    charges = lax.map(
        probe_block, (jnp.arange(n_blocks, dtype=jnp.int32), probe_list, probe_count)
    ).reshape(n_blocks * PB, half_width)
    mix_rows = lax.dynamic_slice_in_dim(w_mix, lax.axis_index("chan") * half_width, half_width, 0)
    mixed = lax.psum(jnp.dot(charges, mix_rows, preferred_element_type=jnp.float32), "chan")
    return jnp.sum(jax.nn.silu(mixed + b_mix) * w_out, axis=1)


def solution(mesh):
    in_specs = (
        P(("image", "brick", "probe"), "chan"),
        P(None, ("image", "brick", "probe")),
        P(None, ("image", "brick", "probe")),
        P(("image", "brick", "probe")),
        P(("image", "brick", "probe")),
        P(("image", "brick", "probe"), None),
        P(("image", "brick", "probe"), None),
        P(("image", "brick", "probe")),
        P(),
        P(),
        P(None, None, None, "chan"),
        P(None, None, None, "chan"),
        P(None, None, "chan"),
        P(),
        P(),
        P(),
    )
    out_specs = P(("image", "brick", "probe"))
    return jax.shard_map(
        per_device, mesh=mesh, in_specs=in_specs, out_specs=out_specs, check_vma=False
    )
```

```python
import functools
import math

import jax
import jax.numpy as jnp
from jax import lax
from jax.experimental import pallas as pl
from jax.experimental.pallas import tpu as pltpu
from jax.sharding import PartitionSpec as P

PB = 128
LANES = 128
FEW_GROUPS = 8
SMALL = 16
ROOT = (2.0 * math.log2(math.e)) ** 0.5
F32 = jnp.float32
BF16 = jnp.bfloat16


def iota(shape, dim):
    return lax.broadcasted_iota(jnp.int32, shape, dim)


def dot(a, b):
    return jnp.dot(a, b, preferred_element_type=F32)


def dot_tn(a, b):
    return lax.dot_general(a, b, (((0,), (0,)), ((), ())), preferred_element_type=F32)


def one_hot(mask):
    return jnp.where(mask, 1.0, 0.0).astype(BF16)


def same(names, row):
    return jnp.where(names == row, jnp.ones_like(names), jnp.zeros_like(names))


def silu(x):
    half_x = 0.5 * x
    return half_x * jnp.tanh(half_x) + half_x


def bell(scaled, center):
    away = scaled - center
    return jnp.exp2(-(away * away))


def lane_atom(lane, fan, tiles):
    return (lane % tiles) * (LANES // fan) + lane // tiles


def pack_kernel(
    fan, atom_s, atom_pos, edge_vec, edge_nbr, border, send, w_msg, w_rad, w_probe,
    b_in, b_mix, w_out, probe_list, probe_count, data_out, weight_out, small_out, natural,
):
    half, atoms = atom_s.shape
    tiles = atoms * fan // LANES
    per_tile = LANES // fan
    part = lax.axis_index("chan")
    perm = one_hot(lane_atom(iota((atoms, LANES), 1), fan, tiles) == iota((atoms, LANES), 0))
    scalars = dot(atom_s[...], perm).astype(BF16)
    vec = edge_vec[...]
    vec_high = vec.astype(BF16).astype(F32)
    length = jnp.sqrt(jnp.sum(vec * vec, axis=0, keepdims=True))
    short = length - jnp.sqrt(jnp.sum(vec_high * vec_high, axis=0, keepdims=True))
    rows = jnp.concatenate([vec_high, short], axis=0)
    for tile in range(tiles):
        for comp in range(4):
            natural[comp * tiles + tile : comp * tiles + tile + 1, :] = rows[
                comp : comp + 1, tile * LANES : (tile + 1) * LANES
            ]
    natural[4 * tiles : 5 * tiles, :] = edge_nbr[...].astype(F32)
    natural[5 * tiles :, :] = jnp.zeros((LANES - 5 * tiles, LANES), F32)
    turned = natural[...].T
    lane = iota((fan, LANES), 1)
    sorted_rows = []
    for comp in range(5):
        rows = jnp.zeros((fan, LANES), F32)
        for a in range(per_tile):
            piece = turned[a * fan : (a + 1) * fan, :]
            shift = (a * tiles - comp * tiles) % LANES
            piece = pltpu.roll(piece, shift, 1) if shift else piece
            rows = jnp.where(lane // tiles == a, piece, rows)
        sorted_rows.append(jnp.where(part == 0, rows[: fan // 2], rows[fan // 2 :]))
    pos = dot(atom_pos[...].astype(BF16), perm)
    blank = jnp.zeros((1, LANES), F32)
    border_row = jnp.concatenate(
        [border[...].astype(F32), jnp.zeros((1, LANES - border.shape[1]), F32)], axis=1
    )
    send_row = jnp.concatenate(
        [send[...].astype(F32), jnp.zeros((1, LANES - send.shape[1]), F32)], axis=1
    )
    rest = jnp.concatenate([pos, border_row, send_row, blank, blank, blank], axis=0)
    others = jnp.concatenate(sorted_rows + [rest], axis=0).astype(BF16)
    for group in range(data_out.shape[0]):
        data_out[group, 0:half, :] = scalars
        data_out[group, half:, :] = others
    at = 0
    for piece in (b_in, b_mix, w_out, probe_list, probe_count):
        rows, cols = piece.shape
        small_out[at : at + rows, 0:cols] = piece[...].astype(F32)
        at += rows
    probe_rows = [w_probe[r].astype(F32) for r in range(w_probe.shape[0])]
    radial = jnp.concatenate([w_rad[...].astype(F32)] + probe_rows, axis=0).T.astype(BF16)
    weight_out[: w_msg.shape[0], :] = w_msg[...]
    weight_out[w_msg.shape[0] :, :] = radial


def pack(
    groups, atom_s, atom_pos, edge_vec, edge_nbr, border_index, send_index, w_msg, w_rad, w_probe,
    b_in, b_mix, w_out, probe_list, probe_count,
):
    atoms, half = atom_s.shape
    fan = edge_nbr.shape[0] // atoms
    return pl.pallas_call(
        functools.partial(pack_kernel, fan),
        out_shape=(
            jax.ShapeDtypeStruct((groups, half + 5 * fan // 2 + 8, LANES), BF16),
            jax.ShapeDtypeStruct((w_msg.size // LANES + half, LANES), BF16),
            jax.ShapeDtypeStruct((SMALL, LANES), F32),
        ),
        scratch_shapes=[pltpu.VMEM((LANES, LANES), F32)],
        name="pack",
    )(
        atom_s.T,
        atom_pos,
        edge_vec,
        edge_nbr.reshape(-1, LANES),
        border_index.reshape(1, -1),
        send_index,
        jnp.transpose(w_msg, (0, 2, 3, 1)).reshape(-1, LANES),
        jnp.transpose(w_rad, (0, 2, 1, 3)).reshape(-1, half),
        w_probe,
        b_in,
        b_mix.reshape(1, -1),
        w_out.reshape(1, -1),
        probe_list,
        probe_count.reshape(1, -1),
    )


def density_kernel(
    sizes,
    data_mine,
    data_other,
    weights_mine,
    weights_other,
    small_from,
    w_in_from,
    w_mix_from,
    density,
    state0,
    own0,
    faces0,
    state1,
    weights,
    small,
    w_in,
    w_mix,
    sems,
):
    groups, fan, rim, half, n_basis, cap, n_blocks = sizes
    layers = w_in.shape[0]
    width = 2 * half
    tiles = LANES * fan // LANES
    root_fan = fan**0.5
    me = lax.axis_index("brick") * lax.axis_size("probe") + lax.axis_index("probe")
    part = lax.axis_index("chan")
    moves = [
        (weights_mine, weights.at[part]),
        (weights_other, weights.at[1 - part]),
        (small_from, small),
        (w_in_from, w_in),
        (w_mix_from, w_mix),
    ]
    moves = [pltpu.make_async_copy(*move, sems.at[i]) for i, move in enumerate(moves)]
    for move in moves:
        move.start()
    every = groups * LANES
    edge_at = half
    n_edge = 5 * fan // 2
    rest_at = half + n_edge

    def data(group, c, rows):
        return (data_mine, data_other)[c][group, rows, :]

    def weight(layer, p):
        at = (layer * 3 + p) * half
        return jnp.concatenate([weights[c, at : at + half, :] for c in range(2)], axis=0)

    def radial_weight(layer, p):
        at = (layer * 3 + p) * n_basis
        return radial_all[:, at : at + n_basis]

    def edge_rows(group):
        return [data(group, c, slice(edge_at, rest_at)).astype(F32) for c in range(2)]

    def border_of(group):
        return data(group, 0, slice(rest_at, rest_at + 8)).astype(F32)[3:4, 0 : 2 * rim]

    centers = iota((n_basis, 1), 0).astype(F32) * (ROOT * 6.0 / (n_basis - 1))

    def basis_of(length, env):
        return (bell(length * ROOT, centers) * env).astype(BF16)

    received = groups * cap
    edges = received * fan
    send_rows = jnp.concatenate(
        [data(g, 0, slice(rest_at, rest_at + 8)).astype(F32)[4:5] for g in range(groups)], axis=0
    )

    def picks(lane_count, per_group):
        lane = iota((LANES, lane_count), 1)
        wanted = me * cap + lane % cap
        spread = dot(send_rows.astype(BF16), one_hot(iota((LANES, lane_count), 0) == wanted))
        lane = iota((groups, lane_count), 1)
        spread = jnp.where(lane // per_group == iota((groups, lane_count), 0), spread, 0.0)
        return jnp.sum(spread, axis=0, keepdims=True)

    per_group = fan * cap
    pick_edges = picks(edges, per_group)
    pick_atoms = picks(received, cap)
    atom_rows = lane_atom(iota((LANES, per_group), 0), fan, tiles).astype(F32)
    chosen = []
    for group in range(groups):
        rows = jnp.concatenate([data(group, c, slice(edge_at, rest_at)) for c in range(2)], axis=0)
        want = pick_edges[:, group * per_group : (group + 1) * per_group]
        chosen.append(dot(rows, one_hot(atom_rows == want)))
    chosen = jnp.concatenate(chosen, axis=1)
    step = fan // 2
    row = iota((2 * n_edge, edges), 0)
    slot_k = (row // n_edge) * step + row % step
    lane_k = (iota((2 * n_edge, edges), 1) % per_group) // cap
    chosen = jnp.where(slot_k == lane_k, chosen, 0.0)
    chosen = jnp.sum(chosen.reshape(2 * 5, step, edges), axis=1)
    chosen = chosen[0:5] + chosen[5:10]
    pick_vec = [chosen[x : x + 1] for x in range(3)]
    nbr = chosen[4:5]
    length = jnp.sqrt(sum(x * x for x in pick_vec)) + chosen[3:4]
    basis1 = basis_of(length, (1.0 - length * length / 36.0) ** 2)

    nbr = nbr.astype(jnp.int32)
    home = iota((1, edges), 1) // per_group
    is_low = (nbr >= LANES) & (nbr < LANES + rim)
    is_up = nbr >= LANES + rim
    owner = jnp.where(
        is_low, (home + groups - 1) % groups, jnp.where(is_up, (home + 1) % groups, home)
    )
    entry = owner * 2 * rim + jnp.where(is_low, nbr - (LANES - rim), nbr - (LANES + rim))
    entry = jnp.where(is_low | is_up, entry, -1)
    border_all = jnp.concatenate(
        [border_of(g) for g in range(groups)], axis=1
    )
    border_all = jnp.broadcast_to(border_all, (16, groups * 2 * rim)).astype(BF16)
    seen = dot(border_all, one_hot(iota((groups * 2 * rim, edges), 0) == entry))[0:1]
    target_atom = jnp.where(entry < 0, nbr, seen.astype(jnp.int32))
    column = iota((every, 1), 0)
    column_name = (column // LANES) * LANES + lane_atom(column % LANES, fan, tiles)
    quad = groups // 2
    window = [[(h * quad + groups - 1 + i) % groups for i in range(quad + 2)] for h in range(2)]
    window_pick = []
    for h in range(2):
        lanes = slice(h * edges // 2, (h + 1) * edges // 2)
        near = lax.rem(owner[:, lanes] + 2 * groups - (h * quad + groups - 1), groups)
        name = near * LANES + target_atom[:, lanes]
        window_pick.append(one_hot(column_name[: (quad + 2) * LANES] == name))
    wanted = (iota((1, received), 1) // cap) * LANES + pick_atoms.astype(jnp.int32)
    chosen_atoms = one_hot(column_name == wanted)

    for move in moves:
        move.wait()
    small_rows = small[...]
    columns = small_rows.T
    radial_at = weights.shape[1] - half
    radial_all = jnp.concatenate([weights[c, radial_at:, :] for c in range(2)], axis=0)

    pos_rows = jnp.concatenate(
        [data(g, 0, slice(rest_at, rest_at + 8)) for g in range(groups)], axis=1
    )
    pos = dot(pos_rows, chosen_atoms) - 1.875
    pos_cols = jnp.concatenate(
        [
            jnp.concatenate([pos, jnp.zeros((8, LANES - received), F32)], axis=1),
            jnp.zeros((LANES - 8, LANES), F32),
        ],
        axis=0,
    ).T
    list_len = width
    list_at = layers + 2
    counts = []
    for block in range(n_blocks):
        live = iota((1, list_len), 1).astype(F32) < small_rows[list_at + n_blocks : list_at + n_blocks + 1, block : block + 1]
        named = jnp.where(live, small_rows[list_at + block : list_at + block + 1], -1.0)
        hits = jnp.where(iota((received, list_len), 0).astype(F32) == named, 1.0, 0.0)
        counts.append(
            jnp.broadcast_to(jnp.sum(hits, axis=1, keepdims=True), (received, PB))
        )
    counts = jnp.concatenate(counts, axis=1)
    probes = n_blocks * PB
    number = me * probes + iota((1, probes), 1)
    grid = [
        (n % 16).astype(F32) * 0.25 - 1.875 for n in (number, number // 16, number // 256)
    ]
    dist_sq = jnp.zeros((received, probes), F32)
    for x in range(3):
        dist_sq = dist_sq + (grid[x] - pos_cols[0:received, x : x + 1]) ** 2
    dist = jnp.sqrt(dist_sq) * ROOT
    envelope = (1.0 - dist_sq / 64.0) ** 2 * counts
    probe_basis = jnp.concatenate(
        [
            (bell(dist, r * (ROOT * 7.0 / (n_basis - 1))) * envelope).astype(BF16)
            for r in range(n_basis)
        ],
        axis=0,
    )
    terms_shape = (2 * n_basis, n_basis * received)
    probe_weight = radial_all[:, 3 * layers * n_basis :]
    w_scalar, w_vector = (
        dot(probe_weight, one_hot(iota(terms_shape, 1) // received * 2 + p == iota(terms_shape, 0)))
        for p in range(2)
    )

    for group in range(groups):
        for c in range(2):
            place = part if c == 0 else 1 - part
            rows = pl.ds(pl.multiple_of(place * half, half), half)
            state0[rows, group * LANES : (group + 1) * LANES] = data(group, c, slice(0, half))
    hidden = silu(dot_tn(w_in[0], state0[...]) + columns[:, 0:1]).astype(BF16)
    weight_ac = jnp.concatenate([weight(0, 0), weight(0, 2)], axis=0)
    messages = dot(weight_ac, hidden).astype(BF16)
    atom_col = lane_atom(iota((LANES, 2 * rim), 0), fan, tiles).astype(F32)
    for group in range(groups):
        own = messages[:, group * LANES : (group + 1) * LANES]
        own0[group] = own
        border_row = border_of(group)
        faces0[group, :, 0 : 2 * rim] = dot(own, one_hot(atom_col == border_row)).astype(BF16)

    row = iota((LANES + 2 * rim, 1), 0)
    names = jnp.where(
        row < LANES,
        lane_atom(row, fan, tiles),
        jnp.where(row < LANES + rim, row + rim, row - rim),
    ).astype(F32)
    names = jnp.broadcast_to(names, (LANES + 2 * rim, LANES)).astype(BF16)
    upper_lane = iota((2 * width, 2 * rim), 1) < rim
    radial_ac = jnp.concatenate([radial_weight(0, 0), radial_weight(0, 2)], axis=0)

    for group in range(groups):
        up = (group + 1) % groups
        low = (group + groups - 1) % groups
        ghosts = jnp.where(
            upper_lane,
            faces0[up, :, 0 : 2 * rim].astype(F32),
            faces0[low, :, 0 : 2 * rim].astype(F32),
        ).astype(BF16)
        table = jnp.concatenate([own0[group], ghosts], axis=1)
        halves = edge_rows(group)
        step = fan // 2
        acc = jnp.zeros((width, LANES), F32)
        acc_vec = [jnp.zeros((width, LANES), F32) for _ in range(3)]
        for c in range(2):
            rows = halves[c]
            vec = [rows[x * step : (x + 1) * step] for x in range(3)]
            nbr = rows[4 * step : 5 * step]
            length_sq = vec[0] * vec[0] + vec[1] * vec[1] + vec[2] * vec[2]
            length = jnp.sqrt(length_sq) + rows[3 * step : 4 * step]
            env = (1.0 - length * length / 36.0) ** 2
            for pair in range(step // 2):
                ks = (2 * pair, 2 * pair + 1)
                picked = jnp.concatenate([same(names, nbr[k : k + 1].astype(BF16)) for k in ks], axis=1)
                basis = jnp.concatenate(
                    [basis_of(length[k : k + 1], env[k : k + 1]) for k in ks], axis=1
                )
                prod = dot(table, picked) * dot(radial_ac, basis)
                for i, k in enumerate(ks):
                    block = prod[:, i * LANES : (i + 1) * LANES]
                    acc = acc + block[:width]
                    for x in range(3):
                        acc_vec[x] = acc_vec[x] + block[width:] * vec[x][k : k + 1]
        lanes = slice(group * LANES, (group + 1) * LANES)
        state1[0:width, lanes] = (state0[:, lanes].astype(F32) + acc / root_fan).astype(BF16)
        for x in range(3):
            state1[(x + 1) * width : (x + 2) * width, lanes] = (acc_vec[x] / root_fan).astype(BF16)

    rows = []
    for h in range(2):
        near_states = jnp.concatenate(
            [state1[:, g * LANES : (g + 1) * LANES] for g in window[h]], axis=1
        )
        rows.append(dot(near_states, window_pick[h]))
    rows = jnp.concatenate(rows, axis=1)
    hidden = silu(dot_tn(w_in[1], rows[:width].astype(BF16)) + columns[:, 1:2]).astype(BF16)
    weight_abc = jnp.concatenate([weight(1, p) for p in range(3)], axis=0)
    messages = dot(weight_abc, hidden).astype(BF16).astype(F32)
    radial_abc = jnp.concatenate([radial_weight(1, p) for p in range(3)], axis=0)
    filters = dot(radial_abc, basis1)
    weighted = messages * filters
    gate = weighted[width : 2 * width]
    along = weighted[2 * width :]
    parts = [weighted[:width]]
    for x in range(3):
        parts.append(rows[(1 + x) * width : (2 + x) * width] * gate + along * pick_vec[x])
    parts = jnp.concatenate(parts, axis=0).astype(BF16)
    edge = iota((edges, received), 0)
    slot = (edge // per_group) * cap + edge % cap
    delta = dot(parts, one_hot(slot == iota((edges, received), 1)))
    final = (dot(state1[...], chosen_atoms) + delta / root_fan).astype(BF16).astype(F32)

    along = final[width : 2 * width] * pos[0:1]
    for x in range(1, 3):
        along = along + final[(x + 1) * width : (x + 2) * width] * pos[x : x + 1]
    def repeat(value):
        return jnp.concatenate([value] * n_basis, axis=1)
    terms = [w_scalar * repeat(final[:width]) - w_vector * repeat(along)]
    for x in range(3):
        terms.append(w_vector * repeat(final[(x + 1) * width : (x + 2) * width]))
    sums = dot(jnp.concatenate(terms, axis=0).astype(BF16), probe_basis)
    charges = sums[:width]
    for x in range(3):
        charges = charges + grid[x] * sums[(x + 1) * width : (x + 2) * width]
    mixed = dot_tn(w_mix[...], charges.astype(BF16)) + columns[:, layers : layers + 1]
    density[...] = jnp.sum(silu(mixed) * columns[:, layers + 1 : layers + 2], axis=0, keepdims=True)


def few_groups(
    atom_s, atom_pos, edge_vec, edge_nbr, border_index, send_index, probe_list, probe_count,
    w_in, b_in, w_msg, w_rad, w_probe, w_mix, b_mix, w_out,
):
    atoms, half = atom_s.shape
    groups = lax.axis_size("brick") * lax.axis_size("probe")
    fan = edge_nbr.shape[0] // atoms
    rim = border_index.shape[0] // 2
    n_basis = w_rad.shape[1]
    cap = send_index.shape[1] // groups
    width = 2 * half
    every = groups * LANES
    data, weights, small = pack(
        groups, atom_s, atom_pos, edge_vec, edge_nbr, border_index, send_index, w_msg, w_rad, w_probe,
        b_in, b_mix, w_out, probe_list, probe_count,
    )
    swap = [(0, 1), (1, 0)]
    weights_other = lax.ppermute(weights, "chan", swap)
    mine = lax.all_to_all(data, ("brick", "probe"), split_axis=0, concat_axis=0, tiled=True)
    other = lax.ppermute(mine, "chan", swap)
    n_probes = probe_list.shape[0] * PB
    density = pl.pallas_call(
        functools.partial(density_kernel, (groups, fan, rim, half, n_basis, cap, probe_list.shape[0])),
        out_shape=jax.ShapeDtypeStruct((1, n_probes), F32),
        in_specs=[pl.BlockSpec(memory_space=pltpu.VMEM)] * 2 + [pl.BlockSpec(memory_space=pltpu.HBM)] * 5,
        scratch_shapes=[
            pltpu.VMEM((width, every), BF16),
            pltpu.VMEM((groups, 2 * width, LANES), BF16),
            pltpu.VMEM((groups, 2 * width, LANES), BF16),
            pltpu.VMEM((4 * width, every), BF16),
            pltpu.VMEM((2,) + weights.shape, BF16),
            pltpu.VMEM(small.shape, F32),
            pltpu.VMEM(w_in.shape, BF16),
            pltpu.VMEM(w_mix.shape, BF16),
            pltpu.SemaphoreType.DMA((5,)),
        ],
        compiler_params=pltpu.CompilerParams(vmem_limit_bytes=40 * 1024 * 1024),
        name="density",
    )(mine, other, weights, weights_other, small, w_in, w_mix)
    return density.reshape(n_probes)


def per_device(*args):
    if lax.axis_size("brick") * lax.axis_size("probe") == FEW_GROUPS:
        return few_groups(*args)
    return many_groups(*args)


def extended(block, sides, width):
    for axis, dim in sides:
        count = lax.axis_size(axis)
        forward = [(i, i + 1) for i in range(count - 1)]
        forward.append((count - 1, 0))
        backward = [(target, source) for source, target in forward]
        low = lax.ppermute(
            lax.slice_in_dim(block, block.shape[dim] - width, None, axis=dim), axis, forward
        )
        high = lax.ppermute(lax.slice_in_dim(block, 0, width, axis=dim), axis, backward)
        block = jnp.concatenate([low, block, high], axis=dim)
    return block


def radial(distance, count, top):
    centers = jnp.arange(count).astype(jnp.float32) * (top / (count - 1))
    return jnp.exp(-2.0 * (distance[..., None] - centers) ** 2)


def make_block(
    recv_rows, recv_pos, w_scalar, w_vector, feat_width, group_no, n_blocks, list_len, n_basis
):

    def probe_block(block_in):
        block_no, listed, live_count = block_in
        index_row = (group_no * n_blocks + block_no) * PB + jnp.arange(PB, dtype=jnp.int32)
        grid_xyz = (
            jnp.stack([index_row % 16, index_row // 16 % 16, index_row // 256 % 16], axis=1).astype(
                jnp.float32
            )
            * 0.25
        )
        atom_xyz = recv_pos[:, listed]
        disp = grid_xyz[:, :, None] - atom_xyz[None]
        dist_sq = jnp.sum(disp * disp, axis=1)
        live = (jnp.arange(list_len, dtype=jnp.int32) < live_count).astype(jnp.float32)
        envelope = (1.0 - dist_sq / 64.0) ** 2 * live[None, :]
        basis = radial(jnp.sqrt(dist_sq), n_basis, 7.0) * envelope[:, :, None]
        scalar_w = basis.astype(jnp.bfloat16).reshape(PB, list_len * n_basis)
        vector_w = (
            (disp[:, :, :, None] * basis[:, None])
            .astype(jnp.bfloat16)
            .reshape(PB, 3 * list_len * n_basis)
        )
        atom_rows = recv_rows[listed]
        atom_terms = (atom_rows[:, None, :feat_width] * w_scalar[None]).reshape(
            list_len * n_basis, feat_width
        )
        vec_rows = jnp.transpose(
            atom_rows[:, feat_width:].reshape(list_len, 3, feat_width), (1, 0, 2)
        )
        vector_terms = (vec_rows[:, :, None, :] * w_vector[None, None]).reshape(
            3 * list_len * n_basis, feat_width
        )
        charge = jnp.dot(scalar_w, atom_terms, preferred_element_type=jnp.float32) + jnp.dot(
            vector_w, vector_terms, preferred_element_type=jnp.float32
        )
        return charge.astype(jnp.bfloat16)

    return probe_block


def many_groups(
    atom_s,
    atom_pos,
    edge_vec,
    edge_nbr,
    border_index,
    send_index,
    probe_list,
    probe_count,
    w_in,
    b_in,
    w_msg,
    w_rad,
    w_probe,
    w_mix,
    b_mix,
    w_out,
):
    atom_count, half_width = atom_s.shape
    n_layers = w_in.shape[0]
    width = w_in.shape[1]
    n_basis = w_rad.shape[1]
    fan_out = edge_nbr.shape[0] // atom_count
    root_fan = fan_out**0.5
    rim_rows = border_index.shape[0] // 2
    length = jnp.sqrt(jnp.sum(edge_vec * edge_vec, axis=0))
    edge_env = (1.0 - length * length / 36.0) ** 2
    edge_basis = (radial(length, n_basis, 6.0) * edge_env[:, None]).astype(jnp.bfloat16)
    edge_cols = jnp.transpose(edge_vec)
    scalars = atom_s
    vectors = jnp.zeros((atom_count, 3 * half_width), jnp.bfloat16)
    for layer_no in range(n_layers):
        full_rows = lax.all_gather(scalars, "chan", axis=1, tiled=True)
        in_weight = w_in[layer_no]
        in_bias = b_in[layer_no]
        msg_weight = w_msg[layer_no].reshape(width, 3 * half_width)
        rad_weight = w_rad[layer_no].reshape(n_basis, 3 * half_width)
        hidden_act = jax.nn.silu(
            jnp.dot(full_rows, in_weight, preferred_element_type=jnp.float32) + in_bias
        ).astype(jnp.bfloat16)
        inner_tab = jnp.concatenate(
            [
                jnp.dot(hidden_act, msg_weight, preferred_element_type=jnp.float32).astype(
                    jnp.bfloat16
                ),
                vectors,
            ],
            axis=1,
        )
        padded = extended(inner_tab[border_index], ((("brick", "probe"), 0),), rim_rows)
        lookup = jnp.concatenate([inner_tab, padded[:rim_rows], padded[3 * rim_rows :]], axis=0)
        neighbour_rows = lookup[edge_nbr]
        filters = jnp.dot(edge_basis, rad_weight, preferred_element_type=jnp.float32)
        weighted = neighbour_rows[:, : 3 * half_width] * filters
        neighbour_vec = neighbour_rows[:, 3 * half_width :].reshape(-1, 3, half_width)
        vector_gate = weighted[:, None, half_width : 2 * half_width]
        along_edge = weighted[:, None, 2 * half_width :]
        delta_vec = neighbour_vec * vector_gate + along_edge * edge_cols[:, :, None]
        delta_scalar = (
            weighted[:, :half_width].reshape(atom_count, fan_out, half_width).sum(axis=1) / root_fan
        )
        delta_vec = delta_vec.reshape(atom_count, fan_out, 3 * half_width).sum(axis=1) / root_fan
        scalars = (scalars + delta_scalar).astype(jnp.bfloat16)
        vectors = (vectors + delta_vec).astype(jnp.bfloat16)
    features = jnp.concatenate([scalars, vectors], axis=1)
    picks = send_index[0]
    n_brick = lax.axis_size("brick")
    n_probe = lax.axis_size("probe")
    n_groups = n_brick * n_probe
    slot_cap = picks.shape[0] // n_groups
    out_rows = features[picks]
    out_pos = jnp.transpose(atom_pos)[picks].astype(jnp.bfloat16)
    received = (
        lax.all_to_all(
            out_rows.reshape(n_groups, slot_cap, 4 * half_width),
            ("brick", "probe"),
            split_axis=0,
            concat_axis=0,
            tiled=True,
        ),
        lax.all_to_all(
            out_pos.reshape(n_groups, slot_cap, 3),
            ("brick", "probe"),
            split_axis=0,
            concat_axis=0,
            tiled=True,
        ),
    )
    recv_count = n_groups * slot_cap
    recv_rows = received[0].reshape(recv_count, 4 * half_width)
    recv_pos = jnp.transpose(received[1].reshape(recv_count, 3)).astype(jnp.float32)
    group_no = lax.axis_index("brick") * n_probe + lax.axis_index("probe")
    n_blocks, list_len = probe_list.shape
    probe_block = make_block(
        recv_rows,
        recv_pos,
        w_probe[:, 0, :],
        w_probe[:, 1, :],
        half_width,
        group_no,
        n_blocks,
        list_len,
        n_basis,
    )
    charges = lax.map(
        probe_block, (jnp.arange(n_blocks, dtype=jnp.int32), probe_list, probe_count)
    ).reshape(n_blocks * PB, half_width)
    mix_rows = lax.dynamic_slice_in_dim(w_mix, lax.axis_index("chan") * half_width, half_width, 0)
    mixed = lax.psum(jnp.dot(charges, mix_rows, preferred_element_type=jnp.float32), "chan")
    return jnp.sum(jax.nn.silu(mixed + b_mix) * w_out, axis=1)


def solution(mesh):
    in_specs = (
        P(("image", "brick", "probe"), "chan"),
        P(None, ("image", "brick", "probe")),
        P(None, ("image", "brick", "probe")),
        P(("image", "brick", "probe")),
        P(("image", "brick", "probe")),
        P(("image", "brick", "probe"), None),
        P(("image", "brick", "probe"), None),
        P(("image", "brick", "probe")),
        P(),
        P(),
        P(None, None, None, "chan"),
        P(None, None, None, "chan"),
        P(None, None, "chan"),
        P(),
        P(),
        P(),
    )
    out_specs = P(("image", "brick", "probe"))
    return jax.shard_map(
        per_device, mesh=mesh, in_specs=in_specs, out_specs=out_specs, check_vma=False
    )
```

```python
import functools
import math

import jax
import jax.numpy as jnp
from jax import lax
from jax.experimental import pallas as pl
from jax.experimental.pallas import tpu as pltpu
from jax.sharding import PartitionSpec as P

PB = 128
LANES = 128
FEW_GROUPS = 8
SMALL = 16
ROOT = (2.0 * math.log2(math.e)) ** 0.5
F32 = jnp.float32
BF16 = jnp.bfloat16


def iota(shape, dim):
    return lax.broadcasted_iota(jnp.int32, shape, dim)


def dot(a, b):
    return jnp.dot(a, b, preferred_element_type=F32)


def dot_tn(a, b):
    return lax.dot_general(a, b, (((0,), (0,)), ((), ())), preferred_element_type=F32)


def one_hot(mask):
    return jnp.where(mask, 1.0, 0.0).astype(BF16)


def same(names, row):
    return jnp.where(names == row, jnp.ones_like(names), jnp.zeros_like(names))


def silu(x):
    half_x = 0.5 * x
    return half_x * jnp.tanh(half_x) + half_x


def bell(scaled, center):
    away = scaled - center
    return jnp.exp2(-(away * away))


def lane_atom(lane, fan, tiles):
    return (lane % tiles) * (LANES // fan) + lane // tiles


def pack_kernel(
    fan, atom_s, atom_pos, edge_vec, edge_nbr, border, send, w_msg, w_rad, w_probe,
    b_in, b_mix, w_out, probe_list, probe_count, data_out, weight_out, small_out, natural,
):
    half, atoms = atom_s.shape
    tiles = atoms * fan // LANES
    per_tile = LANES // fan
    part = lax.axis_index("chan")
    perm = one_hot(lane_atom(iota((atoms, LANES), 1), fan, tiles) == iota((atoms, LANES), 0))
    scalars = dot(atom_s[...], perm).astype(BF16)
    vec = edge_vec[...]
    vec_high = vec.astype(BF16).astype(F32)
    length = jnp.sqrt(jnp.sum(vec * vec, axis=0, keepdims=True))
    short = length - jnp.sqrt(jnp.sum(vec_high * vec_high, axis=0, keepdims=True))
    rows = jnp.concatenate([vec_high, short], axis=0)
    for tile in range(tiles):
        for comp in range(4):
            natural[comp * tiles + tile : comp * tiles + tile + 1, :] = rows[
                comp : comp + 1, tile * LANES : (tile + 1) * LANES
            ]
    natural[4 * tiles : 5 * tiles, :] = edge_nbr[...].astype(F32)
    natural[5 * tiles :, :] = jnp.zeros((LANES - 5 * tiles, LANES), F32)
    turned = natural[...].T
    lane = iota((fan, LANES), 1)
    sorted_rows = []
    for comp in range(5):
        rows = jnp.zeros((fan, LANES), F32)
        for a in range(per_tile):
            piece = turned[a * fan : (a + 1) * fan, :]
            shift = (a * tiles - comp * tiles) % LANES
            piece = pltpu.roll(piece, shift, 1) if shift else piece
            rows = jnp.where(lane // tiles == a, piece, rows)
        sorted_rows.append(jnp.where(part == 0, rows[: fan // 2], rows[fan // 2 :]))
    pos = dot(atom_pos[...].astype(BF16), perm)
    blank = jnp.zeros((1, LANES), F32)
    border_row = jnp.concatenate(
        [border[...].astype(F32), jnp.zeros((1, LANES - border.shape[1]), F32)], axis=1
    )
    send_row = jnp.concatenate(
        [send[...].astype(F32), jnp.zeros((1, LANES - send.shape[1]), F32)], axis=1
    )
    rest = jnp.concatenate([pos, border_row, send_row, blank, blank, blank], axis=0)
    others = jnp.concatenate(sorted_rows + [rest], axis=0).astype(BF16)
    for group in range(data_out.shape[0]):
        data_out[group, 0:half, :] = scalars
        data_out[group, half:, :] = others
    at = 0
    for piece in (b_in, b_mix, w_out, probe_list, probe_count):
        rows, cols = piece.shape
        small_out[at : at + rows, 0:cols] = piece[...].astype(F32)
        at += rows
    probe_rows = [w_probe[r].astype(F32) for r in range(w_probe.shape[0])]
    radial = jnp.concatenate([w_rad[...].astype(F32)] + probe_rows, axis=0).T.astype(BF16)
    weight_out[: w_msg.shape[0], :] = w_msg[...]
    weight_out[w_msg.shape[0] :, :] = radial


def pack(
    groups, atom_s, atom_pos, edge_vec, edge_nbr, border_index, send_index, w_msg, w_rad, w_probe,
    b_in, b_mix, w_out, probe_list, probe_count,
):
    atoms, half = atom_s.shape
    fan = edge_nbr.shape[0] // atoms
    return pl.pallas_call(
        functools.partial(pack_kernel, fan),
        out_shape=(
            jax.ShapeDtypeStruct((groups, half + 5 * fan // 2 + 8, LANES), BF16),
            jax.ShapeDtypeStruct((w_msg.size // LANES + half, LANES), BF16),
            jax.ShapeDtypeStruct((SMALL, LANES), F32),
        ),
        scratch_shapes=[pltpu.VMEM((LANES, LANES), F32)],
        name="pack",
    )(
        atom_s.T,
        atom_pos,
        edge_vec,
        edge_nbr.reshape(-1, LANES),
        border_index.reshape(1, -1),
        send_index,
        jnp.transpose(w_msg, (0, 2, 3, 1)).reshape(-1, LANES),
        jnp.transpose(w_rad, (0, 2, 1, 3)).reshape(-1, half),
        w_probe,
        b_in,
        b_mix.reshape(1, -1),
        w_out.reshape(1, -1),
        probe_list,
        probe_count.reshape(1, -1),
    )


def density_kernel(
    sizes,
    data_mine,
    data_other,
    weights_mine,
    weights_other,
    small,
    w_in,
    w_mix,
    density,
    state0,
    own0,
    faces0,
    state1,
    weights,
):
    groups, fan, rim, half, n_basis, cap, n_blocks = sizes
    layers = w_in.shape[0]
    width = 2 * half
    tiles = LANES * fan // LANES
    root_fan = fan**0.5
    me = lax.axis_index("brick") * lax.axis_size("probe") + lax.axis_index("probe")
    part = lax.axis_index("chan")
    weights[part] = weights_mine[...]
    weights[1 - part] = weights_other[...]
    every = groups * LANES
    edge_at = half
    n_edge = 5 * fan // 2
    rest_at = half + n_edge

    def data(group, c, rows):
        return (data_mine, data_other)[c][group, rows, :]

    def weight(layer, p):
        at = (layer * 3 + p) * half
        return jnp.concatenate([weights[c, at : at + half, :] for c in range(2)], axis=0)

    def radial_weight(layer, p):
        at = (layer * 3 + p) * n_basis
        return radial_all[:, at : at + n_basis]

    def edge_rows(group):
        return [data(group, c, slice(edge_at, rest_at)).astype(F32) for c in range(2)]

    def border_of(group):
        return data(group, 0, slice(rest_at, rest_at + 8)).astype(F32)[3:4, 0 : 2 * rim]

    centers = iota((n_basis, 1), 0).astype(F32) * (ROOT * 6.0 / (n_basis - 1))

    def basis_of(length, env):
        return (bell(length * ROOT, centers) * env).astype(BF16)

    received = groups * cap
    edges = received * fan
    send_rows = jnp.concatenate(
        [data(g, 0, slice(rest_at, rest_at + 8)).astype(F32)[4:5] for g in range(groups)], axis=0
    )

    def picks(lane_count, per_group):
        lane = iota((LANES, lane_count), 1)
        wanted = me * cap + lane % cap
        spread = dot(send_rows.astype(BF16), one_hot(iota((LANES, lane_count), 0) == wanted))
        lane = iota((groups, lane_count), 1)
        spread = jnp.where(lane // per_group == iota((groups, lane_count), 0), spread, 0.0)
        return jnp.sum(spread, axis=0, keepdims=True)

    per_group = fan * cap
    pick_edges = picks(edges, per_group)
    pick_atoms = picks(received, cap)
    atom_rows = lane_atom(iota((LANES, per_group), 0), fan, tiles).astype(F32)
    chosen = []
    for group in range(groups):
        rows = jnp.concatenate([data(group, c, slice(edge_at, rest_at)) for c in range(2)], axis=0)
        want = pick_edges[:, group * per_group : (group + 1) * per_group]
        chosen.append(dot(rows, one_hot(atom_rows == want)))
    chosen = jnp.concatenate(chosen, axis=1)
    step = fan // 2
    row = iota((2 * n_edge, edges), 0)
    slot_k = (row // n_edge) * step + row % step
    lane_k = (iota((2 * n_edge, edges), 1) % per_group) // cap
    chosen = jnp.where(slot_k == lane_k, chosen, 0.0)
    chosen = jnp.sum(chosen.reshape(2 * 5, step, edges), axis=1)
    chosen = chosen[0:5] + chosen[5:10]
    pick_vec = [chosen[x : x + 1] for x in range(3)]
    nbr = chosen[4:5]
    length = jnp.sqrt(sum(x * x for x in pick_vec)) + chosen[3:4]
    basis1 = basis_of(length, (1.0 - length * length / 36.0) ** 2)

    nbr = nbr.astype(jnp.int32)
    home = iota((1, edges), 1) // per_group
    is_low = (nbr >= LANES) & (nbr < LANES + rim)
    is_up = nbr >= LANES + rim
    owner = jnp.where(
        is_low, (home + groups - 1) % groups, jnp.where(is_up, (home + 1) % groups, home)
    )
    entry = owner * 2 * rim + jnp.where(is_low, nbr - (LANES - rim), nbr - (LANES + rim))
    entry = jnp.where(is_low | is_up, entry, -1)
    border_all = jnp.concatenate(
        [border_of(g) for g in range(groups)], axis=1
    )
    border_all = jnp.broadcast_to(border_all, (16, groups * 2 * rim)).astype(BF16)
    seen = dot(border_all, one_hot(iota((groups * 2 * rim, edges), 0) == entry))[0:1]
    target_atom = jnp.where(entry < 0, nbr, seen.astype(jnp.int32))
    column = iota((every, 1), 0)
    column_name = (column // LANES) * LANES + lane_atom(column % LANES, fan, tiles)
    quad = groups // 2
    window = [[(h * quad + groups - 1 + i) % groups for i in range(quad + 2)] for h in range(2)]
    window_pick = []
    for h in range(2):
        lanes = slice(h * edges // 2, (h + 1) * edges // 2)
        near = lax.rem(owner[:, lanes] + 2 * groups - (h * quad + groups - 1), groups)
        name = near * LANES + target_atom[:, lanes]
        window_pick.append(one_hot(column_name[: (quad + 2) * LANES] == name))
    wanted = (iota((1, received), 1) // cap) * LANES + pick_atoms.astype(jnp.int32)
    chosen_atoms = one_hot(column_name == wanted)

    small_rows = small[...]
    columns = small_rows.T
    radial_at = weights.shape[1] - half
    radial_all = jnp.concatenate([weights[c, radial_at:, :] for c in range(2)], axis=0)

    pos_rows = jnp.concatenate(
        [data(g, 0, slice(rest_at, rest_at + 8)) for g in range(groups)], axis=1
    )
    pos = dot(pos_rows, chosen_atoms) - 1.875
    pos_cols = jnp.concatenate(
        [
            jnp.concatenate([pos, jnp.zeros((8, LANES - received), F32)], axis=1),
            jnp.zeros((LANES - 8, LANES), F32),
        ],
        axis=0,
    ).T
    list_len = width
    list_at = layers + 2
    counts = []
    for block in range(n_blocks):
        live = iota((1, list_len), 1).astype(F32) < small_rows[list_at + n_blocks : list_at + n_blocks + 1, block : block + 1]
        named = jnp.where(live, small_rows[list_at + block : list_at + block + 1], -1.0)
        hits = jnp.where(iota((received, list_len), 0).astype(F32) == named, 1.0, 0.0)
        counts.append(
            jnp.broadcast_to(jnp.sum(hits, axis=1, keepdims=True), (received, PB))
        )
    counts = jnp.concatenate(counts, axis=1)
    probes = n_blocks * PB
    number = me * probes + iota((1, probes), 1)
    grid = [
        (n % 16).astype(F32) * 0.25 - 1.875 for n in (number, number // 16, number // 256)
    ]
    dist_sq = jnp.zeros((received, probes), F32)
    for x in range(3):
        dist_sq = dist_sq + (grid[x] - pos_cols[0:received, x : x + 1]) ** 2
    dist = jnp.sqrt(dist_sq) * ROOT
    envelope = (1.0 - dist_sq / 64.0) ** 2 * counts
    probe_basis = jnp.concatenate(
        [
            (bell(dist, r * (ROOT * 7.0 / (n_basis - 1))) * envelope).astype(BF16)
            for r in range(n_basis)
        ],
        axis=0,
    )
    terms_shape = (2 * n_basis, n_basis * received)
    probe_weight = radial_all[:, 3 * layers * n_basis :]
    w_scalar, w_vector = (
        dot(probe_weight, one_hot(iota(terms_shape, 1) // received * 2 + p == iota(terms_shape, 0)))
        for p in range(2)
    )

    for group in range(groups):
        for c in range(2):
            place = part if c == 0 else 1 - part
            rows = pl.ds(pl.multiple_of(place * half, half), half)
            state0[rows, group * LANES : (group + 1) * LANES] = data(group, c, slice(0, half))
    hidden = silu(dot_tn(w_in[0], state0[...]) + columns[:, 0:1]).astype(BF16)
    weight_ac = jnp.concatenate([weight(0, 0), weight(0, 2)], axis=0)
    messages = dot(weight_ac, hidden).astype(BF16)
    atom_col = lane_atom(iota((LANES, 2 * rim), 0), fan, tiles).astype(F32)
    for group in range(groups):
        own = messages[:, group * LANES : (group + 1) * LANES]
        own0[group] = own
        border_row = border_of(group)
        faces0[group, :, 0 : 2 * rim] = dot(own, one_hot(atom_col == border_row)).astype(BF16)

    row = iota((LANES + 2 * rim, 1), 0)
    names = jnp.where(
        row < LANES,
        lane_atom(row, fan, tiles),
        jnp.where(row < LANES + rim, row + rim, row - rim),
    ).astype(F32)
    names = jnp.broadcast_to(names, (LANES + 2 * rim, LANES)).astype(BF16)
    upper_lane = iota((2 * width, 2 * rim), 1) < rim
    radial_ac = jnp.concatenate([radial_weight(0, 0), radial_weight(0, 2)], axis=0)
    radial_rows = jnp.concatenate([jnp.zeros((2 * width, LANES + 2 * rim), BF16), radial_ac], axis=1)
    blank = jnp.zeros((2 * width, n_basis), BF16)

    for group in range(groups):
        up = (group + 1) % groups
        low = (group + groups - 1) % groups
        ghosts = jnp.where(
            upper_lane,
            faces0[up, :, 0 : 2 * rim].astype(F32),
            faces0[low, :, 0 : 2 * rim].astype(F32),
        ).astype(BF16)
        table = jnp.concatenate([own0[group], ghosts, blank], axis=1)
        left = jnp.concatenate([table, radial_rows], axis=0)
        halves = edge_rows(group)
        step = fan // 2
        acc = jnp.zeros((width, LANES), F32)
        acc_vec = [jnp.zeros((width, LANES), F32) for _ in range(3)]
        for c in range(2):
            rows = halves[c]
            vec = [rows[x * step : (x + 1) * step] for x in range(3)]
            nbr = rows[4 * step : 5 * step]
            length_sq = vec[0] * vec[0] + vec[1] * vec[1] + vec[2] * vec[2]
            length = jnp.sqrt(length_sq) + rows[3 * step : 4 * step]
            env = (1.0 - length * length / 36.0) ** 2
            for pair in range(step // 2):
                ks = (2 * pair, 2 * pair + 1)
                picked = jnp.concatenate([same(names, nbr[k : k + 1].astype(BF16)) for k in ks], axis=1)
                basis = jnp.concatenate(
                    [basis_of(length[k : k + 1], env[k : k + 1]) for k in ks], axis=1
                )
                both = dot(left, jnp.concatenate([picked, basis], axis=0))
                prod = both[: 2 * width] * both[2 * width :]
                for i, k in enumerate(ks):
                    block = prod[:, i * LANES : (i + 1) * LANES]
                    acc = acc + block[:width]
                    for x in range(3):
                        acc_vec[x] = acc_vec[x] + block[width:] * vec[x][k : k + 1]
        lanes = slice(group * LANES, (group + 1) * LANES)
        state1[0:width, lanes] = (state0[:, lanes].astype(F32) + acc / root_fan).astype(BF16)
        for x in range(3):
            state1[(x + 1) * width : (x + 2) * width, lanes] = (acc_vec[x] / root_fan).astype(BF16)

    rows = []
    for h in range(2):
        near_states = jnp.concatenate(
            [state1[:, g * LANES : (g + 1) * LANES] for g in window[h]], axis=1
        )
        rows.append(dot(near_states, window_pick[h]))
    rows = jnp.concatenate(rows, axis=1)
    hidden = silu(dot_tn(w_in[1], rows[:width].astype(BF16)) + columns[:, 1:2]).astype(BF16)
    weight_abc = jnp.concatenate([weight(1, p) for p in range(3)], axis=0)
    messages = dot(weight_abc, hidden).astype(BF16).astype(F32)
    radial_abc = jnp.concatenate([radial_weight(1, p) for p in range(3)], axis=0)
    filters = dot(radial_abc, basis1)
    weighted = messages * filters
    gate = weighted[width : 2 * width]
    along = weighted[2 * width :]
    parts = [weighted[:width]]
    for x in range(3):
        parts.append(rows[(1 + x) * width : (2 + x) * width] * gate + along * pick_vec[x])
    parts = jnp.concatenate(parts, axis=0).astype(BF16)
    edge = iota((edges, received), 0)
    slot = (edge // per_group) * cap + edge % cap
    delta = dot(parts, one_hot(slot == iota((edges, received), 1)))
    final = (dot(state1[...], chosen_atoms) + delta / root_fan).astype(BF16).astype(F32)

    along = final[width : 2 * width] * pos[0:1]
    for x in range(1, 3):
        along = along + final[(x + 1) * width : (x + 2) * width] * pos[x : x + 1]
    def repeat(value):
        return jnp.concatenate([value] * n_basis, axis=1)
    terms = [w_scalar * repeat(final[:width]) - w_vector * repeat(along)]
    for x in range(3):
        terms.append(w_vector * repeat(final[(x + 1) * width : (x + 2) * width]))
    sums = dot(jnp.concatenate(terms, axis=0).astype(BF16), probe_basis)
    charges = sums[:width]
    for x in range(3):
        charges = charges + grid[x] * sums[(x + 1) * width : (x + 2) * width]
    mixed = dot_tn(w_mix[...], charges.astype(BF16)) + columns[:, layers : layers + 1]
    density[...] = jnp.sum(silu(mixed) * columns[:, layers + 1 : layers + 2], axis=0, keepdims=True)


def few_groups(
    atom_s, atom_pos, edge_vec, edge_nbr, border_index, send_index, probe_list, probe_count,
    w_in, b_in, w_msg, w_rad, w_probe, w_mix, b_mix, w_out,
):
    atoms, half = atom_s.shape
    groups = lax.axis_size("brick") * lax.axis_size("probe")
    fan = edge_nbr.shape[0] // atoms
    rim = border_index.shape[0] // 2
    n_basis = w_rad.shape[1]
    cap = send_index.shape[1] // groups
    width = 2 * half
    every = groups * LANES
    data, weights, small = pack(
        groups, atom_s, atom_pos, edge_vec, edge_nbr, border_index, send_index, w_msg, w_rad, w_probe,
        b_in, b_mix, w_out, probe_list, probe_count,
    )
    swap = [(0, 1), (1, 0)]
    weights_other = lax.ppermute(weights, "chan", swap)
    mine = lax.all_to_all(data, ("brick", "probe"), split_axis=0, concat_axis=0, tiled=True)
    other = lax.ppermute(mine, "chan", swap)
    n_probes = probe_list.shape[0] * PB
    density = pl.pallas_call(
        functools.partial(density_kernel, (groups, fan, rim, half, n_basis, cap, probe_list.shape[0])),
        out_shape=jax.ShapeDtypeStruct((1, n_probes), F32),
        scratch_shapes=[
            pltpu.VMEM((width, every), BF16),
            pltpu.VMEM((groups, 2 * width, LANES), BF16),
            pltpu.VMEM((groups, 2 * width, LANES), BF16),
            pltpu.VMEM((4 * width, every), BF16),
            pltpu.VMEM((2,) + weights.shape, BF16),
        ],
        compiler_params=pltpu.CompilerParams(vmem_limit_bytes=40 * 1024 * 1024),
        name="density",
    )(mine, other, weights, weights_other, small, w_in, w_mix)
    return density.reshape(n_probes)


def per_device(*args):
    if lax.axis_size("brick") * lax.axis_size("probe") == FEW_GROUPS:
        return few_groups(*args)
    return many_groups(*args)


def extended(block, sides, width):
    for axis, dim in sides:
        count = lax.axis_size(axis)
        forward = [(i, i + 1) for i in range(count - 1)]
        forward.append((count - 1, 0))
        backward = [(target, source) for source, target in forward]
        low = lax.ppermute(
            lax.slice_in_dim(block, block.shape[dim] - width, None, axis=dim), axis, forward
        )
        high = lax.ppermute(lax.slice_in_dim(block, 0, width, axis=dim), axis, backward)
        block = jnp.concatenate([low, block, high], axis=dim)
    return block


def radial(distance, count, top):
    centers = jnp.arange(count).astype(jnp.float32) * (top / (count - 1))
    return jnp.exp(-2.0 * (distance[..., None] - centers) ** 2)


def make_block(
    recv_rows, recv_pos, w_scalar, w_vector, feat_width, group_no, n_blocks, list_len, n_basis
):

    def probe_block(block_in):
        block_no, listed, live_count = block_in
        index_row = (group_no * n_blocks + block_no) * PB + jnp.arange(PB, dtype=jnp.int32)
        grid_xyz = (
            jnp.stack([index_row % 16, index_row // 16 % 16, index_row // 256 % 16], axis=1).astype(
                jnp.float32
            )
            * 0.25
        )
        atom_xyz = recv_pos[:, listed]
        disp = grid_xyz[:, :, None] - atom_xyz[None]
        dist_sq = jnp.sum(disp * disp, axis=1)
        live = (jnp.arange(list_len, dtype=jnp.int32) < live_count).astype(jnp.float32)
        envelope = (1.0 - dist_sq / 64.0) ** 2 * live[None, :]
        basis = radial(jnp.sqrt(dist_sq), n_basis, 7.0) * envelope[:, :, None]
        scalar_w = basis.astype(jnp.bfloat16).reshape(PB, list_len * n_basis)
        vector_w = (
            (disp[:, :, :, None] * basis[:, None])
            .astype(jnp.bfloat16)
            .reshape(PB, 3 * list_len * n_basis)
        )
        atom_rows = recv_rows[listed]
        atom_terms = (atom_rows[:, None, :feat_width] * w_scalar[None]).reshape(
            list_len * n_basis, feat_width
        )
        vec_rows = jnp.transpose(
            atom_rows[:, feat_width:].reshape(list_len, 3, feat_width), (1, 0, 2)
        )
        vector_terms = (vec_rows[:, :, None, :] * w_vector[None, None]).reshape(
            3 * list_len * n_basis, feat_width
        )
        charge = jnp.dot(scalar_w, atom_terms, preferred_element_type=jnp.float32) + jnp.dot(
            vector_w, vector_terms, preferred_element_type=jnp.float32
        )
        return charge.astype(jnp.bfloat16)

    return probe_block


def many_groups(
    atom_s,
    atom_pos,
    edge_vec,
    edge_nbr,
    border_index,
    send_index,
    probe_list,
    probe_count,
    w_in,
    b_in,
    w_msg,
    w_rad,
    w_probe,
    w_mix,
    b_mix,
    w_out,
):
    atom_count, half_width = atom_s.shape
    n_layers = w_in.shape[0]
    width = w_in.shape[1]
    n_basis = w_rad.shape[1]
    fan_out = edge_nbr.shape[0] // atom_count
    root_fan = fan_out**0.5
    rim_rows = border_index.shape[0] // 2
    length = jnp.sqrt(jnp.sum(edge_vec * edge_vec, axis=0))
    edge_env = (1.0 - length * length / 36.0) ** 2
    edge_basis = (radial(length, n_basis, 6.0) * edge_env[:, None]).astype(jnp.bfloat16)
    edge_cols = jnp.transpose(edge_vec)
    scalars = atom_s
    vectors = jnp.zeros((atom_count, 3 * half_width), jnp.bfloat16)
    for layer_no in range(n_layers):
        full_rows = lax.all_gather(scalars, "chan", axis=1, tiled=True)
        in_weight = w_in[layer_no]
        in_bias = b_in[layer_no]
        msg_weight = w_msg[layer_no].reshape(width, 3 * half_width)
        rad_weight = w_rad[layer_no].reshape(n_basis, 3 * half_width)
        hidden_act = jax.nn.silu(
            jnp.dot(full_rows, in_weight, preferred_element_type=jnp.float32) + in_bias
        ).astype(jnp.bfloat16)
        inner_tab = jnp.concatenate(
            [
                jnp.dot(hidden_act, msg_weight, preferred_element_type=jnp.float32).astype(
                    jnp.bfloat16
                ),
                vectors,
            ],
            axis=1,
        )
        padded = extended(inner_tab[border_index], ((("brick", "probe"), 0),), rim_rows)
        lookup = jnp.concatenate([inner_tab, padded[:rim_rows], padded[3 * rim_rows :]], axis=0)
        neighbour_rows = lookup[edge_nbr]
        filters = jnp.dot(edge_basis, rad_weight, preferred_element_type=jnp.float32)
        weighted = neighbour_rows[:, : 3 * half_width] * filters
        neighbour_vec = neighbour_rows[:, 3 * half_width :].reshape(-1, 3, half_width)
        vector_gate = weighted[:, None, half_width : 2 * half_width]
        along_edge = weighted[:, None, 2 * half_width :]
        delta_vec = neighbour_vec * vector_gate + along_edge * edge_cols[:, :, None]
        delta_scalar = (
            weighted[:, :half_width].reshape(atom_count, fan_out, half_width).sum(axis=1) / root_fan
        )
        delta_vec = delta_vec.reshape(atom_count, fan_out, 3 * half_width).sum(axis=1) / root_fan
        scalars = (scalars + delta_scalar).astype(jnp.bfloat16)
        vectors = (vectors + delta_vec).astype(jnp.bfloat16)
    features = jnp.concatenate([scalars, vectors], axis=1)
    picks = send_index[0]
    n_brick = lax.axis_size("brick")
    n_probe = lax.axis_size("probe")
    n_groups = n_brick * n_probe
    slot_cap = picks.shape[0] // n_groups
    out_rows = features[picks]
    out_pos = jnp.transpose(atom_pos)[picks].astype(jnp.bfloat16)
    received = (
        lax.all_to_all(
            out_rows.reshape(n_groups, slot_cap, 4 * half_width),
            ("brick", "probe"),
            split_axis=0,
            concat_axis=0,
            tiled=True,
        ),
        lax.all_to_all(
            out_pos.reshape(n_groups, slot_cap, 3),
            ("brick", "probe"),
            split_axis=0,
            concat_axis=0,
            tiled=True,
        ),
    )
    recv_count = n_groups * slot_cap
    recv_rows = received[0].reshape(recv_count, 4 * half_width)
    recv_pos = jnp.transpose(received[1].reshape(recv_count, 3)).astype(jnp.float32)
    group_no = lax.axis_index("brick") * n_probe + lax.axis_index("probe")
    n_blocks, list_len = probe_list.shape
    probe_block = make_block(
        recv_rows,
        recv_pos,
        w_probe[:, 0, :],
        w_probe[:, 1, :],
        half_width,
        group_no,
        n_blocks,
        list_len,
        n_basis,
    )
    charges = lax.map(
        probe_block, (jnp.arange(n_blocks, dtype=jnp.int32), probe_list, probe_count)
    ).reshape(n_blocks * PB, half_width)
    mix_rows = lax.dynamic_slice_in_dim(w_mix, lax.axis_index("chan") * half_width, half_width, 0)
    mixed = lax.psum(jnp.dot(charges, mix_rows, preferred_element_type=jnp.float32), "chan")
    return jnp.sum(jax.nn.silu(mixed + b_mix) * w_out, axis=1)


def solution(mesh):
    in_specs = (
        P(("image", "brick", "probe"), "chan"),
        P(None, ("image", "brick", "probe")),
        P(None, ("image", "brick", "probe")),
        P(("image", "brick", "probe")),
        P(("image", "brick", "probe")),
        P(("image", "brick", "probe"), None),
        P(("image", "brick", "probe"), None),
        P(("image", "brick", "probe")),
        P(),
        P(),
        P(None, None, None, "chan"),
        P(None, None, None, "chan"),
        P(None, None, "chan"),
        P(),
        P(),
        P(),
    )
    out_specs = P(("image", "brick", "probe"))
    return jax.shard_map(
        per_device, mesh=mesh, in_specs=in_specs, out_specs=out_specs, check_vma=False
    )
```

```python
import functools
import math

import jax
import jax.numpy as jnp
from jax import lax
from jax.experimental import pallas as pl
from jax.experimental.pallas import tpu as pltpu
from jax.sharding import PartitionSpec as P

PB = 128
LANES = 128
FEW_GROUPS = 8
SMALL = 16
ROOT = (2.0 * math.log2(math.e)) ** 0.5
F32 = jnp.float32
BF16 = jnp.bfloat16


def iota(shape, dim):
    return lax.broadcasted_iota(jnp.int32, shape, dim)


def dot(a, b):
    return jnp.dot(a, b, preferred_element_type=F32)


def dot_tn(a, b):
    return lax.dot_general(a, b, (((0,), (0,)), ((), ())), preferred_element_type=F32)


def one_hot(mask):
    return jnp.where(mask, 1.0, 0.0).astype(BF16)


def same(names, row):
    return jnp.where(names == row, jnp.ones_like(names), jnp.zeros_like(names))


def silu(x):
    half_x = 0.5 * x
    return half_x * jnp.tanh(half_x) + half_x


def bell(scaled, center):
    away = scaled - center
    return jnp.exp2(-(away * away))


def lane_atom(lane, fan, tiles):
    return (lane % tiles) * (LANES // fan) + lane // tiles


def pack_kernel(
    fan, atom_s, atom_pos, edge_vec, edge_nbr, border, send, w_msg, w_rad, w_probe,
    b_in, b_mix, w_out, probe_list, probe_count, data_out, weight_out, small_out, natural,
):
    half, atoms = atom_s.shape
    tiles = atoms * fan // LANES
    per_tile = LANES // fan
    part = lax.axis_index("chan")
    perm = one_hot(lane_atom(iota((atoms, LANES), 1), fan, tiles) == iota((atoms, LANES), 0))
    scalars = dot(atom_s[...], perm).astype(BF16)
    vec = edge_vec[...]
    vec_high = vec.astype(BF16).astype(F32)
    length = jnp.sqrt(jnp.sum(vec * vec, axis=0, keepdims=True))
    short = length - jnp.sqrt(jnp.sum(vec_high * vec_high, axis=0, keepdims=True))
    rows = jnp.concatenate([vec_high, short], axis=0)
    for tile in range(tiles):
        for comp in range(4):
            natural[comp * tiles + tile : comp * tiles + tile + 1, :] = rows[
                comp : comp + 1, tile * LANES : (tile + 1) * LANES
            ]
    natural[4 * tiles : 5 * tiles, :] = edge_nbr[...].astype(F32)
    natural[5 * tiles :, :] = jnp.zeros((LANES - 5 * tiles, LANES), F32)
    turned = natural[...].T
    lane = iota((fan, LANES), 1)
    sorted_rows = []
    for comp in range(5):
        rows = jnp.zeros((fan, LANES), F32)
        for a in range(per_tile):
            piece = turned[a * fan : (a + 1) * fan, :]
            shift = (a * tiles - comp * tiles) % LANES
            piece = pltpu.roll(piece, shift, 1) if shift else piece
            rows = jnp.where(lane // tiles == a, piece, rows)
        sorted_rows.append(jnp.where(part == 0, rows[: fan // 2], rows[fan // 2 :]))
    pos = dot(atom_pos[...].astype(BF16), perm)
    blank = jnp.zeros((1, LANES), F32)
    border_row = jnp.concatenate(
        [border[...].astype(F32), jnp.zeros((1, LANES - border.shape[1]), F32)], axis=1
    )
    send_row = jnp.concatenate(
        [send[...].astype(F32), jnp.zeros((1, LANES - send.shape[1]), F32)], axis=1
    )
    rest = jnp.concatenate([pos, border_row, send_row, blank, blank, blank], axis=0)
    others = jnp.concatenate(sorted_rows + [rest], axis=0).astype(BF16)
    for group in range(data_out.shape[0]):
        data_out[group, 0:half, :] = scalars
        data_out[group, half:, :] = others
    at = 0
    for piece in (b_in, b_mix, w_out, probe_list, probe_count):
        rows, cols = piece.shape
        small_out[at : at + rows, 0:cols] = piece[...].astype(F32)
        at += rows
    probe_rows = [w_probe[r].astype(F32) for r in range(w_probe.shape[0])]
    radial = jnp.concatenate([w_rad[...].astype(F32)] + probe_rows, axis=0).T.astype(BF16)
    weight_out[: w_msg.shape[0], :] = w_msg[...]
    weight_out[w_msg.shape[0] :, :] = radial


def pack(
    groups, atom_s, atom_pos, edge_vec, edge_nbr, border_index, send_index, w_msg, w_rad, w_probe,
    b_in, b_mix, w_out, probe_list, probe_count,
):
    atoms, half = atom_s.shape
    fan = edge_nbr.shape[0] // atoms
    return pl.pallas_call(
        functools.partial(pack_kernel, fan),
        out_shape=(
            jax.ShapeDtypeStruct((groups, half + 5 * fan // 2 + 8, LANES), BF16),
            jax.ShapeDtypeStruct((w_msg.size // LANES + half, LANES), BF16),
            jax.ShapeDtypeStruct((SMALL, LANES), F32),
        ),
        scratch_shapes=[pltpu.VMEM((LANES, LANES), F32)],
        name="pack",
    )(
        atom_s.T,
        atom_pos,
        edge_vec,
        edge_nbr.reshape(-1, LANES),
        border_index.reshape(1, -1),
        send_index,
        jnp.transpose(w_msg, (0, 2, 3, 1)).reshape(-1, LANES),
        jnp.transpose(w_rad, (0, 2, 1, 3)).reshape(-1, half),
        w_probe,
        b_in,
        b_mix.reshape(1, -1),
        w_out.reshape(1, -1),
        probe_list,
        probe_count.reshape(1, -1),
    )


def probe_grid(me, probes):
    number = me * probes + iota((1, probes), 1)
    return [(n % 16).astype(F32) * 0.25 - 1.875 for n in (number, number // 16, number // 256)]


def probe_kernel(sizes, list_at, data_mine, small, chosen_rows, probe_basis):
    groups, fan, rim, half, n_basis, cap, n_blocks = sizes
    width = 2 * half
    tiles = fan
    every = groups * LANES
    me = lax.axis_index("brick") * lax.axis_size("probe") + lax.axis_index("probe")
    rest_at = half + 5 * fan // 2
    small_rows = small[...]
    received = groups * cap
    edges = received * fan
    send_rows = jnp.concatenate(
        [data_mine[g, rest_at : rest_at + 8, :].astype(F32)[4:5] for g in range(groups)], axis=0
    )

    def picks(lane_count, per_group):
        lane = iota((LANES, lane_count), 1)
        wanted = me * cap + lane % cap
        spread = dot(send_rows.astype(BF16), one_hot(iota((LANES, lane_count), 0) == wanted))
        lane = iota((groups, lane_count), 1)
        spread = jnp.where(lane // per_group == iota((groups, lane_count), 0), spread, 0.0)
        return jnp.sum(spread, axis=0, keepdims=True)

    per_group = fan * cap
    pick_atoms = picks(received, cap)
    column = iota((every, 1), 0)
    column_name = (column // LANES) * LANES + lane_atom(column % LANES, fan, tiles)
    wanted = (iota((1, received), 1) // cap) * LANES + pick_atoms.astype(jnp.int32)
    chosen_atoms = one_hot(column_name == wanted)

    pos_rows = jnp.concatenate(
        [data_mine[g, rest_at : rest_at + 8, :] for g in range(groups)], axis=1
    )
    pos = dot(pos_rows, chosen_atoms) - 1.875
    chosen_rows[0:1, :] = picks(edges, per_group)
    chosen_rows[1:2, 0:received] = pick_atoms
    chosen_rows[2:5, 0:received] = pos[0:3]
    pos_cols = jnp.concatenate(
        [
            jnp.concatenate([pos, jnp.zeros((8, LANES - received), F32)], axis=1),
            jnp.zeros((LANES - 8, LANES), F32),
        ],
        axis=0,
    ).T
    list_len = width
    counts = []
    for block in range(n_blocks):
        live = iota((1, list_len), 1).astype(F32) < small_rows[list_at + n_blocks : list_at + n_blocks + 1, block : block + 1]
        named = jnp.where(live, small_rows[list_at + block : list_at + block + 1], -1.0)
        hits = jnp.where(iota((received, list_len), 0).astype(F32) == named, 1.0, 0.0)
        counts.append(
            jnp.broadcast_to(jnp.sum(hits, axis=1, keepdims=True), (received, PB))
        )
    counts = jnp.concatenate(counts, axis=1)
    probes = n_blocks * PB
    grid = probe_grid(me, probes)
    dist_sq = jnp.zeros((received, probes), F32)
    for x in range(3):
        dist_sq = dist_sq + (grid[x] - pos_cols[0:received, x : x + 1]) ** 2
    dist = jnp.sqrt(dist_sq) * ROOT
    envelope = (1.0 - dist_sq / 64.0) ** 2 * counts
    probe_basis[...] = jnp.concatenate(
        [
            (bell(dist, r * (ROOT * 7.0 / (n_basis - 1))) * envelope).astype(BF16)
            for r in range(n_basis)
        ],
        axis=0,
    )


def density_kernel(
    sizes,
    data_mine,
    data_other,
    weights_mine,
    weights_other,
    small,
    w_in,
    w_mix,
    chosen_rows,
    probe_basis,
    density,
    state0,
    own0,
    faces0,
    state1,
    weights,
):
    groups, fan, rim, half, n_basis, cap, n_blocks = sizes
    layers = w_in.shape[0]
    width = 2 * half
    tiles = LANES * fan // LANES
    root_fan = fan**0.5
    me = lax.axis_index("brick") * lax.axis_size("probe") + lax.axis_index("probe")
    part = lax.axis_index("chan")
    weights[part] = weights_mine[...]
    weights[1 - part] = weights_other[...]
    every = groups * LANES
    edge_at = half
    n_edge = 5 * fan // 2
    rest_at = half + n_edge

    def data(group, c, rows):
        return (data_mine, data_other)[c][group, rows, :]

    def weight(layer, p):
        at = (layer * 3 + p) * half
        return jnp.concatenate([weights[c, at : at + half, :] for c in range(2)], axis=0)

    def radial_weight(layer, p):
        at = (layer * 3 + p) * n_basis
        return radial_all[:, at : at + n_basis]

    def edge_rows(group):
        return [data(group, c, slice(edge_at, rest_at)).astype(F32) for c in range(2)]

    def border_of(group):
        return data(group, 0, slice(rest_at, rest_at + 8)).astype(F32)[3:4, 0 : 2 * rim]

    centers = iota((n_basis, 1), 0).astype(F32) * (ROOT * 6.0 / (n_basis - 1))

    def basis_of(length, env):
        return (bell(length * ROOT, centers) * env).astype(BF16)

    received = groups * cap
    edges = received * fan
    per_group = fan * cap
    pick_edges = chosen_rows[0:1, :]
    pick_atoms = chosen_rows[1:2, 0:received]
    pos = chosen_rows[2:5, 0:received]
    atom_rows = lane_atom(iota((LANES, per_group), 0), fan, tiles).astype(F32)
    chosen = []
    for group in range(groups):
        rows = jnp.concatenate([data(group, c, slice(edge_at, rest_at)) for c in range(2)], axis=0)
        want = pick_edges[:, group * per_group : (group + 1) * per_group]
        chosen.append(dot(rows, one_hot(atom_rows == want)))
    chosen = jnp.concatenate(chosen, axis=1)
    step = fan // 2
    row = iota((2 * n_edge, edges), 0)
    slot_k = (row // n_edge) * step + row % step
    lane_k = (iota((2 * n_edge, edges), 1) % per_group) // cap
    chosen = jnp.where(slot_k == lane_k, chosen, 0.0)
    chosen = jnp.sum(chosen.reshape(2 * 5, step, edges), axis=1)
    chosen = chosen[0:5] + chosen[5:10]
    pick_vec = [chosen[x : x + 1] for x in range(3)]
    nbr = chosen[4:5]
    length = jnp.sqrt(sum(x * x for x in pick_vec)) + chosen[3:4]
    basis1 = basis_of(length, (1.0 - length * length / 36.0) ** 2)

    nbr = nbr.astype(jnp.int32)
    home = iota((1, edges), 1) // per_group
    is_low = (nbr >= LANES) & (nbr < LANES + rim)
    is_up = nbr >= LANES + rim
    owner = jnp.where(
        is_low, (home + groups - 1) % groups, jnp.where(is_up, (home + 1) % groups, home)
    )
    entry = owner * 2 * rim + jnp.where(is_low, nbr - (LANES - rim), nbr - (LANES + rim))
    entry = jnp.where(is_low | is_up, entry, -1)
    border_all = jnp.concatenate(
        [border_of(g) for g in range(groups)], axis=1
    )
    border_all = jnp.broadcast_to(border_all, (16, groups * 2 * rim)).astype(BF16)
    seen = dot(border_all, one_hot(iota((groups * 2 * rim, edges), 0) == entry))[0:1]
    target_atom = jnp.where(entry < 0, nbr, seen.astype(jnp.int32))
    column = iota((every, 1), 0)
    column_name = (column // LANES) * LANES + lane_atom(column % LANES, fan, tiles)
    quad = groups // 2
    window = [[(h * quad + groups - 1 + i) % groups for i in range(quad + 2)] for h in range(2)]
    window_pick = []
    for h in range(2):
        lanes = slice(h * edges // 2, (h + 1) * edges // 2)
        near = lax.rem(owner[:, lanes] + 2 * groups - (h * quad + groups - 1), groups)
        name = near * LANES + target_atom[:, lanes]
        window_pick.append(one_hot(column_name[: (quad + 2) * LANES] == name))
    wanted = (iota((1, received), 1) // cap) * LANES + pick_atoms.astype(jnp.int32)
    chosen_atoms = one_hot(column_name == wanted)

    small_rows = small[...]
    columns = small_rows.T
    radial_at = weights.shape[1] - half
    radial_all = jnp.concatenate([weights[c, radial_at:, :] for c in range(2)], axis=0)

    terms_shape = (2 * n_basis, n_basis * received)
    probe_weight = radial_all[:, 3 * layers * n_basis :]
    w_scalar, w_vector = (
        dot(probe_weight, one_hot(iota(terms_shape, 1) // received * 2 + p == iota(terms_shape, 0)))
        for p in range(2)
    )

    probes = density.shape[1]
    grid = probe_grid(me, probes)

    for group in range(groups):
        for c in range(2):
            place = part if c == 0 else 1 - part
            rows = pl.ds(pl.multiple_of(place * half, half), half)
            state0[rows, group * LANES : (group + 1) * LANES] = data(group, c, slice(0, half))
    hidden = silu(dot_tn(w_in[0], state0[...]) + columns[:, 0:1]).astype(BF16)
    weight_ac = jnp.concatenate([weight(0, 0), weight(0, 2)], axis=0)
    messages = dot(weight_ac, hidden).astype(BF16)
    atom_col = lane_atom(iota((LANES, 2 * rim), 0), fan, tiles).astype(F32)
    for group in range(groups):
        own = messages[:, group * LANES : (group + 1) * LANES]
        own0[group] = own
        border_row = border_of(group)
        faces0[group, :, 0 : 2 * rim] = dot(own, one_hot(atom_col == border_row)).astype(BF16)

    row = iota((LANES + 2 * rim, 1), 0)
    names = jnp.where(
        row < LANES,
        lane_atom(row, fan, tiles),
        jnp.where(row < LANES + rim, row + rim, row - rim),
    ).astype(F32)
    names = jnp.broadcast_to(names, (LANES + 2 * rim, LANES)).astype(BF16)
    upper_lane = iota((2 * width, 2 * rim), 1) < rim
    radial_ac = jnp.concatenate([radial_weight(0, 0), radial_weight(0, 2)], axis=0)
    radial_rows = jnp.concatenate([jnp.zeros((2 * width, LANES + 2 * rim), BF16), radial_ac], axis=1)
    blank = jnp.zeros((2 * width, n_basis), BF16)

    for group in range(groups):
        up = (group + 1) % groups
        low = (group + groups - 1) % groups
        ghosts = jnp.where(
            upper_lane,
            faces0[up, :, 0 : 2 * rim].astype(F32),
            faces0[low, :, 0 : 2 * rim].astype(F32),
        ).astype(BF16)
        table = jnp.concatenate([own0[group], ghosts, blank], axis=1)
        left = jnp.concatenate(
            [
                block[at : at + 16]
                for at in range(0, 2 * width, 16)
                for block in (table, radial_rows)
            ],
            axis=0,
        )
        halves = edge_rows(group)
        step = fan // 2
        acc = jnp.zeros((width, LANES), F32)
        acc_vec = [jnp.zeros((width, LANES), F32) for _ in range(3)]
        for c in range(2):
            rows = halves[c]
            vec = [rows[x * step : (x + 1) * step] for x in range(3)]
            nbr = rows[4 * step : 5 * step]
            length_sq = vec[0] * vec[0] + vec[1] * vec[1] + vec[2] * vec[2]
            length = jnp.sqrt(length_sq) + rows[3 * step : 4 * step]
            env = (1.0 - length * length / 36.0) ** 2
            for pair in range(step // 2):
                ks = (2 * pair, 2 * pair + 1)
                picked = jnp.concatenate([same(names, nbr[k : k + 1].astype(BF16)) for k in ks], axis=1)
                basis = jnp.concatenate(
                    [basis_of(length[k : k + 1], env[k : k + 1]) for k in ks], axis=1
                )
                both = dot(left, jnp.concatenate([picked, basis], axis=0))
                prod = jnp.concatenate(
                    [both[at : at + 16] * both[at + 16 : at + 32] for at in range(0, 4 * width, 32)],
                    axis=0,
                )
                for i, k in enumerate(ks):
                    block = prod[:, i * LANES : (i + 1) * LANES]
                    acc = acc + block[:width]
                    for x in range(3):
                        acc_vec[x] = acc_vec[x] + block[width:] * vec[x][k : k + 1]
        lanes = slice(group * LANES, (group + 1) * LANES)
        state1[0:width, lanes] = (state0[:, lanes].astype(F32) + acc / root_fan).astype(BF16)
        for x in range(3):
            state1[(x + 1) * width : (x + 2) * width, lanes] = (acc_vec[x] / root_fan).astype(BF16)

    rows = []
    for h in range(2):
        near_states = jnp.concatenate(
            [state1[:, g * LANES : (g + 1) * LANES] for g in window[h]], axis=1
        )
        rows.append(dot(near_states, window_pick[h]))
    rows = jnp.concatenate(rows, axis=1)
    hidden = silu(dot_tn(w_in[1], rows[:width].astype(BF16)) + columns[:, 1:2]).astype(BF16)
    weight_abc = jnp.concatenate([weight(1, p) for p in range(3)], axis=0)
    messages = dot(weight_abc, hidden).astype(BF16).astype(F32)
    radial_abc = jnp.concatenate([radial_weight(1, p) for p in range(3)], axis=0)
    filters = dot(radial_abc, basis1)
    weighted = messages * filters
    gate = weighted[width : 2 * width]
    along = weighted[2 * width :]
    parts = [weighted[:width]]
    for x in range(3):
        parts.append(rows[(1 + x) * width : (2 + x) * width] * gate + along * pick_vec[x])
    parts = jnp.concatenate(parts, axis=0).astype(BF16)
    edge = iota((edges, received), 0)
    slot = (edge // per_group) * cap + edge % cap
    delta = dot(parts, one_hot(slot == iota((edges, received), 1)))
    final = (dot(state1[...], chosen_atoms) + delta / root_fan).astype(BF16).astype(F32)

    along = final[width : 2 * width] * pos[0:1]
    for x in range(1, 3):
        along = along + final[(x + 1) * width : (x + 2) * width] * pos[x : x + 1]
    def repeat(value):
        return jnp.concatenate([value] * n_basis, axis=1)
    terms = [w_scalar * repeat(final[:width]) - w_vector * repeat(along)]
    for x in range(3):
        terms.append(w_vector * repeat(final[(x + 1) * width : (x + 2) * width]))
    sums = dot(jnp.concatenate(terms, axis=0).astype(BF16), probe_basis[...])
    charges = sums[:width]
    for x in range(3):
        charges = charges + grid[x] * sums[(x + 1) * width : (x + 2) * width]
    mixed = dot_tn(w_mix[...], charges.astype(BF16)) + columns[:, layers : layers + 1]
    density[...] = jnp.sum(silu(mixed) * columns[:, layers + 1 : layers + 2], axis=0, keepdims=True)


def few_groups(
    atom_s, atom_pos, edge_vec, edge_nbr, border_index, send_index, probe_list, probe_count,
    w_in, b_in, w_msg, w_rad, w_probe, w_mix, b_mix, w_out,
):
    atoms, half = atom_s.shape
    groups = lax.axis_size("brick") * lax.axis_size("probe")
    fan = edge_nbr.shape[0] // atoms
    rim = border_index.shape[0] // 2
    n_basis = w_rad.shape[1]
    cap = send_index.shape[1] // groups
    width = 2 * half
    every = groups * LANES
    data, weights, small = pack(
        groups, atom_s, atom_pos, edge_vec, edge_nbr, border_index, send_index, w_msg, w_rad, w_probe,
        b_in, b_mix, w_out, probe_list, probe_count,
    )
    swap = [(0, 1), (1, 0)]
    weights_other = lax.ppermute(weights, "chan", swap)
    mine = lax.all_to_all(data, ("brick", "probe"), split_axis=0, concat_axis=0, tiled=True)
    other = lax.ppermute(mine, "chan", swap)
    n_probes = probe_list.shape[0] * PB
    sizes = (groups, fan, rim, half, n_basis, cap, probe_list.shape[0])
    chosen_rows, probe_basis = pl.pallas_call(
        functools.partial(probe_kernel, sizes, w_in.shape[0] + 2),
        out_shape=(
            jax.ShapeDtypeStruct((8, groups * cap * fan), F32),
            jax.ShapeDtypeStruct((n_basis * groups * cap, n_probes), BF16),
        ),
        compiler_params=pltpu.CompilerParams(vmem_limit_bytes=24 * 1024 * 1024),
        name="probe_basis",
    )(mine, small)
    density = pl.pallas_call(
        functools.partial(density_kernel, sizes),
        out_shape=jax.ShapeDtypeStruct((1, n_probes), F32),
        scratch_shapes=[
            pltpu.VMEM((width, every), BF16),
            pltpu.VMEM((groups, 2 * width, LANES), BF16),
            pltpu.VMEM((groups, 2 * width, LANES), BF16),
            pltpu.VMEM((4 * width, every), BF16),
            pltpu.VMEM((2,) + weights.shape, BF16),
        ],
        compiler_params=pltpu.CompilerParams(vmem_limit_bytes=40 * 1024 * 1024),
        name="density",
    )(mine, other, weights, weights_other, small, w_in, w_mix, chosen_rows, probe_basis)
    return density.reshape(n_probes)


def per_device(*args):
    if lax.axis_size("brick") * lax.axis_size("probe") == FEW_GROUPS:
        return few_groups(*args)
    return many_groups(*args)


def extended(block, sides, width):
    for axis, dim in sides:
        count = lax.axis_size(axis)
        forward = [(i, i + 1) for i in range(count - 1)]
        forward.append((count - 1, 0))
        backward = [(target, source) for source, target in forward]
        low = lax.ppermute(
            lax.slice_in_dim(block, block.shape[dim] - width, None, axis=dim), axis, forward
        )
        high = lax.ppermute(lax.slice_in_dim(block, 0, width, axis=dim), axis, backward)
        block = jnp.concatenate([low, block, high], axis=dim)
    return block


def radial(distance, count, top):
    centers = jnp.arange(count).astype(jnp.float32) * (top / (count - 1))
    return jnp.exp(-2.0 * (distance[..., None] - centers) ** 2)


def make_block(
    recv_rows, recv_pos, w_scalar, w_vector, feat_width, group_no, n_blocks, list_len, n_basis
):

    def probe_block(block_in):
        block_no, listed, live_count = block_in
        index_row = (group_no * n_blocks + block_no) * PB + jnp.arange(PB, dtype=jnp.int32)
        grid_xyz = (
            jnp.stack([index_row % 16, index_row // 16 % 16, index_row // 256 % 16], axis=1).astype(
                jnp.float32
            )
            * 0.25
        )
        atom_xyz = recv_pos[:, listed]
        disp = grid_xyz[:, :, None] - atom_xyz[None]
        dist_sq = jnp.sum(disp * disp, axis=1)
        live = (jnp.arange(list_len, dtype=jnp.int32) < live_count).astype(jnp.float32)
        envelope = (1.0 - dist_sq / 64.0) ** 2 * live[None, :]
        basis = radial(jnp.sqrt(dist_sq), n_basis, 7.0) * envelope[:, :, None]
        scalar_w = basis.astype(jnp.bfloat16).reshape(PB, list_len * n_basis)
        vector_w = (
            (disp[:, :, :, None] * basis[:, None])
            .astype(jnp.bfloat16)
            .reshape(PB, 3 * list_len * n_basis)
        )
        atom_rows = recv_rows[listed]
        atom_terms = (atom_rows[:, None, :feat_width] * w_scalar[None]).reshape(
            list_len * n_basis, feat_width
        )
        vec_rows = jnp.transpose(
            atom_rows[:, feat_width:].reshape(list_len, 3, feat_width), (1, 0, 2)
        )
        vector_terms = (vec_rows[:, :, None, :] * w_vector[None, None]).reshape(
            3 * list_len * n_basis, feat_width
        )
        charge = jnp.dot(scalar_w, atom_terms, preferred_element_type=jnp.float32) + jnp.dot(
            vector_w, vector_terms, preferred_element_type=jnp.float32
        )
        return charge.astype(jnp.bfloat16)

    return probe_block


def many_groups(
    atom_s,
    atom_pos,
    edge_vec,
    edge_nbr,
    border_index,
    send_index,
    probe_list,
    probe_count,
    w_in,
    b_in,
    w_msg,
    w_rad,
    w_probe,
    w_mix,
    b_mix,
    w_out,
):
    atom_count, half_width = atom_s.shape
    n_layers = w_in.shape[0]
    width = w_in.shape[1]
    n_basis = w_rad.shape[1]
    fan_out = edge_nbr.shape[0] // atom_count
    root_fan = fan_out**0.5
    rim_rows = border_index.shape[0] // 2
    length = jnp.sqrt(jnp.sum(edge_vec * edge_vec, axis=0))
    edge_env = (1.0 - length * length / 36.0) ** 2
    edge_basis = (radial(length, n_basis, 6.0) * edge_env[:, None]).astype(jnp.bfloat16)
    edge_cols = jnp.transpose(edge_vec)
    scalars = atom_s
    vectors = jnp.zeros((atom_count, 3 * half_width), jnp.bfloat16)
    for layer_no in range(n_layers):
        full_rows = lax.all_gather(scalars, "chan", axis=1, tiled=True)
        in_weight = w_in[layer_no]
        in_bias = b_in[layer_no]
        msg_weight = w_msg[layer_no].reshape(width, 3 * half_width)
        rad_weight = w_rad[layer_no].reshape(n_basis, 3 * half_width)
        hidden_act = jax.nn.silu(
            jnp.dot(full_rows, in_weight, preferred_element_type=jnp.float32) + in_bias
        ).astype(jnp.bfloat16)
        inner_tab = jnp.concatenate(
            [
                jnp.dot(hidden_act, msg_weight, preferred_element_type=jnp.float32).astype(
                    jnp.bfloat16
                ),
                vectors,
            ],
            axis=1,
        )
        padded = extended(inner_tab[border_index], ((("brick", "probe"), 0),), rim_rows)
        lookup = jnp.concatenate([inner_tab, padded[:rim_rows], padded[3 * rim_rows :]], axis=0)
        neighbour_rows = lookup[edge_nbr]
        filters = jnp.dot(edge_basis, rad_weight, preferred_element_type=jnp.float32)
        weighted = neighbour_rows[:, : 3 * half_width] * filters
        neighbour_vec = neighbour_rows[:, 3 * half_width :].reshape(-1, 3, half_width)
        vector_gate = weighted[:, None, half_width : 2 * half_width]
        along_edge = weighted[:, None, 2 * half_width :]
        delta_vec = neighbour_vec * vector_gate + along_edge * edge_cols[:, :, None]
        delta_scalar = (
            weighted[:, :half_width].reshape(atom_count, fan_out, half_width).sum(axis=1) / root_fan
        )
        delta_vec = delta_vec.reshape(atom_count, fan_out, 3 * half_width).sum(axis=1) / root_fan
        scalars = (scalars + delta_scalar).astype(jnp.bfloat16)
        vectors = (vectors + delta_vec).astype(jnp.bfloat16)
    features = jnp.concatenate([scalars, vectors], axis=1)
    picks = send_index[0]
    n_brick = lax.axis_size("brick")
    n_probe = lax.axis_size("probe")
    n_groups = n_brick * n_probe
    slot_cap = picks.shape[0] // n_groups
    out_rows = features[picks]
    out_pos = jnp.transpose(atom_pos)[picks].astype(jnp.bfloat16)
    received = (
        lax.all_to_all(
            out_rows.reshape(n_groups, slot_cap, 4 * half_width),
            ("brick", "probe"),
            split_axis=0,
            concat_axis=0,
            tiled=True,
        ),
        lax.all_to_all(
            out_pos.reshape(n_groups, slot_cap, 3),
            ("brick", "probe"),
            split_axis=0,
            concat_axis=0,
            tiled=True,
        ),
    )
    recv_count = n_groups * slot_cap
    recv_rows = received[0].reshape(recv_count, 4 * half_width)
    recv_pos = jnp.transpose(received[1].reshape(recv_count, 3)).astype(jnp.float32)
    group_no = lax.axis_index("brick") * n_probe + lax.axis_index("probe")
    n_blocks, list_len = probe_list.shape
    probe_block = make_block(
        recv_rows,
        recv_pos,
        w_probe[:, 0, :],
        w_probe[:, 1, :],
        half_width,
        group_no,
        n_blocks,
        list_len,
        n_basis,
    )
    charges = lax.map(
        probe_block, (jnp.arange(n_blocks, dtype=jnp.int32), probe_list, probe_count)
    ).reshape(n_blocks * PB, half_width)
    mix_rows = lax.dynamic_slice_in_dim(w_mix, lax.axis_index("chan") * half_width, half_width, 0)
    mixed = lax.psum(jnp.dot(charges, mix_rows, preferred_element_type=jnp.float32), "chan")
    return jnp.sum(jax.nn.silu(mixed + b_mix) * w_out, axis=1)


def solution(mesh):
    in_specs = (
        P(("image", "brick", "probe"), "chan"),
        P(None, ("image", "brick", "probe")),
        P(None, ("image", "brick", "probe")),
        P(("image", "brick", "probe")),
        P(("image", "brick", "probe")),
        P(("image", "brick", "probe"), None),
        P(("image", "brick", "probe"), None),
        P(("image", "brick", "probe")),
        P(),
        P(),
        P(None, None, None, "chan"),
        P(None, None, None, "chan"),
        P(None, None, "chan"),
        P(),
        P(),
        P(),
    )
    out_specs = P(("image", "brick", "probe"))
    return jax.shard_map(
        per_device, mesh=mesh, in_specs=in_specs, out_specs=out_specs, check_vma=False
    )
```

```python
import functools
import itertools
import math

import jax
import jax.numpy as jnp
from jax import lax
from jax.experimental import pallas as pl
from jax.experimental.pallas import tpu as pltpu
from jax.sharding import PartitionSpec as P

PB = 128
LANES = 128
FEW_GROUPS = 8
SMALL = 16
ROOT = (2.0 * math.log2(math.e)) ** 0.5
F32 = jnp.float32
BF16 = jnp.bfloat16


def iota(shape, dim):
    return lax.broadcasted_iota(jnp.int32, shape, dim)


def dot(a, b):
    return jnp.dot(a, b, preferred_element_type=F32)


def dot_tn(a, b):
    return lax.dot_general(a, b, (((0,), (0,)), ((), ())), preferred_element_type=F32)


def one_hot(mask):
    return jnp.where(mask, 1.0, 0.0).astype(BF16)


def same(names, row):
    return jnp.where(names == row, jnp.ones_like(names), jnp.zeros_like(names))


def silu(x):
    half_x = 0.5 * x
    return half_x * jnp.tanh(half_x) + half_x


def bell(scaled, center):
    away = scaled - center
    return jnp.exp2(-(away * away))


def lane_atom(lane, fan, tiles):
    return (lane % tiles) * (LANES // fan) + lane // tiles


def length_keeping_round(exact):
    choices = []
    for value in exact:
        near = value.astype(BF16).astype(F32)
        step = jnp.where(value > near, 1.01 / 256.0, -1.01 / 256.0) * jnp.abs(near)
        choices.append((near, (near + step).astype(BF16).astype(F32)))
    target = sum(value * value for value in exact)
    best, best_error = None, None
    for picked in itertools.product(*choices):
        error = jnp.abs(sum(value * value for value in picked) - target)
        if best is None:
            best, best_error = picked, error
            continue
        better = error < best_error
        best = tuple(jnp.where(better, new, old) for new, old in zip(picked, best))
        best_error = jnp.where(better, error, best_error)
    return best


def pack_kernel(
    fan, atom_s, atom_pos, edge_vec, edge_nbr, border, send, w_msg, w_rad, w_probe,
    b_in, b_mix, w_out, probe_list, probe_count, data_out, weight_out, small_out, natural,
):
    half, atoms = atom_s.shape
    tiles = atoms * fan // LANES
    per_tile = LANES // fan
    part = lax.axis_index("chan")
    perm = one_hot(lane_atom(iota((atoms, LANES), 1), fan, tiles) == iota((atoms, LANES), 0))
    scalars = dot(atom_s[...], perm).astype(BF16)
    for tile in range(tiles):
        for comp in range(3):
            natural[comp * tiles + tile : comp * tiles + tile + 1, :] = edge_vec[
                comp : comp + 1, tile * LANES : (tile + 1) * LANES
            ]
    exact = [natural[comp * tiles : (comp + 1) * tiles, :] for comp in range(3)]
    for comp, value in enumerate(length_keeping_round(exact)):
        natural[comp * tiles : (comp + 1) * tiles, :] = value
    natural[3 * tiles : 4 * tiles, :] = edge_nbr[...].astype(F32)
    natural[4 * tiles :, :] = jnp.zeros((LANES - 4 * tiles, LANES), F32)
    turned = natural[...].T
    lane = iota((fan, LANES), 1)
    sorted_rows = []
    for comp in range(4):
        rows = jnp.zeros((fan, LANES), F32)
        for a in range(per_tile):
            piece = turned[a * fan : (a + 1) * fan, :]
            shift = (a * tiles - comp * tiles) % LANES
            piece = pltpu.roll(piece, shift, 1) if shift else piece
            rows = jnp.where(lane // tiles == a, piece, rows)
        sorted_rows.append(jnp.where(part == 0, rows[: fan // 2], rows[fan // 2 :]))
    pos = dot(atom_pos[...].astype(BF16), perm)
    blank = jnp.zeros((1, LANES), F32)
    border_row = jnp.concatenate(
        [border[...].astype(F32), jnp.zeros((1, LANES - border.shape[1]), F32)], axis=1
    )
    send_row = jnp.concatenate(
        [send[...].astype(F32), jnp.zeros((1, LANES - send.shape[1]), F32)], axis=1
    )
    rest = jnp.concatenate([pos, border_row, send_row, blank, blank, blank], axis=0)
    others = jnp.concatenate(sorted_rows + [rest], axis=0).astype(BF16)
    for group in range(data_out.shape[0]):
        data_out[group, 0:half, :] = scalars
        data_out[group, half:, :] = others
    at = 0
    for piece in (b_in, b_mix, w_out, probe_list, probe_count):
        rows, cols = piece.shape
        small_out[at : at + rows, 0:cols] = piece[...].astype(F32)
        at += rows
    probe_rows = [w_probe[r].astype(F32) for r in range(w_probe.shape[0])]
    radial = jnp.concatenate([w_rad[...].astype(F32)] + probe_rows, axis=0).T.astype(BF16)
    weight_out[: w_msg.shape[0], :] = w_msg[...]
    weight_out[w_msg.shape[0] :, :] = radial


def pack(
    groups, atom_s, atom_pos, edge_vec, edge_nbr, border_index, send_index, w_msg, w_rad, w_probe,
    b_in, b_mix, w_out, probe_list, probe_count,
):
    atoms, half = atom_s.shape
    fan = edge_nbr.shape[0] // atoms
    return pl.pallas_call(
        functools.partial(pack_kernel, fan),
        out_shape=(
            jax.ShapeDtypeStruct((groups, half + 4 * fan // 2 + 8, LANES), BF16),
            jax.ShapeDtypeStruct((w_msg.size // LANES + half, LANES), BF16),
            jax.ShapeDtypeStruct((SMALL, LANES), F32),
        ),
        scratch_shapes=[pltpu.VMEM((LANES, LANES), F32)],
        name="pack",
    )(
        atom_s.T,
        atom_pos,
        edge_vec,
        edge_nbr.reshape(-1, LANES),
        border_index.reshape(1, -1),
        send_index,
        jnp.transpose(w_msg, (0, 2, 3, 1)).reshape(-1, LANES),
        jnp.transpose(w_rad, (0, 2, 1, 3)).reshape(-1, half),
        w_probe,
        b_in,
        b_mix.reshape(1, -1),
        w_out.reshape(1, -1),
        probe_list,
        probe_count.reshape(1, -1),
    )


def probe_grid(me, probes):
    number = me * probes + iota((1, probes), 1)
    return [(n % 16).astype(F32) * 0.25 - 1.875 for n in (number, number // 16, number // 256)]


def probe_kernel(sizes, list_at, data_mine, small, chosen_rows, probe_basis):
    groups, fan, rim, half, n_basis, cap, n_blocks = sizes
    width = 2 * half
    tiles = fan
    every = groups * LANES
    me = lax.axis_index("brick") * lax.axis_size("probe") + lax.axis_index("probe")
    rest_at = half + 4 * fan // 2
    small_rows = small[...]
    received = groups * cap
    edges = received * fan
    send_rows = jnp.concatenate(
        [data_mine[g, rest_at : rest_at + 8, :].astype(F32)[4:5] for g in range(groups)], axis=0
    )

    def picks(lane_count, per_group):
        lane = iota((LANES, lane_count), 1)
        wanted = me * cap + lane % cap
        spread = dot(send_rows.astype(BF16), one_hot(iota((LANES, lane_count), 0) == wanted))
        lane = iota((groups, lane_count), 1)
        spread = jnp.where(lane // per_group == iota((groups, lane_count), 0), spread, 0.0)
        return jnp.sum(spread, axis=0, keepdims=True)

    per_group = fan * cap
    pick_atoms = picks(received, cap)
    column = iota((every, 1), 0)
    column_name = (column // LANES) * LANES + lane_atom(column % LANES, fan, tiles)
    wanted = (iota((1, received), 1) // cap) * LANES + pick_atoms.astype(jnp.int32)
    chosen_atoms = one_hot(column_name == wanted)

    pos_rows = jnp.concatenate(
        [data_mine[g, rest_at : rest_at + 8, :] for g in range(groups)], axis=1
    )
    pos = dot(pos_rows, chosen_atoms) - 1.875
    chosen_rows[0:1, :] = picks(edges, per_group)
    chosen_rows[1:2, 0:received] = pick_atoms
    chosen_rows[2:5, 0:received] = pos[0:3]
    pos_cols = jnp.concatenate(
        [
            jnp.concatenate([pos, jnp.zeros((8, LANES - received), F32)], axis=1),
            jnp.zeros((LANES - 8, LANES), F32),
        ],
        axis=0,
    ).T
    list_len = width
    counts = []
    for block in range(n_blocks):
        live = iota((1, list_len), 1).astype(F32) < small_rows[list_at + n_blocks : list_at + n_blocks + 1, block : block + 1]
        named = jnp.where(live, small_rows[list_at + block : list_at + block + 1], -1.0)
        hits = jnp.where(iota((received, list_len), 0).astype(F32) == named, 1.0, 0.0)
        counts.append(
            jnp.broadcast_to(jnp.sum(hits, axis=1, keepdims=True), (received, PB))
        )
    counts = jnp.concatenate(counts, axis=1)
    probes = n_blocks * PB
    grid = probe_grid(me, probes)
    dist_sq = jnp.zeros((received, probes), F32)
    for x in range(3):
        dist_sq = dist_sq + (grid[x] - pos_cols[0:received, x : x + 1]) ** 2
    dist = jnp.sqrt(dist_sq) * ROOT
    envelope = (1.0 - dist_sq / 64.0) ** 2 * counts
    probe_basis[...] = jnp.concatenate(
        [
            (bell(dist, r * (ROOT * 7.0 / (n_basis - 1))) * envelope).astype(BF16)
            for r in range(n_basis)
        ],
        axis=0,
    )


def density_kernel(
    sizes,
    data_mine,
    data_other,
    weights_mine,
    weights_other,
    small,
    w_in,
    w_mix,
    chosen_rows,
    probe_basis,
    density,
    state0,
    own0,
    faces0,
    state1,
    weights,
):
    groups, fan, rim, half, n_basis, cap, n_blocks = sizes
    layers = w_in.shape[0]
    width = 2 * half
    tiles = LANES * fan // LANES
    root_fan = fan**0.5
    me = lax.axis_index("brick") * lax.axis_size("probe") + lax.axis_index("probe")
    part = lax.axis_index("chan")
    weights[part] = weights_mine[...]
    weights[1 - part] = weights_other[...]
    every = groups * LANES
    edge_at = half
    n_edge = 4 * fan // 2
    rest_at = half + n_edge

    def data(group, c, rows):
        return (data_mine, data_other)[c][group, rows, :]

    def weight(layer, p):
        at = (layer * 3 + p) * half
        return jnp.concatenate([weights[c, at : at + half, :] for c in range(2)], axis=0)

    def radial_weight(layer, p):
        at = (layer * 3 + p) * n_basis
        return radial_all[:, at : at + n_basis]

    def edge_rows(group):
        return [data(group, c, slice(edge_at, rest_at)).astype(F32) for c in range(2)]

    def border_of(group):
        return data(group, 0, slice(rest_at, rest_at + 8)).astype(F32)[3:4, 0 : 2 * rim]

    centers = iota((n_basis, 1), 0).astype(F32) * (ROOT * 6.0 / (n_basis - 1))

    def basis_of(length, env):
        return (bell(length * ROOT, centers) * env).astype(BF16)

    received = groups * cap
    edges = received * fan
    per_group = fan * cap
    pick_edges = chosen_rows[0:1, :]
    pick_atoms = chosen_rows[1:2, 0:received]
    pos = chosen_rows[2:5, 0:received]
    atom_rows = lane_atom(iota((LANES, per_group), 0), fan, tiles).astype(F32)
    chosen = []
    for group in range(groups):
        rows = jnp.concatenate([data(group, c, slice(edge_at, rest_at)) for c in range(2)], axis=0)
        want = pick_edges[:, group * per_group : (group + 1) * per_group]
        chosen.append(dot(rows, one_hot(atom_rows == want)))
    chosen = jnp.concatenate(chosen, axis=1)
    step = fan // 2
    row = iota((2 * n_edge, edges), 0)
    slot_k = (row // n_edge) * step + row % step
    lane_k = (iota((2 * n_edge, edges), 1) % per_group) // cap
    chosen = jnp.where(slot_k == lane_k, chosen, 0.0)
    chosen = jnp.sum(chosen.reshape(2 * 4, step, edges), axis=1)
    chosen = chosen[0:4] + chosen[4:8]
    pick_vec = [chosen[x : x + 1] for x in range(3)]
    nbr = chosen[3:4]
    length = jnp.sqrt(sum(x * x for x in pick_vec))
    basis1 = basis_of(length, (1.0 - length * length / 36.0) ** 2)

    nbr = nbr.astype(jnp.int32)
    home = iota((1, edges), 1) // per_group
    is_low = (nbr >= LANES) & (nbr < LANES + rim)
    is_up = nbr >= LANES + rim
    owner = jnp.where(
        is_low, (home + groups - 1) % groups, jnp.where(is_up, (home + 1) % groups, home)
    )
    entry = owner * 2 * rim + jnp.where(is_low, nbr - (LANES - rim), nbr - (LANES + rim))
    entry = jnp.where(is_low | is_up, entry, -1)
    border_all = jnp.concatenate(
        [border_of(g) for g in range(groups)], axis=1
    )
    border_all = jnp.broadcast_to(border_all, (16, groups * 2 * rim)).astype(BF16)
    seen = dot(border_all, one_hot(iota((groups * 2 * rim, edges), 0) == entry))[0:1]
    target_atom = jnp.where(entry < 0, nbr, seen.astype(jnp.int32))
    column = iota((every, 1), 0)
    column_name = (column // LANES) * LANES + lane_atom(column % LANES, fan, tiles)
    quad = groups // 2
    window = [[(h * quad + groups - 1 + i) % groups for i in range(quad + 2)] for h in range(2)]
    window_pick = []
    for h in range(2):
        lanes = slice(h * edges // 2, (h + 1) * edges // 2)
        near = lax.rem(owner[:, lanes] + 2 * groups - (h * quad + groups - 1), groups)
        name = near * LANES + target_atom[:, lanes]
        window_pick.append(one_hot(column_name[: (quad + 2) * LANES] == name))
    wanted = (iota((1, received), 1) // cap) * LANES + pick_atoms.astype(jnp.int32)
    chosen_atoms = one_hot(column_name == wanted)

    small_rows = small[...]
    columns = small_rows.T
    radial_at = weights.shape[1] - half
    radial_all = jnp.concatenate([weights[c, radial_at:, :] for c in range(2)], axis=0)

    terms_shape = (2 * n_basis, n_basis * received)
    probe_weight = radial_all[:, 3 * layers * n_basis :]
    w_scalar, w_vector = (
        dot(probe_weight, one_hot(iota(terms_shape, 1) // received * 2 + p == iota(terms_shape, 0)))
        for p in range(2)
    )

    probes = density.shape[1]
    grid = probe_grid(me, probes)

    for group in range(groups):
        for c in range(2):
            place = part if c == 0 else 1 - part
            rows = pl.ds(pl.multiple_of(place * half, half), half)
            state0[rows, group * LANES : (group + 1) * LANES] = data(group, c, slice(0, half))
    hidden = silu(dot_tn(w_in[0], state0[...]) + columns[:, 0:1]).astype(BF16)
    weight_ac = jnp.concatenate([weight(0, 0), weight(0, 2)], axis=0)
    messages = dot(weight_ac, hidden).astype(BF16)
    atom_col = lane_atom(iota((LANES, 2 * rim), 0), fan, tiles).astype(F32)
    for group in range(groups):
        own = messages[:, group * LANES : (group + 1) * LANES]
        own0[group] = own
        border_row = border_of(group)
        faces0[group, :, 0 : 2 * rim] = dot(own, one_hot(atom_col == border_row)).astype(BF16)

    row = iota((LANES + 2 * rim, 1), 0)
    names = jnp.where(
        row < LANES,
        lane_atom(row, fan, tiles),
        jnp.where(row < LANES + rim, row + rim, row - rim),
    ).astype(F32)
    names = jnp.broadcast_to(names, (LANES + 2 * rim, LANES)).astype(BF16)
    upper_lane = iota((2 * width, 2 * rim), 1) < rim
    radial_ac = jnp.concatenate([radial_weight(0, 0), radial_weight(0, 2)], axis=0)
    radial_rows = jnp.concatenate([jnp.zeros((2 * width, LANES + 2 * rim), BF16), radial_ac], axis=1)
    blank = jnp.zeros((2 * width, n_basis), BF16)

    for group in range(groups):
        up = (group + 1) % groups
        low = (group + groups - 1) % groups
        ghosts = jnp.where(
            upper_lane,
            faces0[up, :, 0 : 2 * rim].astype(F32),
            faces0[low, :, 0 : 2 * rim].astype(F32),
        ).astype(BF16)
        table = jnp.concatenate([own0[group], ghosts, blank], axis=1)
        left = jnp.concatenate(
            [
                block[at : at + 16]
                for at in range(0, 2 * width, 16)
                for block in (table, radial_rows)
            ],
            axis=0,
        )
        halves = edge_rows(group)
        step = fan // 2
        acc = jnp.zeros((width, LANES), F32)
        acc_vec = [jnp.zeros((width, LANES), F32) for _ in range(3)]
        for c in range(2):
            rows = halves[c]
            vec = [rows[x * step : (x + 1) * step] for x in range(3)]
            nbr = rows[3 * step : 4 * step]
            length_sq = vec[0] * vec[0] + vec[1] * vec[1] + vec[2] * vec[2]
            length = jnp.sqrt(length_sq)
            env = (1.0 - length * length / 36.0) ** 2
            for pair in range(step // 2):
                ks = (2 * pair, 2 * pair + 1)
                picked = jnp.concatenate([same(names, nbr[k : k + 1].astype(BF16)) for k in ks], axis=1)
                basis = jnp.concatenate(
                    [basis_of(length[k : k + 1], env[k : k + 1]) for k in ks], axis=1
                )
                both = dot(left, jnp.concatenate([picked, basis], axis=0))
                prod = jnp.concatenate(
                    [both[at : at + 16] * both[at + 16 : at + 32] for at in range(0, 4 * width, 32)],
                    axis=0,
                )
                for i, k in enumerate(ks):
                    block = prod[:, i * LANES : (i + 1) * LANES]
                    acc = acc + block[:width]
                    for x in range(3):
                        acc_vec[x] = acc_vec[x] + block[width:] * vec[x][k : k + 1]
        lanes = slice(group * LANES, (group + 1) * LANES)
        state1[0:width, lanes] = (state0[:, lanes].astype(F32) + acc / root_fan).astype(BF16)
        for x in range(3):
            state1[(x + 1) * width : (x + 2) * width, lanes] = (acc_vec[x] / root_fan).astype(BF16)

    rows = []
    for h in range(2):
        near_states = jnp.concatenate(
            [state1[:, g * LANES : (g + 1) * LANES] for g in window[h]], axis=1
        )
        rows.append(dot(near_states, window_pick[h]))
    rows = jnp.concatenate(rows, axis=1)
    hidden = silu(dot_tn(w_in[1], rows[:width].astype(BF16)) + columns[:, 1:2]).astype(BF16)
    weight_abc = jnp.concatenate([weight(1, p) for p in range(3)], axis=0)
    messages = dot(weight_abc, hidden).astype(BF16).astype(F32)
    radial_abc = jnp.concatenate([radial_weight(1, p) for p in range(3)], axis=0)
    filters = dot(radial_abc, basis1)
    weighted = messages * filters
    gate = weighted[width : 2 * width]
    along = weighted[2 * width :]
    parts = [weighted[:width]]
    for x in range(3):
        parts.append(rows[(1 + x) * width : (2 + x) * width] * gate + along * pick_vec[x])
    parts = jnp.concatenate(parts, axis=0).astype(BF16)
    edge = iota((edges, received), 0)
    slot = (edge // per_group) * cap + edge % cap
    delta = dot(parts, one_hot(slot == iota((edges, received), 1)))
    final = (dot(state1[...], chosen_atoms) + delta / root_fan).astype(BF16).astype(F32)

    along = final[width : 2 * width] * pos[0:1]
    for x in range(1, 3):
        along = along + final[(x + 1) * width : (x + 2) * width] * pos[x : x + 1]
    def repeat(value):
        return jnp.concatenate([value] * n_basis, axis=1)
    terms = [w_scalar * repeat(final[:width]) - w_vector * repeat(along)]
    for x in range(3):
        terms.append(w_vector * repeat(final[(x + 1) * width : (x + 2) * width]))
    sums = dot(jnp.concatenate(terms, axis=0).astype(BF16), probe_basis[...])
    charges = sums[:width]
    for x in range(3):
        charges = charges + grid[x] * sums[(x + 1) * width : (x + 2) * width]
    mixed = dot_tn(w_mix[...], charges.astype(BF16)) + columns[:, layers : layers + 1]
    density[...] = jnp.sum(silu(mixed) * columns[:, layers + 1 : layers + 2], axis=0, keepdims=True)


def few_groups(
    atom_s, atom_pos, edge_vec, edge_nbr, border_index, send_index, probe_list, probe_count,
    w_in, b_in, w_msg, w_rad, w_probe, w_mix, b_mix, w_out,
):
    atoms, half = atom_s.shape
    groups = lax.axis_size("brick") * lax.axis_size("probe")
    fan = edge_nbr.shape[0] // atoms
    rim = border_index.shape[0] // 2
    n_basis = w_rad.shape[1]
    cap = send_index.shape[1] // groups
    width = 2 * half
    every = groups * LANES
    data, weights, small = pack(
        groups, atom_s, atom_pos, edge_vec, edge_nbr, border_index, send_index, w_msg, w_rad, w_probe,
        b_in, b_mix, w_out, probe_list, probe_count,
    )
    swap = [(0, 1), (1, 0)]
    weights_other = lax.ppermute(weights, "chan", swap)
    mine = lax.all_to_all(data, ("brick", "probe"), split_axis=0, concat_axis=0, tiled=True)
    other = lax.ppermute(mine, "chan", swap)
    n_probes = probe_list.shape[0] * PB
    sizes = (groups, fan, rim, half, n_basis, cap, probe_list.shape[0])
    chosen_rows, probe_basis = pl.pallas_call(
        functools.partial(probe_kernel, sizes, w_in.shape[0] + 2),
        out_shape=(
            jax.ShapeDtypeStruct((8, groups * cap * fan), F32),
            jax.ShapeDtypeStruct((n_basis * groups * cap, n_probes), BF16),
        ),
        compiler_params=pltpu.CompilerParams(vmem_limit_bytes=24 * 1024 * 1024),
        name="probe_basis",
    )(mine, small)
    density = pl.pallas_call(
        functools.partial(density_kernel, sizes),
        out_shape=jax.ShapeDtypeStruct((1, n_probes), F32),
        scratch_shapes=[
            pltpu.VMEM((width, every), BF16),
            pltpu.VMEM((groups, 2 * width, LANES), BF16),
            pltpu.VMEM((groups, 2 * width, LANES), BF16),
            pltpu.VMEM((4 * width, every), BF16),
            pltpu.VMEM((2,) + weights.shape, BF16),
        ],
        compiler_params=pltpu.CompilerParams(vmem_limit_bytes=40 * 1024 * 1024),
        name="density",
    )(mine, other, weights, weights_other, small, w_in, w_mix, chosen_rows, probe_basis)
    return density.reshape(n_probes)


def per_device(*args):
    if lax.axis_size("brick") * lax.axis_size("probe") == FEW_GROUPS:
        return few_groups(*args)
    return many_groups(*args)


def extended(block, sides, width):
    for axis, dim in sides:
        count = lax.axis_size(axis)
        forward = [(i, i + 1) for i in range(count - 1)]
        forward.append((count - 1, 0))
        backward = [(target, source) for source, target in forward]
        low = lax.ppermute(
            lax.slice_in_dim(block, block.shape[dim] - width, None, axis=dim), axis, forward
        )
        high = lax.ppermute(lax.slice_in_dim(block, 0, width, axis=dim), axis, backward)
        block = jnp.concatenate([low, block, high], axis=dim)
    return block


def radial(distance, count, top):
    centers = jnp.arange(count).astype(jnp.float32) * (top / (count - 1))
    return jnp.exp(-2.0 * (distance[..., None] - centers) ** 2)


def make_block(
    recv_rows, recv_pos, w_scalar, w_vector, feat_width, group_no, n_blocks, list_len, n_basis
):

    def probe_block(block_in):
        block_no, listed, live_count = block_in
        index_row = (group_no * n_blocks + block_no) * PB + jnp.arange(PB, dtype=jnp.int32)
        grid_xyz = (
            jnp.stack([index_row % 16, index_row // 16 % 16, index_row // 256 % 16], axis=1).astype(
                jnp.float32
            )
            * 0.25
        )
        atom_xyz = recv_pos[:, listed]
        disp = grid_xyz[:, :, None] - atom_xyz[None]
        dist_sq = jnp.sum(disp * disp, axis=1)
        live = (jnp.arange(list_len, dtype=jnp.int32) < live_count).astype(jnp.float32)
        envelope = (1.0 - dist_sq / 64.0) ** 2 * live[None, :]
        basis = radial(jnp.sqrt(dist_sq), n_basis, 7.0) * envelope[:, :, None]
        scalar_w = basis.astype(jnp.bfloat16).reshape(PB, list_len * n_basis)
        vector_w = (
            (disp[:, :, :, None] * basis[:, None])
            .astype(jnp.bfloat16)
            .reshape(PB, 3 * list_len * n_basis)
        )
        atom_rows = recv_rows[listed]
        atom_terms = (atom_rows[:, None, :feat_width] * w_scalar[None]).reshape(
            list_len * n_basis, feat_width
        )
        vec_rows = jnp.transpose(
            atom_rows[:, feat_width:].reshape(list_len, 3, feat_width), (1, 0, 2)
        )
        vector_terms = (vec_rows[:, :, None, :] * w_vector[None, None]).reshape(
            3 * list_len * n_basis, feat_width
        )
        charge = jnp.dot(scalar_w, atom_terms, preferred_element_type=jnp.float32) + jnp.dot(
            vector_w, vector_terms, preferred_element_type=jnp.float32
        )
        return charge.astype(jnp.bfloat16)

    return probe_block


def many_groups(
    atom_s,
    atom_pos,
    edge_vec,
    edge_nbr,
    border_index,
    send_index,
    probe_list,
    probe_count,
    w_in,
    b_in,
    w_msg,
    w_rad,
    w_probe,
    w_mix,
    b_mix,
    w_out,
):
    atom_count, half_width = atom_s.shape
    n_layers = w_in.shape[0]
    width = w_in.shape[1]
    n_basis = w_rad.shape[1]
    fan_out = edge_nbr.shape[0] // atom_count
    root_fan = fan_out**0.5
    rim_rows = border_index.shape[0] // 2
    length = jnp.sqrt(jnp.sum(edge_vec * edge_vec, axis=0))
    edge_env = (1.0 - length * length / 36.0) ** 2
    edge_basis = (radial(length, n_basis, 6.0) * edge_env[:, None]).astype(jnp.bfloat16)
    edge_cols = jnp.transpose(edge_vec)
    scalars = atom_s
    vectors = jnp.zeros((atom_count, 3 * half_width), jnp.bfloat16)
    for layer_no in range(n_layers):
        full_rows = lax.all_gather(scalars, "chan", axis=1, tiled=True)
        in_weight = w_in[layer_no]
        in_bias = b_in[layer_no]
        msg_weight = w_msg[layer_no].reshape(width, 3 * half_width)
        rad_weight = w_rad[layer_no].reshape(n_basis, 3 * half_width)
        hidden_act = jax.nn.silu(
            jnp.dot(full_rows, in_weight, preferred_element_type=jnp.float32) + in_bias
        ).astype(jnp.bfloat16)
        inner_tab = jnp.concatenate(
            [
                jnp.dot(hidden_act, msg_weight, preferred_element_type=jnp.float32).astype(
                    jnp.bfloat16
                ),
                vectors,
            ],
            axis=1,
        )
        padded = extended(inner_tab[border_index], ((("brick", "probe"), 0),), rim_rows)
        lookup = jnp.concatenate([inner_tab, padded[:rim_rows], padded[3 * rim_rows :]], axis=0)
        neighbour_rows = lookup[edge_nbr]
        filters = jnp.dot(edge_basis, rad_weight, preferred_element_type=jnp.float32)
        weighted = neighbour_rows[:, : 3 * half_width] * filters
        neighbour_vec = neighbour_rows[:, 3 * half_width :].reshape(-1, 3, half_width)
        vector_gate = weighted[:, None, half_width : 2 * half_width]
        along_edge = weighted[:, None, 2 * half_width :]
        delta_vec = neighbour_vec * vector_gate + along_edge * edge_cols[:, :, None]
        delta_scalar = (
            weighted[:, :half_width].reshape(atom_count, fan_out, half_width).sum(axis=1) / root_fan
        )
        delta_vec = delta_vec.reshape(atom_count, fan_out, 3 * half_width).sum(axis=1) / root_fan
        scalars = (scalars + delta_scalar).astype(jnp.bfloat16)
        vectors = (vectors + delta_vec).astype(jnp.bfloat16)
    features = jnp.concatenate([scalars, vectors], axis=1)
    picks = send_index[0]
    n_brick = lax.axis_size("brick")
    n_probe = lax.axis_size("probe")
    n_groups = n_brick * n_probe
    slot_cap = picks.shape[0] // n_groups
    out_rows = features[picks]
    out_pos = jnp.transpose(atom_pos)[picks].astype(jnp.bfloat16)
    received = (
        lax.all_to_all(
            out_rows.reshape(n_groups, slot_cap, 4 * half_width),
            ("brick", "probe"),
            split_axis=0,
            concat_axis=0,
            tiled=True,
        ),
        lax.all_to_all(
            out_pos.reshape(n_groups, slot_cap, 3),
            ("brick", "probe"),
            split_axis=0,
            concat_axis=0,
            tiled=True,
        ),
    )
    recv_count = n_groups * slot_cap
    recv_rows = received[0].reshape(recv_count, 4 * half_width)
    recv_pos = jnp.transpose(received[1].reshape(recv_count, 3)).astype(jnp.float32)
    group_no = lax.axis_index("brick") * n_probe + lax.axis_index("probe")
    n_blocks, list_len = probe_list.shape
    probe_block = make_block(
        recv_rows,
        recv_pos,
        w_probe[:, 0, :],
        w_probe[:, 1, :],
        half_width,
        group_no,
        n_blocks,
        list_len,
        n_basis,
    )
    charges = lax.map(
        probe_block, (jnp.arange(n_blocks, dtype=jnp.int32), probe_list, probe_count)
    ).reshape(n_blocks * PB, half_width)
    mix_rows = lax.dynamic_slice_in_dim(w_mix, lax.axis_index("chan") * half_width, half_width, 0)
    mixed = lax.psum(jnp.dot(charges, mix_rows, preferred_element_type=jnp.float32), "chan")
    return jnp.sum(jax.nn.silu(mixed + b_mix) * w_out, axis=1)


def solution(mesh):
    in_specs = (
        P(("image", "brick", "probe"), "chan"),
        P(None, ("image", "brick", "probe")),
        P(None, ("image", "brick", "probe")),
        P(("image", "brick", "probe")),
        P(("image", "brick", "probe")),
        P(("image", "brick", "probe"), None),
        P(("image", "brick", "probe"), None),
        P(("image", "brick", "probe")),
        P(),
        P(),
        P(None, None, None, "chan"),
        P(None, None, None, "chan"),
        P(None, None, "chan"),
        P(),
        P(),
        P(),
    )
    out_specs = P(("image", "brick", "probe"))
    return jax.shard_map(
        per_device, mesh=mesh, in_specs=in_specs, out_specs=out_specs, check_vma=False
    )
```

```python
import functools
import itertools
import math

import jax
import jax.numpy as jnp
from jax import lax
from jax.experimental import pallas as pl
from jax.experimental.pallas import tpu as pltpu
from jax.sharding import PartitionSpec as P

PB = 128
LANES = 128
FEW_GROUPS = 8
SMALL = 16
TOGETHER = 4
ROOT = (2.0 * math.log2(math.e)) ** 0.5
F32 = jnp.float32
BF16 = jnp.bfloat16


def iota(shape, dim):
    return lax.broadcasted_iota(jnp.int32, shape, dim)


def dot(a, b):
    return jnp.dot(a, b, preferred_element_type=F32)


def dot_tn(a, b):
    return lax.dot_general(a, b, (((0,), (0,)), ((), ())), preferred_element_type=F32)


def one_hot(mask):
    return jnp.where(mask, 1.0, 0.0).astype(BF16)


def same(names, row):
    return jnp.where(names == row, jnp.ones_like(names), jnp.zeros_like(names))


def silu(x):
    half_x = 0.5 * x
    return half_x * jnp.tanh(half_x) + half_x


def bell(scaled, center):
    away = scaled - center
    return jnp.exp2(-(away * away))


def lane_atom(lane, fan, tiles):
    return (lane % tiles) * (LANES // fan) + lane // tiles


def length_keeping_round(exact):
    choices = []
    for value in exact:
        near = value.astype(BF16).astype(F32)
        step = jnp.where(value > near, 1.01 / 256.0, -1.01 / 256.0) * jnp.abs(near)
        choices.append((near, (near + step).astype(BF16).astype(F32)))
    target = sum(value * value for value in exact)
    best, best_error = None, None
    for picked in itertools.product(*choices):
        error = jnp.abs(sum(value * value for value in picked) - target)
        if best is None:
            best, best_error = picked, error
            continue
        better = error < best_error
        best = tuple(jnp.where(better, new, old) for new, old in zip(picked, best))
        best_error = jnp.where(better, error, best_error)
    return best


def pack_kernel(
    fan, atom_s, atom_pos, edge_vec, edge_nbr, border, send, w_msg, w_rad, w_probe,
    b_in, b_mix, w_out, probe_list, probe_count, data_out, weight_out, small_out, natural,
):
    half, atoms = atom_s.shape
    tiles = atoms * fan // LANES
    per_tile = LANES // fan
    part = lax.axis_index("chan")
    perm = one_hot(lane_atom(iota((atoms, LANES), 1), fan, tiles) == iota((atoms, LANES), 0))
    scalars = dot(atom_s[...], perm).astype(BF16)
    for tile in range(tiles):
        for comp in range(3):
            natural[comp * tiles + tile : comp * tiles + tile + 1, :] = edge_vec[
                comp : comp + 1, tile * LANES : (tile + 1) * LANES
            ]
    exact = [natural[comp * tiles : (comp + 1) * tiles, :] for comp in range(3)]
    for comp, value in enumerate(length_keeping_round(exact)):
        natural[comp * tiles : (comp + 1) * tiles, :] = value
    natural[3 * tiles : 4 * tiles, :] = edge_nbr[...].astype(F32)
    natural[4 * tiles :, :] = jnp.zeros((LANES - 4 * tiles, LANES), F32)
    turned = natural[...].T
    lane = iota((fan, LANES), 1)
    sorted_rows = []
    for comp in range(4):
        rows = jnp.zeros((fan, LANES), F32)
        for a in range(per_tile):
            piece = turned[a * fan : (a + 1) * fan, :]
            shift = (a * tiles - comp * tiles) % LANES
            piece = pltpu.roll(piece, shift, 1) if shift else piece
            rows = jnp.where(lane // tiles == a, piece, rows)
        sorted_rows.append(jnp.where(part == 0, rows[: fan // 2], rows[fan // 2 :]))
    pos = dot(atom_pos[...].astype(BF16), perm)
    blank = jnp.zeros((1, LANES), F32)
    border_row = jnp.concatenate(
        [border[...].astype(F32), jnp.zeros((1, LANES - border.shape[1]), F32)], axis=1
    )
    send_row = jnp.concatenate(
        [send[...].astype(F32), jnp.zeros((1, LANES - send.shape[1]), F32)], axis=1
    )
    rest = jnp.concatenate([pos, border_row, send_row, blank, blank, blank], axis=0)
    others = jnp.concatenate(sorted_rows + [rest], axis=0).astype(BF16)
    for group in range(data_out.shape[0]):
        data_out[group, 0:half, :] = scalars
        data_out[group, half:, :] = others
    at = 0
    for piece in (b_in, b_mix, w_out, probe_list, probe_count):
        rows, cols = piece.shape
        small_out[at : at + rows, 0:cols] = piece[...].astype(F32)
        at += rows
    probe_rows = [w_probe[r].astype(F32) for r in range(w_probe.shape[0])]
    radial = jnp.concatenate([w_rad[...].astype(F32)] + probe_rows, axis=0).T.astype(BF16)
    weight_out[: w_msg.shape[0], :] = w_msg[...]
    weight_out[w_msg.shape[0] :, :] = radial


def pack(
    groups, atom_s, atom_pos, edge_vec, edge_nbr, border_index, send_index, w_msg, w_rad, w_probe,
    b_in, b_mix, w_out, probe_list, probe_count,
):
    atoms, half = atom_s.shape
    fan = edge_nbr.shape[0] // atoms
    return pl.pallas_call(
        functools.partial(pack_kernel, fan),
        out_shape=(
            jax.ShapeDtypeStruct((groups, half + 4 * fan // 2 + 8, LANES), BF16),
            jax.ShapeDtypeStruct((w_msg.size // LANES + half, LANES), BF16),
            jax.ShapeDtypeStruct((SMALL, LANES), F32),
        ),
        scratch_shapes=[pltpu.VMEM((LANES, LANES), F32)],
        name="pack",
    )(
        atom_s.T,
        atom_pos,
        edge_vec,
        edge_nbr.reshape(-1, LANES),
        border_index.reshape(1, -1),
        send_index,
        jnp.transpose(w_msg, (0, 2, 3, 1)).reshape(-1, LANES),
        jnp.transpose(w_rad, (0, 2, 1, 3)).reshape(-1, half),
        w_probe,
        b_in,
        b_mix.reshape(1, -1),
        w_out.reshape(1, -1),
        probe_list,
        probe_count.reshape(1, -1),
    )


def probe_grid(me, probes):
    number = me * probes + iota((1, probes), 1)
    return [(n % 16).astype(F32) * 0.25 - 1.875 for n in (number, number // 16, number // 256)]


def probe_kernel(sizes, list_at, data_mine, small, chosen_rows, probe_basis):
    groups, fan, rim, half, n_basis, cap, n_blocks = sizes
    width = 2 * half
    tiles = fan
    every = groups * LANES
    me = lax.axis_index("brick") * lax.axis_size("probe") + lax.axis_index("probe")
    rest_at = half + 4 * fan // 2
    small_rows = small[...]
    received = groups * cap
    edges = received * fan
    send_rows = jnp.concatenate(
        [data_mine[g, rest_at : rest_at + 8, :].astype(F32)[4:5] for g in range(groups)], axis=0
    )

    def picks(lane_count, per_group):
        lane = iota((LANES, lane_count), 1)
        wanted = me * cap + lane % cap
        spread = dot(send_rows.astype(BF16), one_hot(iota((LANES, lane_count), 0) == wanted))
        lane = iota((groups, lane_count), 1)
        spread = jnp.where(lane // per_group == iota((groups, lane_count), 0), spread, 0.0)
        return jnp.sum(spread, axis=0, keepdims=True)

    per_group = fan * cap
    pick_atoms = picks(received, cap)
    column = iota((every, 1), 0)
    column_name = (column // LANES) * LANES + lane_atom(column % LANES, fan, tiles)
    wanted = (iota((1, received), 1) // cap) * LANES + pick_atoms.astype(jnp.int32)
    chosen_atoms = one_hot(column_name == wanted)

    pos_rows = jnp.concatenate(
        [data_mine[g, rest_at : rest_at + 8, :] for g in range(groups)], axis=1
    )
    pos = dot(pos_rows, chosen_atoms) - 1.875
    chosen_rows[0:1, :] = picks(edges, per_group)
    chosen_rows[1:2, 0:received] = pick_atoms
    chosen_rows[2:5, 0:received] = pos[0:3]
    pos_cols = jnp.concatenate(
        [
            jnp.concatenate([pos, jnp.zeros((8, LANES - received), F32)], axis=1),
            jnp.zeros((LANES - 8, LANES), F32),
        ],
        axis=0,
    ).T
    list_len = width
    counts = []
    for block in range(n_blocks):
        live = iota((1, list_len), 1).astype(F32) < small_rows[list_at + n_blocks : list_at + n_blocks + 1, block : block + 1]
        named = jnp.where(live, small_rows[list_at + block : list_at + block + 1], -1.0)
        hits = jnp.where(iota((received, list_len), 0).astype(F32) == named, 1.0, 0.0)
        counts.append(
            jnp.broadcast_to(jnp.sum(hits, axis=1, keepdims=True), (received, PB))
        )
    counts = jnp.concatenate(counts, axis=1)
    probes = n_blocks * PB
    grid = probe_grid(me, probes)
    dist_sq = jnp.zeros((received, probes), F32)
    for x in range(3):
        dist_sq = dist_sq + (grid[x] - pos_cols[0:received, x : x + 1]) ** 2
    dist = jnp.sqrt(dist_sq) * ROOT
    envelope = (1.0 - dist_sq / 64.0) ** 2 * counts
    probe_basis[...] = jnp.concatenate(
        [
            (bell(dist, r * (ROOT * 7.0 / (n_basis - 1))) * envelope).astype(BF16)
            for r in range(n_basis)
        ],
        axis=0,
    )


def density_kernel(
    sizes,
    data_mine,
    data_other,
    weights_mine,
    weights_other,
    small,
    w_in,
    w_mix,
    chosen_rows,
    probe_basis,
    density,
    state0,
    own0,
    faces0,
    state1,
    weights,
):
    groups, fan, rim, half, n_basis, cap, n_blocks = sizes
    layers = w_in.shape[0]
    width = 2 * half
    tiles = LANES * fan // LANES
    root_fan = fan**0.5
    me = lax.axis_index("brick") * lax.axis_size("probe") + lax.axis_index("probe")
    part = lax.axis_index("chan")
    weights[part] = weights_mine[...]
    weights[1 - part] = weights_other[...]
    every = groups * LANES
    edge_at = half
    n_edge = 4 * fan // 2
    rest_at = half + n_edge

    def data(group, c, rows):
        return (data_mine, data_other)[c][group, rows, :]

    def weight(layer, p):
        at = (layer * 3 + p) * half
        return jnp.concatenate([weights[c, at : at + half, :] for c in range(2)], axis=0)

    def radial_weight(layer, p):
        at = (layer * 3 + p) * n_basis
        return radial_all[:, at : at + n_basis]

    def edge_rows(group):
        return [data(group, c, slice(edge_at, rest_at)).astype(F32) for c in range(2)]

    def border_of(group):
        return data(group, 0, slice(rest_at, rest_at + 8)).astype(F32)[3:4, 0 : 2 * rim]

    centers = iota((n_basis, 1), 0).astype(F32) * (ROOT * 6.0 / (n_basis - 1))

    def basis_of(length, env):
        return (bell(length * ROOT, centers) * env).astype(BF16)

    received = groups * cap
    edges = received * fan
    per_group = fan * cap
    pick_edges = chosen_rows[0:1, :]
    pick_atoms = chosen_rows[1:2, 0:received]
    pos = chosen_rows[2:5, 0:received]
    atom_rows = lane_atom(iota((LANES, per_group), 0), fan, tiles).astype(F32)
    chosen = []
    for group in range(groups):
        rows = jnp.concatenate([data(group, c, slice(edge_at, rest_at)) for c in range(2)], axis=0)
        want = pick_edges[:, group * per_group : (group + 1) * per_group]
        chosen.append(dot(rows, one_hot(atom_rows == want)))
    chosen = jnp.concatenate(chosen, axis=1)
    step = fan // 2
    row = iota((2 * n_edge, edges), 0)
    slot_k = (row // n_edge) * step + row % step
    lane_k = (iota((2 * n_edge, edges), 1) % per_group) // cap
    chosen = jnp.where(slot_k == lane_k, chosen, 0.0)
    chosen = jnp.sum(chosen.reshape(2 * 4, step, edges), axis=1)
    chosen = chosen[0:4] + chosen[4:8]
    pick_vec = [chosen[x : x + 1] for x in range(3)]
    nbr = chosen[3:4]
    length = jnp.sqrt(sum(x * x for x in pick_vec))
    basis1 = basis_of(length, (1.0 - length * length / 36.0) ** 2)

    nbr = nbr.astype(jnp.int32)
    home = iota((1, edges), 1) // per_group
    is_low = (nbr >= LANES) & (nbr < LANES + rim)
    is_up = nbr >= LANES + rim
    owner = jnp.where(
        is_low, (home + groups - 1) % groups, jnp.where(is_up, (home + 1) % groups, home)
    )
    entry = owner * 2 * rim + jnp.where(is_low, nbr - (LANES - rim), nbr - (LANES + rim))
    entry = jnp.where(is_low | is_up, entry, -1)
    border_all = jnp.concatenate(
        [border_of(g) for g in range(groups)], axis=1
    )
    border_all = jnp.broadcast_to(border_all, (16, groups * 2 * rim)).astype(BF16)
    seen = dot(border_all, one_hot(iota((groups * 2 * rim, edges), 0) == entry))[0:1]
    target_atom = jnp.where(entry < 0, nbr, seen.astype(jnp.int32))
    column = iota((every, 1), 0)
    column_name = (column // LANES) * LANES + lane_atom(column % LANES, fan, tiles)
    quad = groups // 2
    window = [[(h * quad + groups - 1 + i) % groups for i in range(quad + 2)] for h in range(2)]
    window_pick = []
    for h in range(2):
        lanes = slice(h * edges // 2, (h + 1) * edges // 2)
        near = lax.rem(owner[:, lanes] + 2 * groups - (h * quad + groups - 1), groups)
        name = near * LANES + target_atom[:, lanes]
        window_pick.append(one_hot(column_name[: (quad + 2) * LANES] == name))
    wanted = (iota((1, received), 1) // cap) * LANES + pick_atoms.astype(jnp.int32)
    chosen_atoms = one_hot(column_name == wanted)

    small_rows = small[...]
    columns = small_rows.T
    radial_at = weights.shape[1] - half
    radial_all = jnp.concatenate([weights[c, radial_at:, :] for c in range(2)], axis=0)

    terms_shape = (2 * n_basis, n_basis * received)
    probe_weight = radial_all[:, 3 * layers * n_basis :]
    w_scalar, w_vector = (
        dot(probe_weight, one_hot(iota(terms_shape, 1) // received * 2 + p == iota(terms_shape, 0)))
        for p in range(2)
    )

    probes = density.shape[1]
    grid = probe_grid(me, probes)

    for group in range(groups):
        for c in range(2):
            place = part if c == 0 else 1 - part
            rows = pl.ds(pl.multiple_of(place * half, half), half)
            state0[rows, group * LANES : (group + 1) * LANES] = data(group, c, slice(0, half))
    hidden = silu(dot_tn(w_in[0], state0[...]) + columns[:, 0:1]).astype(BF16)
    weight_ac = jnp.concatenate([weight(0, 0), weight(0, 2)], axis=0)
    messages = dot(weight_ac, hidden).astype(BF16)
    atom_col = lane_atom(iota((LANES, 2 * rim), 0), fan, tiles).astype(F32)
    for group in range(groups):
        own = messages[:, group * LANES : (group + 1) * LANES]
        own0[group] = own
        border_row = border_of(group)
        faces0[group, :, 0 : 2 * rim] = dot(own, one_hot(atom_col == border_row)).astype(BF16)

    row = iota((LANES + 2 * rim, 1), 0)
    names = jnp.where(
        row < LANES,
        lane_atom(row, fan, tiles),
        jnp.where(row < LANES + rim, row + rim, row - rim),
    ).astype(F32)
    names = jnp.broadcast_to(names, (LANES + 2 * rim, LANES)).astype(BF16)
    upper_lane = iota((2 * width, 2 * rim), 1) < rim
    radial_ac = jnp.concatenate([radial_weight(0, 0), radial_weight(0, 2)], axis=0)
    radial_rows = jnp.concatenate([jnp.zeros((2 * width, LANES + 2 * rim), BF16), radial_ac], axis=1)
    blank = jnp.zeros((2 * width, n_basis), BF16)

    for group in range(groups):
        up = (group + 1) % groups
        low = (group + groups - 1) % groups
        ghosts = jnp.where(
            upper_lane,
            faces0[up, :, 0 : 2 * rim].astype(F32),
            faces0[low, :, 0 : 2 * rim].astype(F32),
        ).astype(BF16)
        table = jnp.concatenate([own0[group], ghosts, blank], axis=1)
        left = jnp.concatenate(
            [
                block[at : at + 16]
                for at in range(0, 2 * width, 16)
                for block in (table, radial_rows)
            ],
            axis=0,
        )
        halves = edge_rows(group)
        step = fan // 2
        acc = jnp.zeros((width, LANES), F32)
        acc_vec = [jnp.zeros((width, LANES), F32) for _ in range(3)]
        for c in range(2):
            rows = halves[c]
            vec = [rows[x * step : (x + 1) * step] for x in range(3)]
            nbr = rows[3 * step : 4 * step]
            length_sq = vec[0] * vec[0] + vec[1] * vec[1] + vec[2] * vec[2]
            length = jnp.sqrt(length_sq)
            env = (1.0 - length * length / 36.0) ** 2
            for first in range(0, step, TOGETHER):
                ks = range(first, first + TOGETHER)
                picked = jnp.concatenate([same(names, nbr[k : k + 1].astype(BF16)) for k in ks], axis=1)
                basis = jnp.concatenate(
                    [basis_of(length[k : k + 1], env[k : k + 1]) for k in ks], axis=1
                )
                both = dot(left, jnp.concatenate([picked, basis], axis=0))
                prod = jnp.concatenate(
                    [both[at : at + 16] * both[at + 16 : at + 32] for at in range(0, 4 * width, 32)],
                    axis=0,
                )
                for i, k in enumerate(ks):
                    block = prod[:, i * LANES : (i + 1) * LANES]
                    acc = acc + block[:width]
                    for x in range(3):
                        acc_vec[x] = acc_vec[x] + block[width:] * vec[x][k : k + 1]
        lanes = slice(group * LANES, (group + 1) * LANES)
        state1[0:width, lanes] = (state0[:, lanes].astype(F32) + acc / root_fan).astype(BF16)
        for x in range(3):
            state1[(x + 1) * width : (x + 2) * width, lanes] = (acc_vec[x] / root_fan).astype(BF16)

    rows = []
    for h in range(2):
        near_states = jnp.concatenate(
            [state1[:, g * LANES : (g + 1) * LANES] for g in window[h]], axis=1
        )
        rows.append(dot(near_states, window_pick[h]))
    rows = jnp.concatenate(rows, axis=1)
    hidden = silu(dot_tn(w_in[1], rows[:width].astype(BF16)) + columns[:, 1:2]).astype(BF16)
    weight_abc = jnp.concatenate([weight(1, p) for p in range(3)], axis=0)
    messages = dot(weight_abc, hidden).astype(BF16).astype(F32)
    radial_abc = jnp.concatenate([radial_weight(1, p) for p in range(3)], axis=0)
    filters = dot(radial_abc, basis1)
    weighted = messages * filters
    gate = weighted[width : 2 * width]
    along = weighted[2 * width :]
    parts = [weighted[:width]]
    for x in range(3):
        parts.append(rows[(1 + x) * width : (2 + x) * width] * gate + along * pick_vec[x])
    parts = jnp.concatenate(parts, axis=0).astype(BF16)
    edge = iota((edges, received), 0)
    slot = (edge // per_group) * cap + edge % cap
    delta = dot(parts, one_hot(slot == iota((edges, received), 1)))
    final = (dot(state1[...], chosen_atoms) + delta / root_fan).astype(BF16).astype(F32)

    along = final[width : 2 * width] * pos[0:1]
    for x in range(1, 3):
        along = along + final[(x + 1) * width : (x + 2) * width] * pos[x : x + 1]
    def repeat(value):
        return jnp.concatenate([value] * n_basis, axis=1)
    terms = [w_scalar * repeat(final[:width]) - w_vector * repeat(along)]
    for x in range(3):
        terms.append(w_vector * repeat(final[(x + 1) * width : (x + 2) * width]))
    sums = dot(jnp.concatenate(terms, axis=0).astype(BF16), probe_basis[...])
    charges = sums[:width]
    for x in range(3):
        charges = charges + grid[x] * sums[(x + 1) * width : (x + 2) * width]
    mixed = dot_tn(w_mix[...], charges.astype(BF16)) + columns[:, layers : layers + 1]
    density[...] = jnp.sum(silu(mixed) * columns[:, layers + 1 : layers + 2], axis=0, keepdims=True)


def few_groups(
    atom_s, atom_pos, edge_vec, edge_nbr, border_index, send_index, probe_list, probe_count,
    w_in, b_in, w_msg, w_rad, w_probe, w_mix, b_mix, w_out,
):
    atoms, half = atom_s.shape
    groups = lax.axis_size("brick") * lax.axis_size("probe")
    fan = edge_nbr.shape[0] // atoms
    rim = border_index.shape[0] // 2
    n_basis = w_rad.shape[1]
    cap = send_index.shape[1] // groups
    width = 2 * half
    every = groups * LANES
    data, weights, small = pack(
        groups, atom_s, atom_pos, edge_vec, edge_nbr, border_index, send_index, w_msg, w_rad, w_probe,
        b_in, b_mix, w_out, probe_list, probe_count,
    )
    swap = [(0, 1), (1, 0)]
    weights_other = lax.ppermute(weights, "chan", swap)
    mine = lax.all_to_all(data, ("brick", "probe"), split_axis=0, concat_axis=0, tiled=True)
    other = lax.ppermute(mine, "chan", swap)
    n_probes = probe_list.shape[0] * PB
    sizes = (groups, fan, rim, half, n_basis, cap, probe_list.shape[0])
    chosen_rows, probe_basis = pl.pallas_call(
        functools.partial(probe_kernel, sizes, w_in.shape[0] + 2),
        out_shape=(
            jax.ShapeDtypeStruct((8, groups * cap * fan), F32),
            jax.ShapeDtypeStruct((n_basis * groups * cap, n_probes), BF16),
        ),
        compiler_params=pltpu.CompilerParams(vmem_limit_bytes=24 * 1024 * 1024),
        name="probe_basis",
    )(mine, small)
    density = pl.pallas_call(
        functools.partial(density_kernel, sizes),
        out_shape=jax.ShapeDtypeStruct((1, n_probes), F32),
        scratch_shapes=[
            pltpu.VMEM((width, every), BF16),
            pltpu.VMEM((groups, 2 * width, LANES), BF16),
            pltpu.VMEM((groups, 2 * width, LANES), BF16),
            pltpu.VMEM((4 * width, every), BF16),
            pltpu.VMEM((2,) + weights.shape, BF16),
        ],
        compiler_params=pltpu.CompilerParams(vmem_limit_bytes=40 * 1024 * 1024),
        name="density",
    )(mine, other, weights, weights_other, small, w_in, w_mix, chosen_rows, probe_basis)
    return density.reshape(n_probes)


def per_device(*args):
    if lax.axis_size("brick") * lax.axis_size("probe") == FEW_GROUPS:
        return few_groups(*args)
    return many_groups(*args)


def extended(block, sides, width):
    for axis, dim in sides:
        count = lax.axis_size(axis)
        forward = [(i, i + 1) for i in range(count - 1)]
        forward.append((count - 1, 0))
        backward = [(target, source) for source, target in forward]
        low = lax.ppermute(
            lax.slice_in_dim(block, block.shape[dim] - width, None, axis=dim), axis, forward
        )
        high = lax.ppermute(lax.slice_in_dim(block, 0, width, axis=dim), axis, backward)
        block = jnp.concatenate([low, block, high], axis=dim)
    return block


def radial(distance, count, top):
    centers = jnp.arange(count).astype(jnp.float32) * (top / (count - 1))
    return jnp.exp(-2.0 * (distance[..., None] - centers) ** 2)


def make_block(
    recv_rows, recv_pos, w_scalar, w_vector, feat_width, group_no, n_blocks, list_len, n_basis
):

    def probe_block(block_in):
        block_no, listed, live_count = block_in
        index_row = (group_no * n_blocks + block_no) * PB + jnp.arange(PB, dtype=jnp.int32)
        grid_xyz = (
            jnp.stack([index_row % 16, index_row // 16 % 16, index_row // 256 % 16], axis=1).astype(
                jnp.float32
            )
            * 0.25
        )
        atom_xyz = recv_pos[:, listed]
        disp = grid_xyz[:, :, None] - atom_xyz[None]
        dist_sq = jnp.sum(disp * disp, axis=1)
        live = (jnp.arange(list_len, dtype=jnp.int32) < live_count).astype(jnp.float32)
        envelope = (1.0 - dist_sq / 64.0) ** 2 * live[None, :]
        basis = radial(jnp.sqrt(dist_sq), n_basis, 7.0) * envelope[:, :, None]
        scalar_w = basis.astype(jnp.bfloat16).reshape(PB, list_len * n_basis)
        vector_w = (
            (disp[:, :, :, None] * basis[:, None])
            .astype(jnp.bfloat16)
            .reshape(PB, 3 * list_len * n_basis)
        )
        atom_rows = recv_rows[listed]
        atom_terms = (atom_rows[:, None, :feat_width] * w_scalar[None]).reshape(
            list_len * n_basis, feat_width
        )
        vec_rows = jnp.transpose(
            atom_rows[:, feat_width:].reshape(list_len, 3, feat_width), (1, 0, 2)
        )
        vector_terms = (vec_rows[:, :, None, :] * w_vector[None, None]).reshape(
            3 * list_len * n_basis, feat_width
        )
        charge = jnp.dot(scalar_w, atom_terms, preferred_element_type=jnp.float32) + jnp.dot(
            vector_w, vector_terms, preferred_element_type=jnp.float32
        )
        return charge.astype(jnp.bfloat16)

    return probe_block


def many_groups(
    atom_s,
    atom_pos,
    edge_vec,
    edge_nbr,
    border_index,
    send_index,
    probe_list,
    probe_count,
    w_in,
    b_in,
    w_msg,
    w_rad,
    w_probe,
    w_mix,
    b_mix,
    w_out,
):
    atom_count, half_width = atom_s.shape
    n_layers = w_in.shape[0]
    width = w_in.shape[1]
    n_basis = w_rad.shape[1]
    fan_out = edge_nbr.shape[0] // atom_count
    root_fan = fan_out**0.5
    rim_rows = border_index.shape[0] // 2
    length = jnp.sqrt(jnp.sum(edge_vec * edge_vec, axis=0))
    edge_env = (1.0 - length * length / 36.0) ** 2
    edge_basis = (radial(length, n_basis, 6.0) * edge_env[:, None]).astype(jnp.bfloat16)
    edge_cols = jnp.transpose(edge_vec)
    scalars = atom_s
    vectors = jnp.zeros((atom_count, 3 * half_width), jnp.bfloat16)
    for layer_no in range(n_layers):
        full_rows = lax.all_gather(scalars, "chan", axis=1, tiled=True)
        in_weight = w_in[layer_no]
        in_bias = b_in[layer_no]
        msg_weight = w_msg[layer_no].reshape(width, 3 * half_width)
        rad_weight = w_rad[layer_no].reshape(n_basis, 3 * half_width)
        hidden_act = jax.nn.silu(
            jnp.dot(full_rows, in_weight, preferred_element_type=jnp.float32) + in_bias
        ).astype(jnp.bfloat16)
        inner_tab = jnp.concatenate(
            [
                jnp.dot(hidden_act, msg_weight, preferred_element_type=jnp.float32).astype(
                    jnp.bfloat16
                ),
                vectors,
            ],
            axis=1,
        )
        padded = extended(inner_tab[border_index], ((("brick", "probe"), 0),), rim_rows)
        lookup = jnp.concatenate([inner_tab, padded[:rim_rows], padded[3 * rim_rows :]], axis=0)
        neighbour_rows = lookup[edge_nbr]
        filters = jnp.dot(edge_basis, rad_weight, preferred_element_type=jnp.float32)
        weighted = neighbour_rows[:, : 3 * half_width] * filters
        neighbour_vec = neighbour_rows[:, 3 * half_width :].reshape(-1, 3, half_width)
        vector_gate = weighted[:, None, half_width : 2 * half_width]
        along_edge = weighted[:, None, 2 * half_width :]
        delta_vec = neighbour_vec * vector_gate + along_edge * edge_cols[:, :, None]
        delta_scalar = (
            weighted[:, :half_width].reshape(atom_count, fan_out, half_width).sum(axis=1) / root_fan
        )
        delta_vec = delta_vec.reshape(atom_count, fan_out, 3 * half_width).sum(axis=1) / root_fan
        scalars = (scalars + delta_scalar).astype(jnp.bfloat16)
        vectors = (vectors + delta_vec).astype(jnp.bfloat16)
    features = jnp.concatenate([scalars, vectors], axis=1)
    picks = send_index[0]
    n_brick = lax.axis_size("brick")
    n_probe = lax.axis_size("probe")
    n_groups = n_brick * n_probe
    slot_cap = picks.shape[0] // n_groups
    out_rows = features[picks]
    out_pos = jnp.transpose(atom_pos)[picks].astype(jnp.bfloat16)
    received = (
        lax.all_to_all(
            out_rows.reshape(n_groups, slot_cap, 4 * half_width),
            ("brick", "probe"),
            split_axis=0,
            concat_axis=0,
            tiled=True,
        ),
        lax.all_to_all(
            out_pos.reshape(n_groups, slot_cap, 3),
            ("brick", "probe"),
            split_axis=0,
            concat_axis=0,
            tiled=True,
        ),
    )
    recv_count = n_groups * slot_cap
    recv_rows = received[0].reshape(recv_count, 4 * half_width)
    recv_pos = jnp.transpose(received[1].reshape(recv_count, 3)).astype(jnp.float32)
    group_no = lax.axis_index("brick") * n_probe + lax.axis_index("probe")
    n_blocks, list_len = probe_list.shape
    probe_block = make_block(
        recv_rows,
        recv_pos,
        w_probe[:, 0, :],
        w_probe[:, 1, :],
        half_width,
        group_no,
        n_blocks,
        list_len,
        n_basis,
    )
    charges = lax.map(
        probe_block, (jnp.arange(n_blocks, dtype=jnp.int32), probe_list, probe_count)
    ).reshape(n_blocks * PB, half_width)
    mix_rows = lax.dynamic_slice_in_dim(w_mix, lax.axis_index("chan") * half_width, half_width, 0)
    mixed = lax.psum(jnp.dot(charges, mix_rows, preferred_element_type=jnp.float32), "chan")
    return jnp.sum(jax.nn.silu(mixed + b_mix) * w_out, axis=1)


def solution(mesh):
    in_specs = (
        P(("image", "brick", "probe"), "chan"),
        P(None, ("image", "brick", "probe")),
        P(None, ("image", "brick", "probe")),
        P(("image", "brick", "probe")),
        P(("image", "brick", "probe")),
        P(("image", "brick", "probe"), None),
        P(("image", "brick", "probe"), None),
        P(("image", "brick", "probe")),
        P(),
        P(),
        P(None, None, None, "chan"),
        P(None, None, None, "chan"),
        P(None, None, "chan"),
        P(),
        P(),
        P(),
    )
    out_specs = P(("image", "brick", "probe"))
    return jax.shard_map(
        per_device, mesh=mesh, in_specs=in_specs, out_specs=out_specs, check_vma=False
    )
```

```python
import functools
import itertools
import math

import jax
import jax.numpy as jnp
from jax import lax
from jax.experimental import pallas as pl
from jax.experimental.pallas import tpu as pltpu
from jax.sharding import PartitionSpec as P

PB = 128
LANES = 128
FEW_GROUPS = 8
SMALL = 16
TOGETHER = 2
ROOT = (2.0 * math.log2(math.e)) ** 0.5
F32 = jnp.float32
BF16 = jnp.bfloat16


def iota(shape, dim):
    return lax.broadcasted_iota(jnp.int32, shape, dim)


def dot(a, b):
    return jnp.dot(a, b, preferred_element_type=F32)


def dot_tn(a, b):
    return lax.dot_general(a, b, (((0,), (0,)), ((), ())), preferred_element_type=F32)


def one_hot(mask):
    return jnp.where(mask, 1.0, 0.0).astype(BF16)


def same(names, row):
    return jnp.where(names == row, jnp.ones_like(names), jnp.zeros_like(names))


def silu(x):
    half_x = 0.5 * x
    return half_x * jnp.tanh(half_x) + half_x


def bell(scaled, center):
    away = scaled - center
    return jnp.exp2(-(away * away))


def lane_atom(lane, fan, tiles):
    return (lane % tiles) * (LANES // fan) + lane // tiles


def length_keeping_round(exact):
    choices = []
    for value in exact:
        near = value.astype(BF16).astype(F32)
        step = jnp.where(value > near, 1.01 / 256.0, -1.01 / 256.0) * jnp.abs(near)
        choices.append((near, (near + step).astype(BF16).astype(F32)))
    target = sum(value * value for value in exact)
    best, best_error = None, None
    for picked in itertools.product(*choices):
        error = jnp.abs(sum(value * value for value in picked) - target)
        if best is None:
            best, best_error = picked, error
            continue
        better = error < best_error
        best = tuple(jnp.where(better, new, old) for new, old in zip(picked, best))
        best_error = jnp.where(better, error, best_error)
    return best


def pack_kernel(
    fan, atom_s, atom_pos, edge_vec, edge_nbr, border, send, w_msg, w_rad, w_probe,
    b_in, b_mix, w_out, probe_list, probe_count, data_out, weight_out, small_out, natural,
):
    half, atoms = atom_s.shape
    tiles = atoms * fan // LANES
    per_tile = LANES // fan
    part = lax.axis_index("chan")
    perm = one_hot(lane_atom(iota((atoms, LANES), 1), fan, tiles) == iota((atoms, LANES), 0))
    scalars = dot(atom_s[...], perm).astype(BF16)
    for tile in range(tiles):
        for comp in range(3):
            natural[comp * tiles + tile : comp * tiles + tile + 1, :] = edge_vec[
                comp : comp + 1, tile * LANES : (tile + 1) * LANES
            ]
    exact = [natural[comp * tiles : (comp + 1) * tiles, :] for comp in range(3)]
    for comp, value in enumerate(length_keeping_round(exact)):
        natural[comp * tiles : (comp + 1) * tiles, :] = value
    natural[3 * tiles : 4 * tiles, :] = edge_nbr[...].astype(F32)
    natural[4 * tiles :, :] = jnp.zeros((LANES - 4 * tiles, LANES), F32)
    turned = natural[...].T
    lane = iota((fan, LANES), 1)
    sorted_rows = []
    for comp in range(4):
        rows = jnp.zeros((fan, LANES), F32)
        for a in range(per_tile):
            piece = turned[a * fan : (a + 1) * fan, :]
            shift = (a * tiles - comp * tiles) % LANES
            piece = pltpu.roll(piece, shift, 1) if shift else piece
            rows = jnp.where(lane // tiles == a, piece, rows)
        sorted_rows.append(rows)
    blank = jnp.zeros((1, LANES), F32)
    every_edge = jnp.concatenate(sorted_rows, axis=0).astype(BF16)
    sorted_rows = [jnp.where(part == 0, rows[: fan // 2], rows[fan // 2 :]) for rows in sorted_rows]
    border_row = jnp.concatenate(
        [border[...].astype(F32), jnp.zeros((1, LANES - border.shape[1]), F32)], axis=1
    )
    picks = send.shape[1]
    groups = data_out.shape[0]
    cap = picks // groups
    block = fan * cap
    lane = iota((picks, groups * block), 1)
    place = (lane // block) * cap + lane % cap
    send_row = jnp.broadcast_to(send[...].astype(F32), (8, picks)).astype(BF16)
    wanted = dot(send_row, one_hot(iota((picks, groups * block), 0) == place))[0:1]
    atom_col = lane_atom(iota((LANES, groups * block), 0), fan, tiles).astype(F32)
    spread = dot(every_edge, one_hot(atom_col == wanted))
    edge_k = iota(spread.shape, 0) % fan
    spread = jnp.where(edge_k == (iota(spread.shape, 1) % block) // cap, spread, 0.0)
    picked = jnp.sum(spread.reshape(4, fan, groups * block), axis=1)
    pick_atom = one_hot(iota((atoms, picks), 0).astype(F32) == send[...].astype(F32))
    facts = [send[...].astype(F32)]
    pos = dot(atom_pos[...].astype(BF16), pick_atom)
    facts += [pos[x : x + 1] for x in range(3)]
    owner = iota((groups, picks), 1) // cap == iota((groups, picks), 0)
    facts = jnp.concatenate([jnp.where(owner, fact, 0.0) for fact in facts], axis=1)
    row = iota((4 * picks, LANES), 0)
    place = (row // picks) * cap + row % cap
    facts = dot(facts.astype(BF16), one_hot(place == iota((4 * picks, LANES), 1)))
    edge_part = jnp.concatenate(sorted_rows, axis=0).astype(BF16)
    for group in range(groups):
        mine = slice(group * block, (group + 1) * block)
        rest = [facts[group : group + 1], border_row]
        for comp in (0, 2):
            rest.append(
                jnp.concatenate([picked[comp : comp + 1, mine], picked[comp + 1 : comp + 2, mine]], axis=1)
            )
        rest = jnp.concatenate(rest + [blank] * 4, axis=0)
        data_out[group, 0:half, :] = scalars
        data_out[group, half : half + 2 * fan, :] = edge_part
        data_out[group, half + 2 * fan :, :] = rest.astype(BF16)
    at = 0
    for piece in (b_in, b_mix, w_out, probe_list, probe_count):
        rows, cols = piece.shape
        small_out[at : at + rows, 0:cols] = piece[...].astype(F32)
        at += rows
    probe_rows = [w_probe[r].astype(F32) for r in range(w_probe.shape[0])]
    radial = jnp.concatenate([w_rad[...].astype(F32)] + probe_rows, axis=0).T.astype(BF16)
    weight_out[: w_msg.shape[0], :] = w_msg[...]
    weight_out[w_msg.shape[0] :, :] = radial


def pack(
    groups, atom_s, atom_pos, edge_vec, edge_nbr, border_index, send_index, w_msg, w_rad, w_probe,
    b_in, b_mix, w_out, probe_list, probe_count,
):
    atoms, half = atom_s.shape
    fan = edge_nbr.shape[0] // atoms
    return pl.pallas_call(
        functools.partial(pack_kernel, fan),
        out_shape=(
            jax.ShapeDtypeStruct((groups, half + 4 * fan // 2 + 8, LANES), BF16),
            jax.ShapeDtypeStruct((w_msg.size // LANES + half, LANES), BF16),
            jax.ShapeDtypeStruct((SMALL, LANES), F32),
        ),
        scratch_shapes=[pltpu.VMEM((LANES, LANES), F32)],
        name="pack",
    )(
        atom_s.T,
        atom_pos,
        edge_vec,
        edge_nbr.reshape(-1, LANES),
        border_index.reshape(1, -1),
        send_index,
        jnp.transpose(w_msg, (0, 2, 3, 1)).reshape(-1, LANES),
        jnp.transpose(w_rad, (0, 2, 1, 3)).reshape(-1, half),
        w_probe,
        b_in,
        b_mix.reshape(1, -1),
        w_out.reshape(1, -1),
        probe_list,
        probe_count.reshape(1, -1),
    )


def probe_grid(me, probes):
    number = me * probes + iota((1, probes), 1)
    return [(n % 16).astype(F32) * 0.25 - 1.875 for n in (number, number // 16, number // 256)]


def index_kernel(sizes, list_at, data_mine, small, facts_out, slots, probe_basis):
    groups, fan, rim, half, n_basis, cap, n_blocks = sizes
    tiles = fan
    received = groups * cap
    per_group = fan * cap
    edges = received * fan
    rest_at = half + 2 * fan
    me = lax.axis_index("brick") * lax.axis_size("probe") + lax.axis_index("probe")
    small_rows = small[...]
    rest = [data_mine[g, rest_at : rest_at + 8, :].astype(F32) for g in range(groups)]
    facts = jnp.concatenate([rows[0:1] for rows in rest], axis=0).astype(BF16)
    lane = iota((LANES, 4 * received), 1)
    wanted = (lane // received) * cap + lane % cap
    facts = dot(facts, one_hot(iota((LANES, 4 * received), 0) == wanted))
    source = (iota(facts.shape, 1) % received) // cap
    facts = jnp.sum(jnp.where(source == iota(facts.shape, 0), facts, 0.0), axis=0, keepdims=True)
    pick_atoms = facts[:, 0:received]
    for comp in range(3):
        rows = [r[2 + comp // 2 : 3 + comp // 2, (comp % 2) * per_group :][:, :per_group] for r in rest]
        facts_out[comp : comp + 1, :] = jnp.concatenate(rows, axis=1)
    nbr = jnp.concatenate([r[3:4, per_group : 2 * per_group] for r in rest], axis=1).astype(jnp.int32)

    home = iota((1, edges), 1) // per_group
    is_low = (nbr >= LANES) & (nbr < LANES + rim)
    is_up = nbr >= LANES + rim
    owner = jnp.where(
        is_low, (home + groups - 1) % groups, jnp.where(is_up, (home + 1) % groups, home)
    )
    entry = owner * 2 * rim + jnp.where(is_low, nbr - (LANES - rim), nbr - (LANES + rim))
    entry = jnp.where(is_low | is_up, entry, -1)
    border_all = jnp.concatenate([r[1:2, 0 : 2 * rim] for r in rest], axis=1)
    border_all = jnp.broadcast_to(border_all, (16, groups * 2 * rim)).astype(BF16)
    seen = dot(border_all, one_hot(iota((groups * 2 * rim, edges), 0) == entry))[0:1]
    target = jnp.where(entry < 0, nbr, seen.astype(jnp.int32))

    column = iota((groups * LANES, 1), 0)
    column_name = (column // LANES) * LANES + lane_atom(column % LANES, fan, tiles)
    home = iota((1, received), 1) // cap
    self_hot = one_hot(column_name == home * LANES + pick_atoms.astype(jnp.int32))
    uses = dot(self_hot, jnp.ones((received, LANES), BF16))
    uses = [uses[g * LANES : (g + 1) * LANES] for g in range(groups)]
    quad = groups // 2
    window_hot, near_groups = [], []
    for h in range(2):
        lanes = slice(h * edges // 2, (h + 1) * edges // 2)
        near = lax.rem(owner[:, lanes] + 2 * groups - (h * quad + groups - 1), groups)
        hot = one_hot(column_name[: (quad + 2) * LANES] == near * LANES + target[:, lanes])
        window_hot.append(hot)
        near_groups.append(near)
        used = dot(hot, jnp.ones((edges // 2, LANES), BF16))
        for i in range(quad + 2):
            g = (h * quad + groups - 1 + i) % groups
            uses[g] = uses[g] + used[i * LANES : (i + 1) * LANES]
    lane = iota((LANES, LANES), 1)
    needed = jnp.zeros((LANES, LANES), F32)
    for g in range(groups):
        needed = jnp.where((lane == g) & (uses[g] > 0.0), 1.0, needed)
    order = dot(one_hot(lane <= iota((LANES, LANES), 0)), needed.astype(BF16))
    slot = jnp.where(needed > 0.0, order - 1.0, -1.0)
    slots[...] = slot
    slot_rows = slot.T
    facts_out[8:9, 0:LANES] = order[LANES - 1 : LANES, :]

    for h in range(2):
        lanes = slice(h * edges // 2, (h + 1) * edges // 2)
        in_window = [(h * quad + groups - 1 + i) % groups for i in range(quad + 2)]
        row = jnp.concatenate([slot_rows[g : g + 1] for g in in_window], axis=1)
        row = jnp.broadcast_to(row, (16, (quad + 2) * LANES)).astype(BF16)
        place = dot(row, window_hot[h])[0:1]
        facts_out[3:4, lanes] = near_groups[h].astype(F32) * LANES + place
    row = jnp.concatenate([slot_rows[g : g + 1] for g in range(groups)], axis=1)
    row = jnp.broadcast_to(row, (16, groups * LANES)).astype(BF16)
    facts_out[7:8, 0:received] = home.astype(F32) * LANES + dot(row, self_hot)[0:1]

    shifted = facts - 1.875
    for x in range(3):
        facts_out[4 + x : 5 + x, 0:received] = shifted[:, (1 + x) * received : (2 + x) * received]
    pos_cols = jnp.broadcast_to(shifted, (LANES, 4 * received)).T
    list_len = LANES
    counts = []
    for block in range(n_blocks):
        limit = small_rows[list_at + n_blocks : list_at + n_blocks + 1, block : block + 1]
        live = iota((1, list_len), 1).astype(F32) < limit
        named = jnp.where(live, small_rows[list_at + block : list_at + block + 1], -1.0)
        hits = jnp.where(iota((received, list_len), 0).astype(F32) == named, 1.0, 0.0)
        counts.append(jnp.broadcast_to(jnp.sum(hits, axis=1, keepdims=True), (received, PB)))
    counts = jnp.concatenate(counts, axis=1)
    probes = n_blocks * PB
    grid = probe_grid(me, probes)
    dist_sq = jnp.zeros((received, probes), F32)
    for x in range(3):
        dist_sq = dist_sq + (grid[x] - pos_cols[(1 + x) * received : (2 + x) * received, 0:1]) ** 2
    dist = jnp.sqrt(dist_sq) * ROOT
    envelope = (1.0 - dist_sq / 64.0) ** 2 * counts
    probe_basis[...] = jnp.concatenate(
        [
            (bell(dist, r * (ROOT * 7.0 / (n_basis - 1))) * envelope).astype(BF16)
            for r in range(n_basis)
        ],
        axis=0,
    )


def density_kernel(
    sizes,
    data_mine,
    data_other,
    weights_mine,
    weights_other,
    small,
    w_in,
    w_mix,
    facts,
    slots,
    probe_basis,
    density,
    state0,
    own0,
    faces0,
    state1,
    weights,
):
    groups, fan, rim, half, n_basis, cap, n_blocks = sizes
    layers = w_in.shape[0]
    width = 2 * half
    tiles = LANES * fan // LANES
    root_fan = fan**0.5
    me = lax.axis_index("brick") * lax.axis_size("probe") + lax.axis_index("probe")
    part = lax.axis_index("chan")
    weights[part] = weights_mine[...]
    weights[1 - part] = weights_other[...]
    every = groups * LANES
    edge_at = half
    n_edge = 4 * fan // 2
    rest_at = half + n_edge

    def data(group, c, rows):
        return (data_mine, data_other)[c][group, rows, :]

    def weight(layer, p):
        at = (layer * 3 + p) * half
        return jnp.concatenate([weights[c, at : at + half, :] for c in range(2)], axis=0)

    def radial_weight(layer, p):
        at = (layer * 3 + p) * n_basis
        return radial_all[:, at : at + n_basis]

    def edge_rows(group):
        return [data(group, c, slice(edge_at, rest_at)).astype(F32) for c in range(2)]

    def border_of(group):
        return data(group, 0, slice(rest_at, rest_at + 8)).astype(F32)[1:2, 0 : 2 * rim]

    centers = iota((n_basis, 1), 0).astype(F32) * (ROOT * 6.0 / (n_basis - 1))

    def basis_of(length, env):
        return (bell(length * ROOT, centers) * env).astype(BF16)

    small_rows = small[...]
    columns = small_rows.T
    radial_at = weights.shape[1] - half
    radial_all = jnp.concatenate([weights[c, radial_at:, :] for c in range(2)], axis=0)

    received = groups * cap
    edges = received * fan
    per_group = fan * cap
    pick_vec = [facts[x : x + 1, :] for x in range(3)]
    pos = facts[4:7, 0:received]
    length = jnp.sqrt(sum(x * x for x in pick_vec))
    basis1 = basis_of(length, (1.0 - length * length / 36.0) ** 2)
    quad = groups // 2
    window = [[(h * quad + groups - 1 + i) % groups for i in range(quad + 2)] for h in range(2)]
    near_row = iota(((quad + 2) * LANES, edges // 2), 0).astype(F32)
    window_pick = [
        one_hot(near_row == facts[3:4, h * edges // 2 : (h + 1) * edges // 2]) for h in range(2)
    ]
    chosen_atoms = one_hot(iota((every, received), 0).astype(F32) == facts[7:8, 0:received])

    terms_shape = (2 * n_basis, n_basis * received)
    probe_weight = radial_all[:, 3 * layers * n_basis :]
    w_scalar, w_vector = (
        dot(probe_weight, one_hot(iota(terms_shape, 1) // received * 2 + p == iota(terms_shape, 0)))
        for p in range(2)
    )

    probes = density.shape[1]
    grid = probe_grid(me, probes)

    for group in range(groups):
        for c in range(2):
            place = part if c == 0 else 1 - part
            rows = pl.ds(pl.multiple_of(place * half, half), half)
            state0[rows, group * LANES : (group + 1) * LANES] = data(group, c, slice(0, half))
    hidden = silu(dot_tn(w_in[0], state0[...]) + columns[:, 0:1]).astype(BF16)
    weight_ac = jnp.concatenate([weight(0, 0), weight(0, 2)], axis=0)
    messages = dot(weight_ac, hidden).astype(BF16)
    atom_col = lane_atom(iota((LANES, 2 * rim), 0), fan, tiles).astype(F32)
    for group in range(groups):
        own = messages[:, group * LANES : (group + 1) * LANES]
        own0[group] = own
        border_row = border_of(group)
        faces0[group, :, 0 : 2 * rim] = dot(own, one_hot(atom_col == border_row)).astype(BF16)

    row = iota((LANES + 2 * rim, 1), 0)
    names = jnp.where(
        row < LANES,
        lane_atom(row, fan, tiles),
        jnp.where(row < LANES + rim, row + rim, row - rim),
    ).astype(F32)
    names = jnp.broadcast_to(names, (LANES + 2 * rim, LANES)).astype(BF16)
    upper_lane = iota((2 * width, 2 * rim), 1) < rim
    radial_ac = jnp.concatenate([radial_weight(0, 0), radial_weight(0, 2)], axis=0)
    radial_rows = jnp.concatenate([jnp.zeros((2 * width, LANES + 2 * rim), BF16), radial_ac], axis=1)
    blank = jnp.zeros((2 * width, n_basis), BF16)

    some = LANES // 2
    step = fan // 2

    def update(group, first_slot):
        up = (group + 1) % groups
        low = (group + groups - 1) % groups
        ghosts = jnp.where(
            upper_lane,
            faces0[up, :, 0 : 2 * rim].astype(F32),
            faces0[low, :, 0 : 2 * rim].astype(F32),
        ).astype(BF16)
        table = jnp.concatenate([own0[group], ghosts, blank], axis=1)
        left = jnp.concatenate(
            [
                block[at : at + 16]
                for at in range(0, 2 * width, 16)
                for block in (table, radial_rows)
            ],
            axis=0,
        )
        lanes = slice(group * LANES, (group + 1) * LANES)
        slot_lane = (iota((LANES, some), 1) + first_slot).astype(F32)
        in_slot = one_hot(slots[:, group : group + 1] == slot_lane)
        source = jnp.concatenate(
            [data(group, c, slice(edge_at, rest_at)) for c in range(2)] + [state0[:, lanes]], axis=0
        )
        source = dot(source, in_slot)
        rows = jnp.concatenate([source[:n_edge], source[n_edge : 2 * n_edge]], axis=1)
        own_scalars = source[2 * n_edge :]
        vec = [rows[x * step : (x + 1) * step] for x in range(3)]
        nbr = rows[3 * step : 4 * step]
        length = jnp.sqrt(vec[0] * vec[0] + vec[1] * vec[1] + vec[2] * vec[2])
        env = (1.0 - length * length / 36.0) ** 2
        acc = jnp.zeros((width, LANES), F32)
        acc_vec = [jnp.zeros((width, LANES), F32) for _ in range(3)]
        for first in range(0, step, TOGETHER):
            ks = range(first, first + TOGETHER)
            picked = jnp.concatenate([same(names, nbr[k : k + 1].astype(BF16)) for k in ks], axis=1)
            basis = jnp.concatenate(
                [basis_of(length[k : k + 1], env[k : k + 1]) for k in ks], axis=1
            )
            both = dot(left, jnp.concatenate([picked, basis], axis=0))
            prod = jnp.concatenate(
                [both[at : at + 16] * both[at + 16 : at + 32] for at in range(0, 4 * width, 32)],
                axis=0,
            )
            for i, k in enumerate(ks):
                block = prod[:, i * LANES : (i + 1) * LANES]
                acc = acc + block[:width]
                for x in range(3):
                    acc_vec[x] = acc_vec[x] + block[width:] * vec[x][k : k + 1]
        acc, *acc_vec = [(a[:, :some] + a[:, some:]) / root_fan for a in [acc] + acc_vec]
        return jnp.concatenate([own_scalars + acc] + acc_vec, axis=0)

    for group in range(groups):
        state = update(group, 0)
        state = jnp.concatenate([state, jnp.zeros_like(state)], axis=1)
        state1[:, group * LANES : (group + 1) * LANES] = state.astype(BF16)

    @pl.when(jnp.max(facts[8:9, 0:groups]) > some)
    def _():
        for group in range(groups):

            @pl.when(jnp.max(facts[8:9, group : group + 1]) > some)
            def _():
                lanes = slice(group * LANES + some, (group + 1) * LANES)
                state1[:, lanes] = update(group, some).astype(BF16)

    rows = []
    for h in range(2):
        near_states = jnp.concatenate(
            [state1[:, g * LANES : (g + 1) * LANES] for g in window[h]], axis=1
        )
        rows.append(dot(near_states, window_pick[h]))
    rows = jnp.concatenate(rows, axis=1)
    hidden = silu(dot_tn(w_in[1], rows[:width].astype(BF16)) + columns[:, 1:2]).astype(BF16)
    weight_abc = jnp.concatenate([weight(1, p) for p in range(3)], axis=0)
    messages = dot(weight_abc, hidden).astype(BF16).astype(F32)
    radial_abc = jnp.concatenate([radial_weight(1, p) for p in range(3)], axis=0)
    filters = dot(radial_abc, basis1)
    weighted = messages * filters
    gate = weighted[width : 2 * width]
    along = weighted[2 * width :]
    parts = [weighted[:width]]
    for x in range(3):
        parts.append(rows[(1 + x) * width : (2 + x) * width] * gate + along * pick_vec[x])
    parts = jnp.concatenate(parts, axis=0).astype(BF16)
    edge = iota((edges, received), 0)
    slot = (edge // per_group) * cap + edge % cap
    delta = dot(parts, one_hot(slot == iota((edges, received), 1)))
    final = (dot(state1[...], chosen_atoms) + delta / root_fan).astype(BF16).astype(F32)

    along = final[width : 2 * width] * pos[0:1]
    for x in range(1, 3):
        along = along + final[(x + 1) * width : (x + 2) * width] * pos[x : x + 1]
    def repeat(value):
        return jnp.concatenate([value] * n_basis, axis=1)
    terms = [w_scalar * repeat(final[:width]) - w_vector * repeat(along)]
    for x in range(3):
        terms.append(w_vector * repeat(final[(x + 1) * width : (x + 2) * width]))
    sums = dot(jnp.concatenate(terms, axis=0).astype(BF16), probe_basis[...])
    charges = sums[:width]
    for x in range(3):
        charges = charges + grid[x] * sums[(x + 1) * width : (x + 2) * width]
    mixed = dot_tn(w_mix[...], charges.astype(BF16)) + columns[:, layers : layers + 1]
    density[...] = jnp.sum(silu(mixed) * columns[:, layers + 1 : layers + 2], axis=0, keepdims=True)


def few_groups(
    atom_s, atom_pos, edge_vec, edge_nbr, border_index, send_index, probe_list, probe_count,
    w_in, b_in, w_msg, w_rad, w_probe, w_mix, b_mix, w_out,
):
    atoms, half = atom_s.shape
    groups = lax.axis_size("brick") * lax.axis_size("probe")
    fan = edge_nbr.shape[0] // atoms
    rim = border_index.shape[0] // 2
    n_basis = w_rad.shape[1]
    cap = send_index.shape[1] // groups
    width = 2 * half
    every = groups * LANES
    data, weights, small = pack(
        groups, atom_s, atom_pos, edge_vec, edge_nbr, border_index, send_index, w_msg, w_rad, w_probe,
        b_in, b_mix, w_out, probe_list, probe_count,
    )
    swap = [(0, 1), (1, 0)]
    weights_other = lax.ppermute(weights, "chan", swap)
    mine = lax.all_to_all(data, ("brick", "probe"), split_axis=0, concat_axis=0, tiled=True)
    other = lax.ppermute(mine, "chan", swap)
    n_probes = probe_list.shape[0] * PB
    sizes = (groups, fan, rim, half, n_basis, cap, probe_list.shape[0])
    facts, slots, probe_basis = pl.pallas_call(
        functools.partial(index_kernel, sizes, w_in.shape[0] + 2),
        out_shape=(
            jax.ShapeDtypeStruct((16, groups * cap * fan), F32),
            jax.ShapeDtypeStruct((LANES, LANES), F32),
            jax.ShapeDtypeStruct((n_basis * groups * cap, n_probes), BF16),
        ),
        compiler_params=pltpu.CompilerParams(vmem_limit_bytes=24 * 1024 * 1024),
        name="index",
    )(mine, small)
    density = pl.pallas_call(
        functools.partial(density_kernel, sizes),
        out_shape=jax.ShapeDtypeStruct((1, n_probes), F32),
        scratch_shapes=[
            pltpu.VMEM((width, every), BF16),
            pltpu.VMEM((groups, 2 * width, LANES), BF16),
            pltpu.VMEM((groups, 2 * width, LANES), BF16),
            pltpu.VMEM((4 * width, every), BF16),
            pltpu.VMEM((2,) + weights.shape, BF16),
        ],
        compiler_params=pltpu.CompilerParams(vmem_limit_bytes=40 * 1024 * 1024),
        name="density",
    )(mine, other, weights, weights_other, small, w_in, w_mix, facts, slots, probe_basis)
    return density.reshape(n_probes)


def per_device(*args):
    if lax.axis_size("brick") * lax.axis_size("probe") == FEW_GROUPS:
        return few_groups(*args)
    return many_groups(*args)


def extended(block, sides, width):
    for axis, dim in sides:
        count = lax.axis_size(axis)
        forward = [(i, i + 1) for i in range(count - 1)]
        forward.append((count - 1, 0))
        backward = [(target, source) for source, target in forward]
        low = lax.ppermute(
            lax.slice_in_dim(block, block.shape[dim] - width, None, axis=dim), axis, forward
        )
        high = lax.ppermute(lax.slice_in_dim(block, 0, width, axis=dim), axis, backward)
        block = jnp.concatenate([low, block, high], axis=dim)
    return block


def radial(distance, count, top):
    centers = jnp.arange(count).astype(jnp.float32) * (top / (count - 1))
    return jnp.exp(-2.0 * (distance[..., None] - centers) ** 2)


def make_block(
    recv_rows, recv_pos, w_scalar, w_vector, feat_width, group_no, n_blocks, list_len, n_basis
):

    def probe_block(block_in):
        block_no, listed, live_count = block_in
        index_row = (group_no * n_blocks + block_no) * PB + jnp.arange(PB, dtype=jnp.int32)
        grid_xyz = (
            jnp.stack([index_row % 16, index_row // 16 % 16, index_row // 256 % 16], axis=1).astype(
                jnp.float32
            )
            * 0.25
        )
        atom_xyz = recv_pos[:, listed]
        disp = grid_xyz[:, :, None] - atom_xyz[None]
        dist_sq = jnp.sum(disp * disp, axis=1)
        live = (jnp.arange(list_len, dtype=jnp.int32) < live_count).astype(jnp.float32)
        envelope = (1.0 - dist_sq / 64.0) ** 2 * live[None, :]
        basis = radial(jnp.sqrt(dist_sq), n_basis, 7.0) * envelope[:, :, None]
        scalar_w = basis.astype(jnp.bfloat16).reshape(PB, list_len * n_basis)
        vector_w = (
            (disp[:, :, :, None] * basis[:, None])
            .astype(jnp.bfloat16)
            .reshape(PB, 3 * list_len * n_basis)
        )
        atom_rows = recv_rows[listed]
        atom_terms = (atom_rows[:, None, :feat_width] * w_scalar[None]).reshape(
            list_len * n_basis, feat_width
        )
        vec_rows = jnp.transpose(
            atom_rows[:, feat_width:].reshape(list_len, 3, feat_width), (1, 0, 2)
        )
        vector_terms = (vec_rows[:, :, None, :] * w_vector[None, None]).reshape(
            3 * list_len * n_basis, feat_width
        )
        charge = jnp.dot(scalar_w, atom_terms, preferred_element_type=jnp.float32) + jnp.dot(
            vector_w, vector_terms, preferred_element_type=jnp.float32
        )
        return charge.astype(jnp.bfloat16)

    return probe_block


def many_groups(
    atom_s,
    atom_pos,
    edge_vec,
    edge_nbr,
    border_index,
    send_index,
    probe_list,
    probe_count,
    w_in,
    b_in,
    w_msg,
    w_rad,
    w_probe,
    w_mix,
    b_mix,
    w_out,
):
    atom_count, half_width = atom_s.shape
    n_layers = w_in.shape[0]
    width = w_in.shape[1]
    n_basis = w_rad.shape[1]
    fan_out = edge_nbr.shape[0] // atom_count
    root_fan = fan_out**0.5
    rim_rows = border_index.shape[0] // 2
    length = jnp.sqrt(jnp.sum(edge_vec * edge_vec, axis=0))
    edge_env = (1.0 - length * length / 36.0) ** 2
    edge_basis = (radial(length, n_basis, 6.0) * edge_env[:, None]).astype(jnp.bfloat16)
    edge_cols = jnp.transpose(edge_vec)
    scalars = atom_s
    vectors = jnp.zeros((atom_count, 3 * half_width), jnp.bfloat16)
    for layer_no in range(n_layers):
        full_rows = lax.all_gather(scalars, "chan", axis=1, tiled=True)
        in_weight = w_in[layer_no]
        in_bias = b_in[layer_no]
        msg_weight = w_msg[layer_no].reshape(width, 3 * half_width)
        rad_weight = w_rad[layer_no].reshape(n_basis, 3 * half_width)
        hidden_act = jax.nn.silu(
            jnp.dot(full_rows, in_weight, preferred_element_type=jnp.float32) + in_bias
        ).astype(jnp.bfloat16)
        inner_tab = jnp.concatenate(
            [
                jnp.dot(hidden_act, msg_weight, preferred_element_type=jnp.float32).astype(
                    jnp.bfloat16
                ),
                vectors,
            ],
            axis=1,
        )
        padded = extended(inner_tab[border_index], ((("brick", "probe"), 0),), rim_rows)
        lookup = jnp.concatenate([inner_tab, padded[:rim_rows], padded[3 * rim_rows :]], axis=0)
        neighbour_rows = lookup[edge_nbr]
        filters = jnp.dot(edge_basis, rad_weight, preferred_element_type=jnp.float32)
        weighted = neighbour_rows[:, : 3 * half_width] * filters
        neighbour_vec = neighbour_rows[:, 3 * half_width :].reshape(-1, 3, half_width)
        vector_gate = weighted[:, None, half_width : 2 * half_width]
        along_edge = weighted[:, None, 2 * half_width :]
        delta_vec = neighbour_vec * vector_gate + along_edge * edge_cols[:, :, None]
        delta_scalar = (
            weighted[:, :half_width].reshape(atom_count, fan_out, half_width).sum(axis=1) / root_fan
        )
        delta_vec = delta_vec.reshape(atom_count, fan_out, 3 * half_width).sum(axis=1) / root_fan
        scalars = (scalars + delta_scalar).astype(jnp.bfloat16)
        vectors = (vectors + delta_vec).astype(jnp.bfloat16)
    features = jnp.concatenate([scalars, vectors], axis=1)
    picks = send_index[0]
    n_brick = lax.axis_size("brick")
    n_probe = lax.axis_size("probe")
    n_groups = n_brick * n_probe
    slot_cap = picks.shape[0] // n_groups
    out_rows = features[picks]
    out_pos = jnp.transpose(atom_pos)[picks].astype(jnp.bfloat16)
    received = (
        lax.all_to_all(
            out_rows.reshape(n_groups, slot_cap, 4 * half_width),
            ("brick", "probe"),
            split_axis=0,
            concat_axis=0,
            tiled=True,
        ),
        lax.all_to_all(
            out_pos.reshape(n_groups, slot_cap, 3),
            ("brick", "probe"),
            split_axis=0,
            concat_axis=0,
            tiled=True,
        ),
    )
    recv_count = n_groups * slot_cap
    recv_rows = received[0].reshape(recv_count, 4 * half_width)
    recv_pos = jnp.transpose(received[1].reshape(recv_count, 3)).astype(jnp.float32)
    group_no = lax.axis_index("brick") * n_probe + lax.axis_index("probe")
    n_blocks, list_len = probe_list.shape
    probe_block = make_block(
        recv_rows,
        recv_pos,
        w_probe[:, 0, :],
        w_probe[:, 1, :],
        half_width,
        group_no,
        n_blocks,
        list_len,
        n_basis,
    )
    charges = lax.map(
        probe_block, (jnp.arange(n_blocks, dtype=jnp.int32), probe_list, probe_count)
    ).reshape(n_blocks * PB, half_width)
    mix_rows = lax.dynamic_slice_in_dim(w_mix, lax.axis_index("chan") * half_width, half_width, 0)
    mixed = lax.psum(jnp.dot(charges, mix_rows, preferred_element_type=jnp.float32), "chan")
    return jnp.sum(jax.nn.silu(mixed + b_mix) * w_out, axis=1)


def solution(mesh):
    in_specs = (
        P(("image", "brick", "probe"), "chan"),
        P(None, ("image", "brick", "probe")),
        P(None, ("image", "brick", "probe")),
        P(("image", "brick", "probe")),
        P(("image", "brick", "probe")),
        P(("image", "brick", "probe"), None),
        P(("image", "brick", "probe"), None),
        P(("image", "brick", "probe")),
        P(),
        P(),
        P(None, None, None, "chan"),
        P(None, None, None, "chan"),
        P(None, None, "chan"),
        P(),
        P(),
        P(),
    )
    out_specs = P(("image", "brick", "probe"))
    return jax.shard_map(
        per_device, mesh=mesh, in_specs=in_specs, out_specs=out_specs, check_vma=False
    )
```

```python
import functools
import itertools
import math

import jax
import jax.numpy as jnp
from jax import lax
from jax.experimental import pallas as pl
from jax.experimental.pallas import tpu as pltpu
from jax.sharding import PartitionSpec as P

PB = 128
LANES = 128
FEW_GROUPS = 8
SMALL = 16
TOGETHER = 2
ROOT = (2.0 * math.log2(math.e)) ** 0.5
F32 = jnp.float32
BF16 = jnp.bfloat16


def iota(shape, dim):
    return lax.broadcasted_iota(jnp.int32, shape, dim)


def dot(a, b):
    return jnp.dot(a, b, preferred_element_type=F32)


def dot_tn(a, b):
    return lax.dot_general(a, b, (((0,), (0,)), ((), ())), preferred_element_type=F32)


def one_hot(mask):
    return jnp.where(mask, 1.0, 0.0).astype(BF16)


def same(names, row):
    return jnp.where(names == row, jnp.ones_like(names), jnp.zeros_like(names))


def silu(x):
    half_x = 0.5 * x
    return half_x * jnp.tanh(half_x) + half_x


def bell(scaled, center):
    away = scaled - center
    return jnp.exp2(-(away * away))


def lane_atom(lane, fan, tiles):
    return (lane % tiles) * (LANES // fan) + lane // tiles


def length_keeping_round(exact):
    choices = []
    for value in exact:
        near = value.astype(BF16).astype(F32)
        step = jnp.where(value > near, 1.01 / 256.0, -1.01 / 256.0) * jnp.abs(near)
        choices.append((near, (near + step).astype(BF16).astype(F32)))
    target = sum(value * value for value in exact)
    best, best_error = None, None
    for picked in itertools.product(*choices):
        error = jnp.abs(sum(value * value for value in picked) - target)
        if best is None:
            best, best_error = picked, error
            continue
        better = error < best_error
        best = tuple(jnp.where(better, new, old) for new, old in zip(picked, best))
        best_error = jnp.where(better, error, best_error)
    return best


def pack_kernel(
    fan, atom_s, atom_pos, edge_vec, edge_nbr, border, send, w_msg, w_rad, w_probe,
    b_in, b_mix, w_out, probe_list, probe_count, data_out, weight_out, small_out, natural,
):
    half, atoms = atom_s.shape
    tiles = atoms * fan // LANES
    per_tile = LANES // fan
    part = lax.axis_index("chan")
    perm = one_hot(lane_atom(iota((atoms, LANES), 1), fan, tiles) == iota((atoms, LANES), 0))
    scalars = dot(atom_s[...], perm).astype(BF16)
    for tile in range(tiles):
        for comp in range(3):
            natural[comp * tiles + tile : comp * tiles + tile + 1, :] = edge_vec[
                comp : comp + 1, tile * LANES : (tile + 1) * LANES
            ]
    exact = [natural[comp * tiles : (comp + 1) * tiles, :] for comp in range(3)]
    for comp, value in enumerate(length_keeping_round(exact)):
        natural[comp * tiles : (comp + 1) * tiles, :] = value
    natural[3 * tiles : 4 * tiles, :] = edge_nbr[...].astype(F32)
    natural[4 * tiles :, :] = jnp.zeros((LANES - 4 * tiles, LANES), F32)
    turned = natural[...].T
    lane = iota((fan, LANES), 1)
    sorted_rows = []
    for comp in range(4):
        rows = jnp.zeros((fan, LANES), F32)
        for a in range(per_tile):
            piece = turned[a * fan : (a + 1) * fan, :]
            shift = (a * tiles - comp * tiles) % LANES
            piece = pltpu.roll(piece, shift, 1) if shift else piece
            rows = jnp.where(lane // tiles == a, piece, rows)
        sorted_rows.append(rows)
    blank = jnp.zeros((1, LANES), F32)
    every_edge = jnp.concatenate(sorted_rows, axis=0).astype(BF16)
    sorted_rows = [jnp.where(part == 0, rows[: fan // 2], rows[fan // 2 :]) for rows in sorted_rows]
    border_row = jnp.concatenate(
        [border[...].astype(F32), jnp.zeros((1, LANES - border.shape[1]), F32)], axis=1
    )
    picks = send.shape[1]
    groups = data_out.shape[0]
    cap = picks // groups
    block = fan * cap
    lane = iota((picks, groups * block), 1)
    place = (lane // block) * cap + lane % cap
    send_row = jnp.broadcast_to(send[...].astype(F32), (8, picks)).astype(BF16)
    wanted = dot(send_row, one_hot(iota((picks, groups * block), 0) == place))[0:1]
    atom_col = lane_atom(iota((LANES, groups * block), 0), fan, tiles).astype(F32)
    spread = dot(every_edge, one_hot(atom_col == wanted))
    edge_k = iota(spread.shape, 0) % fan
    spread = jnp.where(edge_k == (iota(spread.shape, 1) % block) // cap, spread, 0.0)
    picked = jnp.sum(spread.reshape(4, fan, groups * block), axis=1)
    pick_atom = one_hot(iota((atoms, picks), 0).astype(F32) == send[...].astype(F32))
    facts = [send[...].astype(F32)]
    pos = dot(atom_pos[...].astype(BF16), pick_atom)
    facts += [pos[x : x + 1] for x in range(3)]
    owner = iota((groups, picks), 1) // cap == iota((groups, picks), 0)
    facts = jnp.concatenate([jnp.where(owner, fact, 0.0) for fact in facts], axis=1)
    row = iota((4 * picks, LANES), 0)
    place = (row // picks) * cap + row % cap
    facts = dot(facts.astype(BF16), one_hot(place == iota((4 * picks, LANES), 1)))
    edge_part = jnp.concatenate(sorted_rows, axis=0).astype(BF16)
    for group in range(groups):
        mine = slice(group * block, (group + 1) * block)
        rest = [facts[group : group + 1], border_row]
        for comp in (0, 2):
            rest.append(
                jnp.concatenate([picked[comp : comp + 1, mine], picked[comp + 1 : comp + 2, mine]], axis=1)
            )
        rest = jnp.concatenate(rest + [blank] * 4, axis=0)
        data_out[group, 0:half, :] = scalars
        data_out[group, half : half + 2 * fan, :] = edge_part
        data_out[group, half + 2 * fan :, :] = rest.astype(BF16)
    at = 0
    for piece in (b_in, b_mix, w_out, probe_list, probe_count):
        rows, cols = piece.shape
        small_out[at : at + rows, 0:cols] = piece[...].astype(F32)
        at += rows
    probe_rows = [w_probe[r].astype(F32) for r in range(w_probe.shape[0])]
    radial = jnp.concatenate([w_rad[...].astype(F32)] + probe_rows, axis=0).T.astype(BF16)
    weight_out[: w_msg.shape[0], :] = w_msg[...]
    weight_out[w_msg.shape[0] :, :] = radial


def pack(
    groups, atom_s, atom_pos, edge_vec, edge_nbr, border_index, send_index, w_msg, w_rad, w_probe,
    b_in, b_mix, w_out, probe_list, probe_count,
):
    atoms, half = atom_s.shape
    fan = edge_nbr.shape[0] // atoms
    return pl.pallas_call(
        functools.partial(pack_kernel, fan),
        out_shape=(
            jax.ShapeDtypeStruct((groups, half + 4 * fan // 2 + 8, LANES), BF16),
            jax.ShapeDtypeStruct((w_msg.size // LANES + half, LANES), BF16),
            jax.ShapeDtypeStruct((SMALL, LANES), F32),
        ),
        scratch_shapes=[pltpu.VMEM((LANES, LANES), F32)],
        name="pack",
    )(
        atom_s.T,
        atom_pos,
        edge_vec,
        edge_nbr.reshape(-1, LANES),
        border_index.reshape(1, -1),
        send_index,
        jnp.transpose(w_msg, (0, 2, 3, 1)).reshape(-1, LANES),
        jnp.transpose(w_rad, (0, 2, 1, 3)).reshape(-1, half),
        w_probe,
        b_in,
        b_mix.reshape(1, -1),
        w_out.reshape(1, -1),
        probe_list,
        probe_count.reshape(1, -1),
    )


def probe_grid(me, probes):
    number = me * probes + iota((1, probes), 1)
    return [(n % 16).astype(F32) * 0.25 - 1.875 for n in (number, number // 16, number // 256)]


def index_kernel(sizes, list_at, data_mine, small, facts_out, slots, probe_basis):
    groups, fan, rim, half, n_basis, cap, n_blocks = sizes
    tiles = fan
    received = groups * cap
    per_group = fan * cap
    edges = received * fan
    rest_at = half + 2 * fan
    me = lax.axis_index("brick") * lax.axis_size("probe") + lax.axis_index("probe")
    small_rows = small[...]
    rest = [data_mine[g, rest_at : rest_at + 8, :].astype(F32) for g in range(groups)]
    facts = jnp.concatenate([rows[0:1] for rows in rest], axis=0).astype(BF16)
    lane = iota((LANES, 4 * received), 1)
    wanted = (lane // received) * cap + lane % cap
    facts = dot(facts, one_hot(iota((LANES, 4 * received), 0) == wanted))
    source = (iota(facts.shape, 1) % received) // cap
    facts = jnp.sum(jnp.where(source == iota(facts.shape, 0), facts, 0.0), axis=0, keepdims=True)
    pick_atoms = facts[:, 0:received]
    for comp in range(3):
        rows = [r[2 + comp // 2 : 3 + comp // 2, (comp % 2) * per_group :][:, :per_group] for r in rest]
        facts_out[comp : comp + 1, :] = jnp.concatenate(rows, axis=1)
    nbr = jnp.concatenate([r[3:4, per_group : 2 * per_group] for r in rest], axis=1).astype(jnp.int32)

    home = iota((1, edges), 1) // per_group
    is_low = (nbr >= LANES) & (nbr < LANES + rim)
    is_up = nbr >= LANES + rim
    owner = jnp.where(
        is_low, (home + groups - 1) % groups, jnp.where(is_up, (home + 1) % groups, home)
    )
    entry = owner * 2 * rim + jnp.where(is_low, nbr - (LANES - rim), nbr - (LANES + rim))
    entry = jnp.where(is_low | is_up, entry, -1)
    border_all = jnp.concatenate([r[1:2, 0 : 2 * rim] for r in rest], axis=1)
    border_all = jnp.broadcast_to(border_all, (16, groups * 2 * rim)).astype(BF16)
    seen = dot(border_all, one_hot(iota((groups * 2 * rim, edges), 0) == entry))[0:1]
    target = jnp.where(entry < 0, nbr, seen.astype(jnp.int32))

    column = iota((groups * LANES, 1), 0)
    column_name = (column // LANES) * LANES + lane_atom(column % LANES, fan, tiles)
    home = iota((1, received), 1) // cap
    self_hot = one_hot(column_name == home * LANES + pick_atoms.astype(jnp.int32))
    uses = dot(self_hot, jnp.ones((received, LANES), BF16))
    uses = [uses[g * LANES : (g + 1) * LANES] for g in range(groups)]
    quad = groups // 2
    window_hot, near_groups = [], []
    for h in range(2):
        lanes = slice(h * edges // 2, (h + 1) * edges // 2)
        near = lax.rem(owner[:, lanes] + 2 * groups - (h * quad + groups - 1), groups)
        hot = one_hot(column_name[: (quad + 2) * LANES] == near * LANES + target[:, lanes])
        window_hot.append(hot)
        near_groups.append(near)
        used = dot(hot, jnp.ones((edges // 2, LANES), BF16))
        for i in range(quad + 2):
            g = (h * quad + groups - 1 + i) % groups
            uses[g] = uses[g] + used[i * LANES : (i + 1) * LANES]
    lane = iota((LANES, LANES), 1)
    needed = jnp.zeros((LANES, LANES), F32)
    for g in range(groups):
        needed = jnp.where((lane == g) & (uses[g] > 0.0), 1.0, needed)
    order = dot(one_hot(lane <= iota((LANES, LANES), 0)), needed.astype(BF16))
    slot = jnp.where(needed > 0.0, order - 1.0, -1.0)
    slots[...] = slot
    slot_rows = slot.T
    facts_out[8:9, 0:LANES] = order[LANES - 1 : LANES, :]

    for h in range(2):
        lanes = slice(h * edges // 2, (h + 1) * edges // 2)
        in_window = [(h * quad + groups - 1 + i) % groups for i in range(quad + 2)]
        row = jnp.concatenate([slot_rows[g : g + 1] for g in in_window], axis=1)
        row = jnp.broadcast_to(row, (16, (quad + 2) * LANES)).astype(BF16)
        place = dot(row, window_hot[h])[0:1]
        facts_out[3:4, lanes] = near_groups[h].astype(F32) * LANES + place
    row = jnp.concatenate([slot_rows[g : g + 1] for g in range(groups)], axis=1)
    row = jnp.broadcast_to(row, (16, groups * LANES)).astype(BF16)
    facts_out[7:8, 0:received] = home.astype(F32) * LANES + dot(row, self_hot)[0:1]

    shifted = facts - 1.875
    for x in range(3):
        facts_out[4 + x : 5 + x, 0:received] = shifted[:, (1 + x) * received : (2 + x) * received]
    pos_cols = jnp.broadcast_to(shifted, (LANES, 4 * received)).T
    list_len = LANES
    counts = []
    for block in range(n_blocks):
        limit = small_rows[list_at + n_blocks : list_at + n_blocks + 1, block : block + 1]
        live = iota((1, list_len), 1).astype(F32) < limit
        named = jnp.where(live, small_rows[list_at + block : list_at + block + 1], -1.0)
        hits = jnp.where(iota((received, list_len), 0).astype(F32) == named, 1.0, 0.0)
        counts.append(jnp.broadcast_to(jnp.sum(hits, axis=1, keepdims=True), (received, PB)))
    counts = jnp.concatenate(counts, axis=1)
    probes = n_blocks * PB
    grid = probe_grid(me, probes)
    dist_sq = jnp.zeros((received, probes), F32)
    for x in range(3):
        dist_sq = dist_sq + (grid[x] - pos_cols[(1 + x) * received : (2 + x) * received, 0:1]) ** 2
    dist = jnp.sqrt(dist_sq) * ROOT
    envelope = (1.0 - dist_sq * (1.0 / 64.0)) ** 2 * counts
    probe_basis[...] = jnp.concatenate(
        [
            (bell(dist, r * (ROOT * 7.0 / (n_basis - 1))) * envelope).astype(BF16)
            for r in range(n_basis)
        ],
        axis=0,
    )


def density_kernel(
    sizes,
    data_mine,
    data_other,
    weights_mine,
    weights_other,
    small,
    w_in,
    w_mix,
    facts,
    slots,
    probe_basis,
    density,
    state0,
    own0,
    faces0,
    state1,
    weights,
    slot_hot,
):
    groups, fan, rim, half, n_basis, cap, n_blocks = sizes
    layers = w_in.shape[0]
    width = 2 * half
    tiles = LANES * fan // LANES
    root_fan = fan**0.5
    me = lax.axis_index("brick") * lax.axis_size("probe") + lax.axis_index("probe")
    part = lax.axis_index("chan")
    weights[part] = weights_mine[...]
    weights[1 - part] = weights_other[...]
    every = groups * LANES
    edge_at = half
    n_edge = 4 * fan // 2
    rest_at = half + n_edge

    def data(group, c, rows):
        return (data_mine, data_other)[c][group, rows, :]

    def weight(layer, p):
        at = (layer * 3 + p) * half
        return jnp.concatenate([weights[c, at : at + half, :] for c in range(2)], axis=0)

    def radial_weight(layer, p):
        at = (layer * 3 + p) * n_basis
        return radial_all[:, at : at + n_basis]

    def edge_rows(group):
        return [data(group, c, slice(edge_at, rest_at)).astype(F32) for c in range(2)]

    def border_of(group):
        return data(group, 0, slice(rest_at, rest_at + 8)).astype(F32)[1:2, 0 : 2 * rim]

    centers = iota((n_basis, 1), 0).astype(F32) * (ROOT * 6.0 / (n_basis - 1))

    def basis_of(length, env):
        return (bell(length * ROOT, centers) * env).astype(BF16)

    small_rows = small[...]
    columns = small_rows.T
    radial_at = weights.shape[1] - half
    radial_all = jnp.concatenate([weights[c, radial_at:, :] for c in range(2)], axis=0)

    received = groups * cap
    edges = received * fan
    per_group = fan * cap
    pick_vec = [facts[x : x + 1, :] for x in range(3)]
    pos = facts[4:7, 0:received]
    length = jnp.sqrt(sum(x * x for x in pick_vec))
    basis1 = basis_of(length, (1.0 - length * length * (1.0 / 36.0)) ** 2)
    quad = groups // 2
    window = [[(h * quad + groups - 1 + i) % groups for i in range(quad + 2)] for h in range(2)]
    near_row = iota(((quad + 2) * LANES, edges // 2), 0).astype(F32)
    window_pick = [
        one_hot(near_row == facts[3:4, h * edges // 2 : (h + 1) * edges // 2]) for h in range(2)
    ]
    chosen_atoms = one_hot(iota((every, received), 0).astype(F32) == facts[7:8, 0:received])

    terms_shape = (2 * n_basis, n_basis * received)
    probe_weight = radial_all[:, 3 * layers * n_basis :]
    w_scalar, w_vector = (
        dot(probe_weight, one_hot(iota(terms_shape, 1) // received * 2 + p == iota(terms_shape, 0)))
        for p in range(2)
    )

    probes = density.shape[1]
    grid = probe_grid(me, probes)

    for group in range(groups):
        for c in range(2):
            place = part if c == 0 else 1 - part
            rows = pl.ds(pl.multiple_of(place * half, half), half)
            state0[rows, group * LANES : (group + 1) * LANES] = data(group, c, slice(0, half))
    hidden = silu(dot_tn(w_in[0], state0[...]) + columns[:, 0:1]).astype(BF16)
    weight_ac = jnp.concatenate([weight(0, 0), weight(0, 2)], axis=0)
    messages = dot(weight_ac, hidden).astype(BF16)
    atom_col = lane_atom(iota((LANES, 2 * rim), 0), fan, tiles).astype(F32)
    for group in range(groups):
        own = messages[:, group * LANES : (group + 1) * LANES]
        own0[group] = own
        border_row = border_of(group)
        faces0[group, :, 0 : 2 * rim] = dot(own, one_hot(atom_col == border_row)).astype(BF16)

    row = iota((LANES + 2 * rim, 1), 0)
    names = jnp.where(
        row < LANES,
        lane_atom(row, fan, tiles),
        jnp.where(row < LANES + rim, row + rim, row - rim),
    ).astype(F32)
    names = jnp.broadcast_to(names, (LANES + 2 * rim, LANES)).astype(BF16)
    upper_lane = iota((2 * width, 2 * rim), 1) < rim
    radial_ac = jnp.concatenate([radial_weight(0, 0), radial_weight(0, 2)], axis=0)
    radial_rows = jnp.concatenate([jnp.zeros((2 * width, LANES + 2 * rim), BF16), radial_ac], axis=1)
    blank = jnp.zeros((2 * width, n_basis), BF16)

    some = LANES // 2
    step = fan // 2

    for group in range(groups):
        slot_lane = iota((LANES, LANES), 1).astype(F32)
        slot_hot[group] = one_hot(slots[:, group : group + 1] == slot_lane)

    def lanes_of(group):
        return pl.ds(pl.multiple_of(group * LANES, LANES), LANES)

    def update(group, first_slot):
        up = lax.rem(group + 1, groups)
        low = lax.rem(group + groups - 1, groups)
        ghosts = jnp.where(
            upper_lane,
            faces0[up, :, 0 : 2 * rim].astype(F32),
            faces0[low, :, 0 : 2 * rim].astype(F32),
        ).astype(BF16)
        table = jnp.concatenate([own0[group], ghosts, blank], axis=1)
        left = jnp.concatenate(
            [
                block[at : at + 16]
                for at in range(0, 2 * width, 16)
                for block in (table, radial_rows)
            ],
            axis=0,
        )
        in_slot = slot_hot[group, :, first_slot : first_slot + some]
        source = jnp.concatenate(
            [data(group, c, slice(edge_at, rest_at)) for c in range(2)] + [state0[:, lanes_of(group)]],
            axis=0,
        )
        source = dot(source, in_slot)
        rows = jnp.concatenate([source[:n_edge], source[n_edge : 2 * n_edge]], axis=1)
        own_scalars = source[2 * n_edge :]
        vec = [rows[x * step : (x + 1) * step] for x in range(3)]
        nbr = rows[3 * step : 4 * step]
        length = jnp.sqrt(vec[0] * vec[0] + vec[1] * vec[1] + vec[2] * vec[2])
        env = (1.0 - length * length * (1.0 / 36.0)) ** 2
        acc = jnp.zeros((width, LANES), F32)
        acc_vec = [jnp.zeros((width, LANES), F32) for _ in range(3)]
        for first in range(0, step, TOGETHER):
            ks = range(first, first + TOGETHER)
            picked = jnp.concatenate([same(names, nbr[k : k + 1].astype(BF16)) for k in ks], axis=1)
            basis = jnp.concatenate(
                [basis_of(length[k : k + 1], env[k : k + 1]) for k in ks], axis=1
            )
            both = dot(left, jnp.concatenate([picked, basis], axis=0))
            prod = jnp.concatenate(
                [both[at : at + 16] * both[at + 16 : at + 32] for at in range(0, 4 * width, 32)],
                axis=0,
            )
            for i, k in enumerate(ks):
                block = prod[:, i * LANES : (i + 1) * LANES]
                acc = acc + block[:width]
                for x in range(3):
                    acc_vec[x] = acc_vec[x] + block[width:] * vec[x][k : k + 1]
        acc, *acc_vec = [(a[:, :some] + a[:, some:]) * (1.0 / root_fan) for a in [acc] + acc_vec]
        return jnp.concatenate([own_scalars + acc] + acc_vec, axis=0)

    def first_slots(step_no, carry):
        for group in (2 * step_no, 2 * step_no + 1):
            state = update(group, 0)
            state = jnp.concatenate([state, jnp.zeros_like(state)], axis=1)
            state1[:, lanes_of(group)] = state.astype(BF16)
        return carry

    lax.fori_loop(0, groups // 2, first_slots, 0)
    needed = facts[8:9, 0:LANES]

    @pl.when(jnp.max(needed) > some)
    def _():
        def more_slots(group, carry):
            count = jnp.max(jnp.where(iota((1, LANES), 1) == group, needed, 0.0))

            @pl.when(count > some)
            def _():
                state = update(group, some)
                before = state1[:, lanes_of(group)].astype(F32)[:, :some]
                state1[:, lanes_of(group)] = jnp.concatenate([before, state], axis=1).astype(BF16)

            return carry

        lax.fori_loop(0, groups, more_slots, 0)

    rows = []
    for h in range(2):
        near_states = jnp.concatenate(
            [state1[:, g * LANES : (g + 1) * LANES] for g in window[h]], axis=1
        )
        rows.append(dot(near_states, window_pick[h]))
    rows = jnp.concatenate(rows, axis=1)
    hidden = silu(dot_tn(w_in[1], rows[:width].astype(BF16)) + columns[:, 1:2]).astype(BF16)
    weight_abc = jnp.concatenate([weight(1, p) for p in range(3)], axis=0)
    messages = dot(weight_abc, hidden).astype(BF16).astype(F32)
    radial_abc = jnp.concatenate([radial_weight(1, p) for p in range(3)], axis=0)
    filters = dot(radial_abc, basis1)
    weighted = messages * filters
    gate = weighted[width : 2 * width]
    along = weighted[2 * width :]
    parts = [weighted[:width]]
    for x in range(3):
        parts.append(rows[(1 + x) * width : (2 + x) * width] * gate + along * pick_vec[x])
    parts = jnp.concatenate(parts, axis=0).astype(BF16)
    edge = iota((edges, received), 0)
    slot = (edge // per_group) * cap + edge % cap
    delta = dot(parts, one_hot(slot == iota((edges, received), 1)))
    final = (dot(state1[...], chosen_atoms) + delta * (1.0 / root_fan)).astype(BF16)

    spread = one_hot(
        iota((received, n_basis * received), 1) % received == iota((received, n_basis * received), 0)
    )
    final = dot(final, spread)
    pos = jnp.concatenate([pos] * n_basis, axis=1)
    vectors = [final[(x + 1) * width : (x + 2) * width] for x in range(3)]
    along = sum(vectors[x] * pos[x : x + 1] for x in range(3))
    terms = [w_scalar * final[:width] - w_vector * along]
    terms += [w_vector * vector for vector in vectors]
    sums = dot(jnp.concatenate(terms, axis=0).astype(BF16), probe_basis[...])
    charges = sums[:width]
    for x in range(3):
        charges = charges + grid[x] * sums[(x + 1) * width : (x + 2) * width]
    mixed = dot_tn(w_mix[...], charges.astype(BF16)) + columns[:, layers : layers + 1]
    density[...] = jnp.sum(silu(mixed) * columns[:, layers + 1 : layers + 2], axis=0, keepdims=True)


def few_groups(
    atom_s, atom_pos, edge_vec, edge_nbr, border_index, send_index, probe_list, probe_count,
    w_in, b_in, w_msg, w_rad, w_probe, w_mix, b_mix, w_out,
):
    atoms, half = atom_s.shape
    groups = lax.axis_size("brick") * lax.axis_size("probe")
    fan = edge_nbr.shape[0] // atoms
    rim = border_index.shape[0] // 2
    n_basis = w_rad.shape[1]
    cap = send_index.shape[1] // groups
    width = 2 * half
    every = groups * LANES
    data, weights, small = pack(
        groups, atom_s, atom_pos, edge_vec, edge_nbr, border_index, send_index, w_msg, w_rad, w_probe,
        b_in, b_mix, w_out, probe_list, probe_count,
    )
    swap = [(0, 1), (1, 0)]
    weights_other = lax.ppermute(weights, "chan", swap)
    mine = lax.all_to_all(data, ("brick", "probe"), split_axis=0, concat_axis=0, tiled=True)
    other = lax.ppermute(mine, "chan", swap)
    n_probes = probe_list.shape[0] * PB
    sizes = (groups, fan, rim, half, n_basis, cap, probe_list.shape[0])
    facts, slots, probe_basis = pl.pallas_call(
        functools.partial(index_kernel, sizes, w_in.shape[0] + 2),
        out_shape=(
            jax.ShapeDtypeStruct((16, groups * cap * fan), F32),
            jax.ShapeDtypeStruct((LANES, LANES), F32),
            jax.ShapeDtypeStruct((n_basis * groups * cap, n_probes), BF16),
        ),
        compiler_params=pltpu.CompilerParams(vmem_limit_bytes=24 * 1024 * 1024),
        name="index",
    )(mine, small)
    density = pl.pallas_call(
        functools.partial(density_kernel, sizes),
        out_shape=jax.ShapeDtypeStruct((1, n_probes), F32),
        scratch_shapes=[
            pltpu.VMEM((width, every), BF16),
            pltpu.VMEM((groups, 2 * width, LANES), BF16),
            pltpu.VMEM((groups, 2 * width, LANES), BF16),
            pltpu.VMEM((4 * width, every), BF16),
            pltpu.VMEM((2,) + weights.shape, BF16),
            pltpu.VMEM((groups, LANES, LANES), BF16),
        ],
        compiler_params=pltpu.CompilerParams(vmem_limit_bytes=40 * 1024 * 1024),
        name="density",
    )(mine, other, weights, weights_other, small, w_in, w_mix, facts, slots, probe_basis)
    return density.reshape(n_probes)


def per_device(*args):
    if lax.axis_size("brick") * lax.axis_size("probe") == FEW_GROUPS:
        return few_groups(*args)
    return many_groups(*args)


def extended(block, sides, width):
    for axis, dim in sides:
        count = lax.axis_size(axis)
        forward = [(i, i + 1) for i in range(count - 1)]
        forward.append((count - 1, 0))
        backward = [(target, source) for source, target in forward]
        low = lax.ppermute(
            lax.slice_in_dim(block, block.shape[dim] - width, None, axis=dim), axis, forward
        )
        high = lax.ppermute(lax.slice_in_dim(block, 0, width, axis=dim), axis, backward)
        block = jnp.concatenate([low, block, high], axis=dim)
    return block


def radial(distance, count, top):
    centers = jnp.arange(count).astype(jnp.float32) * (top / (count - 1))
    return jnp.exp(-2.0 * (distance[..., None] - centers) ** 2)


def make_block(
    recv_rows, recv_pos, w_scalar, w_vector, feat_width, group_no, n_blocks, list_len, n_basis
):

    def probe_block(block_in):
        block_no, listed, live_count = block_in
        index_row = (group_no * n_blocks + block_no) * PB + jnp.arange(PB, dtype=jnp.int32)
        grid_xyz = (
            jnp.stack([index_row % 16, index_row // 16 % 16, index_row // 256 % 16], axis=1).astype(
                jnp.float32
            )
            * 0.25
        )
        atom_xyz = recv_pos[:, listed]
        disp = grid_xyz[:, :, None] - atom_xyz[None]
        dist_sq = jnp.sum(disp * disp, axis=1)
        live = (jnp.arange(list_len, dtype=jnp.int32) < live_count).astype(jnp.float32)
        envelope = (1.0 - dist_sq / 64.0) ** 2 * live[None, :]
        basis = radial(jnp.sqrt(dist_sq), n_basis, 7.0) * envelope[:, :, None]
        scalar_w = basis.astype(jnp.bfloat16).reshape(PB, list_len * n_basis)
        vector_w = (
            (disp[:, :, :, None] * basis[:, None])
            .astype(jnp.bfloat16)
            .reshape(PB, 3 * list_len * n_basis)
        )
        atom_rows = recv_rows[listed]
        atom_terms = (atom_rows[:, None, :feat_width] * w_scalar[None]).reshape(
            list_len * n_basis, feat_width
        )
        vec_rows = jnp.transpose(
            atom_rows[:, feat_width:].reshape(list_len, 3, feat_width), (1, 0, 2)
        )
        vector_terms = (vec_rows[:, :, None, :] * w_vector[None, None]).reshape(
            3 * list_len * n_basis, feat_width
        )
        charge = jnp.dot(scalar_w, atom_terms, preferred_element_type=jnp.float32) + jnp.dot(
            vector_w, vector_terms, preferred_element_type=jnp.float32
        )
        return charge.astype(jnp.bfloat16)

    return probe_block


def many_groups(
    atom_s,
    atom_pos,
    edge_vec,
    edge_nbr,
    border_index,
    send_index,
    probe_list,
    probe_count,
    w_in,
    b_in,
    w_msg,
    w_rad,
    w_probe,
    w_mix,
    b_mix,
    w_out,
):
    atom_count, half_width = atom_s.shape
    n_layers = w_in.shape[0]
    width = w_in.shape[1]
    n_basis = w_rad.shape[1]
    fan_out = edge_nbr.shape[0] // atom_count
    root_fan = fan_out**0.5
    rim_rows = border_index.shape[0] // 2
    length = jnp.sqrt(jnp.sum(edge_vec * edge_vec, axis=0))
    edge_env = (1.0 - length * length / 36.0) ** 2
    edge_basis = (radial(length, n_basis, 6.0) * edge_env[:, None]).astype(jnp.bfloat16)
    edge_cols = jnp.transpose(edge_vec)
    scalars = atom_s
    vectors = jnp.zeros((atom_count, 3 * half_width), jnp.bfloat16)
    for layer_no in range(n_layers):
        full_rows = lax.all_gather(scalars, "chan", axis=1, tiled=True)
        in_weight = w_in[layer_no]
        in_bias = b_in[layer_no]
        msg_weight = w_msg[layer_no].reshape(width, 3 * half_width)
        rad_weight = w_rad[layer_no].reshape(n_basis, 3 * half_width)
        hidden_act = jax.nn.silu(
            jnp.dot(full_rows, in_weight, preferred_element_type=jnp.float32) + in_bias
        ).astype(jnp.bfloat16)
        inner_tab = jnp.concatenate(
            [
                jnp.dot(hidden_act, msg_weight, preferred_element_type=jnp.float32).astype(
                    jnp.bfloat16
                ),
                vectors,
            ],
            axis=1,
        )
        padded = extended(inner_tab[border_index], ((("brick", "probe"), 0),), rim_rows)
        lookup = jnp.concatenate([inner_tab, padded[:rim_rows], padded[3 * rim_rows :]], axis=0)
        neighbour_rows = lookup[edge_nbr]
        filters = jnp.dot(edge_basis, rad_weight, preferred_element_type=jnp.float32)
        weighted = neighbour_rows[:, : 3 * half_width] * filters
        neighbour_vec = neighbour_rows[:, 3 * half_width :].reshape(-1, 3, half_width)
        vector_gate = weighted[:, None, half_width : 2 * half_width]
        along_edge = weighted[:, None, 2 * half_width :]
        delta_vec = neighbour_vec * vector_gate + along_edge * edge_cols[:, :, None]
        delta_scalar = (
            weighted[:, :half_width].reshape(atom_count, fan_out, half_width).sum(axis=1) / root_fan
        )
        delta_vec = delta_vec.reshape(atom_count, fan_out, 3 * half_width).sum(axis=1) / root_fan
        scalars = (scalars + delta_scalar).astype(jnp.bfloat16)
        vectors = (vectors + delta_vec).astype(jnp.bfloat16)
    features = jnp.concatenate([scalars, vectors], axis=1)
    picks = send_index[0]
    n_brick = lax.axis_size("brick")
    n_probe = lax.axis_size("probe")
    n_groups = n_brick * n_probe
    slot_cap = picks.shape[0] // n_groups
    out_rows = features[picks]
    out_pos = jnp.transpose(atom_pos)[picks].astype(jnp.bfloat16)
    received = (
        lax.all_to_all(
            out_rows.reshape(n_groups, slot_cap, 4 * half_width),
            ("brick", "probe"),
            split_axis=0,
            concat_axis=0,
            tiled=True,
        ),
        lax.all_to_all(
            out_pos.reshape(n_groups, slot_cap, 3),
            ("brick", "probe"),
            split_axis=0,
            concat_axis=0,
            tiled=True,
        ),
    )
    recv_count = n_groups * slot_cap
    recv_rows = received[0].reshape(recv_count, 4 * half_width)
    recv_pos = jnp.transpose(received[1].reshape(recv_count, 3)).astype(jnp.float32)
    group_no = lax.axis_index("brick") * n_probe + lax.axis_index("probe")
    n_blocks, list_len = probe_list.shape
    probe_block = make_block(
        recv_rows,
        recv_pos,
        w_probe[:, 0, :],
        w_probe[:, 1, :],
        half_width,
        group_no,
        n_blocks,
        list_len,
        n_basis,
    )
    charges = lax.map(
        probe_block, (jnp.arange(n_blocks, dtype=jnp.int32), probe_list, probe_count)
    ).reshape(n_blocks * PB, half_width)
    mix_rows = lax.dynamic_slice_in_dim(w_mix, lax.axis_index("chan") * half_width, half_width, 0)
    mixed = lax.psum(jnp.dot(charges, mix_rows, preferred_element_type=jnp.float32), "chan")
    return jnp.sum(jax.nn.silu(mixed + b_mix) * w_out, axis=1)


def solution(mesh):
    in_specs = (
        P(("image", "brick", "probe"), "chan"),
        P(None, ("image", "brick", "probe")),
        P(None, ("image", "brick", "probe")),
        P(("image", "brick", "probe")),
        P(("image", "brick", "probe")),
        P(("image", "brick", "probe"), None),
        P(("image", "brick", "probe"), None),
        P(("image", "brick", "probe")),
        P(),
        P(),
        P(None, None, None, "chan"),
        P(None, None, None, "chan"),
        P(None, None, "chan"),
        P(),
        P(),
        P(),
    )
    out_specs = P(("image", "brick", "probe"))
    return jax.shard_map(
        per_device, mesh=mesh, in_specs=in_specs, out_specs=out_specs, check_vma=False
    )
```

```python
import functools
import itertools
import math

import jax
import jax.numpy as jnp
from jax import lax
from jax.experimental import pallas as pl
from jax.experimental.pallas import tpu as pltpu
from jax.sharding import PartitionSpec as P

PB = 128
LANES = 128
FEW_GROUPS = 8
SMALL = 16
ROOT = (2.0 * math.log2(math.e)) ** 0.5
F32 = jnp.float32
BF16 = jnp.bfloat16


def iota(shape, dim):
    return lax.broadcasted_iota(jnp.int32, shape, dim)


def dot(a, b):
    return jnp.dot(a, b, preferred_element_type=F32)


def dot_tn(a, b):
    return lax.dot_general(a, b, (((0,), (0,)), ((), ())), preferred_element_type=F32)


def one_hot(mask):
    return jnp.where(mask, 1.0, 0.0).astype(BF16)


def same(names, row):
    return jnp.where(names == row, jnp.ones_like(names), jnp.zeros_like(names))


def silu(x):
    half_x = 0.5 * x
    return half_x * jnp.tanh(half_x) + half_x


def bell(scaled, center):
    away = scaled - center
    return jnp.exp2(-(away * away))


def lane_atom(lane, fan, tiles):
    return (lane % tiles) * (LANES // fan) + lane // tiles


def length_keeping_round(exact):
    choices = []
    for value in exact:
        near = value.astype(BF16).astype(F32)
        step = jnp.where(value > near, 1.01 / 256.0, -1.01 / 256.0) * jnp.abs(near)
        choices.append((near, (near + step).astype(BF16).astype(F32)))
    target = sum(value * value for value in exact)
    best, best_error = None, None
    for picked in itertools.product(*choices):
        error = jnp.abs(sum(value * value for value in picked) - target)
        if best is None:
            best, best_error = picked, error
            continue
        better = error < best_error
        best = tuple(jnp.where(better, new, old) for new, old in zip(picked, best))
        best_error = jnp.where(better, error, best_error)
    return best


def pack_kernel(
    fan, atom_s, atom_pos, edge_vec, edge_nbr, border, send, w_msg, w_rad, w_probe,
    b_in, b_mix, w_out, probe_list, probe_count, data_out, weight_out, small_out, natural,
):
    half, atoms = atom_s.shape
    tiles = atoms * fan // LANES
    per_tile = LANES // fan
    part = lax.axis_index("chan")
    perm = one_hot(lane_atom(iota((atoms, LANES), 1), fan, tiles) == iota((atoms, LANES), 0))
    scalars = dot(atom_s[...], perm).astype(BF16)
    for tile in range(tiles):
        for comp in range(3):
            natural[comp * tiles + tile : comp * tiles + tile + 1, :] = edge_vec[
                comp : comp + 1, tile * LANES : (tile + 1) * LANES
            ]
    exact = [natural[comp * tiles : (comp + 1) * tiles, :] for comp in range(3)]
    for comp, value in enumerate(length_keeping_round(exact)):
        natural[comp * tiles : (comp + 1) * tiles, :] = value
    natural[3 * tiles : 4 * tiles, :] = edge_nbr[...].astype(F32)
    natural[4 * tiles :, :] = jnp.zeros((LANES - 4 * tiles, LANES), F32)
    turned = natural[...].T
    lane = iota((fan, LANES), 1)
    sorted_rows = []
    for comp in range(4):
        rows = jnp.zeros((fan, LANES), F32)
        for a in range(per_tile):
            piece = turned[a * fan : (a + 1) * fan, :]
            shift = (a * tiles - comp * tiles) % LANES
            piece = pltpu.roll(piece, shift, 1) if shift else piece
            rows = jnp.where(lane // tiles == a, piece, rows)
        sorted_rows.append(jnp.where(part == 0, rows[: fan // 2], rows[fan // 2 :]))
    pos = dot(atom_pos[...].astype(BF16), perm)
    blank = jnp.zeros((1, LANES), F32)
    border_row = jnp.concatenate(
        [border[...].astype(F32), jnp.zeros((1, LANES - border.shape[1]), F32)], axis=1
    )
    send_row = jnp.concatenate(
        [send[...].astype(F32), jnp.zeros((1, LANES - send.shape[1]), F32)], axis=1
    )
    rest = jnp.concatenate([pos, border_row, send_row, blank, blank, blank], axis=0)
    others = jnp.concatenate(sorted_rows + [rest], axis=0).astype(BF16)
    for group in range(data_out.shape[0]):
        data_out[group, 0:half, :] = scalars
        data_out[group, half:, :] = others
    at = 0
    for piece in (b_in, b_mix, w_out, probe_list, probe_count):
        rows, cols = piece.shape
        small_out[at : at + rows, 0:cols] = piece[...].astype(F32)
        at += rows
    probe_rows = [w_probe[r].astype(F32) for r in range(w_probe.shape[0])]
    radial = jnp.concatenate([w_rad[...].astype(F32)] + probe_rows, axis=0).T.astype(BF16)
    weight_out[: w_msg.shape[0], :] = w_msg[...]
    weight_out[w_msg.shape[0] :, :] = radial


def pack(
    groups, atom_s, atom_pos, edge_vec, edge_nbr, border_index, send_index, w_msg, w_rad, w_probe,
    b_in, b_mix, w_out, probe_list, probe_count,
):
    atoms, half = atom_s.shape
    fan = edge_nbr.shape[0] // atoms
    return pl.pallas_call(
        functools.partial(pack_kernel, fan),
        out_shape=(
            jax.ShapeDtypeStruct((groups, half + 4 * fan // 2 + 8, LANES), BF16),
            jax.ShapeDtypeStruct((w_msg.size // LANES + half, LANES), BF16),
            jax.ShapeDtypeStruct((SMALL, LANES), F32),
        ),
        scratch_shapes=[pltpu.VMEM((LANES, LANES), F32)],
        name="pack",
    )(
        atom_s.T,
        atom_pos,
        edge_vec,
        edge_nbr.reshape(-1, LANES),
        border_index.reshape(1, -1),
        send_index,
        jnp.transpose(w_msg, (0, 2, 3, 1)).reshape(-1, LANES),
        jnp.transpose(w_rad, (0, 2, 1, 3)).reshape(-1, half),
        w_probe,
        b_in,
        b_mix.reshape(1, -1),
        w_out.reshape(1, -1),
        probe_list,
        probe_count.reshape(1, -1),
    )


def probe_grid(me, probes):
    number = me * probes + iota((1, probes), 1)
    return [(n % 16).astype(F32) * 0.25 - 1.875 for n in (number, number // 16, number // 256)]


def probe_kernel(sizes, list_at, data_mine, small, chosen_rows, probe_basis):
    groups, fan, rim, half, n_basis, cap, n_blocks = sizes
    width = 2 * half
    tiles = fan
    every = groups * LANES
    me = lax.axis_index("brick") * lax.axis_size("probe") + lax.axis_index("probe")
    rest_at = half + 4 * fan // 2
    small_rows = small[...]
    received = groups * cap
    edges = received * fan
    send_rows = jnp.concatenate(
        [data_mine[g, rest_at : rest_at + 8, :].astype(F32)[4:5] for g in range(groups)], axis=0
    )

    def picks(lane_count, per_group):
        lane = iota((LANES, lane_count), 1)
        wanted = me * cap + lane % cap
        spread = dot(send_rows.astype(BF16), one_hot(iota((LANES, lane_count), 0) == wanted))
        lane = iota((groups, lane_count), 1)
        spread = jnp.where(lane // per_group == iota((groups, lane_count), 0), spread, 0.0)
        return jnp.sum(spread, axis=0, keepdims=True)

    per_group = fan * cap
    pick_atoms = picks(received, cap)
    column = iota((every, 1), 0)
    column_name = (column // LANES) * LANES + lane_atom(column % LANES, fan, tiles)
    wanted = (iota((1, received), 1) // cap) * LANES + pick_atoms.astype(jnp.int32)
    chosen_atoms = one_hot(column_name == wanted)

    pos_rows = jnp.concatenate(
        [data_mine[g, rest_at : rest_at + 8, :] for g in range(groups)], axis=1
    )
    pos = dot(pos_rows, chosen_atoms) - 1.875
    chosen_rows[0:1, :] = picks(edges, per_group)
    chosen_rows[1:2, 0:received] = pick_atoms
    chosen_rows[2:5, 0:received] = pos[0:3]
    pos_cols = jnp.concatenate(
        [
            jnp.concatenate([pos, jnp.zeros((8, LANES - received), F32)], axis=1),
            jnp.zeros((LANES - 8, LANES), F32),
        ],
        axis=0,
    ).T
    list_len = width
    counts = []
    for block in range(n_blocks):
        live = iota((1, list_len), 1).astype(F32) < small_rows[list_at + n_blocks : list_at + n_blocks + 1, block : block + 1]
        named = jnp.where(live, small_rows[list_at + block : list_at + block + 1], -1.0)
        hits = jnp.where(iota((received, list_len), 0).astype(F32) == named, 1.0, 0.0)
        counts.append(
            jnp.broadcast_to(jnp.sum(hits, axis=1, keepdims=True), (received, PB))
        )
    counts = jnp.concatenate(counts, axis=1)
    probes = n_blocks * PB
    grid = probe_grid(me, probes)
    dist_sq = jnp.zeros((received, probes), F32)
    for x in range(3):
        dist_sq = dist_sq + (grid[x] - pos_cols[0:received, x : x + 1]) ** 2
    dist = jnp.sqrt(dist_sq) * ROOT
    envelope = (1.0 - dist_sq * (1.0 / 64.0)) ** 2 * counts
    probe_basis[...] = jnp.concatenate(
        [
            (bell(dist, r * (ROOT * 7.0 / (n_basis - 1))) * envelope).astype(BF16)
            for r in range(n_basis)
        ],
        axis=0,
    )


def density_kernel(
    sizes,
    data_mine,
    data_other,
    weights_mine,
    weights_other,
    small,
    w_in,
    w_mix,
    chosen_rows,
    probe_basis,
    density,
    state0,
    own0,
    faces0,
    state1,
    weights,
):
    groups, fan, rim, half, n_basis, cap, n_blocks = sizes
    layers = w_in.shape[0]
    width = 2 * half
    tiles = LANES * fan // LANES
    root_fan = fan**0.5
    me = lax.axis_index("brick") * lax.axis_size("probe") + lax.axis_index("probe")
    part = lax.axis_index("chan")
    weights[part] = weights_mine[...]
    weights[1 - part] = weights_other[...]
    every = groups * LANES
    edge_at = half
    n_edge = 4 * fan // 2
    rest_at = half + n_edge

    def data(group, c, rows):
        return (data_mine, data_other)[c][group, rows, :]

    def weight(layer, p):
        at = (layer * 3 + p) * half
        return jnp.concatenate([weights[c, at : at + half, :] for c in range(2)], axis=0)

    def radial_weight(layer, p):
        at = (layer * 3 + p) * n_basis
        return radial_all[:, at : at + n_basis]

    def edge_rows(group):
        return [data(group, c, slice(edge_at, rest_at)).astype(F32) for c in range(2)]

    def border_of(group):
        return data(group, 0, slice(rest_at, rest_at + 8)).astype(F32)[3:4, 0 : 2 * rim]

    centers = iota((n_basis, 1), 0).astype(F32) * (ROOT * 6.0 / (n_basis - 1))

    def basis_of(length, env):
        return (bell(length * ROOT, centers) * env).astype(BF16)

    received = groups * cap
    edges = received * fan
    per_group = fan * cap
    pick_edges = chosen_rows[0:1, :]
    pick_atoms = chosen_rows[1:2, 0:received]
    pos = chosen_rows[2:5, 0:received]
    atom_rows = lane_atom(iota((LANES, per_group), 0), fan, tiles).astype(F32)
    chosen = []
    for group in range(groups):
        rows = jnp.concatenate([data(group, c, slice(edge_at, rest_at)) for c in range(2)], axis=0)
        want = pick_edges[:, group * per_group : (group + 1) * per_group]
        chosen.append(dot(rows, one_hot(atom_rows == want)))
    chosen = jnp.concatenate(chosen, axis=1)
    step = fan // 2
    row = iota((2 * n_edge, edges), 0)
    slot_k = (row // n_edge) * step + row % step
    lane_k = (iota((2 * n_edge, edges), 1) % per_group) // cap
    chosen = jnp.where(slot_k == lane_k, chosen, 0.0)
    chosen = jnp.sum(chosen.reshape(2 * 4, step, edges), axis=1)
    chosen = chosen[0:4] + chosen[4:8]
    pick_vec = [chosen[x : x + 1] for x in range(3)]
    nbr = chosen[3:4]
    length = jnp.sqrt(sum(x * x for x in pick_vec))
    basis1 = basis_of(length, (1.0 - length * length * (1.0 / 36.0)) ** 2)

    nbr = nbr.astype(jnp.int32)
    home = iota((1, edges), 1) // per_group
    is_low = (nbr >= LANES) & (nbr < LANES + rim)
    is_up = nbr >= LANES + rim
    owner = jnp.where(
        is_low, (home + groups - 1) % groups, jnp.where(is_up, (home + 1) % groups, home)
    )
    entry = owner * 2 * rim + jnp.where(is_low, nbr - (LANES - rim), nbr - (LANES + rim))
    entry = jnp.where(is_low | is_up, entry, -1)
    border_all = jnp.concatenate(
        [border_of(g) for g in range(groups)], axis=1
    )
    border_all = jnp.broadcast_to(border_all, (16, groups * 2 * rim)).astype(BF16)
    seen = dot(border_all, one_hot(iota((groups * 2 * rim, edges), 0) == entry))[0:1]
    target_atom = jnp.where(entry < 0, nbr, seen.astype(jnp.int32))
    column = iota((every, 1), 0)
    column_name = (column // LANES) * LANES + lane_atom(column % LANES, fan, tiles)
    quad = groups // 2
    window = [[(h * quad + groups - 1 + i) % groups for i in range(quad + 2)] for h in range(2)]
    window_pick = []
    for h in range(2):
        lanes = slice(h * edges // 2, (h + 1) * edges // 2)
        near = lax.rem(owner[:, lanes] + 2 * groups - (h * quad + groups - 1), groups)
        name = near * LANES + target_atom[:, lanes]
        window_pick.append(one_hot(column_name[: (quad + 2) * LANES] == name))
    wanted = (iota((1, received), 1) // cap) * LANES + pick_atoms.astype(jnp.int32)
    chosen_atoms = one_hot(column_name == wanted)

    small_rows = small[...]
    columns = small_rows.T
    radial_at = weights.shape[1] - half
    radial_all = jnp.concatenate([weights[c, radial_at:, :] for c in range(2)], axis=0)

    terms_shape = (2 * n_basis, n_basis * received)
    probe_weight = radial_all[:, 3 * layers * n_basis :]
    w_scalar, w_vector = (
        dot(probe_weight, one_hot(iota(terms_shape, 1) // received * 2 + p == iota(terms_shape, 0)))
        for p in range(2)
    )

    probes = density.shape[1]
    grid = probe_grid(me, probes)

    for group in range(groups):
        for c in range(2):
            place = part if c == 0 else 1 - part
            rows = pl.ds(pl.multiple_of(place * half, half), half)
            state0[rows, group * LANES : (group + 1) * LANES] = data(group, c, slice(0, half))
    hidden = silu(dot_tn(w_in[0], state0[...]) + columns[:, 0:1]).astype(BF16)
    weight_ac = jnp.concatenate([weight(0, 0), weight(0, 2)], axis=0)
    messages = dot(weight_ac, hidden).astype(BF16)
    atom_col = lane_atom(iota((LANES, 2 * rim), 0), fan, tiles).astype(F32)
    for group in range(groups):
        own = messages[:, group * LANES : (group + 1) * LANES]
        own0[group] = own
        border_row = border_of(group)
        faces0[group, :, 0 : 2 * rim] = dot(own, one_hot(atom_col == border_row)).astype(BF16)

    row = iota((LANES + 2 * rim, 1), 0)
    names = jnp.where(
        row < LANES,
        lane_atom(row, fan, tiles),
        jnp.where(row < LANES + rim, row + rim, row - rim),
    ).astype(F32)
    names = jnp.broadcast_to(names, (LANES + 2 * rim, LANES)).astype(BF16)
    upper_lane = iota((2 * width, 2 * rim), 1) < rim
    radial_ac = jnp.concatenate([radial_weight(0, 0), radial_weight(0, 2)], axis=0)
    radial_rows = jnp.concatenate([jnp.zeros((2 * width, LANES + 2 * rim), BF16), radial_ac], axis=1)
    blank = jnp.zeros((2 * width, n_basis), BF16)

    for group in range(groups):
        up = (group + 1) % groups
        low = (group + groups - 1) % groups
        ghosts = jnp.where(
            upper_lane,
            faces0[up, :, 0 : 2 * rim].astype(F32),
            faces0[low, :, 0 : 2 * rim].astype(F32),
        ).astype(BF16)
        table = jnp.concatenate([own0[group], ghosts, blank], axis=1)
        left = jnp.concatenate(
            [
                block[at : at + 16]
                for at in range(0, 2 * width, 16)
                for block in (table, radial_rows)
            ],
            axis=0,
        )
        halves = edge_rows(group)
        step = fan // 2
        acc = jnp.zeros((width, LANES), F32)
        acc_vec = [jnp.zeros((width, LANES), F32) for _ in range(3)]
        for c in range(2):
            rows = halves[c]
            vec = [rows[x * step : (x + 1) * step] for x in range(3)]
            nbr = rows[3 * step : 4 * step]
            length_sq = vec[0] * vec[0] + vec[1] * vec[1] + vec[2] * vec[2]
            length = jnp.sqrt(length_sq)
            env = (1.0 - length * length * (1.0 / 36.0)) ** 2
            for pair in range(step // 2):
                ks = (2 * pair, 2 * pair + 1)
                picked = jnp.concatenate([same(names, nbr[k : k + 1].astype(BF16)) for k in ks], axis=1)
                basis = jnp.concatenate(
                    [basis_of(length[k : k + 1], env[k : k + 1]) for k in ks], axis=1
                )
                both = dot(left, jnp.concatenate([picked, basis], axis=0))
                prod = jnp.concatenate(
                    [both[at : at + 16] * both[at + 16 : at + 32] for at in range(0, 4 * width, 32)],
                    axis=0,
                )
                for i, k in enumerate(ks):
                    block = prod[:, i * LANES : (i + 1) * LANES]
                    acc = acc + block[:width]
                    for x in range(3):
                        acc_vec[x] = acc_vec[x] + block[width:] * vec[x][k : k + 1]
        lanes = slice(group * LANES, (group + 1) * LANES)
        state1[0:width, lanes] = (state0[:, lanes].astype(F32) + acc * (1.0 / root_fan)).astype(BF16)
        for x in range(3):
            state1[(x + 1) * width : (x + 2) * width, lanes] = (acc_vec[x] * (1.0 / root_fan)).astype(BF16)

    rows = []
    for h in range(2):
        near_states = jnp.concatenate(
            [state1[:, g * LANES : (g + 1) * LANES] for g in window[h]], axis=1
        )
        rows.append(dot(near_states, window_pick[h]))
    rows = jnp.concatenate(rows, axis=1)
    hidden = silu(dot_tn(w_in[1], rows[:width].astype(BF16)) + columns[:, 1:2]).astype(BF16)
    weight_abc = jnp.concatenate([weight(1, p) for p in range(3)], axis=0)
    messages = dot(weight_abc, hidden).astype(BF16).astype(F32)
    radial_abc = jnp.concatenate([radial_weight(1, p) for p in range(3)], axis=0)
    filters = dot(radial_abc, basis1)
    weighted = messages * filters
    gate = weighted[width : 2 * width]
    along = weighted[2 * width :]
    parts = [weighted[:width]]
    for x in range(3):
        parts.append(rows[(1 + x) * width : (2 + x) * width] * gate + along * pick_vec[x])
    parts = jnp.concatenate(parts, axis=0).astype(BF16)
    edge = iota((edges, received), 0)
    slot = (edge // per_group) * cap + edge % cap
    delta = dot(parts, one_hot(slot == iota((edges, received), 1)))
    final = (dot(state1[...], chosen_atoms) + delta * (1.0 / root_fan)).astype(BF16)

    spread = one_hot(
        iota((received, n_basis * received), 1) % received == iota((received, n_basis * received), 0)
    )
    final = dot(final, spread)
    pos = jnp.concatenate([pos] * n_basis, axis=1)
    vectors = [final[(x + 1) * width : (x + 2) * width] for x in range(3)]
    along = sum(vectors[x] * pos[x : x + 1] for x in range(3))
    terms = [w_scalar * final[:width] - w_vector * along]
    terms += [w_vector * vector for vector in vectors]
    sums = dot(jnp.concatenate(terms, axis=0).astype(BF16), probe_basis[...])
    charges = sums[:width]
    for x in range(3):
        charges = charges + grid[x] * sums[(x + 1) * width : (x + 2) * width]
    mixed = dot_tn(w_mix[...], charges.astype(BF16)) + columns[:, layers : layers + 1]
    density[...] = jnp.sum(silu(mixed) * columns[:, layers + 1 : layers + 2], axis=0, keepdims=True)


def few_groups(
    atom_s, atom_pos, edge_vec, edge_nbr, border_index, send_index, probe_list, probe_count,
    w_in, b_in, w_msg, w_rad, w_probe, w_mix, b_mix, w_out,
):
    atoms, half = atom_s.shape
    groups = lax.axis_size("brick") * lax.axis_size("probe")
    fan = edge_nbr.shape[0] // atoms
    rim = border_index.shape[0] // 2
    n_basis = w_rad.shape[1]
    cap = send_index.shape[1] // groups
    width = 2 * half
    every = groups * LANES
    data, weights, small = pack(
        groups, atom_s, atom_pos, edge_vec, edge_nbr, border_index, send_index, w_msg, w_rad, w_probe,
        b_in, b_mix, w_out, probe_list, probe_count,
    )
    swap = [(0, 1), (1, 0)]
    weights_other = lax.ppermute(weights, "chan", swap)
    mine = lax.all_to_all(data, ("brick", "probe"), split_axis=0, concat_axis=0, tiled=True)
    other = lax.ppermute(mine, "chan", swap)
    n_probes = probe_list.shape[0] * PB
    sizes = (groups, fan, rim, half, n_basis, cap, probe_list.shape[0])
    chosen_rows, probe_basis = pl.pallas_call(
        functools.partial(probe_kernel, sizes, w_in.shape[0] + 2),
        out_shape=(
            jax.ShapeDtypeStruct((8, groups * cap * fan), F32),
            jax.ShapeDtypeStruct((n_basis * groups * cap, n_probes), BF16),
        ),
        compiler_params=pltpu.CompilerParams(vmem_limit_bytes=24 * 1024 * 1024),
        name="probe_basis",
    )(mine, small)
    density = pl.pallas_call(
        functools.partial(density_kernel, sizes),
        out_shape=jax.ShapeDtypeStruct((1, n_probes), F32),
        scratch_shapes=[
            pltpu.VMEM((width, every), BF16),
            pltpu.VMEM((groups, 2 * width, LANES), BF16),
            pltpu.VMEM((groups, 2 * width, LANES), BF16),
            pltpu.VMEM((4 * width, every), BF16),
            pltpu.VMEM((2,) + weights.shape, BF16),
        ],
        compiler_params=pltpu.CompilerParams(vmem_limit_bytes=40 * 1024 * 1024),
        name="density",
    )(mine, other, weights, weights_other, small, w_in, w_mix, chosen_rows, probe_basis)
    return density.reshape(n_probes)


def per_device(*args):
    if lax.axis_size("brick") * lax.axis_size("probe") == FEW_GROUPS:
        return few_groups(*args)
    return many_groups(*args)


def extended(block, sides, width):
    for axis, dim in sides:
        count = lax.axis_size(axis)
        forward = [(i, i + 1) for i in range(count - 1)]
        forward.append((count - 1, 0))
        backward = [(target, source) for source, target in forward]
        low = lax.ppermute(
            lax.slice_in_dim(block, block.shape[dim] - width, None, axis=dim), axis, forward
        )
        high = lax.ppermute(lax.slice_in_dim(block, 0, width, axis=dim), axis, backward)
        block = jnp.concatenate([low, block, high], axis=dim)
    return block


def radial(distance, count, top):
    centers = jnp.arange(count).astype(jnp.float32) * (top / (count - 1))
    return jnp.exp(-2.0 * (distance[..., None] - centers) ** 2)


def make_block(
    recv_rows, recv_pos, w_scalar, w_vector, feat_width, group_no, n_blocks, list_len, n_basis
):

    def probe_block(block_in):
        block_no, listed, live_count = block_in
        index_row = (group_no * n_blocks + block_no) * PB + jnp.arange(PB, dtype=jnp.int32)
        grid_xyz = (
            jnp.stack([index_row % 16, index_row // 16 % 16, index_row // 256 % 16], axis=1).astype(
                jnp.float32
            )
            * 0.25
        )
        atom_xyz = recv_pos[:, listed]
        disp = grid_xyz[:, :, None] - atom_xyz[None]
        dist_sq = jnp.sum(disp * disp, axis=1)
        live = (jnp.arange(list_len, dtype=jnp.int32) < live_count).astype(jnp.float32)
        envelope = (1.0 - dist_sq / 64.0) ** 2 * live[None, :]
        basis = radial(jnp.sqrt(dist_sq), n_basis, 7.0) * envelope[:, :, None]
        scalar_w = basis.astype(jnp.bfloat16).reshape(PB, list_len * n_basis)
        vector_w = (
            (disp[:, :, :, None] * basis[:, None])
            .astype(jnp.bfloat16)
            .reshape(PB, 3 * list_len * n_basis)
        )
        atom_rows = recv_rows[listed]
        atom_terms = (atom_rows[:, None, :feat_width] * w_scalar[None]).reshape(
            list_len * n_basis, feat_width
        )
        vec_rows = jnp.transpose(
            atom_rows[:, feat_width:].reshape(list_len, 3, feat_width), (1, 0, 2)
        )
        vector_terms = (vec_rows[:, :, None, :] * w_vector[None, None]).reshape(
            3 * list_len * n_basis, feat_width
        )
        charge = jnp.dot(scalar_w, atom_terms, preferred_element_type=jnp.float32) + jnp.dot(
            vector_w, vector_terms, preferred_element_type=jnp.float32
        )
        return charge.astype(jnp.bfloat16)

    return probe_block


def many_groups(
    atom_s,
    atom_pos,
    edge_vec,
    edge_nbr,
    border_index,
    send_index,
    probe_list,
    probe_count,
    w_in,
    b_in,
    w_msg,
    w_rad,
    w_probe,
    w_mix,
    b_mix,
    w_out,
):
    atom_count, half_width = atom_s.shape
    n_layers = w_in.shape[0]
    width = w_in.shape[1]
    n_basis = w_rad.shape[1]
    fan_out = edge_nbr.shape[0] // atom_count
    root_fan = fan_out**0.5
    rim_rows = border_index.shape[0] // 2
    length = jnp.sqrt(jnp.sum(edge_vec * edge_vec, axis=0))
    edge_env = (1.0 - length * length / 36.0) ** 2
    edge_basis = (radial(length, n_basis, 6.0) * edge_env[:, None]).astype(jnp.bfloat16)
    edge_cols = jnp.transpose(edge_vec)
    scalars = atom_s
    vectors = jnp.zeros((atom_count, 3 * half_width), jnp.bfloat16)
    for layer_no in range(n_layers):
        full_rows = lax.all_gather(scalars, "chan", axis=1, tiled=True)
        in_weight = w_in[layer_no]
        in_bias = b_in[layer_no]
        msg_weight = w_msg[layer_no].reshape(width, 3 * half_width)
        rad_weight = w_rad[layer_no].reshape(n_basis, 3 * half_width)
        hidden_act = jax.nn.silu(
            jnp.dot(full_rows, in_weight, preferred_element_type=jnp.float32) + in_bias
        ).astype(jnp.bfloat16)
        inner_tab = jnp.concatenate(
            [
                jnp.dot(hidden_act, msg_weight, preferred_element_type=jnp.float32).astype(
                    jnp.bfloat16
                ),
                vectors,
            ],
            axis=1,
        )
        padded = extended(inner_tab[border_index], ((("brick", "probe"), 0),), rim_rows)
        lookup = jnp.concatenate([inner_tab, padded[:rim_rows], padded[3 * rim_rows :]], axis=0)
        neighbour_rows = lookup[edge_nbr]
        filters = jnp.dot(edge_basis, rad_weight, preferred_element_type=jnp.float32)
        weighted = neighbour_rows[:, : 3 * half_width] * filters
        neighbour_vec = neighbour_rows[:, 3 * half_width :].reshape(-1, 3, half_width)
        vector_gate = weighted[:, None, half_width : 2 * half_width]
        along_edge = weighted[:, None, 2 * half_width :]
        delta_vec = neighbour_vec * vector_gate + along_edge * edge_cols[:, :, None]
        delta_scalar = (
            weighted[:, :half_width].reshape(atom_count, fan_out, half_width).sum(axis=1) / root_fan
        )
        delta_vec = delta_vec.reshape(atom_count, fan_out, 3 * half_width).sum(axis=1) / root_fan
        scalars = (scalars + delta_scalar).astype(jnp.bfloat16)
        vectors = (vectors + delta_vec).astype(jnp.bfloat16)
    features = jnp.concatenate([scalars, vectors], axis=1)
    picks = send_index[0]
    n_brick = lax.axis_size("brick")
    n_probe = lax.axis_size("probe")
    n_groups = n_brick * n_probe
    slot_cap = picks.shape[0] // n_groups
    out_rows = features[picks]
    out_pos = jnp.transpose(atom_pos)[picks].astype(jnp.bfloat16)
    received = (
        lax.all_to_all(
            out_rows.reshape(n_groups, slot_cap, 4 * half_width),
            ("brick", "probe"),
            split_axis=0,
            concat_axis=0,
            tiled=True,
        ),
        lax.all_to_all(
            out_pos.reshape(n_groups, slot_cap, 3),
            ("brick", "probe"),
            split_axis=0,
            concat_axis=0,
            tiled=True,
        ),
    )
    recv_count = n_groups * slot_cap
    recv_rows = received[0].reshape(recv_count, 4 * half_width)
    recv_pos = jnp.transpose(received[1].reshape(recv_count, 3)).astype(jnp.float32)
    group_no = lax.axis_index("brick") * n_probe + lax.axis_index("probe")
    n_blocks, list_len = probe_list.shape
    probe_block = make_block(
        recv_rows,
        recv_pos,
        w_probe[:, 0, :],
        w_probe[:, 1, :],
        half_width,
        group_no,
        n_blocks,
        list_len,
        n_basis,
    )
    charges = lax.map(
        probe_block, (jnp.arange(n_blocks, dtype=jnp.int32), probe_list, probe_count)
    ).reshape(n_blocks * PB, half_width)
    mix_rows = lax.dynamic_slice_in_dim(w_mix, lax.axis_index("chan") * half_width, half_width, 0)
    mixed = lax.psum(jnp.dot(charges, mix_rows, preferred_element_type=jnp.float32), "chan")
    return jnp.sum(jax.nn.silu(mixed + b_mix) * w_out, axis=1)


def solution(mesh):
    in_specs = (
        P(("image", "brick", "probe"), "chan"),
        P(None, ("image", "brick", "probe")),
        P(None, ("image", "brick", "probe")),
        P(("image", "brick", "probe")),
        P(("image", "brick", "probe")),
        P(("image", "brick", "probe"), None),
        P(("image", "brick", "probe"), None),
        P(("image", "brick", "probe")),
        P(),
        P(),
        P(None, None, None, "chan"),
        P(None, None, None, "chan"),
        P(None, None, "chan"),
        P(),
        P(),
        P(),
    )
    out_specs = P(("image", "brick", "probe"))
    return jax.shard_map(
        per_device, mesh=mesh, in_specs=in_specs, out_specs=out_specs, check_vma=False
    )
```

```python
import functools
import itertools
import math

import jax
import jax.numpy as jnp
from jax import lax
from jax.experimental import pallas as pl
from jax.experimental.pallas import tpu as pltpu
from jax.sharding import PartitionSpec as P

PB = 128
LANES = 128
FEW_GROUPS = 8
SMALL = 16
ROOT = (2.0 * math.log2(math.e)) ** 0.5
F32 = jnp.float32
BF16 = jnp.bfloat16


def iota(shape, dim):
    return lax.broadcasted_iota(jnp.int32, shape, dim)


def dot(a, b):
    return jnp.dot(a, b, preferred_element_type=F32)


def dot_tn(a, b):
    return lax.dot_general(a, b, (((0,), (0,)), ((), ())), preferred_element_type=F32)


def one_hot(mask):
    return jnp.where(mask, 1.0, 0.0).astype(BF16)


def same(names, row):
    return jnp.where(names == row, jnp.ones_like(names), jnp.zeros_like(names))


def silu(x):
    half_x = 0.5 * x
    return half_x * jnp.tanh(half_x) + half_x


def bell(scaled, center):
    away = scaled - center
    return jnp.exp2(-(away * away))


def lane_atom(lane, fan, tiles):
    return (lane % tiles) * (LANES // fan) + lane // tiles


def length_keeping_round(exact):
    choices = []
    for value in exact:
        near = value.astype(BF16).astype(F32)
        step = jnp.where(value > near, 1.01 / 256.0, -1.01 / 256.0) * jnp.abs(near)
        choices.append((near, (near + step).astype(BF16).astype(F32)))
    target = sum(value * value for value in exact)
    best, best_error = None, None
    for picked in itertools.product(*choices):
        error = jnp.abs(sum(value * value for value in picked) - target)
        if best is None:
            best, best_error = picked, error
            continue
        better = error < best_error
        best = tuple(jnp.where(better, new, old) for new, old in zip(picked, best))
        best_error = jnp.where(better, error, best_error)
    return best


def pack_kernel(
    fan, atom_s, atom_pos, edge_vec, edge_nbr, border, send, w_msg, w_rad, w_probe,
    b_in, b_mix, w_out, probe_list, probe_count, data_out, weight_out, small_out, natural,
):
    half, atoms = atom_s.shape
    tiles = atoms * fan // LANES
    per_tile = LANES // fan
    part = lax.axis_index("chan")
    perm = one_hot(lane_atom(iota((atoms, LANES), 1), fan, tiles) == iota((atoms, LANES), 0))
    scalars = dot(atom_s[...], perm).astype(BF16)
    for tile in range(tiles):
        for comp in range(3):
            natural[comp * tiles + tile : comp * tiles + tile + 1, :] = edge_vec[
                comp : comp + 1, tile * LANES : (tile + 1) * LANES
            ]
    exact = [natural[comp * tiles : (comp + 1) * tiles, :] for comp in range(3)]
    for comp, value in enumerate(length_keeping_round(exact)):
        natural[comp * tiles : (comp + 1) * tiles, :] = value
    natural[3 * tiles : 4 * tiles, :] = edge_nbr[...].astype(F32)
    natural[4 * tiles :, :] = jnp.zeros((LANES - 4 * tiles, LANES), F32)
    turned = natural[...].T
    lane = iota((fan, LANES), 1)
    sorted_rows = []
    for comp in range(4):
        rows = jnp.zeros((fan, LANES), F32)
        for a in range(per_tile):
            piece = turned[a * fan : (a + 1) * fan, :]
            shift = (a * tiles - comp * tiles) % LANES
            piece = pltpu.roll(piece, shift, 1) if shift else piece
            rows = jnp.where(lane // tiles == a, piece, rows)
        sorted_rows.append(jnp.where(part == 0, rows[: fan // 2], rows[fan // 2 :]))
    pos = dot(atom_pos[...].astype(BF16), perm)
    blank = jnp.zeros((1, LANES), F32)
    border_row = jnp.concatenate(
        [border[...].astype(F32), jnp.zeros((1, LANES - border.shape[1]), F32)], axis=1
    )
    send_row = jnp.concatenate(
        [send[...].astype(F32), jnp.zeros((1, LANES - send.shape[1]), F32)], axis=1
    )
    rest = jnp.concatenate([pos, border_row, send_row, blank, blank, blank], axis=0)
    others = jnp.concatenate(sorted_rows + [rest], axis=0).astype(BF16)
    data_out[0:half, :] = scalars
    data_out[half:, :] = others
    at = 0
    for piece in (b_in, b_mix, w_out, probe_list, probe_count):
        rows, cols = piece.shape
        small_out[at : at + rows, 0:cols] = piece[...].astype(F32)
        at += rows
    probe_rows = [w_probe[r].astype(F32) for r in range(w_probe.shape[0])]
    radial = jnp.concatenate([w_rad[...].astype(F32)] + probe_rows, axis=0).T.astype(BF16)
    weight_out[: w_msg.shape[0], :] = w_msg[...]
    weight_out[w_msg.shape[0] :, :] = radial


def pack(
    atom_s, atom_pos, edge_vec, edge_nbr, border_index, send_index, w_msg, w_rad, w_probe,
    b_in, b_mix, w_out, probe_list, probe_count,
):
    atoms, half = atom_s.shape
    fan = edge_nbr.shape[0] // atoms
    return pl.pallas_call(
        functools.partial(pack_kernel, fan),
        out_shape=(
            jax.ShapeDtypeStruct((half + 4 * fan // 2 + 8, LANES), BF16),
            jax.ShapeDtypeStruct((w_msg.size // LANES + half, LANES), BF16),
            jax.ShapeDtypeStruct((SMALL, LANES), F32),
        ),
        scratch_shapes=[pltpu.VMEM((LANES, LANES), F32)],
        name="pack",
    )(
        atom_s.T,
        atom_pos,
        edge_vec,
        edge_nbr.reshape(-1, LANES),
        border_index.reshape(1, -1),
        send_index,
        jnp.transpose(w_msg, (0, 2, 3, 1)).reshape(-1, LANES),
        jnp.transpose(w_rad, (0, 2, 1, 3)).reshape(-1, half),
        w_probe,
        b_in,
        b_mix.reshape(1, -1),
        w_out.reshape(1, -1),
        probe_list,
        probe_count.reshape(1, -1),
    )


def merge_kernel(*refs):
    bricks = len(refs) - 1
    for shift in range(bricks):
        source = lax.rem(lax.axis_index("brick") + bricks - shift, bricks)
        refs[-1][source] = refs[shift][...]


def probe_grid(me, probes):
    number = me * probes + iota((1, probes), 1)
    return [(n % 16).astype(F32) * 0.25 - 1.875 for n in (number, number // 16, number // 256)]


def probe_kernel(sizes, list_at, data_mine, data_beside, small, chosen_rows, probe_basis):
    groups, fan, rim, half, n_basis, cap, n_blocks = sizes
    width = 2 * half
    tiles = fan
    every = groups * LANES
    me = lax.axis_index("brick") * lax.axis_size("probe") + lax.axis_index("probe")
    rest_at = half + 4 * fan // 2
    small_rows = small[...]
    received = groups * cap
    edges = received * fan
    column_no = lax.axis_index("probe")
    rest = []
    for g in range(groups):
        here, there = (x[g // 2, rest_at : rest_at + 8, :].astype(F32) for x in (data_mine, data_beside))
        rest.append(jnp.where(column_no == g % 2, here, there))
    send_rows = jnp.concatenate([rows[4:5] for rows in rest], axis=0)

    def picks(lane_count, per_group):
        lane = iota((LANES, lane_count), 1)
        wanted = me * cap + lane % cap
        spread = dot(send_rows.astype(BF16), one_hot(iota((LANES, lane_count), 0) == wanted))
        lane = iota((groups, lane_count), 1)
        spread = jnp.where(lane // per_group == iota((groups, lane_count), 0), spread, 0.0)
        return jnp.sum(spread, axis=0, keepdims=True)

    per_group = fan * cap
    pick_atoms = picks(received, cap)
    column = iota((every, 1), 0)
    column_name = (column // LANES) * LANES + lane_atom(column % LANES, fan, tiles)
    wanted = (iota((1, received), 1) // cap) * LANES + pick_atoms.astype(jnp.int32)
    chosen_atoms = one_hot(column_name == wanted)

    pos_rows = jnp.concatenate(rest, axis=1).astype(BF16)
    pos = dot(pos_rows, chosen_atoms) - 1.875
    chosen_rows[0:1, :] = picks(edges, per_group)
    chosen_rows[1:2, 0:received] = pick_atoms
    chosen_rows[2:5, 0:received] = pos[0:3]
    pos_cols = jnp.concatenate(
        [
            jnp.concatenate([pos, jnp.zeros((8, LANES - received), F32)], axis=1),
            jnp.zeros((LANES - 8, LANES), F32),
        ],
        axis=0,
    ).T
    list_len = width
    counts = []
    for block in range(n_blocks):
        live = iota((1, list_len), 1).astype(F32) < small_rows[list_at + n_blocks : list_at + n_blocks + 1, block : block + 1]
        named = jnp.where(live, small_rows[list_at + block : list_at + block + 1], -1.0)
        hits = jnp.where(iota((received, list_len), 0).astype(F32) == named, 1.0, 0.0)
        counts.append(
            jnp.broadcast_to(jnp.sum(hits, axis=1, keepdims=True), (received, PB))
        )
    counts = jnp.concatenate(counts, axis=1)
    probes = n_blocks * PB
    grid = probe_grid(me, probes)
    dist_sq = jnp.zeros((received, probes), F32)
    for x in range(3):
        dist_sq = dist_sq + (grid[x] - pos_cols[0:received, x : x + 1]) ** 2
    dist = jnp.sqrt(dist_sq) * ROOT
    envelope = (1.0 - dist_sq / 64.0) ** 2 * counts
    probe_basis[...] = jnp.concatenate(
        [
            (bell(dist, r * (ROOT * 7.0 / (n_basis - 1))) * envelope).astype(BF16)
            for r in range(n_basis)
        ],
        axis=0,
    )


def density_kernel(
    sizes,
    data_mine,
    data_beside,
    data_other,
    data_across,
    weights_mine,
    weights_other,
    small,
    w_in,
    w_mix,
    chosen_rows,
    probe_basis,
    density,
    state0,
    own0,
    faces0,
    state1,
    weights,
    data_all,
):
    groups, fan, rim, half, n_basis, cap, n_blocks = sizes
    layers = w_in.shape[0]
    width = 2 * half
    tiles = LANES * fan // LANES
    root_fan = fan**0.5
    me = lax.axis_index("brick") * lax.axis_size("probe") + lax.axis_index("probe")
    part = lax.axis_index("chan")
    weights[part] = weights_mine[...]
    weights[1 - part] = weights_other[...]
    column = lax.axis_index("probe")
    data_all[part, column] = data_mine[...]
    data_all[part, 1 - column] = data_beside[...]
    data_all[1 - part, column] = data_other[...]
    data_all[1 - part, 1 - column] = data_across[...]
    every = groups * LANES
    edge_at = half
    n_edge = 4 * fan // 2
    rest_at = half + n_edge

    def data(group, c, rows):
        return data_all[c, group % 2, group // 2, rows, :]

    def weight(layer, p):
        at = (layer * 3 + p) * half
        return jnp.concatenate([weights[c, at : at + half, :] for c in range(2)], axis=0)

    def radial_weight(layer, p):
        at = (layer * 3 + p) * n_basis
        return radial_all[:, at : at + n_basis]

    def edge_rows(group):
        return [data(group, c, slice(edge_at, rest_at)).astype(F32) for c in range(2)]

    def border_of(group):
        return data(group, 0, slice(rest_at, rest_at + 8)).astype(F32)[3:4, 0 : 2 * rim]

    centers = iota((n_basis, 1), 0).astype(F32) * (ROOT * 6.0 / (n_basis - 1))

    def basis_of(length, env):
        return (bell(length * ROOT, centers) * env).astype(BF16)

    received = groups * cap
    edges = received * fan
    per_group = fan * cap
    pick_edges = chosen_rows[0:1, :]
    pick_atoms = chosen_rows[1:2, 0:received]
    pos = chosen_rows[2:5, 0:received]
    atom_rows = lane_atom(iota((LANES, per_group), 0), fan, tiles).astype(F32)
    chosen = []
    for group in range(groups):
        rows = jnp.concatenate([data(group, c, slice(edge_at, rest_at)) for c in range(2)], axis=0)
        want = pick_edges[:, group * per_group : (group + 1) * per_group]
        chosen.append(dot(rows, one_hot(atom_rows == want)))
    chosen = jnp.concatenate(chosen, axis=1)
    step = fan // 2
    row = iota((2 * n_edge, edges), 0)
    slot_k = (row // n_edge) * step + row % step
    lane_k = (iota((2 * n_edge, edges), 1) % per_group) // cap
    chosen = jnp.where(slot_k == lane_k, chosen, 0.0)
    chosen = jnp.sum(chosen.reshape(2 * 4, step, edges), axis=1)
    chosen = chosen[0:4] + chosen[4:8]
    pick_vec = [chosen[x : x + 1] for x in range(3)]
    nbr = chosen[3:4]
    length = jnp.sqrt(sum(x * x for x in pick_vec))
    basis1 = basis_of(length, (1.0 - length * length / 36.0) ** 2)

    nbr = nbr.astype(jnp.int32)
    home = iota((1, edges), 1) // per_group
    is_low = (nbr >= LANES) & (nbr < LANES + rim)
    is_up = nbr >= LANES + rim
    owner = jnp.where(
        is_low, (home + groups - 1) % groups, jnp.where(is_up, (home + 1) % groups, home)
    )
    entry = owner * 2 * rim + jnp.where(is_low, nbr - (LANES - rim), nbr - (LANES + rim))
    entry = jnp.where(is_low | is_up, entry, -1)
    border_all = jnp.concatenate(
        [border_of(g) for g in range(groups)], axis=1
    )
    border_all = jnp.broadcast_to(border_all, (16, groups * 2 * rim)).astype(BF16)
    seen = dot(border_all, one_hot(iota((groups * 2 * rim, edges), 0) == entry))[0:1]
    target_atom = jnp.where(entry < 0, nbr, seen.astype(jnp.int32))
    column = iota((every, 1), 0)
    column_name = (column // LANES) * LANES + lane_atom(column % LANES, fan, tiles)
    quad = groups // 2
    window = [[(h * quad + groups - 1 + i) % groups for i in range(quad + 2)] for h in range(2)]
    window_pick = []
    for h in range(2):
        lanes = slice(h * edges // 2, (h + 1) * edges // 2)
        near = lax.rem(owner[:, lanes] + 2 * groups - (h * quad + groups - 1), groups)
        name = near * LANES + target_atom[:, lanes]
        window_pick.append(one_hot(column_name[: (quad + 2) * LANES] == name))
    wanted = (iota((1, received), 1) // cap) * LANES + pick_atoms.astype(jnp.int32)
    chosen_atoms = one_hot(column_name == wanted)

    small_rows = small[...]
    columns = small_rows.T
    radial_at = weights.shape[1] - half
    radial_all = jnp.concatenate([weights[c, radial_at:, :] for c in range(2)], axis=0)

    terms_shape = (2 * n_basis, n_basis * received)
    probe_weight = radial_all[:, 3 * layers * n_basis :]
    w_scalar, w_vector = (
        dot(probe_weight, one_hot(iota(terms_shape, 1) // received * 2 + p == iota(terms_shape, 0)))
        for p in range(2)
    )

    probes = density.shape[1]
    grid = probe_grid(me, probes)

    for group in range(groups):
        for c in range(2):
            rows = slice(c * half, (c + 1) * half)
            state0[rows, group * LANES : (group + 1) * LANES] = data(group, c, slice(0, half))
    hidden = silu(dot_tn(w_in[0], state0[...]) + columns[:, 0:1]).astype(BF16)
    weight_ac = jnp.concatenate([weight(0, 0), weight(0, 2)], axis=0)
    messages = dot(weight_ac, hidden).astype(BF16)
    atom_col = lane_atom(iota((LANES, 2 * rim), 0), fan, tiles).astype(F32)
    for group in range(groups):
        own = messages[:, group * LANES : (group + 1) * LANES]
        own0[group] = own
        border_row = border_of(group)
        faces0[group, :, 0 : 2 * rim] = dot(own, one_hot(atom_col == border_row)).astype(BF16)

    row = iota((LANES + 2 * rim, 1), 0)
    names = jnp.where(
        row < LANES,
        lane_atom(row, fan, tiles),
        jnp.where(row < LANES + rim, row + rim, row - rim),
    ).astype(F32)
    names = jnp.broadcast_to(names, (LANES + 2 * rim, LANES)).astype(BF16)
    upper_lane = iota((2 * width, 2 * rim), 1) < rim
    radial_ac = jnp.concatenate([radial_weight(0, 0), radial_weight(0, 2)], axis=0)
    radial_rows = jnp.concatenate([jnp.zeros((2 * width, LANES + 2 * rim), BF16), radial_ac], axis=1)
    blank = jnp.zeros((2 * width, n_basis), BF16)

    for group in range(groups):
        up = (group + 1) % groups
        low = (group + groups - 1) % groups
        ghosts = jnp.where(
            upper_lane,
            faces0[up, :, 0 : 2 * rim].astype(F32),
            faces0[low, :, 0 : 2 * rim].astype(F32),
        ).astype(BF16)
        table = jnp.concatenate([own0[group], ghosts, blank], axis=1)
        left = jnp.concatenate(
            [
                block[at : at + 16]
                for at in range(0, 2 * width, 16)
                for block in (table, radial_rows)
            ],
            axis=0,
        )
        halves = edge_rows(group)
        step = fan // 2
        acc = jnp.zeros((width, LANES), F32)
        acc_vec = [jnp.zeros((width, LANES), F32) for _ in range(3)]
        for c in range(2):
            rows = halves[c]
            vec = [rows[x * step : (x + 1) * step] for x in range(3)]
            nbr = rows[3 * step : 4 * step]
            length_sq = vec[0] * vec[0] + vec[1] * vec[1] + vec[2] * vec[2]
            length = jnp.sqrt(length_sq)
            env = (1.0 - length * length / 36.0) ** 2
            for pair in range(step // 2):
                ks = (2 * pair, 2 * pair + 1)
                picked = jnp.concatenate([same(names, nbr[k : k + 1].astype(BF16)) for k in ks], axis=1)
                basis = jnp.concatenate(
                    [basis_of(length[k : k + 1], env[k : k + 1]) for k in ks], axis=1
                )
                both = dot(left, jnp.concatenate([picked, basis], axis=0))
                prod = jnp.concatenate(
                    [both[at : at + 16] * both[at + 16 : at + 32] for at in range(0, 4 * width, 32)],
                    axis=0,
                )
                for i, k in enumerate(ks):
                    block = prod[:, i * LANES : (i + 1) * LANES]
                    acc = acc + block[:width]
                    for x in range(3):
                        acc_vec[x] = acc_vec[x] + block[width:] * vec[x][k : k + 1]
        lanes = slice(group * LANES, (group + 1) * LANES)
        state1[0:width, lanes] = (state0[:, lanes].astype(F32) + acc / root_fan).astype(BF16)
        for x in range(3):
            state1[(x + 1) * width : (x + 2) * width, lanes] = (acc_vec[x] / root_fan).astype(BF16)

    rows = []
    for h in range(2):
        near_states = jnp.concatenate(
            [state1[:, g * LANES : (g + 1) * LANES] for g in window[h]], axis=1
        )
        rows.append(dot(near_states, window_pick[h]))
    rows = jnp.concatenate(rows, axis=1)
    hidden = silu(dot_tn(w_in[1], rows[:width].astype(BF16)) + columns[:, 1:2]).astype(BF16)
    weight_abc = jnp.concatenate([weight(1, p) for p in range(3)], axis=0)
    messages = dot(weight_abc, hidden).astype(BF16).astype(F32)
    radial_abc = jnp.concatenate([radial_weight(1, p) for p in range(3)], axis=0)
    filters = dot(radial_abc, basis1)
    weighted = messages * filters
    gate = weighted[width : 2 * width]
    along = weighted[2 * width :]
    parts = [weighted[:width]]
    for x in range(3):
        parts.append(rows[(1 + x) * width : (2 + x) * width] * gate + along * pick_vec[x])
    parts = jnp.concatenate(parts, axis=0).astype(BF16)
    edge = iota((edges, received), 0)
    slot = (edge // per_group) * cap + edge % cap
    delta = dot(parts, one_hot(slot == iota((edges, received), 1)))
    final = (dot(state1[...], chosen_atoms) + delta / root_fan).astype(BF16).astype(F32)

    along = final[width : 2 * width] * pos[0:1]
    for x in range(1, 3):
        along = along + final[(x + 1) * width : (x + 2) * width] * pos[x : x + 1]
    def repeat(value):
        return jnp.concatenate([value] * n_basis, axis=1)
    terms = [w_scalar * repeat(final[:width]) - w_vector * repeat(along)]
    for x in range(3):
        terms.append(w_vector * repeat(final[(x + 1) * width : (x + 2) * width]))
    sums = dot(jnp.concatenate(terms, axis=0).astype(BF16), probe_basis[...])
    charges = sums[:width]
    for x in range(3):
        charges = charges + grid[x] * sums[(x + 1) * width : (x + 2) * width]
    mixed = dot_tn(w_mix[...], charges.astype(BF16)) + columns[:, layers : layers + 1]
    density[...] = jnp.sum(silu(mixed) * columns[:, layers + 1 : layers + 2], axis=0, keepdims=True)


def few_groups(
    atom_s, atom_pos, edge_vec, edge_nbr, border_index, send_index, probe_list, probe_count,
    w_in, b_in, w_msg, w_rad, w_probe, w_mix, b_mix, w_out,
):
    atoms, half = atom_s.shape
    groups = lax.axis_size("brick") * lax.axis_size("probe")
    fan = edge_nbr.shape[0] // atoms
    rim = border_index.shape[0] // 2
    n_basis = w_rad.shape[1]
    cap = send_index.shape[1] // groups
    width = 2 * half
    every = groups * LANES
    data, weights, small = pack(
        atom_s, atom_pos, edge_vec, edge_nbr, border_index, send_index, w_msg, w_rad, w_probe,
        b_in, b_mix, w_out, probe_list, probe_count,
    )
    swap = [(0, 1), (1, 0)]
    bricks = lax.axis_size("brick")
    blocks = [data]
    for shift in range(1, bricks):
        blocks.append(lax.ppermute(data, "brick", [(i, (i + shift) % bricks) for i in range(bricks)]))
    weights_other = lax.ppermute(weights, "chan", swap)
    mine = pl.pallas_call(
        merge_kernel,
        out_shape=jax.ShapeDtypeStruct((bricks,) + data.shape, BF16),
        compiler_params=pltpu.CompilerParams(vmem_limit_bytes=24 * 1024 * 1024),
        name="merge",
    )(*blocks)
    beside = lax.ppermute(mine, "probe", swap)
    other = lax.ppermute(mine, "chan", swap)
    across = lax.ppermute(beside, "chan", swap)
    n_probes = probe_list.shape[0] * PB
    sizes = (groups, fan, rim, half, n_basis, cap, probe_list.shape[0])
    chosen_rows, probe_basis = pl.pallas_call(
        functools.partial(probe_kernel, sizes, w_in.shape[0] + 2),
        out_shape=(
            jax.ShapeDtypeStruct((8, groups * cap * fan), F32),
            jax.ShapeDtypeStruct((n_basis * groups * cap, n_probes), BF16),
        ),
        compiler_params=pltpu.CompilerParams(vmem_limit_bytes=24 * 1024 * 1024),
        name="probe_basis",
    )(mine, beside, small)
    density = pl.pallas_call(
        functools.partial(density_kernel, sizes),
        out_shape=jax.ShapeDtypeStruct((1, n_probes), F32),
        scratch_shapes=[
            pltpu.VMEM((width, every), BF16),
            pltpu.VMEM((groups, 2 * width, LANES), BF16),
            pltpu.VMEM((groups, 2 * width, LANES), BF16),
            pltpu.VMEM((4 * width, every), BF16),
            pltpu.VMEM((2,) + weights.shape, BF16),
            pltpu.VMEM((2, 2, bricks) + data.shape, BF16),
        ],
        compiler_params=pltpu.CompilerParams(vmem_limit_bytes=40 * 1024 * 1024),
        name="density",
    )(mine, beside, other, across, weights, weights_other, small, w_in, w_mix, chosen_rows, probe_basis)
    return density.reshape(n_probes)


def per_device(*args):
    columns = lax.axis_size("probe")
    if columns == 2 and lax.axis_size("brick") * columns == FEW_GROUPS:
        return few_groups(*args)
    return many_groups(*args)


def extended(block, sides, width):
    for axis, dim in sides:
        count = lax.axis_size(axis)
        forward = [(i, i + 1) for i in range(count - 1)]
        forward.append((count - 1, 0))
        backward = [(target, source) for source, target in forward]
        low = lax.ppermute(
            lax.slice_in_dim(block, block.shape[dim] - width, None, axis=dim), axis, forward
        )
        high = lax.ppermute(lax.slice_in_dim(block, 0, width, axis=dim), axis, backward)
        block = jnp.concatenate([low, block, high], axis=dim)
    return block


def radial(distance, count, top):
    centers = jnp.arange(count).astype(jnp.float32) * (top / (count - 1))
    return jnp.exp(-2.0 * (distance[..., None] - centers) ** 2)


def make_block(
    recv_rows, recv_pos, w_scalar, w_vector, feat_width, group_no, n_blocks, list_len, n_basis
):

    def probe_block(block_in):
        block_no, listed, live_count = block_in
        index_row = (group_no * n_blocks + block_no) * PB + jnp.arange(PB, dtype=jnp.int32)
        grid_xyz = (
            jnp.stack([index_row % 16, index_row // 16 % 16, index_row // 256 % 16], axis=1).astype(
                jnp.float32
            )
            * 0.25
        )
        atom_xyz = recv_pos[:, listed]
        disp = grid_xyz[:, :, None] - atom_xyz[None]
        dist_sq = jnp.sum(disp * disp, axis=1)
        live = (jnp.arange(list_len, dtype=jnp.int32) < live_count).astype(jnp.float32)
        envelope = (1.0 - dist_sq / 64.0) ** 2 * live[None, :]
        basis = radial(jnp.sqrt(dist_sq), n_basis, 7.0) * envelope[:, :, None]
        scalar_w = basis.astype(jnp.bfloat16).reshape(PB, list_len * n_basis)
        vector_w = (
            (disp[:, :, :, None] * basis[:, None])
            .astype(jnp.bfloat16)
            .reshape(PB, 3 * list_len * n_basis)
        )
        atom_rows = recv_rows[listed]
        atom_terms = (atom_rows[:, None, :feat_width] * w_scalar[None]).reshape(
            list_len * n_basis, feat_width
        )
        vec_rows = jnp.transpose(
            atom_rows[:, feat_width:].reshape(list_len, 3, feat_width), (1, 0, 2)
        )
        vector_terms = (vec_rows[:, :, None, :] * w_vector[None, None]).reshape(
            3 * list_len * n_basis, feat_width
        )
        charge = jnp.dot(scalar_w, atom_terms, preferred_element_type=jnp.float32) + jnp.dot(
            vector_w, vector_terms, preferred_element_type=jnp.float32
        )
        return charge.astype(jnp.bfloat16)

    return probe_block


def many_groups(
    atom_s,
    atom_pos,
    edge_vec,
    edge_nbr,
    border_index,
    send_index,
    probe_list,
    probe_count,
    w_in,
    b_in,
    w_msg,
    w_rad,
    w_probe,
    w_mix,
    b_mix,
    w_out,
):
    atom_count, half_width = atom_s.shape
    n_layers = w_in.shape[0]
    width = w_in.shape[1]
    n_basis = w_rad.shape[1]
    fan_out = edge_nbr.shape[0] // atom_count
    root_fan = fan_out**0.5
    rim_rows = border_index.shape[0] // 2
    length = jnp.sqrt(jnp.sum(edge_vec * edge_vec, axis=0))
    edge_env = (1.0 - length * length / 36.0) ** 2
    edge_basis = (radial(length, n_basis, 6.0) * edge_env[:, None]).astype(jnp.bfloat16)
    edge_cols = jnp.transpose(edge_vec)
    scalars = atom_s
    vectors = jnp.zeros((atom_count, 3 * half_width), jnp.bfloat16)
    for layer_no in range(n_layers):
        full_rows = lax.all_gather(scalars, "chan", axis=1, tiled=True)
        in_weight = w_in[layer_no]
        in_bias = b_in[layer_no]
        msg_weight = w_msg[layer_no].reshape(width, 3 * half_width)
        rad_weight = w_rad[layer_no].reshape(n_basis, 3 * half_width)
        hidden_act = jax.nn.silu(
            jnp.dot(full_rows, in_weight, preferred_element_type=jnp.float32) + in_bias
        ).astype(jnp.bfloat16)
        inner_tab = jnp.concatenate(
            [
                jnp.dot(hidden_act, msg_weight, preferred_element_type=jnp.float32).astype(
                    jnp.bfloat16
                ),
                vectors,
            ],
            axis=1,
        )
        padded = extended(inner_tab[border_index], ((("brick", "probe"), 0),), rim_rows)
        lookup = jnp.concatenate([inner_tab, padded[:rim_rows], padded[3 * rim_rows :]], axis=0)
        neighbour_rows = lookup[edge_nbr]
        filters = jnp.dot(edge_basis, rad_weight, preferred_element_type=jnp.float32)
        weighted = neighbour_rows[:, : 3 * half_width] * filters
        neighbour_vec = neighbour_rows[:, 3 * half_width :].reshape(-1, 3, half_width)
        vector_gate = weighted[:, None, half_width : 2 * half_width]
        along_edge = weighted[:, None, 2 * half_width :]
        delta_vec = neighbour_vec * vector_gate + along_edge * edge_cols[:, :, None]
        delta_scalar = (
            weighted[:, :half_width].reshape(atom_count, fan_out, half_width).sum(axis=1) / root_fan
        )
        delta_vec = delta_vec.reshape(atom_count, fan_out, 3 * half_width).sum(axis=1) / root_fan
        scalars = (scalars + delta_scalar).astype(jnp.bfloat16)
        vectors = (vectors + delta_vec).astype(jnp.bfloat16)
    features = jnp.concatenate([scalars, vectors], axis=1)
    picks = send_index[0]
    n_brick = lax.axis_size("brick")
    n_probe = lax.axis_size("probe")
    n_groups = n_brick * n_probe
    slot_cap = picks.shape[0] // n_groups
    out_rows = features[picks]
    out_pos = jnp.transpose(atom_pos)[picks].astype(jnp.bfloat16)
    received = (
        lax.all_to_all(
            out_rows.reshape(n_groups, slot_cap, 4 * half_width),
            ("brick", "probe"),
            split_axis=0,
            concat_axis=0,
            tiled=True,
        ),
        lax.all_to_all(
            out_pos.reshape(n_groups, slot_cap, 3),
            ("brick", "probe"),
            split_axis=0,
            concat_axis=0,
            tiled=True,
        ),
    )
    recv_count = n_groups * slot_cap
    recv_rows = received[0].reshape(recv_count, 4 * half_width)
    recv_pos = jnp.transpose(received[1].reshape(recv_count, 3)).astype(jnp.float32)
    group_no = lax.axis_index("brick") * n_probe + lax.axis_index("probe")
    n_blocks, list_len = probe_list.shape
    probe_block = make_block(
        recv_rows,
        recv_pos,
        w_probe[:, 0, :],
        w_probe[:, 1, :],
        half_width,
        group_no,
        n_blocks,
        list_len,
        n_basis,
    )
    charges = lax.map(
        probe_block, (jnp.arange(n_blocks, dtype=jnp.int32), probe_list, probe_count)
    ).reshape(n_blocks * PB, half_width)
    mix_rows = lax.dynamic_slice_in_dim(w_mix, lax.axis_index("chan") * half_width, half_width, 0)
    mixed = lax.psum(jnp.dot(charges, mix_rows, preferred_element_type=jnp.float32), "chan")
    return jnp.sum(jax.nn.silu(mixed + b_mix) * w_out, axis=1)


def solution(mesh):
    in_specs = (
        P(("image", "brick", "probe"), "chan"),
        P(None, ("image", "brick", "probe")),
        P(None, ("image", "brick", "probe")),
        P(("image", "brick", "probe")),
        P(("image", "brick", "probe")),
        P(("image", "brick", "probe"), None),
        P(("image", "brick", "probe"), None),
        P(("image", "brick", "probe")),
        P(),
        P(),
        P(None, None, None, "chan"),
        P(None, None, None, "chan"),
        P(None, None, "chan"),
        P(),
        P(),
        P(),
    )
    out_specs = P(("image", "brick", "probe"))
    return jax.shard_map(
        per_device, mesh=mesh, in_specs=in_specs, out_specs=out_specs, check_vma=False
    )
```

```python
import functools
import itertools
import math

import jax
import jax.numpy as jnp
from jax import lax
from jax.experimental import pallas as pl
from jax.experimental.pallas import tpu as pltpu
from jax.sharding import PartitionSpec as P

PB = 128
LANES = 128
FEW_GROUPS = 8
SMALL = 16
ROOT = (2.0 * math.log2(math.e)) ** 0.5
F32 = jnp.float32
BF16 = jnp.bfloat16


def iota(shape, dim):
    return lax.broadcasted_iota(jnp.int32, shape, dim)


def dot(a, b):
    return jnp.dot(a, b, preferred_element_type=F32)


def dot_tn(a, b):
    return lax.dot_general(a, b, (((0,), (0,)), ((), ())), preferred_element_type=F32)


def one_hot(mask):
    return jnp.where(mask, 1.0, 0.0).astype(BF16)


def same(names, row):
    return jnp.where(names == row, jnp.ones_like(names), jnp.zeros_like(names))


def silu(x):
    half_x = 0.5 * x
    return half_x * jnp.tanh(half_x) + half_x


def bell(scaled, center):
    away = scaled - center
    return jnp.exp2(-(away * away))


def lane_atom(lane, fan, tiles):
    return (lane % tiles) * (LANES // fan) + lane // tiles


def length_keeping_round(exact):
    choices = []
    for value in exact:
        near = value.astype(BF16).astype(F32)
        step = jnp.where(value > near, 1.01 / 256.0, -1.01 / 256.0) * jnp.abs(near)
        choices.append((near, (near + step).astype(BF16).astype(F32)))
    target = sum(value * value for value in exact)
    best, best_error = None, None
    for picked in itertools.product(*choices):
        error = jnp.abs(sum(value * value for value in picked) - target)
        if best is None:
            best, best_error = picked, error
            continue
        better = error < best_error
        best = tuple(jnp.where(better, new, old) for new, old in zip(picked, best))
        best_error = jnp.where(better, error, best_error)
    return best


def pack_kernel(
    fan, atom_s, atom_pos, edge_vec, edge_nbr, border, send, w_msg, w_rad, w_probe,
    b_in, b_mix, w_out, probe_list, probe_count, data_out, weight_out, small_out, natural,
):
    half, atoms = atom_s.shape
    tiles = atoms * fan // LANES
    per_tile = LANES // fan
    part = lax.axis_index("chan")
    perm = one_hot(lane_atom(iota((atoms, LANES), 1), fan, tiles) == iota((atoms, LANES), 0))
    scalars = dot(atom_s[...], perm).astype(BF16)
    for tile in range(tiles):
        for comp in range(3):
            natural[comp * tiles + tile : comp * tiles + tile + 1, :] = edge_vec[
                comp : comp + 1, tile * LANES : (tile + 1) * LANES
            ]
    exact = [natural[comp * tiles : (comp + 1) * tiles, :] for comp in range(3)]
    for comp, value in enumerate(length_keeping_round(exact)):
        natural[comp * tiles : (comp + 1) * tiles, :] = value
    natural[3 * tiles : 4 * tiles, :] = edge_nbr[...].astype(F32)
    natural[4 * tiles :, :] = jnp.zeros((LANES - 4 * tiles, LANES), F32)
    turned = natural[...].T
    lane = iota((fan, LANES), 1)
    sorted_rows = []
    for comp in range(4):
        rows = jnp.zeros((fan, LANES), F32)
        for a in range(per_tile):
            piece = turned[a * fan : (a + 1) * fan, :]
            shift = (a * tiles - comp * tiles) % LANES
            piece = pltpu.roll(piece, shift, 1) if shift else piece
            rows = jnp.where(lane // tiles == a, piece, rows)
        sorted_rows.append(jnp.where(part == 0, rows[: fan // 2], rows[fan // 2 :]))
    pos = dot(atom_pos[...].astype(BF16), perm)
    blank = jnp.zeros((1, LANES), F32)
    border_row = jnp.concatenate(
        [border[...].astype(F32), jnp.zeros((1, LANES - border.shape[1]), F32)], axis=1
    )
    send_row = jnp.concatenate(
        [send[...].astype(F32), jnp.zeros((1, LANES - send.shape[1]), F32)], axis=1
    )
    rest = jnp.concatenate([pos, border_row, send_row, blank, blank, blank], axis=0)
    others = jnp.concatenate(sorted_rows + [rest], axis=0).astype(BF16)
    data_out[0:half, :] = scalars
    data_out[half:, :] = others
    weight_out[weight_out.shape[0] - data_out.shape[0] :, :] = data_out[...]
    at = 0
    for piece in (b_in, b_mix, w_out, probe_list, probe_count):
        rows, cols = piece.shape
        small_out[at : at + rows, 0:cols] = piece[...].astype(F32)
        at += rows
    probe_rows = [w_probe[r].astype(F32) for r in range(w_probe.shape[0])]
    radial = jnp.concatenate([w_rad[...].astype(F32)] + probe_rows, axis=0).T.astype(BF16)
    weight_out[: w_msg.shape[0], :] = w_msg[...]
    weight_out[w_msg.shape[0] : w_msg.shape[0] + half, :] = radial


def pack(
    atom_s, atom_pos, edge_vec, edge_nbr, border_index, send_index, w_msg, w_rad, w_probe,
    b_in, b_mix, w_out, probe_list, probe_count,
):
    atoms, half = atom_s.shape
    fan = edge_nbr.shape[0] // atoms
    return pl.pallas_call(
        functools.partial(pack_kernel, fan),
        out_shape=(
            jax.ShapeDtypeStruct((half + 4 * fan // 2 + 8, LANES), BF16),
            jax.ShapeDtypeStruct((w_msg.size // LANES + half + half + 4 * fan // 2 + 8, LANES), BF16),
            jax.ShapeDtypeStruct((SMALL, LANES), F32),
        ),
        scratch_shapes=[pltpu.VMEM((LANES, LANES), F32)],
        name="pack",
    )(
        atom_s.T,
        atom_pos,
        edge_vec,
        edge_nbr.reshape(-1, LANES),
        border_index.reshape(1, -1),
        send_index,
        jnp.transpose(w_msg, (0, 2, 3, 1)).reshape(-1, LANES),
        jnp.transpose(w_rad, (0, 2, 1, 3)).reshape(-1, half),
        w_probe,
        b_in,
        b_mix.reshape(1, -1),
        w_out.reshape(1, -1),
        probe_list,
        probe_count.reshape(1, -1),
    )


def merge_kernel(*refs):
    far = refs[-1]
    for shift in range(far.shape[0]):
        far[shift] = refs[shift][...]


def by_brick(own, far, put):
    bricks = far.shape[0] + 1
    brick = lax.axis_index("brick")
    put(brick, own)
    for shift in range(1, bricks):
        put(lax.rem(brick + bricks - shift, bricks), far[shift - 1])


def probe_grid(me, probes):
    number = me * probes + iota((1, probes), 1)
    return [(n % 16).astype(F32) * 0.25 - 1.875 for n in (number, number // 16, number // 256)]


def probe_kernel(
    sizes, list_at, own, own_beside, far, far_beside, small, chosen_rows, probe_basis, rest_rows
):
    groups, fan, rim, half, n_basis, cap, n_blocks = sizes
    width = 2 * half
    tiles = fan
    every = groups * LANES
    me = lax.axis_index("brick") * lax.axis_size("probe") + lax.axis_index("probe")
    rest_at = half + 4 * fan // 2
    small_rows = small[...]
    received = groups * cap
    edges = received * fan
    column = lax.axis_index("probe")
    rows = slice(rest_at, rest_at + 8)
    for place, (near, away) in ((column, (own, far)), (1 - column, (own_beside, far_beside))):

        def put(brick, value, place=place):
            rest_rows[2 * brick + place] = value.astype(F32)

        by_brick(near[rows, :], away[:, rows, :], put)
    rest = [rest_rows[g] for g in range(groups)]
    send_rows = jnp.concatenate([rows[4:5] for rows in rest], axis=0)

    def picks(lane_count, per_group):
        lane = iota((LANES, lane_count), 1)
        wanted = me * cap + lane % cap
        spread = dot(send_rows.astype(BF16), one_hot(iota((LANES, lane_count), 0) == wanted))
        lane = iota((groups, lane_count), 1)
        spread = jnp.where(lane // per_group == iota((groups, lane_count), 0), spread, 0.0)
        return jnp.sum(spread, axis=0, keepdims=True)

    per_group = fan * cap
    pick_atoms = picks(received, cap)
    column = iota((every, 1), 0)
    column_name = (column // LANES) * LANES + lane_atom(column % LANES, fan, tiles)
    wanted = (iota((1, received), 1) // cap) * LANES + pick_atoms.astype(jnp.int32)
    chosen_atoms = one_hot(column_name == wanted)

    pos_rows = jnp.concatenate(rest, axis=1).astype(BF16)
    pos = dot(pos_rows, chosen_atoms) - 1.875
    chosen_rows[0:1, :] = picks(edges, per_group)
    chosen_rows[1:2, 0:received] = pick_atoms
    chosen_rows[2:5, 0:received] = pos[0:3]
    pos_cols = jnp.concatenate(
        [
            jnp.concatenate([pos, jnp.zeros((8, LANES - received), F32)], axis=1),
            jnp.zeros((LANES - 8, LANES), F32),
        ],
        axis=0,
    ).T
    list_len = width
    counts = []
    for block in range(n_blocks):
        live = iota((1, list_len), 1).astype(F32) < small_rows[list_at + n_blocks : list_at + n_blocks + 1, block : block + 1]
        named = jnp.where(live, small_rows[list_at + block : list_at + block + 1], -1.0)
        hits = jnp.where(iota((received, list_len), 0).astype(F32) == named, 1.0, 0.0)
        counts.append(
            jnp.broadcast_to(jnp.sum(hits, axis=1, keepdims=True), (received, PB))
        )
    counts = jnp.concatenate(counts, axis=1)
    probes = n_blocks * PB
    grid = probe_grid(me, probes)
    dist_sq = jnp.zeros((received, probes), F32)
    for x in range(3):
        dist_sq = dist_sq + (grid[x] - pos_cols[0:received, x : x + 1]) ** 2
    dist = jnp.sqrt(dist_sq) * ROOT
    envelope = (1.0 - dist_sq / 64.0) ** 2 * counts
    probe_basis[...] = jnp.concatenate(
        [
            (bell(dist, r * (ROOT * 7.0 / (n_basis - 1))) * envelope).astype(BF16)
            for r in range(n_basis)
        ],
        axis=0,
    )


def density_kernel(
    sizes,
    own,
    own_beside,
    own_across,
    far,
    far_beside,
    far_other,
    far_across,
    weights_mine,
    weights_other,
    small,
    w_in,
    w_mix,
    chosen_rows,
    probe_basis,
    density,
    state0,
    own0,
    faces0,
    state1,
    weights,
    data_all,
):
    groups, fan, rim, half, n_basis, cap, n_blocks = sizes
    layers = w_in.shape[0]
    width = 2 * half
    tiles = LANES * fan // LANES
    root_fan = fan**0.5
    me = lax.axis_index("brick") * lax.axis_size("probe") + lax.axis_index("probe")
    part = lax.axis_index("chan")
    weight_rows = weights.shape[1]
    weights[part] = weights_mine[0:weight_rows, :]
    weights[1 - part] = weights_other[0:weight_rows, :]
    column = lax.axis_index("probe")
    own_other = weights_other[weight_rows:, :]
    for core, place, near, away in (
        (part, column, own[...], far),
        (part, 1 - column, own_beside[...], far_beside),
        (1 - part, column, own_other, far_other),
        (1 - part, 1 - column, own_across[...], far_across),
    ):

        def put(brick, value, core=core, place=place):
            data_all[core, place, brick] = value

        by_brick(near, away, put)
    every = groups * LANES
    edge_at = half
    n_edge = 4 * fan // 2
    rest_at = half + n_edge

    def data(group, c, rows):
        return data_all[c, group % 2, group // 2, rows, :]

    def weight(layer, p):
        at = (layer * 3 + p) * half
        return jnp.concatenate([weights[c, at : at + half, :] for c in range(2)], axis=0)

    def radial_weight(layer, p):
        at = (layer * 3 + p) * n_basis
        return radial_all[:, at : at + n_basis]

    def edge_rows(group):
        return [data(group, c, slice(edge_at, rest_at)).astype(F32) for c in range(2)]

    def border_of(group):
        return data(group, 0, slice(rest_at, rest_at + 8)).astype(F32)[3:4, 0 : 2 * rim]

    centers = iota((n_basis, 1), 0).astype(F32) * (ROOT * 6.0 / (n_basis - 1))

    def basis_of(length, env):
        return (bell(length * ROOT, centers) * env).astype(BF16)

    received = groups * cap
    edges = received * fan
    per_group = fan * cap
    pick_edges = chosen_rows[0:1, :]
    pick_atoms = chosen_rows[1:2, 0:received]
    pos = chosen_rows[2:5, 0:received]
    atom_rows = lane_atom(iota((LANES, per_group), 0), fan, tiles).astype(F32)
    chosen = []
    for group in range(groups):
        rows = jnp.concatenate([data(group, c, slice(edge_at, rest_at)) for c in range(2)], axis=0)
        want = pick_edges[:, group * per_group : (group + 1) * per_group]
        chosen.append(dot(rows, one_hot(atom_rows == want)))
    chosen = jnp.concatenate(chosen, axis=1)
    step = fan // 2
    row = iota((2 * n_edge, edges), 0)
    slot_k = (row // n_edge) * step + row % step
    lane_k = (iota((2 * n_edge, edges), 1) % per_group) // cap
    chosen = jnp.where(slot_k == lane_k, chosen, 0.0)
    chosen = jnp.sum(chosen.reshape(2 * 4, step, edges), axis=1)
    chosen = chosen[0:4] + chosen[4:8]
    pick_vec = [chosen[x : x + 1] for x in range(3)]
    nbr = chosen[3:4]
    length = jnp.sqrt(sum(x * x for x in pick_vec))
    basis1 = basis_of(length, (1.0 - length * length / 36.0) ** 2)

    nbr = nbr.astype(jnp.int32)
    home = iota((1, edges), 1) // per_group
    is_low = (nbr >= LANES) & (nbr < LANES + rim)
    is_up = nbr >= LANES + rim
    owner = jnp.where(
        is_low, (home + groups - 1) % groups, jnp.where(is_up, (home + 1) % groups, home)
    )
    entry = owner * 2 * rim + jnp.where(is_low, nbr - (LANES - rim), nbr - (LANES + rim))
    entry = jnp.where(is_low | is_up, entry, -1)
    border_all = jnp.concatenate(
        [border_of(g) for g in range(groups)], axis=1
    )
    border_all = jnp.broadcast_to(border_all, (16, groups * 2 * rim)).astype(BF16)
    seen = dot(border_all, one_hot(iota((groups * 2 * rim, edges), 0) == entry))[0:1]
    target_atom = jnp.where(entry < 0, nbr, seen.astype(jnp.int32))
    column = iota((every, 1), 0)
    column_name = (column // LANES) * LANES + lane_atom(column % LANES, fan, tiles)
    quad = groups // 2
    window = [[(h * quad + groups - 1 + i) % groups for i in range(quad + 2)] for h in range(2)]
    window_pick = []
    for h in range(2):
        lanes = slice(h * edges // 2, (h + 1) * edges // 2)
        near = lax.rem(owner[:, lanes] + 2 * groups - (h * quad + groups - 1), groups)
        name = near * LANES + target_atom[:, lanes]
        window_pick.append(one_hot(column_name[: (quad + 2) * LANES] == name))
    wanted = (iota((1, received), 1) // cap) * LANES + pick_atoms.astype(jnp.int32)
    chosen_atoms = one_hot(column_name == wanted)

    small_rows = small[...]
    columns = small_rows.T
    radial_at = weights.shape[1] - half
    radial_all = jnp.concatenate([weights[c, radial_at:, :] for c in range(2)], axis=0)

    terms_shape = (2 * n_basis, n_basis * received)
    probe_weight = radial_all[:, 3 * layers * n_basis :]
    w_scalar, w_vector = (
        dot(probe_weight, one_hot(iota(terms_shape, 1) // received * 2 + p == iota(terms_shape, 0)))
        for p in range(2)
    )

    probes = density.shape[1]
    grid = probe_grid(me, probes)

    for group in range(groups):
        for c in range(2):
            rows = slice(c * half, (c + 1) * half)
            state0[rows, group * LANES : (group + 1) * LANES] = data(group, c, slice(0, half))
    hidden = silu(dot_tn(w_in[0], state0[...]) + columns[:, 0:1]).astype(BF16)
    weight_ac = jnp.concatenate([weight(0, 0), weight(0, 2)], axis=0)
    messages = dot(weight_ac, hidden).astype(BF16)
    atom_col = lane_atom(iota((LANES, 2 * rim), 0), fan, tiles).astype(F32)
    for group in range(groups):
        own = messages[:, group * LANES : (group + 1) * LANES]
        own0[group] = own
        border_row = border_of(group)
        faces0[group, :, 0 : 2 * rim] = dot(own, one_hot(atom_col == border_row)).astype(BF16)

    row = iota((LANES + 2 * rim, 1), 0)
    names = jnp.where(
        row < LANES,
        lane_atom(row, fan, tiles),
        jnp.where(row < LANES + rim, row + rim, row - rim),
    ).astype(F32)
    names = jnp.broadcast_to(names, (LANES + 2 * rim, LANES)).astype(BF16)
    upper_lane = iota((2 * width, 2 * rim), 1) < rim
    radial_ac = jnp.concatenate([radial_weight(0, 0), radial_weight(0, 2)], axis=0)
    radial_rows = jnp.concatenate([jnp.zeros((2 * width, LANES + 2 * rim), BF16), radial_ac], axis=1)
    blank = jnp.zeros((2 * width, n_basis), BF16)

    for group in range(groups):
        up = (group + 1) % groups
        low = (group + groups - 1) % groups
        ghosts = jnp.where(
            upper_lane,
            faces0[up, :, 0 : 2 * rim].astype(F32),
            faces0[low, :, 0 : 2 * rim].astype(F32),
        ).astype(BF16)
        table = jnp.concatenate([own0[group], ghosts, blank], axis=1)
        left = jnp.concatenate(
            [
                block[at : at + 16]
                for at in range(0, 2 * width, 16)
                for block in (table, radial_rows)
            ],
            axis=0,
        )
        halves = edge_rows(group)
        step = fan // 2
        acc = jnp.zeros((width, LANES), F32)
        acc_vec = [jnp.zeros((width, LANES), F32) for _ in range(3)]
        for c in range(2):
            rows = halves[c]
            vec = [rows[x * step : (x + 1) * step] for x in range(3)]
            nbr = rows[3 * step : 4 * step]
            length_sq = vec[0] * vec[0] + vec[1] * vec[1] + vec[2] * vec[2]
            length = jnp.sqrt(length_sq)
            env = (1.0 - length * length / 36.0) ** 2
            for pair in range(step // 2):
                ks = (2 * pair, 2 * pair + 1)
                picked = jnp.concatenate([same(names, nbr[k : k + 1].astype(BF16)) for k in ks], axis=1)
                basis = jnp.concatenate(
                    [basis_of(length[k : k + 1], env[k : k + 1]) for k in ks], axis=1
                )
                both = dot(left, jnp.concatenate([picked, basis], axis=0))
                prod = jnp.concatenate(
                    [both[at : at + 16] * both[at + 16 : at + 32] for at in range(0, 4 * width, 32)],
                    axis=0,
                )
                for i, k in enumerate(ks):
                    block = prod[:, i * LANES : (i + 1) * LANES]
                    acc = acc + block[:width]
                    for x in range(3):
                        acc_vec[x] = acc_vec[x] + block[width:] * vec[x][k : k + 1]
        lanes = slice(group * LANES, (group + 1) * LANES)
        state1[0:width, lanes] = (state0[:, lanes].astype(F32) + acc / root_fan).astype(BF16)
        for x in range(3):
            state1[(x + 1) * width : (x + 2) * width, lanes] = (acc_vec[x] / root_fan).astype(BF16)

    rows = []
    for h in range(2):
        near_states = jnp.concatenate(
            [state1[:, g * LANES : (g + 1) * LANES] for g in window[h]], axis=1
        )
        rows.append(dot(near_states, window_pick[h]))
    rows = jnp.concatenate(rows, axis=1)
    hidden = silu(dot_tn(w_in[1], rows[:width].astype(BF16)) + columns[:, 1:2]).astype(BF16)
    weight_abc = jnp.concatenate([weight(1, p) for p in range(3)], axis=0)
    messages = dot(weight_abc, hidden).astype(BF16).astype(F32)
    radial_abc = jnp.concatenate([radial_weight(1, p) for p in range(3)], axis=0)
    filters = dot(radial_abc, basis1)
    weighted = messages * filters
    gate = weighted[width : 2 * width]
    along = weighted[2 * width :]
    parts = [weighted[:width]]
    for x in range(3):
        parts.append(rows[(1 + x) * width : (2 + x) * width] * gate + along * pick_vec[x])
    parts = jnp.concatenate(parts, axis=0).astype(BF16)
    edge = iota((edges, received), 0)
    slot = (edge // per_group) * cap + edge % cap
    delta = dot(parts, one_hot(slot == iota((edges, received), 1)))
    final = (dot(state1[...], chosen_atoms) + delta / root_fan).astype(BF16).astype(F32)

    along = final[width : 2 * width] * pos[0:1]
    for x in range(1, 3):
        along = along + final[(x + 1) * width : (x + 2) * width] * pos[x : x + 1]
    def repeat(value):
        return jnp.concatenate([value] * n_basis, axis=1)
    terms = [w_scalar * repeat(final[:width]) - w_vector * repeat(along)]
    for x in range(3):
        terms.append(w_vector * repeat(final[(x + 1) * width : (x + 2) * width]))
    sums = dot(jnp.concatenate(terms, axis=0).astype(BF16), probe_basis[...])
    charges = sums[:width]
    for x in range(3):
        charges = charges + grid[x] * sums[(x + 1) * width : (x + 2) * width]
    mixed = dot_tn(w_mix[...], charges.astype(BF16)) + columns[:, layers : layers + 1]
    density[...] = jnp.sum(silu(mixed) * columns[:, layers + 1 : layers + 2], axis=0, keepdims=True)


def few_groups(
    atom_s, atom_pos, edge_vec, edge_nbr, border_index, send_index, probe_list, probe_count,
    w_in, b_in, w_msg, w_rad, w_probe, w_mix, b_mix, w_out,
):
    atoms, half = atom_s.shape
    groups = lax.axis_size("brick") * lax.axis_size("probe")
    fan = edge_nbr.shape[0] // atoms
    rim = border_index.shape[0] // 2
    n_basis = w_rad.shape[1]
    cap = send_index.shape[1] // groups
    width = 2 * half
    every = groups * LANES
    data, weights, small = pack(
        atom_s, atom_pos, edge_vec, edge_nbr, border_index, send_index, w_msg, w_rad, w_probe,
        b_in, b_mix, w_out, probe_list, probe_count,
    )
    swap = [(0, 1), (1, 0)]
    bricks = lax.axis_size("brick")
    blocks = [
        lax.ppermute(data, "brick", [(i, (i + shift) % bricks) for i in range(bricks)])
        for shift in range(1, bricks)
    ]
    weights_other = lax.ppermute(weights, "chan", swap)
    own_beside = lax.ppermute(data, "probe", swap)
    own_across = lax.ppermute(own_beside, "chan", swap)
    far = pl.pallas_call(
        merge_kernel,
        out_shape=jax.ShapeDtypeStruct((bricks - 1,) + data.shape, BF16),
        in_specs=[pl.BlockSpec(memory_space=pltpu.VMEM)] * len(blocks)
        + [pl.BlockSpec(memory_space=pl.ANY)] * 3,
        compiler_params=pltpu.CompilerParams(vmem_limit_bytes=24 * 1024 * 1024),
        name="merge",
    )(*blocks, own_beside, own_across, weights_other)
    far_beside = lax.ppermute(far, "probe", swap)
    far_other = lax.ppermute(far, "chan", swap)
    far_across = lax.ppermute(far_beside, "chan", swap)
    n_probes = probe_list.shape[0] * PB
    sizes = (groups, fan, rim, half, n_basis, cap, probe_list.shape[0])
    chosen_rows, probe_basis = pl.pallas_call(
        functools.partial(probe_kernel, sizes, w_in.shape[0] + 2),
        out_shape=(
            jax.ShapeDtypeStruct((8, groups * cap * fan), F32),
            jax.ShapeDtypeStruct((n_basis * groups * cap, n_probes), BF16),
        ),
        compiler_params=pltpu.CompilerParams(vmem_limit_bytes=24 * 1024 * 1024),
        scratch_shapes=[pltpu.VMEM((groups, 8, LANES), F32)],
        name="probe_basis",
    )(data, own_beside, far, far_beside, small)
    density = pl.pallas_call(
        functools.partial(density_kernel, sizes),
        out_shape=jax.ShapeDtypeStruct((1, n_probes), F32),
        scratch_shapes=[
            pltpu.VMEM((width, every), BF16),
            pltpu.VMEM((groups, 2 * width, LANES), BF16),
            pltpu.VMEM((groups, 2 * width, LANES), BF16),
            pltpu.VMEM((4 * width, every), BF16),
            pltpu.VMEM((2, weights.shape[0] - data.shape[0], LANES), BF16),
            pltpu.VMEM((2, 2, bricks) + data.shape, BF16),
        ],
        compiler_params=pltpu.CompilerParams(vmem_limit_bytes=40 * 1024 * 1024),
        name="density",
    )(
        data, own_beside, own_across, far, far_beside, far_other, far_across, weights, weights_other,
        small, w_in, w_mix, chosen_rows, probe_basis)
    return density.reshape(n_probes)


def per_device(*args):
    columns = lax.axis_size("probe")
    if columns == 2 and lax.axis_size("brick") * columns == FEW_GROUPS:
        return few_groups(*args)
    return many_groups(*args)


def extended(block, sides, width):
    for axis, dim in sides:
        count = lax.axis_size(axis)
        forward = [(i, i + 1) for i in range(count - 1)]
        forward.append((count - 1, 0))
        backward = [(target, source) for source, target in forward]
        low = lax.ppermute(
            lax.slice_in_dim(block, block.shape[dim] - width, None, axis=dim), axis, forward
        )
        high = lax.ppermute(lax.slice_in_dim(block, 0, width, axis=dim), axis, backward)
        block = jnp.concatenate([low, block, high], axis=dim)
    return block


def radial(distance, count, top):
    centers = jnp.arange(count).astype(jnp.float32) * (top / (count - 1))
    return jnp.exp(-2.0 * (distance[..., None] - centers) ** 2)


def make_block(
    recv_rows, recv_pos, w_scalar, w_vector, feat_width, group_no, n_blocks, list_len, n_basis
):

    def probe_block(block_in):
        block_no, listed, live_count = block_in
        index_row = (group_no * n_blocks + block_no) * PB + jnp.arange(PB, dtype=jnp.int32)
        grid_xyz = (
            jnp.stack([index_row % 16, index_row // 16 % 16, index_row // 256 % 16], axis=1).astype(
                jnp.float32
            )
            * 0.25
        )
        atom_xyz = recv_pos[:, listed]
        disp = grid_xyz[:, :, None] - atom_xyz[None]
        dist_sq = jnp.sum(disp * disp, axis=1)
        live = (jnp.arange(list_len, dtype=jnp.int32) < live_count).astype(jnp.float32)
        envelope = (1.0 - dist_sq / 64.0) ** 2 * live[None, :]
        basis = radial(jnp.sqrt(dist_sq), n_basis, 7.0) * envelope[:, :, None]
        scalar_w = basis.astype(jnp.bfloat16).reshape(PB, list_len * n_basis)
        vector_w = (
            (disp[:, :, :, None] * basis[:, None])
            .astype(jnp.bfloat16)
            .reshape(PB, 3 * list_len * n_basis)
        )
        atom_rows = recv_rows[listed]
        atom_terms = (atom_rows[:, None, :feat_width] * w_scalar[None]).reshape(
            list_len * n_basis, feat_width
        )
        vec_rows = jnp.transpose(
            atom_rows[:, feat_width:].reshape(list_len, 3, feat_width), (1, 0, 2)
        )
        vector_terms = (vec_rows[:, :, None, :] * w_vector[None, None]).reshape(
            3 * list_len * n_basis, feat_width
        )
        charge = jnp.dot(scalar_w, atom_terms, preferred_element_type=jnp.float32) + jnp.dot(
            vector_w, vector_terms, preferred_element_type=jnp.float32
        )
        return charge.astype(jnp.bfloat16)

    return probe_block


def many_groups(
    atom_s,
    atom_pos,
    edge_vec,
    edge_nbr,
    border_index,
    send_index,
    probe_list,
    probe_count,
    w_in,
    b_in,
    w_msg,
    w_rad,
    w_probe,
    w_mix,
    b_mix,
    w_out,
):
    atom_count, half_width = atom_s.shape
    n_layers = w_in.shape[0]
    width = w_in.shape[1]
    n_basis = w_rad.shape[1]
    fan_out = edge_nbr.shape[0] // atom_count
    root_fan = fan_out**0.5
    rim_rows = border_index.shape[0] // 2
    length = jnp.sqrt(jnp.sum(edge_vec * edge_vec, axis=0))
    edge_env = (1.0 - length * length / 36.0) ** 2
    edge_basis = (radial(length, n_basis, 6.0) * edge_env[:, None]).astype(jnp.bfloat16)
    edge_cols = jnp.transpose(edge_vec)
    scalars = atom_s
    vectors = jnp.zeros((atom_count, 3 * half_width), jnp.bfloat16)
    for layer_no in range(n_layers):
        full_rows = lax.all_gather(scalars, "chan", axis=1, tiled=True)
        in_weight = w_in[layer_no]
        in_bias = b_in[layer_no]
        msg_weight = w_msg[layer_no].reshape(width, 3 * half_width)
        rad_weight = w_rad[layer_no].reshape(n_basis, 3 * half_width)
        hidden_act = jax.nn.silu(
            jnp.dot(full_rows, in_weight, preferred_element_type=jnp.float32) + in_bias
        ).astype(jnp.bfloat16)
        inner_tab = jnp.concatenate(
            [
                jnp.dot(hidden_act, msg_weight, preferred_element_type=jnp.float32).astype(
                    jnp.bfloat16
                ),
                vectors,
            ],
            axis=1,
        )
        padded = extended(inner_tab[border_index], ((("brick", "probe"), 0),), rim_rows)
        lookup = jnp.concatenate([inner_tab, padded[:rim_rows], padded[3 * rim_rows :]], axis=0)
        neighbour_rows = lookup[edge_nbr]
        filters = jnp.dot(edge_basis, rad_weight, preferred_element_type=jnp.float32)
        weighted = neighbour_rows[:, : 3 * half_width] * filters
        neighbour_vec = neighbour_rows[:, 3 * half_width :].reshape(-1, 3, half_width)
        vector_gate = weighted[:, None, half_width : 2 * half_width]
        along_edge = weighted[:, None, 2 * half_width :]
        delta_vec = neighbour_vec * vector_gate + along_edge * edge_cols[:, :, None]
        delta_scalar = (
            weighted[:, :half_width].reshape(atom_count, fan_out, half_width).sum(axis=1) / root_fan
        )
        delta_vec = delta_vec.reshape(atom_count, fan_out, 3 * half_width).sum(axis=1) / root_fan
        scalars = (scalars + delta_scalar).astype(jnp.bfloat16)
        vectors = (vectors + delta_vec).astype(jnp.bfloat16)
    features = jnp.concatenate([scalars, vectors], axis=1)
    picks = send_index[0]
    n_brick = lax.axis_size("brick")
    n_probe = lax.axis_size("probe")
    n_groups = n_brick * n_probe
    slot_cap = picks.shape[0] // n_groups
    out_rows = features[picks]
    out_pos = jnp.transpose(atom_pos)[picks].astype(jnp.bfloat16)
    received = (
        lax.all_to_all(
            out_rows.reshape(n_groups, slot_cap, 4 * half_width),
            ("brick", "probe"),
            split_axis=0,
            concat_axis=0,
            tiled=True,
        ),
        lax.all_to_all(
            out_pos.reshape(n_groups, slot_cap, 3),
            ("brick", "probe"),
            split_axis=0,
            concat_axis=0,
            tiled=True,
        ),
    )
    recv_count = n_groups * slot_cap
    recv_rows = received[0].reshape(recv_count, 4 * half_width)
    recv_pos = jnp.transpose(received[1].reshape(recv_count, 3)).astype(jnp.float32)
    group_no = lax.axis_index("brick") * n_probe + lax.axis_index("probe")
    n_blocks, list_len = probe_list.shape
    probe_block = make_block(
        recv_rows,
        recv_pos,
        w_probe[:, 0, :],
        w_probe[:, 1, :],
        half_width,
        group_no,
        n_blocks,
        list_len,
        n_basis,
    )
    charges = lax.map(
        probe_block, (jnp.arange(n_blocks, dtype=jnp.int32), probe_list, probe_count)
    ).reshape(n_blocks * PB, half_width)
    mix_rows = lax.dynamic_slice_in_dim(w_mix, lax.axis_index("chan") * half_width, half_width, 0)
    mixed = lax.psum(jnp.dot(charges, mix_rows, preferred_element_type=jnp.float32), "chan")
    return jnp.sum(jax.nn.silu(mixed + b_mix) * w_out, axis=1)


def solution(mesh):
    in_specs = (
        P(("image", "brick", "probe"), "chan"),
        P(None, ("image", "brick", "probe")),
        P(None, ("image", "brick", "probe")),
        P(("image", "brick", "probe")),
        P(("image", "brick", "probe")),
        P(("image", "brick", "probe"), None),
        P(("image", "brick", "probe"), None),
        P(("image", "brick", "probe")),
        P(),
        P(),
        P(None, None, None, "chan"),
        P(None, None, None, "chan"),
        P(None, None, "chan"),
        P(),
        P(),
        P(),
    )
    out_specs = P(("image", "brick", "probe"))
    return jax.shard_map(
        per_device, mesh=mesh, in_specs=in_specs, out_specs=out_specs, check_vma=False
    )
```

```python
import functools
import itertools
import math

import jax
import jax.numpy as jnp
from jax import lax
from jax.experimental import pallas as pl
from jax.experimental.pallas import tpu as pltpu
from jax.sharding import PartitionSpec as P

PB = 128
LANES = 128
FEW_GROUPS = 8
SMALL = 16
TOGETHER = 4
ROOT = (2.0 * math.log2(math.e)) ** 0.5
F32 = jnp.float32
BF16 = jnp.bfloat16


def iota(shape, dim):
    return lax.broadcasted_iota(jnp.int32, shape, dim)


def dot(a, b):
    return jnp.dot(a, b, preferred_element_type=F32)


def dot_tn(a, b):
    return lax.dot_general(a, b, (((0,), (0,)), ((), ())), preferred_element_type=F32)


def one_hot(mask):
    return jnp.where(mask, 1.0, 0.0).astype(BF16)


def same(names, row):
    return jnp.where(names == row, jnp.ones_like(names), jnp.zeros_like(names))


def silu(x):
    half_x = 0.5 * x
    return half_x * jnp.tanh(half_x) + half_x


def bell(scaled, center):
    away = scaled - center
    return jnp.exp2(-(away * away))


def place_of(group, groups):
    return (group % 2) * (groups // 2) + group // 2


def lane_atom(lane, fan, tiles):
    return (lane % tiles) * (LANES // fan) + lane // tiles


def length_keeping_round(exact):
    choices = []
    for value in exact:
        near = value.astype(BF16).astype(F32)
        step = jnp.where(value > near, 1.01 / 256.0, -1.01 / 256.0) * jnp.abs(near)
        choices.append((near, (near + step).astype(BF16).astype(F32)))
    target = sum(value * value for value in exact)
    best, best_error = None, None
    for picked in itertools.product(*choices):
        error = jnp.abs(sum(value * value for value in picked) - target)
        if best is None:
            best, best_error = picked, error
            continue
        better = error < best_error
        best = tuple(jnp.where(better, new, old) for new, old in zip(picked, best))
        best_error = jnp.where(better, error, best_error)
    return best


def pack_kernel(
    fan, atom_s, atom_pos, edge_vec, edge_nbr, border, send, w_msg, w_rad, w_probe,
    b_in, b_mix, w_out, probe_list, probe_count, data_out, weight_out, small_out, natural,
):
    half, atoms = atom_s.shape
    tiles = atoms * fan // LANES
    per_tile = LANES // fan
    part = lax.axis_index("chan")
    perm = one_hot(lane_atom(iota((atoms, LANES), 1), fan, tiles) == iota((atoms, LANES), 0))
    scalars = dot(atom_s[...], perm).astype(BF16)
    for tile in range(tiles):
        for comp in range(3):
            natural[comp * tiles + tile : comp * tiles + tile + 1, :] = edge_vec[
                comp : comp + 1, tile * LANES : (tile + 1) * LANES
            ]
    exact = [natural[comp * tiles : (comp + 1) * tiles, :] for comp in range(3)]
    for comp, value in enumerate(length_keeping_round(exact)):
        natural[comp * tiles : (comp + 1) * tiles, :] = value
    natural[3 * tiles : 4 * tiles, :] = edge_nbr[...].astype(F32)
    natural[4 * tiles :, :] = jnp.zeros((LANES - 4 * tiles, LANES), F32)
    turned = natural[...].T
    lane = iota((fan, LANES), 1)
    sorted_rows = []
    for comp in range(4):
        rows = jnp.zeros((fan, LANES), F32)
        for a in range(per_tile):
            piece = turned[a * fan : (a + 1) * fan, :]
            shift = (a * tiles - comp * tiles) % LANES
            piece = pltpu.roll(piece, shift, 1) if shift else piece
            rows = jnp.where(lane // tiles == a, piece, rows)
        sorted_rows.append(jnp.where(part == 0, rows[: fan // 2], rows[fan // 2 :]))
    pos = dot(atom_pos[...].astype(BF16), perm)
    blank = jnp.zeros((1, LANES), F32)
    border_row = jnp.concatenate(
        [border[...].astype(F32), jnp.zeros((1, LANES - border.shape[1]), F32)], axis=1
    )
    send_row = jnp.concatenate(
        [send[...].astype(F32), jnp.zeros((1, LANES - send.shape[1]), F32)], axis=1
    )
    rest = jnp.concatenate([pos, border_row, send_row, blank, blank, blank], axis=0)
    others = jnp.concatenate(sorted_rows + [rest], axis=0).astype(BF16)
    for group in range(data_out.shape[0]):
        data_out[group, 0:half, :] = scalars
        data_out[group, half:, :] = others
    at = 0
    for piece in (b_in, b_mix, w_out, probe_list, probe_count):
        rows, cols = piece.shape
        small_out[at : at + rows, 0:cols] = piece[...].astype(F32)
        at += rows
    probe_rows = [w_probe[r].astype(F32) for r in range(w_probe.shape[0])]
    radial = jnp.concatenate([w_rad[...].astype(F32)] + probe_rows, axis=0).T.astype(BF16)
    weight_out[: w_msg.shape[0], :] = w_msg[...]
    weight_out[w_msg.shape[0] :, :] = radial


def pack(
    groups, atom_s, atom_pos, edge_vec, edge_nbr, border_index, send_index, w_msg, w_rad, w_probe,
    b_in, b_mix, w_out, probe_list, probe_count,
):
    atoms, half = atom_s.shape
    fan = edge_nbr.shape[0] // atoms
    return pl.pallas_call(
        functools.partial(pack_kernel, fan),
        out_shape=(
            jax.ShapeDtypeStruct((groups, half + 4 * fan // 2 + 8, LANES), BF16),
            jax.ShapeDtypeStruct((w_msg.size // LANES + half, LANES), BF16),
            jax.ShapeDtypeStruct((SMALL, LANES), F32),
        ),
        scratch_shapes=[pltpu.VMEM((LANES, LANES), F32)],
        name="pack",
    )(
        atom_s.T,
        atom_pos,
        edge_vec,
        edge_nbr.reshape(-1, LANES),
        border_index.reshape(1, -1),
        send_index,
        jnp.transpose(w_msg, (0, 2, 3, 1)).reshape(-1, LANES),
        jnp.transpose(w_rad, (0, 2, 1, 3)).reshape(-1, half),
        w_probe,
        b_in,
        b_mix.reshape(1, -1),
        w_out.reshape(1, -1),
        probe_list,
        probe_count.reshape(1, -1),
    )


def probe_grid(me, probes):
    number = me * probes + iota((1, probes), 1)
    return [(n % 16).astype(F32) * 0.25 - 1.875 for n in (number, number // 16, number // 256)]


def probe_kernel(sizes, list_at, data_mine, small, chosen_rows, probe_basis):
    groups, fan, rim, half, n_basis, cap, n_blocks = sizes
    width = 2 * half
    tiles = fan
    every = groups * LANES
    me = lax.axis_index("brick") * lax.axis_size("probe") + lax.axis_index("probe")
    rest_at = half + 4 * fan // 2
    small_rows = small[...]
    received = groups * cap
    edges = received * fan
    send_rows = jnp.concatenate(
        [data_mine[place_of(g, groups), rest_at : rest_at + 8, :].astype(F32)[4:5] for g in range(groups)], axis=0
    )

    def picks(lane_count, per_group):
        lane = iota((LANES, lane_count), 1)
        wanted = me * cap + lane % cap
        spread = dot(send_rows.astype(BF16), one_hot(iota((LANES, lane_count), 0) == wanted))
        lane = iota((groups, lane_count), 1)
        spread = jnp.where(lane // per_group == iota((groups, lane_count), 0), spread, 0.0)
        return jnp.sum(spread, axis=0, keepdims=True)

    per_group = fan * cap
    pick_atoms = picks(received, cap)
    column = iota((every, 1), 0)
    column_name = (column // LANES) * LANES + lane_atom(column % LANES, fan, tiles)
    wanted = (iota((1, received), 1) // cap) * LANES + pick_atoms.astype(jnp.int32)
    chosen_atoms = one_hot(column_name == wanted)

    pos_rows = jnp.concatenate(
        [data_mine[place_of(g, groups), rest_at : rest_at + 8, :] for g in range(groups)], axis=1
    )
    pos = dot(pos_rows, chosen_atoms) - 1.875
    chosen_rows[0:1, :] = picks(edges, per_group)
    chosen_rows[1:2, 0:received] = pick_atoms
    chosen_rows[2:5, 0:received] = pos[0:3]
    pos_cols = jnp.concatenate(
        [
            jnp.concatenate([pos, jnp.zeros((8, LANES - received), F32)], axis=1),
            jnp.zeros((LANES - 8, LANES), F32),
        ],
        axis=0,
    ).T
    list_len = width
    counts = []
    for block in range(n_blocks):
        live = iota((1, list_len), 1).astype(F32) < small_rows[list_at + n_blocks : list_at + n_blocks + 1, block : block + 1]
        named = jnp.where(live, small_rows[list_at + block : list_at + block + 1], -1.0)
        hits = jnp.where(iota((received, list_len), 0).astype(F32) == named, 1.0, 0.0)
        counts.append(
            jnp.broadcast_to(jnp.sum(hits, axis=1, keepdims=True), (received, PB))
        )
    counts = jnp.concatenate(counts, axis=1)
    probes = n_blocks * PB
    grid = probe_grid(me, probes)
    dist_sq = jnp.zeros((received, probes), F32)
    for x in range(3):
        dist_sq = dist_sq + (grid[x] - pos_cols[0:received, x : x + 1]) ** 2
    dist = jnp.sqrt(dist_sq) * ROOT
    envelope = (1.0 - dist_sq / 64.0) ** 2 * counts
    probe_basis[...] = jnp.concatenate(
        [
            (bell(dist, r * (ROOT * 7.0 / (n_basis - 1))) * envelope).astype(BF16)
            for r in range(n_basis)
        ],
        axis=0,
    )


def density_kernel(
    sizes,
    data_mine,
    data_other,
    weights_mine,
    weights_other,
    small,
    w_in,
    w_mix,
    chosen_rows,
    probe_basis,
    density,
    state0,
    own0,
    faces0,
    state1,
    weights,
):
    groups, fan, rim, half, n_basis, cap, n_blocks = sizes
    layers = w_in.shape[0]
    width = 2 * half
    tiles = LANES * fan // LANES
    root_fan = fan**0.5
    me = lax.axis_index("brick") * lax.axis_size("probe") + lax.axis_index("probe")
    part = lax.axis_index("chan")
    weights[part] = weights_mine[...]
    weights[1 - part] = weights_other[...]
    every = groups * LANES
    edge_at = half
    n_edge = 4 * fan // 2
    rest_at = half + n_edge

    def data(group, c, rows):
        return (data_mine, data_other)[c][place_of(group, groups), rows, :]

    def weight(layer, p):
        at = (layer * 3 + p) * half
        return jnp.concatenate([weights[c, at : at + half, :] for c in range(2)], axis=0)

    def radial_weight(layer, p):
        at = (layer * 3 + p) * n_basis
        return radial_all[:, at : at + n_basis]

    def edge_rows(group):
        return [data(group, c, slice(edge_at, rest_at)).astype(F32) for c in range(2)]

    def border_of(group):
        return data(group, 0, slice(rest_at, rest_at + 8)).astype(F32)[3:4, 0 : 2 * rim]

    centers = iota((n_basis, 1), 0).astype(F32) * (ROOT * 6.0 / (n_basis - 1))

    def basis_of(length, env):
        return (bell(length * ROOT, centers) * env).astype(BF16)

    received = groups * cap
    edges = received * fan
    per_group = fan * cap
    pick_edges = chosen_rows[0:1, :]
    pick_atoms = chosen_rows[1:2, 0:received]
    pos = chosen_rows[2:5, 0:received]
    atom_rows = lane_atom(iota((LANES, per_group), 0), fan, tiles).astype(F32)
    chosen = []
    for group in range(groups):
        rows = jnp.concatenate([data(group, c, slice(edge_at, rest_at)) for c in range(2)], axis=0)
        want = pick_edges[:, group * per_group : (group + 1) * per_group]
        chosen.append(dot(rows, one_hot(atom_rows == want)))
    chosen = jnp.concatenate(chosen, axis=1)
    step = fan // 2
    row = iota((2 * n_edge, edges), 0)
    slot_k = (row // n_edge) * step + row % step
    lane_k = (iota((2 * n_edge, edges), 1) % per_group) // cap
    chosen = jnp.where(slot_k == lane_k, chosen, 0.0)
    chosen = jnp.sum(chosen.reshape(2 * 4, step, edges), axis=1)
    chosen = chosen[0:4] + chosen[4:8]
    pick_vec = [chosen[x : x + 1] for x in range(3)]
    nbr = chosen[3:4]
    length = jnp.sqrt(sum(x * x for x in pick_vec))
    basis1 = basis_of(length, (1.0 - length * length / 36.0) ** 2)

    nbr = nbr.astype(jnp.int32)
    home = iota((1, edges), 1) // per_group
    is_low = (nbr >= LANES) & (nbr < LANES + rim)
    is_up = nbr >= LANES + rim
    owner = jnp.where(
        is_low, (home + groups - 1) % groups, jnp.where(is_up, (home + 1) % groups, home)
    )
    entry = owner * 2 * rim + jnp.where(is_low, nbr - (LANES - rim), nbr - (LANES + rim))
    entry = jnp.where(is_low | is_up, entry, -1)
    border_all = jnp.concatenate(
        [border_of(g) for g in range(groups)], axis=1
    )
    border_all = jnp.broadcast_to(border_all, (16, groups * 2 * rim)).astype(BF16)
    seen = dot(border_all, one_hot(iota((groups * 2 * rim, edges), 0) == entry))[0:1]
    target_atom = jnp.where(entry < 0, nbr, seen.astype(jnp.int32))
    column = iota((every, 1), 0)
    column_name = (column // LANES) * LANES + lane_atom(column % LANES, fan, tiles)
    quad = groups // 2
    window = [[(h * quad + groups - 1 + i) % groups for i in range(quad + 2)] for h in range(2)]
    window_pick = []
    for h in range(2):
        lanes = slice(h * edges // 2, (h + 1) * edges // 2)
        near = lax.rem(owner[:, lanes] + 2 * groups - (h * quad + groups - 1), groups)
        name = near * LANES + target_atom[:, lanes]
        window_pick.append(one_hot(column_name[: (quad + 2) * LANES] == name))
    wanted = (iota((1, received), 1) // cap) * LANES + pick_atoms.astype(jnp.int32)
    chosen_atoms = one_hot(column_name == wanted)

    small_rows = small[...]
    columns = small_rows.T
    radial_at = weights.shape[1] - half
    radial_all = jnp.concatenate([weights[c, radial_at:, :] for c in range(2)], axis=0)

    terms_shape = (2 * n_basis, n_basis * received)
    probe_weight = radial_all[:, 3 * layers * n_basis :]
    w_scalar, w_vector = (
        dot(probe_weight, one_hot(iota(terms_shape, 1) // received * 2 + p == iota(terms_shape, 0)))
        for p in range(2)
    )

    probes = density.shape[1]
    grid = probe_grid(me, probes)

    for group in range(groups):
        for c in range(2):
            place = part if c == 0 else 1 - part
            rows = pl.ds(pl.multiple_of(place * half, half), half)
            state0[rows, group * LANES : (group + 1) * LANES] = data(group, c, slice(0, half))
    hidden = silu(dot_tn(w_in[0], state0[...]) + columns[:, 0:1]).astype(BF16)
    weight_ac = jnp.concatenate([weight(0, 0), weight(0, 2)], axis=0)
    messages = dot(weight_ac, hidden).astype(BF16)
    atom_col = lane_atom(iota((LANES, 2 * rim), 0), fan, tiles).astype(F32)
    for group in range(groups):
        own = messages[:, group * LANES : (group + 1) * LANES]
        own0[group] = own
        border_row = border_of(group)
        faces0[group, :, 0 : 2 * rim] = dot(own, one_hot(atom_col == border_row)).astype(BF16)

    row = iota((LANES + 2 * rim, 1), 0)
    names = jnp.where(
        row < LANES,
        lane_atom(row, fan, tiles),
        jnp.where(row < LANES + rim, row + rim, row - rim),
    ).astype(F32)
    names = jnp.broadcast_to(names, (LANES + 2 * rim, LANES)).astype(BF16)
    upper_lane = iota((2 * width, 2 * rim), 1) < rim
    radial_ac = jnp.concatenate([radial_weight(0, 0), radial_weight(0, 2)], axis=0)
    radial_rows = jnp.concatenate([jnp.zeros((2 * width, LANES + 2 * rim), BF16), radial_ac], axis=1)
    blank = jnp.zeros((2 * width, n_basis), BF16)

    for group in range(groups):
        up = (group + 1) % groups
        low = (group + groups - 1) % groups
        ghosts = jnp.where(
            upper_lane,
            faces0[up, :, 0 : 2 * rim].astype(F32),
            faces0[low, :, 0 : 2 * rim].astype(F32),
        ).astype(BF16)
        table = jnp.concatenate([own0[group], ghosts, blank], axis=1)
        left = jnp.concatenate(
            [
                block[at : at + 16]
                for at in range(0, 2 * width, 16)
                for block in (table, radial_rows)
            ],
            axis=0,
        )
        halves = edge_rows(group)
        step = fan // 2
        acc = jnp.zeros((width, LANES), F32)
        acc_vec = [jnp.zeros((width, LANES), F32) for _ in range(3)]
        for c in range(2):
            rows = halves[c]
            vec = [rows[x * step : (x + 1) * step] for x in range(3)]
            nbr = rows[3 * step : 4 * step]
            length_sq = vec[0] * vec[0] + vec[1] * vec[1] + vec[2] * vec[2]
            length = jnp.sqrt(length_sq)
            env = (1.0 - length * length / 36.0) ** 2
            for first in range(0, step, TOGETHER):
                ks = range(first, first + TOGETHER)
                picked = jnp.concatenate([same(names, nbr[k : k + 1].astype(BF16)) for k in ks], axis=1)
                basis = jnp.concatenate(
                    [basis_of(length[k : k + 1], env[k : k + 1]) for k in ks], axis=1
                )
                both = dot(left, jnp.concatenate([picked, basis], axis=0))
                prod = jnp.concatenate(
                    [both[at : at + 16] * both[at + 16 : at + 32] for at in range(0, 4 * width, 32)],
                    axis=0,
                )
                for i, k in enumerate(ks):
                    block = prod[:, i * LANES : (i + 1) * LANES]
                    acc = acc + block[:width]
                    for x in range(3):
                        acc_vec[x] = acc_vec[x] + block[width:] * vec[x][k : k + 1]
        lanes = slice(group * LANES, (group + 1) * LANES)
        state1[0:width, lanes] = (state0[:, lanes].astype(F32) + acc / root_fan).astype(BF16)
        for x in range(3):
            state1[(x + 1) * width : (x + 2) * width, lanes] = (acc_vec[x] / root_fan).astype(BF16)

    rows = []
    for h in range(2):
        near_states = jnp.concatenate(
            [state1[:, g * LANES : (g + 1) * LANES] for g in window[h]], axis=1
        )
        rows.append(dot(near_states, window_pick[h]))
    rows = jnp.concatenate(rows, axis=1)
    hidden = silu(dot_tn(w_in[1], rows[:width].astype(BF16)) + columns[:, 1:2]).astype(BF16)
    weight_abc = jnp.concatenate([weight(1, p) for p in range(3)], axis=0)
    messages = dot(weight_abc, hidden).astype(BF16).astype(F32)
    radial_abc = jnp.concatenate([radial_weight(1, p) for p in range(3)], axis=0)
    filters = dot(radial_abc, basis1)
    weighted = messages * filters
    gate = weighted[width : 2 * width]
    along = weighted[2 * width :]
    parts = [weighted[:width]]
    for x in range(3):
        parts.append(rows[(1 + x) * width : (2 + x) * width] * gate + along * pick_vec[x])
    parts = jnp.concatenate(parts, axis=0).astype(BF16)
    edge = iota((edges, received), 0)
    slot = (edge // per_group) * cap + edge % cap
    delta = dot(parts, one_hot(slot == iota((edges, received), 1)))
    final = (dot(state1[...], chosen_atoms) + delta / root_fan).astype(BF16).astype(F32)

    along = final[width : 2 * width] * pos[0:1]
    for x in range(1, 3):
        along = along + final[(x + 1) * width : (x + 2) * width] * pos[x : x + 1]
    def repeat(value):
        return jnp.concatenate([value] * n_basis, axis=1)
    terms = [w_scalar * repeat(final[:width]) - w_vector * repeat(along)]
    for x in range(3):
        terms.append(w_vector * repeat(final[(x + 1) * width : (x + 2) * width]))
    sums = dot(jnp.concatenate(terms, axis=0).astype(BF16), probe_basis[...])
    charges = sums[:width]
    for x in range(3):
        charges = charges + grid[x] * sums[(x + 1) * width : (x + 2) * width]
    mixed = dot_tn(w_mix[...], charges.astype(BF16)) + columns[:, layers : layers + 1]
    density[...] = jnp.sum(silu(mixed) * columns[:, layers + 1 : layers + 2], axis=0, keepdims=True)


def few_groups(
    atom_s, atom_pos, edge_vec, edge_nbr, border_index, send_index, probe_list, probe_count,
    w_in, b_in, w_msg, w_rad, w_probe, w_mix, b_mix, w_out,
):
    atoms, half = atom_s.shape
    groups = lax.axis_size("brick") * lax.axis_size("probe")
    fan = edge_nbr.shape[0] // atoms
    rim = border_index.shape[0] // 2
    n_basis = w_rad.shape[1]
    cap = send_index.shape[1] // groups
    width = 2 * half
    every = groups * LANES
    data, weights, small = pack(
        groups, atom_s, atom_pos, edge_vec, edge_nbr, border_index, send_index, w_msg, w_rad, w_probe,
        b_in, b_mix, w_out, probe_list, probe_count,
    )
    swap = [(0, 1), (1, 0)]
    weights_other = lax.ppermute(weights, "chan", swap)
    mine = lax.all_to_all(data, ("probe", "brick"), split_axis=0, concat_axis=0, tiled=True)
    other = lax.ppermute(mine, "chan", swap)
    n_probes = probe_list.shape[0] * PB
    sizes = (groups, fan, rim, half, n_basis, cap, probe_list.shape[0])
    chosen_rows, probe_basis = pl.pallas_call(
        functools.partial(probe_kernel, sizes, w_in.shape[0] + 2),
        out_shape=(
            jax.ShapeDtypeStruct((8, groups * cap * fan), F32),
            jax.ShapeDtypeStruct((n_basis * groups * cap, n_probes), BF16),
        ),
        compiler_params=pltpu.CompilerParams(vmem_limit_bytes=24 * 1024 * 1024),
        name="probe_basis",
    )(mine, small)
    density = pl.pallas_call(
        functools.partial(density_kernel, sizes),
        out_shape=jax.ShapeDtypeStruct((1, n_probes), F32),
        scratch_shapes=[
            pltpu.VMEM((width, every), BF16),
            pltpu.VMEM((groups, 2 * width, LANES), BF16),
            pltpu.VMEM((groups, 2 * width, LANES), BF16),
            pltpu.VMEM((4 * width, every), BF16),
            pltpu.VMEM((2,) + weights.shape, BF16),
        ],
        compiler_params=pltpu.CompilerParams(vmem_limit_bytes=40 * 1024 * 1024),
        name="density",
    )(mine, other, weights, weights_other, small, w_in, w_mix, chosen_rows, probe_basis)
    return density.reshape(n_probes)


def per_device(*args):
    columns = lax.axis_size("probe")
    if columns == 2 and lax.axis_size("brick") * columns == FEW_GROUPS:
        return few_groups(*args)
    return many_groups(*args)


def extended(block, sides, width):
    for axis, dim in sides:
        count = lax.axis_size(axis)
        forward = [(i, i + 1) for i in range(count - 1)]
        forward.append((count - 1, 0))
        backward = [(target, source) for source, target in forward]
        low = lax.ppermute(
            lax.slice_in_dim(block, block.shape[dim] - width, None, axis=dim), axis, forward
        )
        high = lax.ppermute(lax.slice_in_dim(block, 0, width, axis=dim), axis, backward)
        block = jnp.concatenate([low, block, high], axis=dim)
    return block


def radial(distance, count, top):
    centers = jnp.arange(count).astype(jnp.float32) * (top / (count - 1))
    return jnp.exp(-2.0 * (distance[..., None] - centers) ** 2)


def make_block(
    recv_rows, recv_pos, w_scalar, w_vector, feat_width, group_no, n_blocks, list_len, n_basis
):

    def probe_block(block_in):
        block_no, listed, live_count = block_in
        index_row = (group_no * n_blocks + block_no) * PB + jnp.arange(PB, dtype=jnp.int32)
        grid_xyz = (
            jnp.stack([index_row % 16, index_row // 16 % 16, index_row // 256 % 16], axis=1).astype(
                jnp.float32
            )
            * 0.25
        )
        atom_xyz = recv_pos[:, listed]
        disp = grid_xyz[:, :, None] - atom_xyz[None]
        dist_sq = jnp.sum(disp * disp, axis=1)
        live = (jnp.arange(list_len, dtype=jnp.int32) < live_count).astype(jnp.float32)
        envelope = (1.0 - dist_sq / 64.0) ** 2 * live[None, :]
        basis = radial(jnp.sqrt(dist_sq), n_basis, 7.0) * envelope[:, :, None]
        scalar_w = basis.astype(jnp.bfloat16).reshape(PB, list_len * n_basis)
        vector_w = (
            (disp[:, :, :, None] * basis[:, None])
            .astype(jnp.bfloat16)
            .reshape(PB, 3 * list_len * n_basis)
        )
        atom_rows = recv_rows[listed]
        atom_terms = (atom_rows[:, None, :feat_width] * w_scalar[None]).reshape(
            list_len * n_basis, feat_width
        )
        vec_rows = jnp.transpose(
            atom_rows[:, feat_width:].reshape(list_len, 3, feat_width), (1, 0, 2)
        )
        vector_terms = (vec_rows[:, :, None, :] * w_vector[None, None]).reshape(
            3 * list_len * n_basis, feat_width
        )
        charge = jnp.dot(scalar_w, atom_terms, preferred_element_type=jnp.float32) + jnp.dot(
            vector_w, vector_terms, preferred_element_type=jnp.float32
        )
        return charge.astype(jnp.bfloat16)

    return probe_block


def many_groups(
    atom_s,
    atom_pos,
    edge_vec,
    edge_nbr,
    border_index,
    send_index,
    probe_list,
    probe_count,
    w_in,
    b_in,
    w_msg,
    w_rad,
    w_probe,
    w_mix,
    b_mix,
    w_out,
):
    atom_count, half_width = atom_s.shape
    n_layers = w_in.shape[0]
    width = w_in.shape[1]
    n_basis = w_rad.shape[1]
    fan_out = edge_nbr.shape[0] // atom_count
    root_fan = fan_out**0.5
    rim_rows = border_index.shape[0] // 2
    length = jnp.sqrt(jnp.sum(edge_vec * edge_vec, axis=0))
    edge_env = (1.0 - length * length / 36.0) ** 2
    edge_basis = (radial(length, n_basis, 6.0) * edge_env[:, None]).astype(jnp.bfloat16)
    edge_cols = jnp.transpose(edge_vec)
    scalars = atom_s
    vectors = jnp.zeros((atom_count, 3 * half_width), jnp.bfloat16)
    for layer_no in range(n_layers):
        full_rows = lax.all_gather(scalars, "chan", axis=1, tiled=True)
        in_weight = w_in[layer_no]
        in_bias = b_in[layer_no]
        msg_weight = w_msg[layer_no].reshape(width, 3 * half_width)
        rad_weight = w_rad[layer_no].reshape(n_basis, 3 * half_width)
        hidden_act = jax.nn.silu(
            jnp.dot(full_rows, in_weight, preferred_element_type=jnp.float32) + in_bias
        ).astype(jnp.bfloat16)
        inner_tab = jnp.concatenate(
            [
                jnp.dot(hidden_act, msg_weight, preferred_element_type=jnp.float32).astype(
                    jnp.bfloat16
                ),
                vectors,
            ],
            axis=1,
        )
        padded = extended(inner_tab[border_index], ((("brick", "probe"), 0),), rim_rows)
        lookup = jnp.concatenate([inner_tab, padded[:rim_rows], padded[3 * rim_rows :]], axis=0)
        neighbour_rows = lookup[edge_nbr]
        filters = jnp.dot(edge_basis, rad_weight, preferred_element_type=jnp.float32)
        weighted = neighbour_rows[:, : 3 * half_width] * filters
        neighbour_vec = neighbour_rows[:, 3 * half_width :].reshape(-1, 3, half_width)
        vector_gate = weighted[:, None, half_width : 2 * half_width]
        along_edge = weighted[:, None, 2 * half_width :]
        delta_vec = neighbour_vec * vector_gate + along_edge * edge_cols[:, :, None]
        delta_scalar = (
            weighted[:, :half_width].reshape(atom_count, fan_out, half_width).sum(axis=1) / root_fan
        )
        delta_vec = delta_vec.reshape(atom_count, fan_out, 3 * half_width).sum(axis=1) / root_fan
        scalars = (scalars + delta_scalar).astype(jnp.bfloat16)
        vectors = (vectors + delta_vec).astype(jnp.bfloat16)
    features = jnp.concatenate([scalars, vectors], axis=1)
    picks = send_index[0]
    n_brick = lax.axis_size("brick")
    n_probe = lax.axis_size("probe")
    n_groups = n_brick * n_probe
    slot_cap = picks.shape[0] // n_groups
    out_rows = features[picks]
    out_pos = jnp.transpose(atom_pos)[picks].astype(jnp.bfloat16)
    received = (
        lax.all_to_all(
            out_rows.reshape(n_groups, slot_cap, 4 * half_width),
            ("brick", "probe"),
            split_axis=0,
            concat_axis=0,
            tiled=True,
        ),
        lax.all_to_all(
            out_pos.reshape(n_groups, slot_cap, 3),
            ("brick", "probe"),
            split_axis=0,
            concat_axis=0,
            tiled=True,
        ),
    )
    recv_count = n_groups * slot_cap
    recv_rows = received[0].reshape(recv_count, 4 * half_width)
    recv_pos = jnp.transpose(received[1].reshape(recv_count, 3)).astype(jnp.float32)
    group_no = lax.axis_index("brick") * n_probe + lax.axis_index("probe")
    n_blocks, list_len = probe_list.shape
    probe_block = make_block(
        recv_rows,
        recv_pos,
        w_probe[:, 0, :],
        w_probe[:, 1, :],
        half_width,
        group_no,
        n_blocks,
        list_len,
        n_basis,
    )
    charges = lax.map(
        probe_block, (jnp.arange(n_blocks, dtype=jnp.int32), probe_list, probe_count)
    ).reshape(n_blocks * PB, half_width)
    mix_rows = lax.dynamic_slice_in_dim(w_mix, lax.axis_index("chan") * half_width, half_width, 0)
    mixed = lax.psum(jnp.dot(charges, mix_rows, preferred_element_type=jnp.float32), "chan")
    return jnp.sum(jax.nn.silu(mixed + b_mix) * w_out, axis=1)


def solution(mesh):
    in_specs = (
        P(("image", "brick", "probe"), "chan"),
        P(None, ("image", "brick", "probe")),
        P(None, ("image", "brick", "probe")),
        P(("image", "brick", "probe")),
        P(("image", "brick", "probe")),
        P(("image", "brick", "probe"), None),
        P(("image", "brick", "probe"), None),
        P(("image", "brick", "probe")),
        P(),
        P(),
        P(None, None, None, "chan"),
        P(None, None, None, "chan"),
        P(None, None, "chan"),
        P(),
        P(),
        P(),
    )
    out_specs = P(("image", "brick", "probe"))
    return jax.shard_map(
        per_device, mesh=mesh, in_specs=in_specs, out_specs=out_specs, check_vma=False
    )
```

```python
import functools
import itertools
import math

import jax
import jax.numpy as jnp
from jax import lax
from jax.experimental import pallas as pl
from jax.experimental.pallas import tpu as pltpu
from jax.sharding import PartitionSpec as P

PB = 128
LANES = 128
FEW_GROUPS = 8
SMALL = 16
TOGETHER = 4
ROOT = (2.0 * math.log2(math.e)) ** 0.5
F32 = jnp.float32
BF16 = jnp.bfloat16


def iota(shape, dim):
    return lax.broadcasted_iota(jnp.int32, shape, dim)


def dot(a, b):
    return jnp.dot(a, b, preferred_element_type=F32)


def dot_tn(a, b):
    return lax.dot_general(a, b, (((0,), (0,)), ((), ())), preferred_element_type=F32)


def one_hot(mask):
    return jnp.where(mask, 1.0, 0.0).astype(BF16)


def same(names, row):
    return jnp.where(names == row, jnp.ones_like(names), jnp.zeros_like(names))


def silu(x):
    half_x = 0.5 * x
    return half_x * jnp.tanh(half_x) + half_x


def bell(scaled, center):
    away = scaled - center
    return jnp.exp2(-(away * away))


def lane_atom(lane, fan, tiles):
    return (lane % tiles) * (LANES // fan) + lane // tiles


def length_keeping_round(exact):
    choices = []
    for value in exact:
        near = value.astype(BF16).astype(F32)
        step = jnp.where(value > near, 1.01 / 256.0, -1.01 / 256.0) * jnp.abs(near)
        choices.append((near, (near + step).astype(BF16).astype(F32)))
    target = sum(value * value for value in exact)
    best, best_error = None, None
    for picked in itertools.product(*choices):
        error = jnp.abs(sum(value * value for value in picked) - target)
        if best is None:
            best, best_error = picked, error
            continue
        better = error < best_error
        best = tuple(jnp.where(better, new, old) for new, old in zip(picked, best))
        best_error = jnp.where(better, error, best_error)
    return best


def pack_kernel(
    fan, atom_s, atom_pos, edge_vec, edge_nbr, border, send, w_msg, w_rad, w_probe,
    b_in, b_mix, w_out, probe_list, probe_count, data_out, weight_out, small_out, natural,
):
    half, atoms = atom_s.shape
    tiles = atoms * fan // LANES
    per_tile = LANES // fan
    part = lax.axis_index("chan")
    perm = one_hot(lane_atom(iota((atoms, LANES), 1), fan, tiles) == iota((atoms, LANES), 0))
    scalars = dot(atom_s[...], perm).astype(BF16)
    for tile in range(tiles):
        for comp in range(3):
            natural[comp * tiles + tile : comp * tiles + tile + 1, :] = edge_vec[
                comp : comp + 1, tile * LANES : (tile + 1) * LANES
            ]
    exact = [natural[comp * tiles : (comp + 1) * tiles, :] for comp in range(3)]
    for comp, value in enumerate(length_keeping_round(exact)):
        natural[comp * tiles : (comp + 1) * tiles, :] = value
    natural[3 * tiles : 4 * tiles, :] = edge_nbr[...].astype(F32)
    natural[4 * tiles :, :] = jnp.zeros((LANES - 4 * tiles, LANES), F32)
    turned = natural[...].T
    lane = iota((fan, LANES), 1)
    sorted_rows = []
    for comp in range(4):
        rows = jnp.zeros((fan, LANES), F32)
        for a in range(per_tile):
            piece = turned[a * fan : (a + 1) * fan, :]
            shift = (a * tiles - comp * tiles) % LANES
            piece = pltpu.roll(piece, shift, 1) if shift else piece
            rows = jnp.where(lane // tiles == a, piece, rows)
        sorted_rows.append(jnp.where(part == 0, rows[: fan // 2], rows[fan // 2 :]))
    pos = dot(atom_pos[...].astype(BF16), perm)
    blank = jnp.zeros((1, LANES), F32)
    border_row = jnp.concatenate(
        [border[...].astype(F32), jnp.zeros((1, LANES - border.shape[1]), F32)], axis=1
    )
    send_row = jnp.concatenate(
        [send[...].astype(F32), jnp.zeros((1, LANES - send.shape[1]), F32)], axis=1
    )
    rest = jnp.concatenate([pos, border_row, send_row, blank, blank, blank], axis=0)
    others = jnp.concatenate(sorted_rows + [rest], axis=0).astype(BF16)
    for group in range(data_out.shape[0]):
        data_out[group, 0:half, :] = scalars
        data_out[group, half:, :] = others
    at = 0
    for piece in (b_in, b_mix, w_out, probe_list, probe_count):
        rows, cols = piece.shape
        small_out[at : at + rows, 0:cols] = piece[...].astype(F32)
        at += rows
    probe_rows = [w_probe[r].astype(F32) for r in range(w_probe.shape[0])]
    radial = jnp.concatenate([w_rad[...].astype(F32)] + probe_rows, axis=0).T.astype(BF16)
    weight_out[: w_msg.shape[0], :] = w_msg[...]
    weight_out[w_msg.shape[0] :, :] = radial


def pack(
    groups, atom_s, atom_pos, edge_vec, edge_nbr, border_index, send_index, w_msg, w_rad, w_probe,
    b_in, b_mix, w_out, probe_list, probe_count,
):
    atoms, half = atom_s.shape
    fan = edge_nbr.shape[0] // atoms
    return pl.pallas_call(
        functools.partial(pack_kernel, fan),
        out_shape=(
            jax.ShapeDtypeStruct((groups, half + 4 * fan // 2 + 8, LANES), BF16),
            jax.ShapeDtypeStruct((w_msg.size // LANES + half, LANES), BF16),
            jax.ShapeDtypeStruct((SMALL, LANES), F32),
        ),
        scratch_shapes=[pltpu.VMEM((LANES, LANES), F32)],
        name="pack",
    )(
        atom_s.T,
        atom_pos,
        edge_vec,
        edge_nbr.reshape(-1, LANES),
        border_index.reshape(1, -1),
        send_index,
        jnp.transpose(w_msg, (0, 2, 3, 1)).reshape(-1, LANES),
        jnp.transpose(w_rad, (0, 2, 1, 3)).reshape(-1, half),
        w_probe,
        b_in,
        b_mix.reshape(1, -1),
        w_out.reshape(1, -1),
        probe_list,
        probe_count.reshape(1, -1),
    )


def after_kernel(block, there, same_block):
    pass


def probe_grid(me, probes):
    number = me * probes + iota((1, probes), 1)
    return [(n % 16).astype(F32) * 0.25 - 1.875 for n in (number, number // 16, number // 256)]


def probe_kernel(sizes, list_at, data_mine, small, chosen_rows, probe_basis):
    groups, fan, rim, half, n_basis, cap, n_blocks = sizes
    width = 2 * half
    tiles = fan
    every = groups * LANES
    me = lax.axis_index("brick") * lax.axis_size("probe") + lax.axis_index("probe")
    rest_at = half + 4 * fan // 2
    small_rows = small[...]
    received = groups * cap
    edges = received * fan
    send_rows = jnp.concatenate(
        [data_mine[g, rest_at : rest_at + 8, :].astype(F32)[4:5] for g in range(groups)], axis=0
    )

    def picks(lane_count, per_group):
        lane = iota((LANES, lane_count), 1)
        wanted = me * cap + lane % cap
        spread = dot(send_rows.astype(BF16), one_hot(iota((LANES, lane_count), 0) == wanted))
        lane = iota((groups, lane_count), 1)
        spread = jnp.where(lane // per_group == iota((groups, lane_count), 0), spread, 0.0)
        return jnp.sum(spread, axis=0, keepdims=True)

    per_group = fan * cap
    pick_atoms = picks(received, cap)
    column = iota((every, 1), 0)
    column_name = (column // LANES) * LANES + lane_atom(column % LANES, fan, tiles)
    wanted = (iota((1, received), 1) // cap) * LANES + pick_atoms.astype(jnp.int32)
    chosen_atoms = one_hot(column_name == wanted)

    pos_rows = jnp.concatenate(
        [data_mine[g, rest_at : rest_at + 8, :] for g in range(groups)], axis=1
    )
    pos = dot(pos_rows, chosen_atoms) - 1.875
    chosen_rows[0:1, :] = picks(edges, per_group)
    chosen_rows[1:2, 0:received] = pick_atoms
    chosen_rows[2:5, 0:received] = pos[0:3]
    pos_cols = jnp.concatenate(
        [
            jnp.concatenate([pos, jnp.zeros((8, LANES - received), F32)], axis=1),
            jnp.zeros((LANES - 8, LANES), F32),
        ],
        axis=0,
    ).T
    list_len = width
    counts = []
    for block in range(n_blocks):
        live = iota((1, list_len), 1).astype(F32) < small_rows[list_at + n_blocks : list_at + n_blocks + 1, block : block + 1]
        named = jnp.where(live, small_rows[list_at + block : list_at + block + 1], -1.0)
        hits = jnp.where(iota((received, list_len), 0).astype(F32) == named, 1.0, 0.0)
        counts.append(
            jnp.broadcast_to(jnp.sum(hits, axis=1, keepdims=True), (received, PB))
        )
    counts = jnp.concatenate(counts, axis=1)
    probes = n_blocks * PB
    grid = probe_grid(me, probes)
    dist_sq = jnp.zeros((received, probes), F32)
    for x in range(3):
        dist_sq = dist_sq + (grid[x] - pos_cols[0:received, x : x + 1]) ** 2
    dist = jnp.sqrt(dist_sq) * ROOT
    envelope = (1.0 - dist_sq / 64.0) ** 2 * counts
    probe_basis[...] = jnp.concatenate(
        [
            (bell(dist, r * (ROOT * 7.0 / (n_basis - 1))) * envelope).astype(BF16)
            for r in range(n_basis)
        ],
        axis=0,
    )


def density_kernel(
    sizes,
    data_mine,
    data_other,
    weights_mine,
    weights_other,
    small,
    w_in,
    w_mix,
    chosen_rows,
    probe_basis,
    density,
    state0,
    own0,
    faces0,
    state1,
    weights,
):
    groups, fan, rim, half, n_basis, cap, n_blocks = sizes
    layers = w_in.shape[0]
    width = 2 * half
    tiles = LANES * fan // LANES
    root_fan = fan**0.5
    me = lax.axis_index("brick") * lax.axis_size("probe") + lax.axis_index("probe")
    part = lax.axis_index("chan")
    weights[part] = weights_mine[...]
    weights[1 - part] = weights_other[...]
    every = groups * LANES
    edge_at = half
    n_edge = 4 * fan // 2
    rest_at = half + n_edge

    def data(group, c, rows):
        return (data_mine, data_other)[c][group, rows, :]

    def weight(layer, p):
        at = (layer * 3 + p) * half
        return jnp.concatenate([weights[c, at : at + half, :] for c in range(2)], axis=0)

    def radial_weight(layer, p):
        at = (layer * 3 + p) * n_basis
        return radial_all[:, at : at + n_basis]

    def edge_rows(group):
        return [data(group, c, slice(edge_at, rest_at)).astype(F32) for c in range(2)]

    def border_of(group):
        return data(group, 0, slice(rest_at, rest_at + 8)).astype(F32)[3:4, 0 : 2 * rim]

    centers = iota((n_basis, 1), 0).astype(F32) * (ROOT * 6.0 / (n_basis - 1))

    def basis_of(length, env):
        return (bell(length * ROOT, centers) * env).astype(BF16)

    received = groups * cap
    edges = received * fan
    per_group = fan * cap
    pick_edges = chosen_rows[0:1, :]
    pick_atoms = chosen_rows[1:2, 0:received]
    pos = chosen_rows[2:5, 0:received]
    atom_rows = lane_atom(iota((LANES, per_group), 0), fan, tiles).astype(F32)
    chosen = []
    for group in range(groups):
        rows = jnp.concatenate([data(group, c, slice(edge_at, rest_at)) for c in range(2)], axis=0)
        want = pick_edges[:, group * per_group : (group + 1) * per_group]
        chosen.append(dot(rows, one_hot(atom_rows == want)))
    chosen = jnp.concatenate(chosen, axis=1)
    step = fan // 2
    row = iota((2 * n_edge, edges), 0)
    slot_k = (row // n_edge) * step + row % step
    lane_k = (iota((2 * n_edge, edges), 1) % per_group) // cap
    chosen = jnp.where(slot_k == lane_k, chosen, 0.0)
    chosen = jnp.sum(chosen.reshape(2 * 4, step, edges), axis=1)
    chosen = chosen[0:4] + chosen[4:8]
    pick_vec = [chosen[x : x + 1] for x in range(3)]
    nbr = chosen[3:4]
    length = jnp.sqrt(sum(x * x for x in pick_vec))
    basis1 = basis_of(length, (1.0 - length * length / 36.0) ** 2)

    nbr = nbr.astype(jnp.int32)
    home = iota((1, edges), 1) // per_group
    is_low = (nbr >= LANES) & (nbr < LANES + rim)
    is_up = nbr >= LANES + rim
    owner = jnp.where(
        is_low, (home + groups - 1) % groups, jnp.where(is_up, (home + 1) % groups, home)
    )
    entry = owner * 2 * rim + jnp.where(is_low, nbr - (LANES - rim), nbr - (LANES + rim))
    entry = jnp.where(is_low | is_up, entry, -1)
    border_all = jnp.concatenate(
        [border_of(g) for g in range(groups)], axis=1
    )
    border_all = jnp.broadcast_to(border_all, (16, groups * 2 * rim)).astype(BF16)
    seen = dot(border_all, one_hot(iota((groups * 2 * rim, edges), 0) == entry))[0:1]
    target_atom = jnp.where(entry < 0, nbr, seen.astype(jnp.int32))
    column = iota((every, 1), 0)
    column_name = (column // LANES) * LANES + lane_atom(column % LANES, fan, tiles)
    quad = groups // 2
    window = [[(h * quad + groups - 1 + i) % groups for i in range(quad + 2)] for h in range(2)]
    window_pick = []
    for h in range(2):
        lanes = slice(h * edges // 2, (h + 1) * edges // 2)
        near = lax.rem(owner[:, lanes] + 2 * groups - (h * quad + groups - 1), groups)
        name = near * LANES + target_atom[:, lanes]
        window_pick.append(one_hot(column_name[: (quad + 2) * LANES] == name))
    wanted = (iota((1, received), 1) // cap) * LANES + pick_atoms.astype(jnp.int32)
    chosen_atoms = one_hot(column_name == wanted)

    small_rows = small[...]
    columns = small_rows.T
    radial_at = weights.shape[1] - half
    radial_all = jnp.concatenate([weights[c, radial_at:, :] for c in range(2)], axis=0)

    terms_shape = (2 * n_basis, n_basis * received)
    probe_weight = radial_all[:, 3 * layers * n_basis :]
    w_scalar, w_vector = (
        dot(probe_weight, one_hot(iota(terms_shape, 1) // received * 2 + p == iota(terms_shape, 0)))
        for p in range(2)
    )

    probes = density.shape[1]
    grid = probe_grid(me, probes)

    for group in range(groups):
        for c in range(2):
            place = part if c == 0 else 1 - part
            rows = pl.ds(pl.multiple_of(place * half, half), half)
            state0[rows, group * LANES : (group + 1) * LANES] = data(group, c, slice(0, half))
    hidden = silu(dot_tn(w_in[0], state0[...]) + columns[:, 0:1]).astype(BF16)
    weight_ac = jnp.concatenate([weight(0, 0), weight(0, 2)], axis=0)
    messages = dot(weight_ac, hidden).astype(BF16)
    atom_col = lane_atom(iota((LANES, 2 * rim), 0), fan, tiles).astype(F32)
    for group in range(groups):
        own = messages[:, group * LANES : (group + 1) * LANES]
        own0[group] = own
        border_row = border_of(group)
        faces0[group, :, 0 : 2 * rim] = dot(own, one_hot(atom_col == border_row)).astype(BF16)

    row = iota((LANES + 2 * rim, 1), 0)
    names = jnp.where(
        row < LANES,
        lane_atom(row, fan, tiles),
        jnp.where(row < LANES + rim, row + rim, row - rim),
    ).astype(F32)
    names = jnp.broadcast_to(names, (LANES + 2 * rim, LANES)).astype(BF16)
    upper_lane = iota((2 * width, 2 * rim), 1) < rim
    radial_ac = jnp.concatenate([radial_weight(0, 0), radial_weight(0, 2)], axis=0)
    radial_rows = jnp.concatenate([jnp.zeros((2 * width, LANES + 2 * rim), BF16), radial_ac], axis=1)
    blank = jnp.zeros((2 * width, n_basis), BF16)

    for group in range(groups):
        up = (group + 1) % groups
        low = (group + groups - 1) % groups
        ghosts = jnp.where(
            upper_lane,
            faces0[up, :, 0 : 2 * rim].astype(F32),
            faces0[low, :, 0 : 2 * rim].astype(F32),
        ).astype(BF16)
        table = jnp.concatenate([own0[group], ghosts, blank], axis=1)
        left = jnp.concatenate(
            [
                block[at : at + 16]
                for at in range(0, 2 * width, 16)
                for block in (table, radial_rows)
            ],
            axis=0,
        )
        halves = edge_rows(group)
        step = fan // 2
        acc = jnp.zeros((width, LANES), F32)
        acc_vec = [jnp.zeros((width, LANES), F32) for _ in range(3)]
        for c in range(2):
            rows = halves[c]
            vec = [rows[x * step : (x + 1) * step] for x in range(3)]
            nbr = rows[3 * step : 4 * step]
            length_sq = vec[0] * vec[0] + vec[1] * vec[1] + vec[2] * vec[2]
            length = jnp.sqrt(length_sq)
            env = (1.0 - length * length / 36.0) ** 2
            for first in range(0, step, TOGETHER):
                ks = range(first, first + TOGETHER)
                picked = jnp.concatenate([same(names, nbr[k : k + 1].astype(BF16)) for k in ks], axis=1)
                basis = jnp.concatenate(
                    [basis_of(length[k : k + 1], env[k : k + 1]) for k in ks], axis=1
                )
                both = dot(left, jnp.concatenate([picked, basis], axis=0))
                prod = jnp.concatenate(
                    [both[at : at + 16] * both[at + 16 : at + 32] for at in range(0, 4 * width, 32)],
                    axis=0,
                )
                for i, k in enumerate(ks):
                    block = prod[:, i * LANES : (i + 1) * LANES]
                    acc = acc + block[:width]
                    for x in range(3):
                        acc_vec[x] = acc_vec[x] + block[width:] * vec[x][k : k + 1]
        lanes = slice(group * LANES, (group + 1) * LANES)
        state1[0:width, lanes] = (state0[:, lanes].astype(F32) + acc / root_fan).astype(BF16)
        for x in range(3):
            state1[(x + 1) * width : (x + 2) * width, lanes] = (acc_vec[x] / root_fan).astype(BF16)

    rows = []
    for h in range(2):
        near_states = jnp.concatenate(
            [state1[:, g * LANES : (g + 1) * LANES] for g in window[h]], axis=1
        )
        rows.append(dot(near_states, window_pick[h]))
    rows = jnp.concatenate(rows, axis=1)
    hidden = silu(dot_tn(w_in[1], rows[:width].astype(BF16)) + columns[:, 1:2]).astype(BF16)
    weight_abc = jnp.concatenate([weight(1, p) for p in range(3)], axis=0)
    messages = dot(weight_abc, hidden).astype(BF16).astype(F32)
    radial_abc = jnp.concatenate([radial_weight(1, p) for p in range(3)], axis=0)
    filters = dot(radial_abc, basis1)
    weighted = messages * filters
    gate = weighted[width : 2 * width]
    along = weighted[2 * width :]
    parts = [weighted[:width]]
    for x in range(3):
        parts.append(rows[(1 + x) * width : (2 + x) * width] * gate + along * pick_vec[x])
    parts = jnp.concatenate(parts, axis=0).astype(BF16)
    edge = iota((edges, received), 0)
    slot = (edge // per_group) * cap + edge % cap
    delta = dot(parts, one_hot(slot == iota((edges, received), 1)))
    final = (dot(state1[...], chosen_atoms) + delta / root_fan).astype(BF16).astype(F32)

    along = final[width : 2 * width] * pos[0:1]
    for x in range(1, 3):
        along = along + final[(x + 1) * width : (x + 2) * width] * pos[x : x + 1]
    def repeat(value):
        return jnp.concatenate([value] * n_basis, axis=1)
    terms = [w_scalar * repeat(final[:width]) - w_vector * repeat(along)]
    for x in range(3):
        terms.append(w_vector * repeat(final[(x + 1) * width : (x + 2) * width]))
    sums = dot(jnp.concatenate(terms, axis=0).astype(BF16), probe_basis[...])
    charges = sums[:width]
    for x in range(3):
        charges = charges + grid[x] * sums[(x + 1) * width : (x + 2) * width]
    mixed = dot_tn(w_mix[...], charges.astype(BF16)) + columns[:, layers : layers + 1]
    density[...] = jnp.sum(silu(mixed) * columns[:, layers + 1 : layers + 2], axis=0, keepdims=True)


def few_groups(
    atom_s, atom_pos, edge_vec, edge_nbr, border_index, send_index, probe_list, probe_count,
    w_in, b_in, w_msg, w_rad, w_probe, w_mix, b_mix, w_out,
):
    atoms, half = atom_s.shape
    groups = lax.axis_size("brick") * lax.axis_size("probe")
    fan = edge_nbr.shape[0] // atoms
    rim = border_index.shape[0] // 2
    n_basis = w_rad.shape[1]
    cap = send_index.shape[1] // groups
    width = 2 * half
    every = groups * LANES
    data, weights, small = pack(
        groups, atom_s, atom_pos, edge_vec, edge_nbr, border_index, send_index, w_msg, w_rad, w_probe,
        b_in, b_mix, w_out, probe_list, probe_count,
    )
    swap = [(0, 1), (1, 0)]
    weights_other = lax.ppermute(weights, "chan", swap)
    mine = lax.all_to_all(data, ("brick", "probe"), split_axis=0, concat_axis=0, tiled=True)
    anywhere = pl.BlockSpec(memory_space=pl.ANY)
    mine = pl.pallas_call(
        after_kernel,
        out_shape=jax.ShapeDtypeStruct(mine.shape, BF16),
        in_specs=[anywhere] * 2,
        out_specs=anywhere,
        input_output_aliases={0: 0},
        compiler_params=pltpu.CompilerParams(vmem_limit_bytes=16 * 1024 * 1024),
        name="after",
    )(mine, weights_other)
    other = lax.ppermute(mine, "chan", swap)
    n_probes = probe_list.shape[0] * PB
    sizes = (groups, fan, rim, half, n_basis, cap, probe_list.shape[0])
    chosen_rows, probe_basis = pl.pallas_call(
        functools.partial(probe_kernel, sizes, w_in.shape[0] + 2),
        out_shape=(
            jax.ShapeDtypeStruct((8, groups * cap * fan), F32),
            jax.ShapeDtypeStruct((n_basis * groups * cap, n_probes), BF16),
        ),
        compiler_params=pltpu.CompilerParams(vmem_limit_bytes=24 * 1024 * 1024),
        name="probe_basis",
    )(mine, small)
    density = pl.pallas_call(
        functools.partial(density_kernel, sizes),
        out_shape=jax.ShapeDtypeStruct((1, n_probes), F32),
        scratch_shapes=[
            pltpu.VMEM((width, every), BF16),
            pltpu.VMEM((groups, 2 * width, LANES), BF16),
            pltpu.VMEM((groups, 2 * width, LANES), BF16),
            pltpu.VMEM((4 * width, every), BF16),
            pltpu.VMEM((2,) + weights.shape, BF16),
        ],
        compiler_params=pltpu.CompilerParams(vmem_limit_bytes=40 * 1024 * 1024),
        name="density",
    )(mine, other, weights, weights_other, small, w_in, w_mix, chosen_rows, probe_basis)
    return density.reshape(n_probes)


def per_device(*args):
    if lax.axis_size("brick") * lax.axis_size("probe") == FEW_GROUPS:
        return few_groups(*args)
    return many_groups(*args)


def extended(block, sides, width):
    for axis, dim in sides:
        count = lax.axis_size(axis)
        forward = [(i, i + 1) for i in range(count - 1)]
        forward.append((count - 1, 0))
        backward = [(target, source) for source, target in forward]
        low = lax.ppermute(
            lax.slice_in_dim(block, block.shape[dim] - width, None, axis=dim), axis, forward
        )
        high = lax.ppermute(lax.slice_in_dim(block, 0, width, axis=dim), axis, backward)
        block = jnp.concatenate([low, block, high], axis=dim)
    return block


def radial(distance, count, top):
    centers = jnp.arange(count).astype(jnp.float32) * (top / (count - 1))
    return jnp.exp(-2.0 * (distance[..., None] - centers) ** 2)


def make_block(
    recv_rows, recv_pos, w_scalar, w_vector, feat_width, group_no, n_blocks, list_len, n_basis
):

    def probe_block(block_in):
        block_no, listed, live_count = block_in
        index_row = (group_no * n_blocks + block_no) * PB + jnp.arange(PB, dtype=jnp.int32)
        grid_xyz = (
            jnp.stack([index_row % 16, index_row // 16 % 16, index_row // 256 % 16], axis=1).astype(
                jnp.float32
            )
            * 0.25
        )
        atom_xyz = recv_pos[:, listed]
        disp = grid_xyz[:, :, None] - atom_xyz[None]
        dist_sq = jnp.sum(disp * disp, axis=1)
        live = (jnp.arange(list_len, dtype=jnp.int32) < live_count).astype(jnp.float32)
        envelope = (1.0 - dist_sq / 64.0) ** 2 * live[None, :]
        basis = radial(jnp.sqrt(dist_sq), n_basis, 7.0) * envelope[:, :, None]
        scalar_w = basis.astype(jnp.bfloat16).reshape(PB, list_len * n_basis)
        vector_w = (
            (disp[:, :, :, None] * basis[:, None])
            .astype(jnp.bfloat16)
            .reshape(PB, 3 * list_len * n_basis)
        )
        atom_rows = recv_rows[listed]
        atom_terms = (atom_rows[:, None, :feat_width] * w_scalar[None]).reshape(
            list_len * n_basis, feat_width
        )
        vec_rows = jnp.transpose(
            atom_rows[:, feat_width:].reshape(list_len, 3, feat_width), (1, 0, 2)
        )
        vector_terms = (vec_rows[:, :, None, :] * w_vector[None, None]).reshape(
            3 * list_len * n_basis, feat_width
        )
        charge = jnp.dot(scalar_w, atom_terms, preferred_element_type=jnp.float32) + jnp.dot(
            vector_w, vector_terms, preferred_element_type=jnp.float32
        )
        return charge.astype(jnp.bfloat16)

    return probe_block


def many_groups(
    atom_s,
    atom_pos,
    edge_vec,
    edge_nbr,
    border_index,
    send_index,
    probe_list,
    probe_count,
    w_in,
    b_in,
    w_msg,
    w_rad,
    w_probe,
    w_mix,
    b_mix,
    w_out,
):
    atom_count, half_width = atom_s.shape
    n_layers = w_in.shape[0]
    width = w_in.shape[1]
    n_basis = w_rad.shape[1]
    fan_out = edge_nbr.shape[0] // atom_count
    root_fan = fan_out**0.5
    rim_rows = border_index.shape[0] // 2
    length = jnp.sqrt(jnp.sum(edge_vec * edge_vec, axis=0))
    edge_env = (1.0 - length * length / 36.0) ** 2
    edge_basis = (radial(length, n_basis, 6.0) * edge_env[:, None]).astype(jnp.bfloat16)
    edge_cols = jnp.transpose(edge_vec)
    scalars = atom_s
    vectors = jnp.zeros((atom_count, 3 * half_width), jnp.bfloat16)
    for layer_no in range(n_layers):
        full_rows = lax.all_gather(scalars, "chan", axis=1, tiled=True)
        in_weight = w_in[layer_no]
        in_bias = b_in[layer_no]
        msg_weight = w_msg[layer_no].reshape(width, 3 * half_width)
        rad_weight = w_rad[layer_no].reshape(n_basis, 3 * half_width)
        hidden_act = jax.nn.silu(
            jnp.dot(full_rows, in_weight, preferred_element_type=jnp.float32) + in_bias
        ).astype(jnp.bfloat16)
        inner_tab = jnp.concatenate(
            [
                jnp.dot(hidden_act, msg_weight, preferred_element_type=jnp.float32).astype(
                    jnp.bfloat16
                ),
                vectors,
            ],
            axis=1,
        )
        padded = extended(inner_tab[border_index], ((("brick", "probe"), 0),), rim_rows)
        lookup = jnp.concatenate([inner_tab, padded[:rim_rows], padded[3 * rim_rows :]], axis=0)
        neighbour_rows = lookup[edge_nbr]
        filters = jnp.dot(edge_basis, rad_weight, preferred_element_type=jnp.float32)
        weighted = neighbour_rows[:, : 3 * half_width] * filters
        neighbour_vec = neighbour_rows[:, 3 * half_width :].reshape(-1, 3, half_width)
        vector_gate = weighted[:, None, half_width : 2 * half_width]
        along_edge = weighted[:, None, 2 * half_width :]
        delta_vec = neighbour_vec * vector_gate + along_edge * edge_cols[:, :, None]
        delta_scalar = (
            weighted[:, :half_width].reshape(atom_count, fan_out, half_width).sum(axis=1) / root_fan
        )
        delta_vec = delta_vec.reshape(atom_count, fan_out, 3 * half_width).sum(axis=1) / root_fan
        scalars = (scalars + delta_scalar).astype(jnp.bfloat16)
        vectors = (vectors + delta_vec).astype(jnp.bfloat16)
    features = jnp.concatenate([scalars, vectors], axis=1)
    picks = send_index[0]
    n_brick = lax.axis_size("brick")
    n_probe = lax.axis_size("probe")
    n_groups = n_brick * n_probe
    slot_cap = picks.shape[0] // n_groups
    out_rows = features[picks]
    out_pos = jnp.transpose(atom_pos)[picks].astype(jnp.bfloat16)
    received = (
        lax.all_to_all(
            out_rows.reshape(n_groups, slot_cap, 4 * half_width),
            ("brick", "probe"),
            split_axis=0,
            concat_axis=0,
            tiled=True,
        ),
        lax.all_to_all(
            out_pos.reshape(n_groups, slot_cap, 3),
            ("brick", "probe"),
            split_axis=0,
            concat_axis=0,
            tiled=True,
        ),
    )
    recv_count = n_groups * slot_cap
    recv_rows = received[0].reshape(recv_count, 4 * half_width)
    recv_pos = jnp.transpose(received[1].reshape(recv_count, 3)).astype(jnp.float32)
    group_no = lax.axis_index("brick") * n_probe + lax.axis_index("probe")
    n_blocks, list_len = probe_list.shape
    probe_block = make_block(
        recv_rows,
        recv_pos,
        w_probe[:, 0, :],
        w_probe[:, 1, :],
        half_width,
        group_no,
        n_blocks,
        list_len,
        n_basis,
    )
    charges = lax.map(
        probe_block, (jnp.arange(n_blocks, dtype=jnp.int32), probe_list, probe_count)
    ).reshape(n_blocks * PB, half_width)
    mix_rows = lax.dynamic_slice_in_dim(w_mix, lax.axis_index("chan") * half_width, half_width, 0)
    mixed = lax.psum(jnp.dot(charges, mix_rows, preferred_element_type=jnp.float32), "chan")
    return jnp.sum(jax.nn.silu(mixed + b_mix) * w_out, axis=1)


def solution(mesh):
    in_specs = (
        P(("image", "brick", "probe"), "chan"),
        P(None, ("image", "brick", "probe")),
        P(None, ("image", "brick", "probe")),
        P(("image", "brick", "probe")),
        P(("image", "brick", "probe")),
        P(("image", "brick", "probe"), None),
        P(("image", "brick", "probe"), None),
        P(("image", "brick", "probe")),
        P(),
        P(),
        P(None, None, None, "chan"),
        P(None, None, None, "chan"),
        P(None, None, "chan"),
        P(),
        P(),
        P(),
    )
    out_specs = P(("image", "brick", "probe"))
    return jax.shard_map(
        per_device, mesh=mesh, in_specs=in_specs, out_specs=out_specs, check_vma=False
    )
```

```python
import functools
import itertools
import math

import jax
import jax.numpy as jnp
from jax import lax
from jax.experimental import pallas as pl
from jax.experimental.pallas import tpu as pltpu
from jax.sharding import PartitionSpec as P

PB = 128
LANES = 128
FEW_GROUPS = 8
SMALL = 16
TOGETHER = 4
ROOT = (2.0 * math.log2(math.e)) ** 0.5
F32 = jnp.float32
BF16 = jnp.bfloat16


def iota(shape, dim):
    return lax.broadcasted_iota(jnp.int32, shape, dim)


def dot(a, b):
    return jnp.dot(a, b, preferred_element_type=F32)


def dot_tn(a, b):
    return lax.dot_general(a, b, (((0,), (0,)), ((), ())), preferred_element_type=F32)


def one_hot(mask):
    return jnp.where(mask, 1.0, 0.0).astype(BF16)


def same(names, row):
    return jnp.where(names == row, jnp.ones_like(names), jnp.zeros_like(names))


def silu(x):
    half_x = 0.5 * x
    return half_x * jnp.tanh(half_x) + half_x


def bell(scaled, center):
    away = scaled - center
    return jnp.exp2(-(away * away))


def lane_atom(lane, fan, tiles):
    return (lane % tiles) * (LANES // fan) + lane // tiles


def length_keeping_round(exact):
    choices = []
    for value in exact:
        near = value.astype(BF16).astype(F32)
        step = jnp.where(value > near, 1.01 / 256.0, -1.01 / 256.0) * jnp.abs(near)
        choices.append((near, (near + step).astype(BF16).astype(F32)))
    target = sum(value * value for value in exact)
    best, best_error = None, None
    for picked in itertools.product(*choices):
        error = jnp.abs(sum(value * value for value in picked) - target)
        if best is None:
            best, best_error = picked, error
            continue
        better = error < best_error
        best = tuple(jnp.where(better, new, old) for new, old in zip(picked, best))
        best_error = jnp.where(better, error, best_error)
    return best


def pack_kernel(
    fan, atom_s, atom_pos, edge_vec, edge_nbr, border, send, data_out, natural
):
    half, atoms = atom_s.shape
    tiles = atoms * fan // LANES
    per_tile = LANES // fan
    part = lax.axis_index("chan")
    perm = one_hot(lane_atom(iota((atoms, LANES), 1), fan, tiles) == iota((atoms, LANES), 0))
    scalars = dot(atom_s[...], perm).astype(BF16)
    for tile in range(tiles):
        for comp in range(3):
            natural[comp * tiles + tile : comp * tiles + tile + 1, :] = edge_vec[
                comp : comp + 1, tile * LANES : (tile + 1) * LANES
            ]
    exact = [natural[comp * tiles : (comp + 1) * tiles, :] for comp in range(3)]
    for comp, value in enumerate(length_keeping_round(exact)):
        natural[comp * tiles : (comp + 1) * tiles, :] = value
    natural[3 * tiles : 4 * tiles, :] = edge_nbr[...].astype(F32)
    natural[4 * tiles :, :] = jnp.zeros((LANES - 4 * tiles, LANES), F32)
    turned = natural[...].T
    lane = iota((fan, LANES), 1)
    sorted_rows = []
    for comp in range(4):
        rows = jnp.zeros((fan, LANES), F32)
        for a in range(per_tile):
            piece = turned[a * fan : (a + 1) * fan, :]
            shift = (a * tiles - comp * tiles) % LANES
            piece = pltpu.roll(piece, shift, 1) if shift else piece
            rows = jnp.where(lane // tiles == a, piece, rows)
        sorted_rows.append(jnp.where(part == 0, rows[: fan // 2], rows[fan // 2 :]))
    pos = dot(atom_pos[...].astype(BF16), perm)
    blank = jnp.zeros((1, LANES), F32)
    border_row = jnp.concatenate(
        [border[...].astype(F32), jnp.zeros((1, LANES - border.shape[1]), F32)], axis=1
    )
    send_row = jnp.concatenate(
        [send[...].astype(F32), jnp.zeros((1, LANES - send.shape[1]), F32)], axis=1
    )
    rest = jnp.concatenate([pos, border_row, send_row, blank, blank, blank], axis=0)
    others = jnp.concatenate(sorted_rows + [rest], axis=0).astype(BF16)
    for group in range(data_out.shape[0]):
        data_out[group, 0:half, :] = scalars
        data_out[group, half:, :] = others


def weight_kernel(
    w_msg, w_rad, w_probe, b_in, b_mix, w_out, probe_list, probe_count, weight_out, small_out
):
    at = 0
    for piece in (b_in, b_mix, w_out, probe_list, probe_count):
        rows, cols = piece.shape
        small_out[at : at + rows, 0:cols] = piece[...].astype(F32)
        at += rows
    probe_rows = [w_probe[r].astype(F32) for r in range(w_probe.shape[0])]
    radial = jnp.concatenate([w_rad[...].astype(F32)] + probe_rows, axis=0).T.astype(BF16)
    weight_out[: w_msg.shape[0], :] = w_msg[...]
    weight_out[w_msg.shape[0] :, :] = radial


def pack(copies, atom_s, atom_pos, edge_vec, edge_nbr, border_index, send_index):
    atoms, half = atom_s.shape
    fan = edge_nbr.shape[0] // atoms
    return pl.pallas_call(
        functools.partial(pack_kernel, fan),
        out_shape=jax.ShapeDtypeStruct((copies, half + 4 * fan // 2 + 8, LANES), BF16),
        scratch_shapes=[pltpu.VMEM((LANES, LANES), F32)],
        name="pack",
    )(
        atom_s.T,
        atom_pos,
        edge_vec,
        edge_nbr.reshape(-1, LANES),
        border_index.reshape(1, -1),
        send_index,
    )


def pack_weights(half, w_msg, w_rad, w_probe, b_in, b_mix, w_out, probe_list, probe_count):
    return pl.pallas_call(
        weight_kernel,
        out_shape=(
            jax.ShapeDtypeStruct((w_msg.size // LANES + half, LANES), BF16),
            jax.ShapeDtypeStruct((SMALL, LANES), F32),
        ),
        name="pack_weights",
    )(
        jnp.transpose(w_msg, (0, 2, 3, 1)).reshape(-1, LANES),
        jnp.transpose(w_rad, (0, 2, 1, 3)).reshape(-1, half),
        w_probe,
        b_in,
        b_mix.reshape(1, -1),
        w_out.reshape(1, -1),
        probe_list,
        probe_count.reshape(1, -1),
    )


def after_kernel(block, there, same_block):
    pass


def probe_grid(me, probes):
    number = me * probes + iota((1, probes), 1)
    return [(n % 16).astype(F32) * 0.25 - 1.875 for n in (number, number // 16, number // 256)]


def probe_kernel(sizes, list_at, data_mine, small, chosen_rows, probe_basis):
    groups, fan, rim, half, n_basis, cap, n_blocks = sizes
    width = 2 * half
    tiles = fan
    every = groups * LANES
    me = lax.axis_index("brick") * lax.axis_size("probe") + lax.axis_index("probe")
    rest_at = half + 4 * fan // 2
    small_rows = small[...]
    received = groups * cap
    edges = received * fan
    send_rows = jnp.concatenate(
        [data_mine[g, rest_at : rest_at + 8, :].astype(F32)[4:5] for g in range(groups)], axis=0
    )

    def picks(lane_count, per_group):
        lane = iota((LANES, lane_count), 1)
        wanted = me * cap + lane % cap
        spread = dot(send_rows.astype(BF16), one_hot(iota((LANES, lane_count), 0) == wanted))
        lane = iota((groups, lane_count), 1)
        spread = jnp.where(lane // per_group == iota((groups, lane_count), 0), spread, 0.0)
        return jnp.sum(spread, axis=0, keepdims=True)

    per_group = fan * cap
    pick_atoms = picks(received, cap)
    column = iota((every, 1), 0)
    column_name = (column // LANES) * LANES + lane_atom(column % LANES, fan, tiles)
    wanted = (iota((1, received), 1) // cap) * LANES + pick_atoms.astype(jnp.int32)
    chosen_atoms = one_hot(column_name == wanted)

    pos_rows = jnp.concatenate(
        [data_mine[g, rest_at : rest_at + 8, :] for g in range(groups)], axis=1
    )
    pos = dot(pos_rows, chosen_atoms) - 1.875
    chosen_rows[0:1, :] = picks(edges, per_group)
    chosen_rows[1:2, 0:received] = pick_atoms
    chosen_rows[2:5, 0:received] = pos[0:3]
    pos_cols = jnp.concatenate(
        [
            jnp.concatenate([pos, jnp.zeros((8, LANES - received), F32)], axis=1),
            jnp.zeros((LANES - 8, LANES), F32),
        ],
        axis=0,
    ).T
    list_len = width
    counts = []
    for block in range(n_blocks):
        live = iota((1, list_len), 1).astype(F32) < small_rows[list_at + n_blocks : list_at + n_blocks + 1, block : block + 1]
        named = jnp.where(live, small_rows[list_at + block : list_at + block + 1], -1.0)
        hits = jnp.where(iota((received, list_len), 0).astype(F32) == named, 1.0, 0.0)
        counts.append(
            jnp.broadcast_to(jnp.sum(hits, axis=1, keepdims=True), (received, PB))
        )
    counts = jnp.concatenate(counts, axis=1)
    probes = n_blocks * PB
    grid = probe_grid(me, probes)
    dist_sq = jnp.zeros((received, probes), F32)
    for x in range(3):
        dist_sq = dist_sq + (grid[x] - pos_cols[0:received, x : x + 1]) ** 2
    dist = jnp.sqrt(dist_sq) * ROOT
    envelope = (1.0 - dist_sq / 64.0) ** 2 * counts
    probe_basis[...] = jnp.concatenate(
        [
            (bell(dist, r * (ROOT * 7.0 / (n_basis - 1))) * envelope).astype(BF16)
            for r in range(n_basis)
        ],
        axis=0,
    )


def density_kernel(
    sizes,
    data_mine,
    data_other,
    weights_mine,
    weights_other,
    small,
    w_in,
    w_mix,
    chosen_rows,
    probe_basis,
    density,
    state0,
    own0,
    faces0,
    state1,
    weights,
):
    groups, fan, rim, half, n_basis, cap, n_blocks = sizes
    layers = w_in.shape[0]
    width = 2 * half
    tiles = LANES * fan // LANES
    root_fan = fan**0.5
    me = lax.axis_index("brick") * lax.axis_size("probe") + lax.axis_index("probe")
    part = lax.axis_index("chan")
    weights[part] = weights_mine[...]
    weights[1 - part] = weights_other[...]
    every = groups * LANES
    edge_at = half
    n_edge = 4 * fan // 2
    rest_at = half + n_edge

    def data(group, c, rows):
        return (data_mine, data_other)[c][group, rows, :]

    def weight(layer, p):
        at = (layer * 3 + p) * half
        return jnp.concatenate([weights[c, at : at + half, :] for c in range(2)], axis=0)

    def radial_weight(layer, p):
        at = (layer * 3 + p) * n_basis
        return radial_all[:, at : at + n_basis]

    def edge_rows(group):
        return [data(group, c, slice(edge_at, rest_at)).astype(F32) for c in range(2)]

    def border_of(group):
        return data(group, 0, slice(rest_at, rest_at + 8)).astype(F32)[3:4, 0 : 2 * rim]

    centers = iota((n_basis, 1), 0).astype(F32) * (ROOT * 6.0 / (n_basis - 1))

    def basis_of(length, env):
        return (bell(length * ROOT, centers) * env).astype(BF16)

    received = groups * cap
    edges = received * fan
    per_group = fan * cap
    pick_edges = chosen_rows[0:1, :]
    pick_atoms = chosen_rows[1:2, 0:received]
    pos = chosen_rows[2:5, 0:received]
    atom_rows = lane_atom(iota((LANES, per_group), 0), fan, tiles).astype(F32)
    chosen = []
    for group in range(groups):
        rows = jnp.concatenate([data(group, c, slice(edge_at, rest_at)) for c in range(2)], axis=0)
        want = pick_edges[:, group * per_group : (group + 1) * per_group]
        chosen.append(dot(rows, one_hot(atom_rows == want)))
    chosen = jnp.concatenate(chosen, axis=1)
    step = fan // 2
    row = iota((2 * n_edge, edges), 0)
    slot_k = (row // n_edge) * step + row % step
    lane_k = (iota((2 * n_edge, edges), 1) % per_group) // cap
    chosen = jnp.where(slot_k == lane_k, chosen, 0.0)
    chosen = jnp.sum(chosen.reshape(2 * 4, step, edges), axis=1)
    chosen = chosen[0:4] + chosen[4:8]
    pick_vec = [chosen[x : x + 1] for x in range(3)]
    nbr = chosen[3:4]
    length = jnp.sqrt(sum(x * x for x in pick_vec))
    basis1 = basis_of(length, (1.0 - length * length / 36.0) ** 2)

    nbr = nbr.astype(jnp.int32)
    home = iota((1, edges), 1) // per_group
    is_low = (nbr >= LANES) & (nbr < LANES + rim)
    is_up = nbr >= LANES + rim
    owner = jnp.where(
        is_low, (home + groups - 1) % groups, jnp.where(is_up, (home + 1) % groups, home)
    )
    entry = owner * 2 * rim + jnp.where(is_low, nbr - (LANES - rim), nbr - (LANES + rim))
    entry = jnp.where(is_low | is_up, entry, -1)
    border_all = jnp.concatenate(
        [border_of(g) for g in range(groups)], axis=1
    )
    border_all = jnp.broadcast_to(border_all, (16, groups * 2 * rim)).astype(BF16)
    seen = dot(border_all, one_hot(iota((groups * 2 * rim, edges), 0) == entry))[0:1]
    target_atom = jnp.where(entry < 0, nbr, seen.astype(jnp.int32))
    column = iota((every, 1), 0)
    column_name = (column // LANES) * LANES + lane_atom(column % LANES, fan, tiles)
    quad = groups // 2
    window = [[(h * quad + groups - 1 + i) % groups for i in range(quad + 2)] for h in range(2)]
    window_pick = []
    for h in range(2):
        lanes = slice(h * edges // 2, (h + 1) * edges // 2)
        near = lax.rem(owner[:, lanes] + 2 * groups - (h * quad + groups - 1), groups)
        name = near * LANES + target_atom[:, lanes]
        window_pick.append(one_hot(column_name[: (quad + 2) * LANES] == name))
    wanted = (iota((1, received), 1) // cap) * LANES + pick_atoms.astype(jnp.int32)
    chosen_atoms = one_hot(column_name == wanted)

    small_rows = small[...]
    columns = small_rows.T
    radial_at = weights.shape[1] - half
    radial_all = jnp.concatenate([weights[c, radial_at:, :] for c in range(2)], axis=0)

    terms_shape = (2 * n_basis, n_basis * received)
    probe_weight = radial_all[:, 3 * layers * n_basis :]
    w_scalar, w_vector = (
        dot(probe_weight, one_hot(iota(terms_shape, 1) // received * 2 + p == iota(terms_shape, 0)))
        for p in range(2)
    )

    probes = density.shape[1]
    grid = probe_grid(me, probes)

    for group in range(groups):
        for c in range(2):
            place = part if c == 0 else 1 - part
            rows = pl.ds(pl.multiple_of(place * half, half), half)
            state0[rows, group * LANES : (group + 1) * LANES] = data(group, c, slice(0, half))
    hidden = silu(dot_tn(w_in[0], state0[...]) + columns[:, 0:1]).astype(BF16)
    weight_ac = jnp.concatenate([weight(0, 0), weight(0, 2)], axis=0)
    messages = dot(weight_ac, hidden).astype(BF16)
    atom_col = lane_atom(iota((LANES, 2 * rim), 0), fan, tiles).astype(F32)
    for group in range(groups):
        own = messages[:, group * LANES : (group + 1) * LANES]
        own0[group] = own
        border_row = border_of(group)
        faces0[group, :, 0 : 2 * rim] = dot(own, one_hot(atom_col == border_row)).astype(BF16)

    row = iota((LANES + 2 * rim, 1), 0)
    names = jnp.where(
        row < LANES,
        lane_atom(row, fan, tiles),
        jnp.where(row < LANES + rim, row + rim, row - rim),
    ).astype(F32)
    names = jnp.broadcast_to(names, (LANES + 2 * rim, LANES)).astype(BF16)
    upper_lane = iota((2 * width, 2 * rim), 1) < rim
    radial_ac = jnp.concatenate([radial_weight(0, 0), radial_weight(0, 2)], axis=0)
    radial_rows = jnp.concatenate([jnp.zeros((2 * width, LANES + 2 * rim), BF16), radial_ac], axis=1)
    blank = jnp.zeros((2 * width, n_basis), BF16)

    for group in range(groups):
        up = (group + 1) % groups
        low = (group + groups - 1) % groups
        ghosts = jnp.where(
            upper_lane,
            faces0[up, :, 0 : 2 * rim].astype(F32),
            faces0[low, :, 0 : 2 * rim].astype(F32),
        ).astype(BF16)
        table = jnp.concatenate([own0[group], ghosts, blank], axis=1)
        left = jnp.concatenate(
            [
                block[at : at + 16]
                for at in range(0, 2 * width, 16)
                for block in (table, radial_rows)
            ],
            axis=0,
        )
        halves = edge_rows(group)
        step = fan // 2
        acc = jnp.zeros((width, LANES), F32)
        acc_vec = [jnp.zeros((width, LANES), F32) for _ in range(3)]
        for c in range(2):
            rows = halves[c]
            vec = [rows[x * step : (x + 1) * step] for x in range(3)]
            nbr = rows[3 * step : 4 * step]
            length_sq = vec[0] * vec[0] + vec[1] * vec[1] + vec[2] * vec[2]
            length = jnp.sqrt(length_sq)
            env = (1.0 - length * length / 36.0) ** 2
            for first in range(0, step, TOGETHER):
                ks = range(first, first + TOGETHER)
                picked = jnp.concatenate([same(names, nbr[k : k + 1].astype(BF16)) for k in ks], axis=1)
                basis = jnp.concatenate(
                    [basis_of(length[k : k + 1], env[k : k + 1]) for k in ks], axis=1
                )
                both = dot(left, jnp.concatenate([picked, basis], axis=0))
                prod = jnp.concatenate(
                    [both[at : at + 16] * both[at + 16 : at + 32] for at in range(0, 4 * width, 32)],
                    axis=0,
                )
                for i, k in enumerate(ks):
                    block = prod[:, i * LANES : (i + 1) * LANES]
                    acc = acc + block[:width]
                    for x in range(3):
                        acc_vec[x] = acc_vec[x] + block[width:] * vec[x][k : k + 1]
        lanes = slice(group * LANES, (group + 1) * LANES)
        state1[0:width, lanes] = (state0[:, lanes].astype(F32) + acc / root_fan).astype(BF16)
        for x in range(3):
            state1[(x + 1) * width : (x + 2) * width, lanes] = (acc_vec[x] / root_fan).astype(BF16)

    rows = []
    for h in range(2):
        near_states = jnp.concatenate(
            [state1[:, g * LANES : (g + 1) * LANES] for g in window[h]], axis=1
        )
        rows.append(dot(near_states, window_pick[h]))
    rows = jnp.concatenate(rows, axis=1)
    hidden = silu(dot_tn(w_in[1], rows[:width].astype(BF16)) + columns[:, 1:2]).astype(BF16)
    weight_abc = jnp.concatenate([weight(1, p) for p in range(3)], axis=0)
    messages = dot(weight_abc, hidden).astype(BF16).astype(F32)
    radial_abc = jnp.concatenate([radial_weight(1, p) for p in range(3)], axis=0)
    filters = dot(radial_abc, basis1)
    weighted = messages * filters
    gate = weighted[width : 2 * width]
    along = weighted[2 * width :]
    parts = [weighted[:width]]
    for x in range(3):
        parts.append(rows[(1 + x) * width : (2 + x) * width] * gate + along * pick_vec[x])
    parts = jnp.concatenate(parts, axis=0).astype(BF16)
    edge = iota((edges, received), 0)
    slot = (edge // per_group) * cap + edge % cap
    delta = dot(parts, one_hot(slot == iota((edges, received), 1)))
    final = (dot(state1[...], chosen_atoms) + delta / root_fan).astype(BF16).astype(F32)

    along = final[width : 2 * width] * pos[0:1]
    for x in range(1, 3):
        along = along + final[(x + 1) * width : (x + 2) * width] * pos[x : x + 1]
    def repeat(value):
        return jnp.concatenate([value] * n_basis, axis=1)
    terms = [w_scalar * repeat(final[:width]) - w_vector * repeat(along)]
    for x in range(3):
        terms.append(w_vector * repeat(final[(x + 1) * width : (x + 2) * width]))
    sums = dot(jnp.concatenate(terms, axis=0).astype(BF16), probe_basis[...])
    charges = sums[:width]
    for x in range(3):
        charges = charges + grid[x] * sums[(x + 1) * width : (x + 2) * width]
    mixed = dot_tn(w_mix[...], charges.astype(BF16)) + columns[:, layers : layers + 1]
    density[...] = jnp.sum(silu(mixed) * columns[:, layers + 1 : layers + 2], axis=0, keepdims=True)


def few_groups(
    atom_s, atom_pos, edge_vec, edge_nbr, border_index, send_index, probe_list, probe_count,
    w_in, b_in, w_msg, w_rad, w_probe, w_mix, b_mix, w_out,
):
    atoms, half = atom_s.shape
    groups = lax.axis_size("brick") * lax.axis_size("probe")
    fan = edge_nbr.shape[0] // atoms
    rim = border_index.shape[0] // 2
    n_basis = w_rad.shape[1]
    cap = send_index.shape[1] // groups
    width = 2 * half
    every = groups * LANES
    data = pack(groups, atom_s, atom_pos, edge_vec, edge_nbr, border_index, send_index)
    weights, small = pack_weights(
        half, w_msg, w_rad, w_probe, b_in, b_mix, w_out, probe_list, probe_count
    )
    swap = [(0, 1), (1, 0)]
    weights_other = lax.ppermute(weights, "chan", swap)
    mine = lax.all_to_all(data, ("brick", "probe"), split_axis=0, concat_axis=0, tiled=True)
    anywhere = pl.BlockSpec(memory_space=pl.ANY)
    mine = pl.pallas_call(
        after_kernel,
        out_shape=jax.ShapeDtypeStruct(mine.shape, BF16),
        in_specs=[anywhere] * 2,
        out_specs=anywhere,
        input_output_aliases={0: 0},
        compiler_params=pltpu.CompilerParams(vmem_limit_bytes=16 * 1024 * 1024),
        name="after",
    )(mine, weights_other)
    other = lax.ppermute(mine, "chan", swap)
    n_probes = probe_list.shape[0] * PB
    sizes = (groups, fan, rim, half, n_basis, cap, probe_list.shape[0])
    chosen_rows, probe_basis = pl.pallas_call(
        functools.partial(probe_kernel, sizes, w_in.shape[0] + 2),
        out_shape=(
            jax.ShapeDtypeStruct((8, groups * cap * fan), F32),
            jax.ShapeDtypeStruct((n_basis * groups * cap, n_probes), BF16),
        ),
        compiler_params=pltpu.CompilerParams(vmem_limit_bytes=24 * 1024 * 1024),
        name="probe_basis",
    )(mine, small)
    density = pl.pallas_call(
        functools.partial(density_kernel, sizes),
        out_shape=jax.ShapeDtypeStruct((1, n_probes), F32),
        scratch_shapes=[
            pltpu.VMEM((width, every), BF16),
            pltpu.VMEM((groups, 2 * width, LANES), BF16),
            pltpu.VMEM((groups, 2 * width, LANES), BF16),
            pltpu.VMEM((4 * width, every), BF16),
            pltpu.VMEM((2,) + weights.shape, BF16),
        ],
        compiler_params=pltpu.CompilerParams(vmem_limit_bytes=40 * 1024 * 1024),
        name="density",
    )(mine, other, weights, weights_other, small, w_in, w_mix, chosen_rows, probe_basis)
    return density.reshape(n_probes)


def per_device(*args):
    if lax.axis_size("brick") * lax.axis_size("probe") == FEW_GROUPS:
        return few_groups(*args)
    return many_groups(*args)


def extended(block, sides, width):
    for axis, dim in sides:
        count = lax.axis_size(axis)
        forward = [(i, i + 1) for i in range(count - 1)]
        forward.append((count - 1, 0))
        backward = [(target, source) for source, target in forward]
        low = lax.ppermute(
            lax.slice_in_dim(block, block.shape[dim] - width, None, axis=dim), axis, forward
        )
        high = lax.ppermute(lax.slice_in_dim(block, 0, width, axis=dim), axis, backward)
        block = jnp.concatenate([low, block, high], axis=dim)
    return block


def radial(distance, count, top):
    centers = jnp.arange(count).astype(jnp.float32) * (top / (count - 1))
    return jnp.exp(-2.0 * (distance[..., None] - centers) ** 2)


def make_block(
    recv_rows, recv_pos, w_scalar, w_vector, feat_width, group_no, n_blocks, list_len, n_basis
):

    def probe_block(block_in):
        block_no, listed, live_count = block_in
        index_row = (group_no * n_blocks + block_no) * PB + jnp.arange(PB, dtype=jnp.int32)
        grid_xyz = (
            jnp.stack([index_row % 16, index_row // 16 % 16, index_row // 256 % 16], axis=1).astype(
                jnp.float32
            )
            * 0.25
        )
        atom_xyz = recv_pos[:, listed]
        disp = grid_xyz[:, :, None] - atom_xyz[None]
        dist_sq = jnp.sum(disp * disp, axis=1)
        live = (jnp.arange(list_len, dtype=jnp.int32) < live_count).astype(jnp.float32)
        envelope = (1.0 - dist_sq / 64.0) ** 2 * live[None, :]
        basis = radial(jnp.sqrt(dist_sq), n_basis, 7.0) * envelope[:, :, None]
        scalar_w = basis.astype(jnp.bfloat16).reshape(PB, list_len * n_basis)
        vector_w = (
            (disp[:, :, :, None] * basis[:, None])
            .astype(jnp.bfloat16)
            .reshape(PB, 3 * list_len * n_basis)
        )
        atom_rows = recv_rows[listed]
        atom_terms = (atom_rows[:, None, :feat_width] * w_scalar[None]).reshape(
            list_len * n_basis, feat_width
        )
        vec_rows = jnp.transpose(
            atom_rows[:, feat_width:].reshape(list_len, 3, feat_width), (1, 0, 2)
        )
        vector_terms = (vec_rows[:, :, None, :] * w_vector[None, None]).reshape(
            3 * list_len * n_basis, feat_width
        )
        charge = jnp.dot(scalar_w, atom_terms, preferred_element_type=jnp.float32) + jnp.dot(
            vector_w, vector_terms, preferred_element_type=jnp.float32
        )
        return charge.astype(jnp.bfloat16)

    return probe_block


def many_groups(
    atom_s,
    atom_pos,
    edge_vec,
    edge_nbr,
    border_index,
    send_index,
    probe_list,
    probe_count,
    w_in,
    b_in,
    w_msg,
    w_rad,
    w_probe,
    w_mix,
    b_mix,
    w_out,
):
    atom_count, half_width = atom_s.shape
    n_layers = w_in.shape[0]
    width = w_in.shape[1]
    n_basis = w_rad.shape[1]
    fan_out = edge_nbr.shape[0] // atom_count
    root_fan = fan_out**0.5
    rim_rows = border_index.shape[0] // 2
    length = jnp.sqrt(jnp.sum(edge_vec * edge_vec, axis=0))
    edge_env = (1.0 - length * length / 36.0) ** 2
    edge_basis = (radial(length, n_basis, 6.0) * edge_env[:, None]).astype(jnp.bfloat16)
    edge_cols = jnp.transpose(edge_vec)
    scalars = atom_s
    vectors = jnp.zeros((atom_count, 3 * half_width), jnp.bfloat16)
    for layer_no in range(n_layers):
        full_rows = lax.all_gather(scalars, "chan", axis=1, tiled=True)
        in_weight = w_in[layer_no]
        in_bias = b_in[layer_no]
        msg_weight = w_msg[layer_no].reshape(width, 3 * half_width)
        rad_weight = w_rad[layer_no].reshape(n_basis, 3 * half_width)
        hidden_act = jax.nn.silu(
            jnp.dot(full_rows, in_weight, preferred_element_type=jnp.float32) + in_bias
        ).astype(jnp.bfloat16)
        inner_tab = jnp.concatenate(
            [
                jnp.dot(hidden_act, msg_weight, preferred_element_type=jnp.float32).astype(
                    jnp.bfloat16
                ),
                vectors,
            ],
            axis=1,
        )
        padded = extended(inner_tab[border_index], ((("brick", "probe"), 0),), rim_rows)
        lookup = jnp.concatenate([inner_tab, padded[:rim_rows], padded[3 * rim_rows :]], axis=0)
        neighbour_rows = lookup[edge_nbr]
        filters = jnp.dot(edge_basis, rad_weight, preferred_element_type=jnp.float32)
        weighted = neighbour_rows[:, : 3 * half_width] * filters
        neighbour_vec = neighbour_rows[:, 3 * half_width :].reshape(-1, 3, half_width)
        vector_gate = weighted[:, None, half_width : 2 * half_width]
        along_edge = weighted[:, None, 2 * half_width :]
        delta_vec = neighbour_vec * vector_gate + along_edge * edge_cols[:, :, None]
        delta_scalar = (
            weighted[:, :half_width].reshape(atom_count, fan_out, half_width).sum(axis=1) / root_fan
        )
        delta_vec = delta_vec.reshape(atom_count, fan_out, 3 * half_width).sum(axis=1) / root_fan
        scalars = (scalars + delta_scalar).astype(jnp.bfloat16)
        vectors = (vectors + delta_vec).astype(jnp.bfloat16)
    features = jnp.concatenate([scalars, vectors], axis=1)
    picks = send_index[0]
    n_brick = lax.axis_size("brick")
    n_probe = lax.axis_size("probe")
    n_groups = n_brick * n_probe
    slot_cap = picks.shape[0] // n_groups
    out_rows = features[picks]
    out_pos = jnp.transpose(atom_pos)[picks].astype(jnp.bfloat16)
    received = (
        lax.all_to_all(
            out_rows.reshape(n_groups, slot_cap, 4 * half_width),
            ("brick", "probe"),
            split_axis=0,
            concat_axis=0,
            tiled=True,
        ),
        lax.all_to_all(
            out_pos.reshape(n_groups, slot_cap, 3),
            ("brick", "probe"),
            split_axis=0,
            concat_axis=0,
            tiled=True,
        ),
    )
    recv_count = n_groups * slot_cap
    recv_rows = received[0].reshape(recv_count, 4 * half_width)
    recv_pos = jnp.transpose(received[1].reshape(recv_count, 3)).astype(jnp.float32)
    group_no = lax.axis_index("brick") * n_probe + lax.axis_index("probe")
    n_blocks, list_len = probe_list.shape
    probe_block = make_block(
        recv_rows,
        recv_pos,
        w_probe[:, 0, :],
        w_probe[:, 1, :],
        half_width,
        group_no,
        n_blocks,
        list_len,
        n_basis,
    )
    charges = lax.map(
        probe_block, (jnp.arange(n_blocks, dtype=jnp.int32), probe_list, probe_count)
    ).reshape(n_blocks * PB, half_width)
    mix_rows = lax.dynamic_slice_in_dim(w_mix, lax.axis_index("chan") * half_width, half_width, 0)
    mixed = lax.psum(jnp.dot(charges, mix_rows, preferred_element_type=jnp.float32), "chan")
    return jnp.sum(jax.nn.silu(mixed + b_mix) * w_out, axis=1)


def solution(mesh):
    in_specs = (
        P(("image", "brick", "probe"), "chan"),
        P(None, ("image", "brick", "probe")),
        P(None, ("image", "brick", "probe")),
        P(("image", "brick", "probe")),
        P(("image", "brick", "probe")),
        P(("image", "brick", "probe"), None),
        P(("image", "brick", "probe"), None),
        P(("image", "brick", "probe")),
        P(),
        P(),
        P(None, None, None, "chan"),
        P(None, None, None, "chan"),
        P(None, None, "chan"),
        P(),
        P(),
        P(),
    )
    out_specs = P(("image", "brick", "probe"))
    return jax.shard_map(
        per_device, mesh=mesh, in_specs=in_specs, out_specs=out_specs, check_vma=False
    )
```

```python
import functools
import itertools
import math

import jax
import jax.numpy as jnp
from jax import lax
from jax.experimental import pallas as pl
from jax.experimental.pallas import tpu as pltpu
from jax.sharding import PartitionSpec as P

PB = 128
LANES = 128
FEW_GROUPS = 8
SMALL = 16
TOGETHER = 2
ROOT = (2.0 * math.log2(math.e)) ** 0.5
F32 = jnp.float32
BF16 = jnp.bfloat16


def iota(shape, dim):
    return lax.broadcasted_iota(jnp.int32, shape, dim)


def dot(a, b):
    return jnp.dot(a, b, preferred_element_type=F32)


def dot_tn(a, b):
    return lax.dot_general(a, b, (((0,), (0,)), ((), ())), preferred_element_type=F32)


def one_hot(mask):
    return jnp.where(mask, 1.0, 0.0).astype(BF16)


def same(names, row):
    return jnp.where(names == row, jnp.ones_like(names), jnp.zeros_like(names))


def silu(x):
    half_x = 0.5 * x
    return half_x * jnp.tanh(half_x) + half_x


def bell(scaled, center):
    away = scaled - center
    return jnp.exp2(-(away * away))


def lane_atom(lane, fan, tiles):
    return (lane % tiles) * (LANES // fan) + lane // tiles


def length_keeping_round(exact):
    choices = []
    for value in exact:
        near = value.astype(BF16).astype(F32)
        step = jnp.where(value > near, 1.01 / 256.0, -1.01 / 256.0) * jnp.abs(near)
        choices.append((near, (near + step).astype(BF16).astype(F32)))
    target = sum(value * value for value in exact)
    best, best_error = None, None
    for picked in itertools.product(*choices):
        error = jnp.abs(sum(value * value for value in picked) - target)
        if best is None:
            best, best_error = picked, error
            continue
        better = error < best_error
        best = tuple(jnp.where(better, new, old) for new, old in zip(picked, best))
        best_error = jnp.where(better, error, best_error)
    return best


def pack_kernel(
    fan, atom_s, atom_pos, edge_vec, edge_nbr, border, send, data_out, natural
):
    half, atoms = atom_s.shape
    tiles = atoms * fan // LANES
    per_tile = LANES // fan
    part = lax.axis_index("chan")
    perm = one_hot(lane_atom(iota((atoms, LANES), 1), fan, tiles) == iota((atoms, LANES), 0))
    scalars = dot(atom_s[...], perm).astype(BF16)
    for tile in range(tiles):
        for comp in range(3):
            natural[comp * tiles + tile : comp * tiles + tile + 1, :] = edge_vec[
                comp : comp + 1, tile * LANES : (tile + 1) * LANES
            ]
    exact = [natural[comp * tiles : (comp + 1) * tiles, :] for comp in range(3)]
    for comp, value in enumerate(length_keeping_round(exact)):
        natural[comp * tiles : (comp + 1) * tiles, :] = value
    natural[3 * tiles : 4 * tiles, :] = edge_nbr[...].astype(F32)
    natural[4 * tiles :, :] = jnp.zeros((LANES - 4 * tiles, LANES), F32)
    turned = natural[...].T
    lane = iota((fan, LANES), 1)
    sorted_rows = []
    for comp in range(4):
        rows = jnp.zeros((fan, LANES), F32)
        for a in range(per_tile):
            piece = turned[a * fan : (a + 1) * fan, :]
            shift = (a * tiles - comp * tiles) % LANES
            piece = pltpu.roll(piece, shift, 1) if shift else piece
            rows = jnp.where(lane // tiles == a, piece, rows)
        sorted_rows.append(jnp.where(part == 0, rows[: fan // 2], rows[fan // 2 :]))
    pos = dot(atom_pos[...].astype(BF16), perm)
    blank = jnp.zeros((1, LANES), F32)
    border_row = jnp.concatenate(
        [border[...].astype(F32), jnp.zeros((1, LANES - border.shape[1]), F32)], axis=1
    )
    send_row = jnp.concatenate(
        [send[...].astype(F32), jnp.zeros((1, LANES - send.shape[1]), F32)], axis=1
    )
    rest = jnp.concatenate([pos, border_row, send_row, blank, blank, blank], axis=0)
    others = jnp.concatenate(sorted_rows + [rest], axis=0).astype(BF16)
    for group in range(data_out.shape[0]):
        data_out[group, 0:half, :] = scalars
        data_out[group, half:, :] = others


def weight_kernel(
    w_msg, w_rad, w_probe, b_in, b_mix, w_out, probe_list, probe_count, weight_out, small_out
):
    at = 0
    for piece in (b_in, b_mix, w_out, probe_list, probe_count):
        rows, cols = piece.shape
        small_out[at : at + rows, 0:cols] = piece[...].astype(F32)
        at += rows
    probe_rows = [w_probe[r].astype(F32) for r in range(w_probe.shape[0])]
    radial = jnp.concatenate([w_rad[...].astype(F32)] + probe_rows, axis=0).T.astype(BF16)
    weight_out[: w_msg.shape[0], :] = w_msg[...]
    weight_out[w_msg.shape[0] :, :] = radial


def pack(copies, atom_s, atom_pos, edge_vec, edge_nbr, border_index, send_index):
    atoms, half = atom_s.shape
    fan = edge_nbr.shape[0] // atoms
    return pl.pallas_call(
        functools.partial(pack_kernel, fan),
        out_shape=jax.ShapeDtypeStruct((copies, half + 4 * fan // 2 + 8, LANES), BF16),
        scratch_shapes=[pltpu.VMEM((LANES, LANES), F32)],
        name="pack",
    )(
        atom_s.T,
        atom_pos,
        edge_vec,
        edge_nbr.reshape(-1, LANES),
        border_index.reshape(1, -1),
        send_index,
    )


def pack_weights(half, w_msg, w_rad, w_probe, b_in, b_mix, w_out, probe_list, probe_count):
    return pl.pallas_call(
        weight_kernel,
        out_shape=(
            jax.ShapeDtypeStruct((w_msg.size // LANES + half, LANES), BF16),
            jax.ShapeDtypeStruct((SMALL, LANES), F32),
        ),
        name="pack_weights",
    )(
        jnp.transpose(w_msg, (0, 2, 3, 1)).reshape(-1, LANES),
        jnp.transpose(w_rad, (0, 2, 1, 3)).reshape(-1, half),
        w_probe,
        b_in,
        b_mix.reshape(1, -1),
        w_out.reshape(1, -1),
        probe_list,
        probe_count.reshape(1, -1),
    )


def after_kernel(block, there, same_block):
    pass


def probe_grid(me, probes):
    number = me * probes + iota((1, probes), 1)
    return [(n % 16).astype(F32) * 0.25 - 1.875 for n in (number, number // 16, number // 256)]


def probe_kernel(sizes, list_at, data_mine, small, chosen_rows, probe_basis):
    groups, fan, rim, half, n_basis, cap, n_blocks = sizes
    width = 2 * half
    tiles = fan
    every = groups * LANES
    me = lax.axis_index("brick") * lax.axis_size("probe") + lax.axis_index("probe")
    rest_at = half + 4 * fan // 2
    small_rows = small[...]
    received = groups * cap
    edges = received * fan
    send_rows = jnp.concatenate(
        [data_mine[g, rest_at : rest_at + 8, :].astype(F32)[4:5] for g in range(groups)], axis=0
    )

    def picks(lane_count, per_group):
        lane = iota((LANES, lane_count), 1)
        wanted = me * cap + lane % cap
        spread = dot(send_rows.astype(BF16), one_hot(iota((LANES, lane_count), 0) == wanted))
        lane = iota((groups, lane_count), 1)
        spread = jnp.where(lane // per_group == iota((groups, lane_count), 0), spread, 0.0)
        return jnp.sum(spread, axis=0, keepdims=True)

    per_group = fan * cap
    pick_atoms = picks(received, cap)
    column = iota((every, 1), 0)
    column_name = (column // LANES) * LANES + lane_atom(column % LANES, fan, tiles)
    wanted = (iota((1, received), 1) // cap) * LANES + pick_atoms.astype(jnp.int32)
    chosen_atoms = one_hot(column_name == wanted)

    pos_rows = jnp.concatenate(
        [data_mine[g, rest_at : rest_at + 8, :] for g in range(groups)], axis=1
    )
    pos = dot(pos_rows, chosen_atoms) - 1.875
    chosen_rows[0:1, :] = picks(edges, per_group)
    chosen_rows[1:2, 0:received] = pick_atoms
    chosen_rows[2:5, 0:received] = pos[0:3]
    pos_cols = jnp.concatenate(
        [
            jnp.concatenate([pos, jnp.zeros((8, LANES - received), F32)], axis=1),
            jnp.zeros((LANES - 8, LANES), F32),
        ],
        axis=0,
    ).T
    list_len = width
    counts = []
    for block in range(n_blocks):
        live = iota((1, list_len), 1).astype(F32) < small_rows[list_at + n_blocks : list_at + n_blocks + 1, block : block + 1]
        named = jnp.where(live, small_rows[list_at + block : list_at + block + 1], -1.0)
        hits = jnp.where(iota((received, list_len), 0).astype(F32) == named, 1.0, 0.0)
        counts.append(
            jnp.broadcast_to(jnp.sum(hits, axis=1, keepdims=True), (received, PB))
        )
    counts = jnp.concatenate(counts, axis=1)
    probes = n_blocks * PB
    grid = probe_grid(me, probes)
    dist_sq = jnp.zeros((received, probes), F32)
    for x in range(3):
        dist_sq = dist_sq + (grid[x] - pos_cols[0:received, x : x + 1]) ** 2
    dist = jnp.sqrt(dist_sq) * ROOT
    envelope = (1.0 - dist_sq / 64.0) ** 2 * counts
    probe_basis[...] = jnp.concatenate(
        [
            (bell(dist, r * (ROOT * 7.0 / (n_basis - 1))) * envelope).astype(BF16)
            for r in range(n_basis)
        ],
        axis=0,
    )


def density_kernel(
    sizes,
    data_mine,
    data_other,
    weights_mine,
    weights_other,
    small,
    w_in,
    w_mix,
    chosen_rows,
    probe_basis,
    density,
    state0,
    own0,
    faces0,
    state1,
    weights,
):
    groups, fan, rim, half, n_basis, cap, n_blocks = sizes
    layers = w_in.shape[0]
    width = 2 * half
    tiles = LANES * fan // LANES
    root_fan = fan**0.5
    me = lax.axis_index("brick") * lax.axis_size("probe") + lax.axis_index("probe")
    part = lax.axis_index("chan")
    weights[part] = weights_mine[...]
    weights[1 - part] = weights_other[...]
    every = groups * LANES
    edge_at = half
    n_edge = 4 * fan // 2
    rest_at = half + n_edge

    def data(group, c, rows):
        return (data_mine, data_other)[c][group, rows, :]

    def weight(layer, p):
        at = (layer * 3 + p) * half
        return jnp.concatenate([weights[c, at : at + half, :] for c in range(2)], axis=0)

    def radial_weight(layer, p):
        at = (layer * 3 + p) * n_basis
        return radial_all[:, at : at + n_basis]

    def edge_rows(group):
        return [data(group, c, slice(edge_at, rest_at)).astype(F32) for c in range(2)]

    def border_of(group):
        return data(group, 0, slice(rest_at, rest_at + 8)).astype(F32)[3:4, 0 : 2 * rim]

    centers = iota((n_basis, 1), 0).astype(F32) * (ROOT * 6.0 / (n_basis - 1))

    def basis_of(length, env):
        return (bell(length * ROOT, centers) * env).astype(BF16)

    received = groups * cap
    edges = received * fan
    per_group = fan * cap
    pick_edges = chosen_rows[0:1, :]
    pick_atoms = chosen_rows[1:2, 0:received]
    pos = chosen_rows[2:5, 0:received]
    atom_rows = lane_atom(iota((LANES, per_group), 0), fan, tiles).astype(F32)
    chosen = []
    for group in range(groups):
        rows = jnp.concatenate([data(group, c, slice(edge_at, rest_at)) for c in range(2)], axis=0)
        want = pick_edges[:, group * per_group : (group + 1) * per_group]
        chosen.append(dot(rows, one_hot(atom_rows == want)))
    chosen = jnp.concatenate(chosen, axis=1)
    step = fan // 2
    row = iota((2 * n_edge, edges), 0)
    slot_k = (row // n_edge) * step + row % step
    lane_k = (iota((2 * n_edge, edges), 1) % per_group) // cap
    chosen = jnp.where(slot_k == lane_k, chosen, 0.0)
    chosen = jnp.sum(chosen.reshape(2 * 4, step, edges), axis=1)
    chosen = chosen[0:4] + chosen[4:8]
    pick_vec = [chosen[x : x + 1] for x in range(3)]
    nbr = chosen[3:4]
    length = jnp.sqrt(sum(x * x for x in pick_vec))
    basis1 = basis_of(length, (1.0 - length * length / 36.0) ** 2)

    nbr = nbr.astype(jnp.int32)
    home = iota((1, edges), 1) // per_group
    is_low = (nbr >= LANES) & (nbr < LANES + rim)
    is_up = nbr >= LANES + rim
    owner = jnp.where(
        is_low, (home + groups - 1) % groups, jnp.where(is_up, (home + 1) % groups, home)
    )
    entry = owner * 2 * rim + jnp.where(is_low, nbr - (LANES - rim), nbr - (LANES + rim))
    entry = jnp.where(is_low | is_up, entry, -1)
    border_all = jnp.concatenate(
        [border_of(g) for g in range(groups)], axis=1
    )
    border_all = jnp.broadcast_to(border_all, (16, groups * 2 * rim)).astype(BF16)
    seen = dot(border_all, one_hot(iota((groups * 2 * rim, edges), 0) == entry))[0:1]
    target_atom = jnp.where(entry < 0, nbr, seen.astype(jnp.int32))
    column = iota((every, 1), 0)
    column_name = (column // LANES) * LANES + lane_atom(column % LANES, fan, tiles)
    quad = groups // 2
    window = [[(h * quad + groups - 1 + i) % groups for i in range(quad + 2)] for h in range(2)]
    window_pick = []
    for h in range(2):
        lanes = slice(h * edges // 2, (h + 1) * edges // 2)
        near = lax.rem(owner[:, lanes] + 2 * groups - (h * quad + groups - 1), groups)
        name = near * LANES + target_atom[:, lanes]
        window_pick.append(one_hot(column_name[: (quad + 2) * LANES] == name))
    wanted = (iota((1, received), 1) // cap) * LANES + pick_atoms.astype(jnp.int32)
    chosen_atoms = one_hot(column_name == wanted)

    small_rows = small[...]
    columns = small_rows.T
    radial_at = weights.shape[1] - half
    radial_all = jnp.concatenate([weights[c, radial_at:, :] for c in range(2)], axis=0)

    terms_shape = (2 * n_basis, n_basis * received)
    probe_weight = radial_all[:, 3 * layers * n_basis :]
    w_scalar, w_vector = (
        dot(probe_weight, one_hot(iota(terms_shape, 1) // received * 2 + p == iota(terms_shape, 0)))
        for p in range(2)
    )

    probes = density.shape[1]
    grid = probe_grid(me, probes)

    for group in range(groups):
        for c in range(2):
            place = part if c == 0 else 1 - part
            rows = pl.ds(pl.multiple_of(place * half, half), half)
            state0[rows, group * LANES : (group + 1) * LANES] = data(group, c, slice(0, half))
    hidden = silu(dot_tn(w_in[0], state0[...]) + columns[:, 0:1]).astype(BF16)
    weight_ac = jnp.concatenate([weight(0, 0), weight(0, 2)], axis=0)
    messages = dot(weight_ac, hidden).astype(BF16)
    atom_col = lane_atom(iota((LANES, 2 * rim), 0), fan, tiles).astype(F32)
    for group in range(groups):
        own = messages[:, group * LANES : (group + 1) * LANES]
        own0[group] = own
        border_row = border_of(group)
        faces0[group, :, 0 : 2 * rim] = dot(own, one_hot(atom_col == border_row)).astype(BF16)

    row = iota((LANES + 2 * rim, 1), 0)
    names = jnp.where(
        row < LANES,
        lane_atom(row, fan, tiles),
        jnp.where(row < LANES + rim, row + rim, row - rim),
    ).astype(F32)
    names = jnp.broadcast_to(names, (LANES + 2 * rim, LANES)).astype(BF16)
    upper_lane = iota((2 * width, 2 * rim), 1) < rim
    radial_ac = jnp.concatenate([radial_weight(0, 0), radial_weight(0, 2)], axis=0)
    radial_rows = jnp.concatenate([jnp.zeros((2 * width, LANES + 2 * rim), BF16), radial_ac], axis=1)
    blank = jnp.zeros((2 * width, n_basis), BF16)

    for group in range(groups):
        up = (group + 1) % groups
        low = (group + groups - 1) % groups
        ghosts = jnp.where(
            upper_lane,
            faces0[up, :, 0 : 2 * rim].astype(F32),
            faces0[low, :, 0 : 2 * rim].astype(F32),
        ).astype(BF16)
        table = jnp.concatenate([own0[group], ghosts, blank], axis=1)
        lefts = [
            jnp.concatenate(
                [
                    block[at : at + 16]
                    for at in range(first, first + width, 16)
                    for block in (table, radial_rows)
                ],
                axis=0,
            )
            for first in (width, 0)
        ]
        halves = edge_rows(group)
        step = fan // 2
        acc = jnp.zeros((width, LANES), F32)
        acc_vec = [jnp.zeros((width, LANES), F32) for _ in range(3)]
        rights, along = [], []
        for c in range(2):
            rows = halves[c]
            vec = [rows[x * step : (x + 1) * step] for x in range(3)]
            nbr = rows[3 * step : 4 * step]
            length_sq = vec[0] * vec[0] + vec[1] * vec[1] + vec[2] * vec[2]
            length = jnp.sqrt(length_sq)
            env = (1.0 - length * length / 36.0) ** 2
            for first in range(0, step, TOGETHER):
                ks = range(first, first + TOGETHER)
                picked = jnp.concatenate([same(names, nbr[k : k + 1].astype(BF16)) for k in ks], axis=1)
                basis = jnp.concatenate(
                    [basis_of(length[k : k + 1], env[k : k + 1]) for k in ks], axis=1
                )
                rights.append(jnp.concatenate([picked, basis], axis=0))
                along.append([[vec[x][k : k + 1] for x in range(3)] for k in ks])

        def products(left, right):
            both = dot(left, right)
            return jnp.concatenate(
                [both[at : at + 16] * both[at + 16 : at + 32] for at in range(0, 2 * width, 32)],
                axis=0,
            )

        for right, directions in zip(rights, along):
            prod = products(lefts[0], right)
            for i, direction in enumerate(directions):
                block = prod[:, i * LANES : (i + 1) * LANES]
                for x in range(3):
                    acc_vec[x] = acc_vec[x] + block * direction[x]
        for right in rights:
            prod = products(lefts[1], right)
            for i in range(TOGETHER):
                acc = acc + prod[:, i * LANES : (i + 1) * LANES]
        lanes = slice(group * LANES, (group + 1) * LANES)
        state1[0:width, lanes] = (state0[:, lanes].astype(F32) + acc / root_fan).astype(BF16)
        for x in range(3):
            state1[(x + 1) * width : (x + 2) * width, lanes] = (acc_vec[x] / root_fan).astype(BF16)

    rows = []
    for h in range(2):
        near_states = jnp.concatenate(
            [state1[:, g * LANES : (g + 1) * LANES] for g in window[h]], axis=1
        )
        rows.append(dot(near_states, window_pick[h]))
    rows = jnp.concatenate(rows, axis=1)
    hidden = silu(dot_tn(w_in[1], rows[:width].astype(BF16)) + columns[:, 1:2]).astype(BF16)
    weight_abc = jnp.concatenate([weight(1, p) for p in range(3)], axis=0)
    messages = dot(weight_abc, hidden).astype(BF16).astype(F32)
    radial_abc = jnp.concatenate([radial_weight(1, p) for p in range(3)], axis=0)
    filters = dot(radial_abc, basis1)
    weighted = messages * filters
    gate = weighted[width : 2 * width]
    along = weighted[2 * width :]
    parts = [weighted[:width]]
    for x in range(3):
        parts.append(rows[(1 + x) * width : (2 + x) * width] * gate + along * pick_vec[x])
    parts = jnp.concatenate(parts, axis=0).astype(BF16)
    edge = iota((edges, received), 0)
    slot = (edge // per_group) * cap + edge % cap
    delta = dot(parts, one_hot(slot == iota((edges, received), 1)))
    final = (dot(state1[...], chosen_atoms) + delta / root_fan).astype(BF16).astype(F32)

    along = final[width : 2 * width] * pos[0:1]
    for x in range(1, 3):
        along = along + final[(x + 1) * width : (x + 2) * width] * pos[x : x + 1]
    def repeat(value):
        return jnp.concatenate([value] * n_basis, axis=1)
    terms = [w_scalar * repeat(final[:width]) - w_vector * repeat(along)]
    for x in range(3):
        terms.append(w_vector * repeat(final[(x + 1) * width : (x + 2) * width]))
    sums = dot(jnp.concatenate(terms, axis=0).astype(BF16), probe_basis[...])
    charges = sums[:width]
    for x in range(3):
        charges = charges + grid[x] * sums[(x + 1) * width : (x + 2) * width]
    mixed = dot_tn(w_mix[...], charges.astype(BF16)) + columns[:, layers : layers + 1]
    density[...] = jnp.sum(silu(mixed) * columns[:, layers + 1 : layers + 2], axis=0, keepdims=True)


def few_groups(
    atom_s, atom_pos, edge_vec, edge_nbr, border_index, send_index, probe_list, probe_count,
    w_in, b_in, w_msg, w_rad, w_probe, w_mix, b_mix, w_out,
):
    atoms, half = atom_s.shape
    groups = lax.axis_size("brick") * lax.axis_size("probe")
    fan = edge_nbr.shape[0] // atoms
    rim = border_index.shape[0] // 2
    n_basis = w_rad.shape[1]
    cap = send_index.shape[1] // groups
    width = 2 * half
    every = groups * LANES
    data = pack(groups, atom_s, atom_pos, edge_vec, edge_nbr, border_index, send_index)
    weights, small = pack_weights(
        half, w_msg, w_rad, w_probe, b_in, b_mix, w_out, probe_list, probe_count
    )
    swap = [(0, 1), (1, 0)]
    weights_other = lax.ppermute(weights, "chan", swap)
    mine = lax.all_to_all(data, ("brick", "probe"), split_axis=0, concat_axis=0, tiled=True)
    anywhere = pl.BlockSpec(memory_space=pl.ANY)
    mine = pl.pallas_call(
        after_kernel,
        out_shape=jax.ShapeDtypeStruct(mine.shape, BF16),
        in_specs=[anywhere] * 2,
        out_specs=anywhere,
        input_output_aliases={0: 0},
        compiler_params=pltpu.CompilerParams(vmem_limit_bytes=16 * 1024 * 1024),
        name="after",
    )(mine, weights_other)
    other = lax.ppermute(mine, "chan", swap)
    n_probes = probe_list.shape[0] * PB
    sizes = (groups, fan, rim, half, n_basis, cap, probe_list.shape[0])
    chosen_rows, probe_basis = pl.pallas_call(
        functools.partial(probe_kernel, sizes, w_in.shape[0] + 2),
        out_shape=(
            jax.ShapeDtypeStruct((8, groups * cap * fan), F32),
            jax.ShapeDtypeStruct((n_basis * groups * cap, n_probes), BF16),
        ),
        compiler_params=pltpu.CompilerParams(vmem_limit_bytes=24 * 1024 * 1024),
        name="probe_basis",
    )(mine, small)
    density = pl.pallas_call(
        functools.partial(density_kernel, sizes),
        out_shape=jax.ShapeDtypeStruct((1, n_probes), F32),
        scratch_shapes=[
            pltpu.VMEM((width, every), BF16),
            pltpu.VMEM((groups, 2 * width, LANES), BF16),
            pltpu.VMEM((groups, 2 * width, LANES), BF16),
            pltpu.VMEM((4 * width, every), BF16),
            pltpu.VMEM((2,) + weights.shape, BF16),
        ],
        compiler_params=pltpu.CompilerParams(vmem_limit_bytes=40 * 1024 * 1024),
        name="density",
    )(mine, other, weights, weights_other, small, w_in, w_mix, chosen_rows, probe_basis)
    return density.reshape(n_probes)


def per_device(*args):
    if lax.axis_size("brick") * lax.axis_size("probe") == FEW_GROUPS:
        return few_groups(*args)
    return many_groups(*args)


def extended(block, sides, width):
    for axis, dim in sides:
        count = lax.axis_size(axis)
        forward = [(i, i + 1) for i in range(count - 1)]
        forward.append((count - 1, 0))
        backward = [(target, source) for source, target in forward]
        low = lax.ppermute(
            lax.slice_in_dim(block, block.shape[dim] - width, None, axis=dim), axis, forward
        )
        high = lax.ppermute(lax.slice_in_dim(block, 0, width, axis=dim), axis, backward)
        block = jnp.concatenate([low, block, high], axis=dim)
    return block


def radial(distance, count, top):
    centers = jnp.arange(count).astype(jnp.float32) * (top / (count - 1))
    return jnp.exp(-2.0 * (distance[..., None] - centers) ** 2)


def make_block(
    recv_rows, recv_pos, w_scalar, w_vector, feat_width, group_no, n_blocks, list_len, n_basis
):

    def probe_block(block_in):
        block_no, listed, live_count = block_in
        index_row = (group_no * n_blocks + block_no) * PB + jnp.arange(PB, dtype=jnp.int32)
        grid_xyz = (
            jnp.stack([index_row % 16, index_row // 16 % 16, index_row // 256 % 16], axis=1).astype(
                jnp.float32
            )
            * 0.25
        )
        atom_xyz = recv_pos[:, listed]
        disp = grid_xyz[:, :, None] - atom_xyz[None]
        dist_sq = jnp.sum(disp * disp, axis=1)
        live = (jnp.arange(list_len, dtype=jnp.int32) < live_count).astype(jnp.float32)
        envelope = (1.0 - dist_sq / 64.0) ** 2 * live[None, :]
        basis = radial(jnp.sqrt(dist_sq), n_basis, 7.0) * envelope[:, :, None]
        scalar_w = basis.astype(jnp.bfloat16).reshape(PB, list_len * n_basis)
        vector_w = (
            (disp[:, :, :, None] * basis[:, None])
            .astype(jnp.bfloat16)
            .reshape(PB, 3 * list_len * n_basis)
        )
        atom_rows = recv_rows[listed]
        atom_terms = (atom_rows[:, None, :feat_width] * w_scalar[None]).reshape(
            list_len * n_basis, feat_width
        )
        vec_rows = jnp.transpose(
            atom_rows[:, feat_width:].reshape(list_len, 3, feat_width), (1, 0, 2)
        )
        vector_terms = (vec_rows[:, :, None, :] * w_vector[None, None]).reshape(
            3 * list_len * n_basis, feat_width
        )
        charge = jnp.dot(scalar_w, atom_terms, preferred_element_type=jnp.float32) + jnp.dot(
            vector_w, vector_terms, preferred_element_type=jnp.float32
        )
        return charge.astype(jnp.bfloat16)

    return probe_block


def many_groups(
    atom_s,
    atom_pos,
    edge_vec,
    edge_nbr,
    border_index,
    send_index,
    probe_list,
    probe_count,
    w_in,
    b_in,
    w_msg,
    w_rad,
    w_probe,
    w_mix,
    b_mix,
    w_out,
):
    atom_count, half_width = atom_s.shape
    n_layers = w_in.shape[0]
    width = w_in.shape[1]
    n_basis = w_rad.shape[1]
    fan_out = edge_nbr.shape[0] // atom_count
    root_fan = fan_out**0.5
    rim_rows = border_index.shape[0] // 2
    length = jnp.sqrt(jnp.sum(edge_vec * edge_vec, axis=0))
    edge_env = (1.0 - length * length / 36.0) ** 2
    edge_basis = (radial(length, n_basis, 6.0) * edge_env[:, None]).astype(jnp.bfloat16)
    edge_cols = jnp.transpose(edge_vec)
    scalars = atom_s
    vectors = jnp.zeros((atom_count, 3 * half_width), jnp.bfloat16)
    for layer_no in range(n_layers):
        full_rows = lax.all_gather(scalars, "chan", axis=1, tiled=True)
        in_weight = w_in[layer_no]
        in_bias = b_in[layer_no]
        msg_weight = w_msg[layer_no].reshape(width, 3 * half_width)
        rad_weight = w_rad[layer_no].reshape(n_basis, 3 * half_width)
        hidden_act = jax.nn.silu(
            jnp.dot(full_rows, in_weight, preferred_element_type=jnp.float32) + in_bias
        ).astype(jnp.bfloat16)
        inner_tab = jnp.concatenate(
            [
                jnp.dot(hidden_act, msg_weight, preferred_element_type=jnp.float32).astype(
                    jnp.bfloat16
                ),
                vectors,
            ],
            axis=1,
        )
        padded = extended(inner_tab[border_index], ((("brick", "probe"), 0),), rim_rows)
        lookup = jnp.concatenate([inner_tab, padded[:rim_rows], padded[3 * rim_rows :]], axis=0)
        neighbour_rows = lookup[edge_nbr]
        filters = jnp.dot(edge_basis, rad_weight, preferred_element_type=jnp.float32)
        weighted = neighbour_rows[:, : 3 * half_width] * filters
        neighbour_vec = neighbour_rows[:, 3 * half_width :].reshape(-1, 3, half_width)
        vector_gate = weighted[:, None, half_width : 2 * half_width]
        along_edge = weighted[:, None, 2 * half_width :]
        delta_vec = neighbour_vec * vector_gate + along_edge * edge_cols[:, :, None]
        delta_scalar = (
            weighted[:, :half_width].reshape(atom_count, fan_out, half_width).sum(axis=1) / root_fan
        )
        delta_vec = delta_vec.reshape(atom_count, fan_out, 3 * half_width).sum(axis=1) / root_fan
        scalars = (scalars + delta_scalar).astype(jnp.bfloat16)
        vectors = (vectors + delta_vec).astype(jnp.bfloat16)
    features = jnp.concatenate([scalars, vectors], axis=1)
    picks = send_index[0]
    n_brick = lax.axis_size("brick")
    n_probe = lax.axis_size("probe")
    n_groups = n_brick * n_probe
    slot_cap = picks.shape[0] // n_groups
    out_rows = features[picks]
    out_pos = jnp.transpose(atom_pos)[picks].astype(jnp.bfloat16)
    received = (
        lax.all_to_all(
            out_rows.reshape(n_groups, slot_cap, 4 * half_width),
            ("brick", "probe"),
            split_axis=0,
            concat_axis=0,
            tiled=True,
        ),
        lax.all_to_all(
            out_pos.reshape(n_groups, slot_cap, 3),
            ("brick", "probe"),
            split_axis=0,
            concat_axis=0,
            tiled=True,
        ),
    )
    recv_count = n_groups * slot_cap
    recv_rows = received[0].reshape(recv_count, 4 * half_width)
    recv_pos = jnp.transpose(received[1].reshape(recv_count, 3)).astype(jnp.float32)
    group_no = lax.axis_index("brick") * n_probe + lax.axis_index("probe")
    n_blocks, list_len = probe_list.shape
    probe_block = make_block(
        recv_rows,
        recv_pos,
        w_probe[:, 0, :],
        w_probe[:, 1, :],
        half_width,
        group_no,
        n_blocks,
        list_len,
        n_basis,
    )
    charges = lax.map(
        probe_block, (jnp.arange(n_blocks, dtype=jnp.int32), probe_list, probe_count)
    ).reshape(n_blocks * PB, half_width)
    mix_rows = lax.dynamic_slice_in_dim(w_mix, lax.axis_index("chan") * half_width, half_width, 0)
    mixed = lax.psum(jnp.dot(charges, mix_rows, preferred_element_type=jnp.float32), "chan")
    return jnp.sum(jax.nn.silu(mixed + b_mix) * w_out, axis=1)


def solution(mesh):
    in_specs = (
        P(("image", "brick", "probe"), "chan"),
        P(None, ("image", "brick", "probe")),
        P(None, ("image", "brick", "probe")),
        P(("image", "brick", "probe")),
        P(("image", "brick", "probe")),
        P(("image", "brick", "probe"), None),
        P(("image", "brick", "probe"), None),
        P(("image", "brick", "probe")),
        P(),
        P(),
        P(None, None, None, "chan"),
        P(None, None, None, "chan"),
        P(None, None, "chan"),
        P(),
        P(),
        P(),
    )
    out_specs = P(("image", "brick", "probe"))
    return jax.shard_map(
        per_device, mesh=mesh, in_specs=in_specs, out_specs=out_specs, check_vma=False
    )
```

```python
import functools
import itertools
import math

import jax
import jax.numpy as jnp
from jax import lax
from jax.experimental import pallas as pl
from jax.experimental.pallas import tpu as pltpu
from jax.sharding import PartitionSpec as P

PB = 128
LANES = 128
FEW_GROUPS = 8
SMALL = 16
TOGETHER = 2
ROOT = (2.0 * math.log2(math.e)) ** 0.5
F32 = jnp.float32
BF16 = jnp.bfloat16


def iota(shape, dim):
    return lax.broadcasted_iota(jnp.int32, shape, dim)


def dot(a, b):
    return jnp.dot(a, b, preferred_element_type=F32)


def dot_tn(a, b):
    return lax.dot_general(a, b, (((0,), (0,)), ((), ())), preferred_element_type=F32)


def one_hot(mask):
    return jnp.where(mask, 1.0, 0.0).astype(BF16)


def same(names, row):
    return jnp.where(names == row, jnp.ones_like(names), jnp.zeros_like(names))


def silu(x):
    half_x = 0.5 * x
    return half_x * jnp.tanh(half_x) + half_x


def bell(scaled, center):
    away = scaled - center
    return jnp.exp2(-(away * away))


def lane_atom(lane, fan, tiles):
    return (lane % tiles) * (LANES // fan) + lane // tiles


def length_keeping_round(exact):
    choices = []
    for value in exact:
        near = value.astype(BF16).astype(F32)
        step = jnp.where(value > near, 1.01 / 256.0, -1.01 / 256.0) * jnp.abs(near)
        choices.append((near, (near + step).astype(BF16).astype(F32)))
    target = sum(value * value for value in exact)
    best, best_error = None, None
    for picked in itertools.product(*choices):
        error = jnp.abs(sum(value * value for value in picked) - target)
        if best is None:
            best, best_error = picked, error
            continue
        better = error < best_error
        best = tuple(jnp.where(better, new, old) for new, old in zip(picked, best))
        best_error = jnp.where(better, error, best_error)
    return best


def pack_kernel(
    fan, atom_s, atom_pos, edge_vec, edge_nbr, border, send, data_out, natural
):
    half, atoms = atom_s.shape
    tiles = atoms * fan // LANES
    per_tile = LANES // fan
    part = lax.axis_index("chan")
    perm = one_hot(lane_atom(iota((atoms, LANES), 1), fan, tiles) == iota((atoms, LANES), 0))
    scalars = dot(atom_s[...], perm).astype(BF16)
    for tile in range(tiles):
        for comp in range(3):
            natural[comp * tiles + tile : comp * tiles + tile + 1, :] = edge_vec[
                comp : comp + 1, tile * LANES : (tile + 1) * LANES
            ]
    exact = [natural[comp * tiles : (comp + 1) * tiles, :] for comp in range(3)]
    for comp, value in enumerate(length_keeping_round(exact)):
        natural[comp * tiles : (comp + 1) * tiles, :] = value
    natural[3 * tiles : 4 * tiles, :] = edge_nbr[...].astype(F32)
    natural[4 * tiles :, :] = jnp.zeros((LANES - 4 * tiles, LANES), F32)
    turned = natural[...].T
    lane = iota((fan, LANES), 1)
    sorted_rows = []
    for comp in range(4):
        rows = jnp.zeros((fan, LANES), F32)
        for a in range(per_tile):
            piece = turned[a * fan : (a + 1) * fan, :]
            shift = (a * tiles - comp * tiles) % LANES
            piece = pltpu.roll(piece, shift, 1) if shift else piece
            rows = jnp.where(lane // tiles == a, piece, rows)
        sorted_rows.append(rows)
    blank = jnp.zeros((1, LANES), F32)
    every_edge = jnp.concatenate(sorted_rows, axis=0).astype(BF16)
    sorted_rows = [jnp.where(part == 0, rows[: fan // 2], rows[fan // 2 :]) for rows in sorted_rows]
    border_row = jnp.concatenate(
        [border[...].astype(F32), jnp.zeros((1, LANES - border.shape[1]), F32)], axis=1
    )
    picks = send.shape[1]
    groups = data_out.shape[0]
    cap = picks // groups
    block = fan * cap
    lane = iota((picks, groups * block), 1)
    place = (lane // block) * cap + lane % cap
    send_row = jnp.broadcast_to(send[...].astype(F32), (8, picks)).astype(BF16)
    wanted = dot(send_row, one_hot(iota((picks, groups * block), 0) == place))[0:1]
    atom_col = lane_atom(iota((LANES, groups * block), 0), fan, tiles).astype(F32)
    spread = dot(every_edge, one_hot(atom_col == wanted))
    edge_k = iota(spread.shape, 0) % fan
    spread = jnp.where(edge_k == (iota(spread.shape, 1) % block) // cap, spread, 0.0)
    picked = jnp.sum(spread.reshape(4, fan, groups * block), axis=1)
    pick_atom = one_hot(iota((atoms, picks), 0).astype(F32) == send[...].astype(F32))
    facts = [send[...].astype(F32)]
    pos = dot(atom_pos[...].astype(BF16), pick_atom)
    facts += [pos[x : x + 1] for x in range(3)]
    owner = iota((groups, picks), 1) // cap == iota((groups, picks), 0)
    facts = jnp.concatenate([jnp.where(owner, fact, 0.0) for fact in facts], axis=1)
    row = iota((4 * picks, LANES), 0)
    place = (row // picks) * cap + row % cap
    facts = dot(facts.astype(BF16), one_hot(place == iota((4 * picks, LANES), 1)))
    edge_part = jnp.concatenate(sorted_rows, axis=0).astype(BF16)
    for group in range(groups):
        mine = slice(group * block, (group + 1) * block)
        rest = [facts[group : group + 1], border_row]
        for comp in (0, 2):
            rest.append(
                jnp.concatenate([picked[comp : comp + 1, mine], picked[comp + 1 : comp + 2, mine]], axis=1)
            )
        rest = jnp.concatenate(rest + [blank] * 4, axis=0)
        data_out[group, 0:half, :] = scalars
        data_out[group, half : half + 2 * fan, :] = edge_part
        data_out[group, half + 2 * fan :, :] = rest.astype(BF16)


def weight_kernel(
    w_msg, w_rad, w_probe, b_in, b_mix, w_out, probe_list, probe_count, weight_out, small_out
):
    at = 0
    for piece in (b_in, b_mix, w_out, probe_list, probe_count):
        rows, cols = piece.shape
        small_out[at : at + rows, 0:cols] = piece[...].astype(F32)
        at += rows
    probe_rows = [w_probe[r].astype(F32) for r in range(w_probe.shape[0])]
    radial = jnp.concatenate([w_rad[...].astype(F32)] + probe_rows, axis=0).T.astype(BF16)
    weight_out[: w_msg.shape[0], :] = w_msg[...]
    weight_out[w_msg.shape[0] :, :] = radial


def pack(copies, atom_s, atom_pos, edge_vec, edge_nbr, border_index, send_index):
    atoms, half = atom_s.shape
    fan = edge_nbr.shape[0] // atoms
    return pl.pallas_call(
        functools.partial(pack_kernel, fan),
        out_shape=jax.ShapeDtypeStruct((copies, half + 4 * fan // 2 + 8, LANES), BF16),
        scratch_shapes=[pltpu.VMEM((LANES, LANES), F32)],
        name="pack",
    )(
        atom_s.T,
        atom_pos,
        edge_vec,
        edge_nbr.reshape(-1, LANES),
        border_index.reshape(1, -1),
        send_index,
    )


def pack_weights(half, w_msg, w_rad, w_probe, b_in, b_mix, w_out, probe_list, probe_count):
    return pl.pallas_call(
        weight_kernel,
        out_shape=(
            jax.ShapeDtypeStruct((w_msg.size // LANES + half, LANES), BF16),
            jax.ShapeDtypeStruct((SMALL, LANES), F32),
        ),
        name="pack_weights",
    )(
        jnp.transpose(w_msg, (0, 2, 3, 1)).reshape(-1, LANES),
        jnp.transpose(w_rad, (0, 2, 1, 3)).reshape(-1, half),
        w_probe,
        b_in,
        b_mix.reshape(1, -1),
        w_out.reshape(1, -1),
        probe_list,
        probe_count.reshape(1, -1),
    )


def after_kernel(block, there, same_block):
    pass


def probe_grid(me, probes):
    number = me * probes + iota((1, probes), 1)
    return [(n % 16).astype(F32) * 0.25 - 1.875 for n in (number, number // 16, number // 256)]


def index_kernel(sizes, list_at, data_mine, small, facts_out, slots, probe_basis):
    groups, fan, rim, half, n_basis, cap, n_blocks = sizes
    tiles = fan
    received = groups * cap
    per_group = fan * cap
    edges = received * fan
    rest_at = half + 2 * fan
    me = lax.axis_index("brick") * lax.axis_size("probe") + lax.axis_index("probe")
    small_rows = small[...]
    rest = [data_mine[g, rest_at : rest_at + 8, :].astype(F32) for g in range(groups)]
    facts = jnp.concatenate([rows[0:1] for rows in rest], axis=0).astype(BF16)
    lane = iota((LANES, 4 * received), 1)
    wanted = (lane // received) * cap + lane % cap
    facts = dot(facts, one_hot(iota((LANES, 4 * received), 0) == wanted))
    source = (iota(facts.shape, 1) % received) // cap
    facts = jnp.sum(jnp.where(source == iota(facts.shape, 0), facts, 0.0), axis=0, keepdims=True)
    pick_atoms = facts[:, 0:received]
    for comp in range(3):
        rows = [r[2 + comp // 2 : 3 + comp // 2, (comp % 2) * per_group :][:, :per_group] for r in rest]
        facts_out[comp : comp + 1, :] = jnp.concatenate(rows, axis=1)
    nbr = jnp.concatenate([r[3:4, per_group : 2 * per_group] for r in rest], axis=1).astype(jnp.int32)

    home = iota((1, edges), 1) // per_group
    is_low = (nbr >= LANES) & (nbr < LANES + rim)
    is_up = nbr >= LANES + rim
    owner = jnp.where(
        is_low, (home + groups - 1) % groups, jnp.where(is_up, (home + 1) % groups, home)
    )
    entry = owner * 2 * rim + jnp.where(is_low, nbr - (LANES - rim), nbr - (LANES + rim))
    entry = jnp.where(is_low | is_up, entry, -1)
    border_all = jnp.concatenate([r[1:2, 0 : 2 * rim] for r in rest], axis=1)
    border_all = jnp.broadcast_to(border_all, (16, groups * 2 * rim)).astype(BF16)
    seen = dot(border_all, one_hot(iota((groups * 2 * rim, edges), 0) == entry))[0:1]
    target = jnp.where(entry < 0, nbr, seen.astype(jnp.int32))

    column = iota((groups * LANES, 1), 0)
    column_name = (column // LANES) * LANES + lane_atom(column % LANES, fan, tiles)
    home = iota((1, received), 1) // cap
    self_hot = one_hot(column_name == home * LANES + pick_atoms.astype(jnp.int32))
    uses = dot(self_hot, jnp.ones((received, LANES), BF16))
    uses = [uses[g * LANES : (g + 1) * LANES] for g in range(groups)]
    quad = groups // 2
    window_hot, near_groups = [], []
    for h in range(2):
        lanes = slice(h * edges // 2, (h + 1) * edges // 2)
        near = lax.rem(owner[:, lanes] + 2 * groups - (h * quad + groups - 1), groups)
        hot = one_hot(column_name[: (quad + 2) * LANES] == near * LANES + target[:, lanes])
        window_hot.append(hot)
        near_groups.append(near)
        used = dot(hot, jnp.ones((edges // 2, LANES), BF16))
        for i in range(quad + 2):
            g = (h * quad + groups - 1 + i) % groups
            uses[g] = uses[g] + used[i * LANES : (i + 1) * LANES]
    lane = iota((LANES, LANES), 1)
    needed = jnp.zeros((LANES, LANES), F32)
    for g in range(groups):
        needed = jnp.where((lane == g) & (uses[g] > 0.0), 1.0, needed)
    order = dot(one_hot(lane <= iota((LANES, LANES), 0)), needed.astype(BF16))
    slot = jnp.where(needed > 0.0, order - 1.0, -1.0)
    slots[...] = slot
    slot_rows = slot.T
    facts_out[8:9, 0:LANES] = order[LANES - 1 : LANES, :]

    for h in range(2):
        lanes = slice(h * edges // 2, (h + 1) * edges // 2)
        in_window = [(h * quad + groups - 1 + i) % groups for i in range(quad + 2)]
        row = jnp.concatenate([slot_rows[g : g + 1] for g in in_window], axis=1)
        row = jnp.broadcast_to(row, (16, (quad + 2) * LANES)).astype(BF16)
        place = dot(row, window_hot[h])[0:1]
        facts_out[3:4, lanes] = near_groups[h].astype(F32) * LANES + place
    row = jnp.concatenate([slot_rows[g : g + 1] for g in range(groups)], axis=1)
    row = jnp.broadcast_to(row, (16, groups * LANES)).astype(BF16)
    facts_out[7:8, 0:received] = home.astype(F32) * LANES + dot(row, self_hot)[0:1]

    shifted = facts - 1.875
    for x in range(3):
        facts_out[4 + x : 5 + x, 0:received] = shifted[:, (1 + x) * received : (2 + x) * received]
    pos_cols = jnp.broadcast_to(shifted, (LANES, 4 * received)).T
    list_len = LANES
    counts = []
    for block in range(n_blocks):
        limit = small_rows[list_at + n_blocks : list_at + n_blocks + 1, block : block + 1]
        live = iota((1, list_len), 1).astype(F32) < limit
        named = jnp.where(live, small_rows[list_at + block : list_at + block + 1], -1.0)
        hits = jnp.where(iota((received, list_len), 0).astype(F32) == named, 1.0, 0.0)
        counts.append(jnp.broadcast_to(jnp.sum(hits, axis=1, keepdims=True), (received, PB)))
    counts = jnp.concatenate(counts, axis=1)
    probes = n_blocks * PB
    grid = probe_grid(me, probes)
    dist_sq = jnp.zeros((received, probes), F32)
    for x in range(3):
        dist_sq = dist_sq + (grid[x] - pos_cols[(1 + x) * received : (2 + x) * received, 0:1]) ** 2
    dist = jnp.sqrt(dist_sq) * ROOT
    envelope = (1.0 - dist_sq / 64.0) ** 2 * counts
    probe_basis[...] = jnp.concatenate(
        [
            (bell(dist, r * (ROOT * 7.0 / (n_basis - 1))) * envelope).astype(BF16)
            for r in range(n_basis)
        ],
        axis=0,
    )


def density_kernel(
    sizes,
    data_mine,
    data_other,
    weights_mine,
    weights_other,
    small,
    w_in,
    w_mix,
    facts,
    slots,
    probe_basis,
    density,
    state0,
    own0,
    faces0,
    state1,
    weights,
):
    groups, fan, rim, half, n_basis, cap, n_blocks = sizes
    layers = w_in.shape[0]
    width = 2 * half
    tiles = LANES * fan // LANES
    root_fan = fan**0.5
    me = lax.axis_index("brick") * lax.axis_size("probe") + lax.axis_index("probe")
    part = lax.axis_index("chan")
    weights[part] = weights_mine[...]
    weights[1 - part] = weights_other[...]
    every = groups * LANES
    edge_at = half
    n_edge = 4 * fan // 2
    rest_at = half + n_edge

    def data(group, c, rows):
        return (data_mine, data_other)[c][group, rows, :]

    def weight(layer, p):
        at = (layer * 3 + p) * half
        return jnp.concatenate([weights[c, at : at + half, :] for c in range(2)], axis=0)

    def radial_weight(layer, p):
        at = (layer * 3 + p) * n_basis
        return radial_all[:, at : at + n_basis]

    def edge_rows(group):
        return [data(group, c, slice(edge_at, rest_at)).astype(F32) for c in range(2)]

    def border_of(group):
        return data(group, 0, slice(rest_at, rest_at + 8)).astype(F32)[1:2, 0 : 2 * rim]

    centers = iota((n_basis, 1), 0).astype(F32) * (ROOT * 6.0 / (n_basis - 1))

    def basis_of(length, env):
        return (bell(length * ROOT, centers) * env).astype(BF16)

    small_rows = small[...]
    columns = small_rows.T
    radial_at = weights.shape[1] - half
    radial_all = jnp.concatenate([weights[c, radial_at:, :] for c in range(2)], axis=0)

    received = groups * cap
    edges = received * fan
    per_group = fan * cap
    pick_vec = [facts[x : x + 1, :] for x in range(3)]
    pos = facts[4:7, 0:received]
    length = jnp.sqrt(sum(x * x for x in pick_vec))
    basis1 = basis_of(length, (1.0 - length * length / 36.0) ** 2)
    quad = groups // 2
    window = [[(h * quad + groups - 1 + i) % groups for i in range(quad + 2)] for h in range(2)]
    near_row = iota(((quad + 2) * LANES, edges // 2), 0).astype(F32)
    window_pick = [
        one_hot(near_row == facts[3:4, h * edges // 2 : (h + 1) * edges // 2]) for h in range(2)
    ]
    chosen_atoms = one_hot(iota((every, received), 0).astype(F32) == facts[7:8, 0:received])

    terms_shape = (2 * n_basis, n_basis * received)
    probe_weight = radial_all[:, 3 * layers * n_basis :]
    w_scalar, w_vector = (
        dot(probe_weight, one_hot(iota(terms_shape, 1) // received * 2 + p == iota(terms_shape, 0)))
        for p in range(2)
    )

    probes = density.shape[1]
    grid = probe_grid(me, probes)

    for group in range(groups):
        for c in range(2):
            place = part if c == 0 else 1 - part
            rows = pl.ds(pl.multiple_of(place * half, half), half)
            state0[rows, group * LANES : (group + 1) * LANES] = data(group, c, slice(0, half))
    hidden = silu(dot_tn(w_in[0], state0[...]) + columns[:, 0:1]).astype(BF16)
    weight_ac = jnp.concatenate([weight(0, 0), weight(0, 2)], axis=0)
    messages = dot(weight_ac, hidden).astype(BF16)
    atom_col = lane_atom(iota((LANES, 2 * rim), 0), fan, tiles).astype(F32)
    for group in range(groups):
        own = messages[:, group * LANES : (group + 1) * LANES]
        own0[group] = own
        border_row = border_of(group)
        faces0[group, :, 0 : 2 * rim] = dot(own, one_hot(atom_col == border_row)).astype(BF16)

    row = iota((LANES + 2 * rim, 1), 0)
    names = jnp.where(
        row < LANES,
        lane_atom(row, fan, tiles),
        jnp.where(row < LANES + rim, row + rim, row - rim),
    ).astype(F32)
    names = jnp.broadcast_to(names, (LANES + 2 * rim, LANES)).astype(BF16)
    upper_lane = iota((2 * width, 2 * rim), 1) < rim
    radial_ac = jnp.concatenate([radial_weight(0, 0), radial_weight(0, 2)], axis=0)
    radial_rows = jnp.concatenate([jnp.zeros((2 * width, LANES + 2 * rim), BF16), radial_ac], axis=1)
    blank = jnp.zeros((2 * width, n_basis), BF16)

    some = LANES // 2
    step = fan // 2

    def update(group, first_slot):
        up = (group + 1) % groups
        low = (group + groups - 1) % groups
        ghosts = jnp.where(
            upper_lane,
            faces0[up, :, 0 : 2 * rim].astype(F32),
            faces0[low, :, 0 : 2 * rim].astype(F32),
        ).astype(BF16)
        table = jnp.concatenate([own0[group], ghosts, blank], axis=1)
        left = jnp.concatenate(
            [
                block[at : at + 16]
                for at in range(0, 2 * width, 16)
                for block in (table, radial_rows)
            ],
            axis=0,
        )
        lanes = slice(group * LANES, (group + 1) * LANES)
        slot_lane = (iota((LANES, some), 1) + first_slot).astype(F32)
        in_slot = one_hot(slots[:, group : group + 1] == slot_lane)
        source = jnp.concatenate(
            [data(group, c, slice(edge_at, rest_at)) for c in range(2)] + [state0[:, lanes]], axis=0
        )
        source = dot(source, in_slot)
        rows = jnp.concatenate([source[:n_edge], source[n_edge : 2 * n_edge]], axis=1)
        own_scalars = source[2 * n_edge :]
        vec = [rows[x * step : (x + 1) * step] for x in range(3)]
        nbr = rows[3 * step : 4 * step]
        length = jnp.sqrt(vec[0] * vec[0] + vec[1] * vec[1] + vec[2] * vec[2])
        env = (1.0 - length * length / 36.0) ** 2
        acc = jnp.zeros((width, LANES), F32)
        acc_vec = [jnp.zeros((width, LANES), F32) for _ in range(3)]
        for first in range(0, step, TOGETHER):
            ks = range(first, first + TOGETHER)
            picked = jnp.concatenate([same(names, nbr[k : k + 1].astype(BF16)) for k in ks], axis=1)
            basis = jnp.concatenate(
                [basis_of(length[k : k + 1], env[k : k + 1]) for k in ks], axis=1
            )
            both = dot(left, jnp.concatenate([picked, basis], axis=0))
            prod = jnp.concatenate(
                [both[at : at + 16] * both[at + 16 : at + 32] for at in range(0, 4 * width, 32)],
                axis=0,
            )
            for i, k in enumerate(ks):
                block = prod[:, i * LANES : (i + 1) * LANES]
                acc = acc + block[:width]
                for x in range(3):
                    acc_vec[x] = acc_vec[x] + block[width:] * vec[x][k : k + 1]
        acc, *acc_vec = [(a[:, :some] + a[:, some:]) / root_fan for a in [acc] + acc_vec]
        return jnp.concatenate([own_scalars + acc] + acc_vec, axis=0)

    for group in range(groups):
        state = update(group, 0)
        state = jnp.concatenate([state, jnp.zeros_like(state)], axis=1)
        state1[:, group * LANES : (group + 1) * LANES] = state.astype(BF16)

    @pl.when(jnp.max(facts[8:9, 0:groups]) > some)
    def _():
        for group in range(groups):

            @pl.when(jnp.max(facts[8:9, group : group + 1]) > some)
            def _():
                lanes = slice(group * LANES + some, (group + 1) * LANES)
                state1[:, lanes] = update(group, some).astype(BF16)

    rows = []
    for h in range(2):
        near_states = jnp.concatenate(
            [state1[:, g * LANES : (g + 1) * LANES] for g in window[h]], axis=1
        )
        rows.append(dot(near_states, window_pick[h]))
    rows = jnp.concatenate(rows, axis=1)
    hidden = silu(dot_tn(w_in[1], rows[:width].astype(BF16)) + columns[:, 1:2]).astype(BF16)
    weight_abc = jnp.concatenate([weight(1, p) for p in range(3)], axis=0)
    messages = dot(weight_abc, hidden).astype(BF16).astype(F32)
    radial_abc = jnp.concatenate([radial_weight(1, p) for p in range(3)], axis=0)
    filters = dot(radial_abc, basis1)
    weighted = messages * filters
    gate = weighted[width : 2 * width]
    along = weighted[2 * width :]
    parts = [weighted[:width]]
    for x in range(3):
        parts.append(rows[(1 + x) * width : (2 + x) * width] * gate + along * pick_vec[x])
    parts = jnp.concatenate(parts, axis=0).astype(BF16)
    edge = iota((edges, received), 0)
    slot = (edge // per_group) * cap + edge % cap
    delta = dot(parts, one_hot(slot == iota((edges, received), 1)))
    final = (dot(state1[...], chosen_atoms) + delta / root_fan).astype(BF16).astype(F32)

    along = final[width : 2 * width] * pos[0:1]
    for x in range(1, 3):
        along = along + final[(x + 1) * width : (x + 2) * width] * pos[x : x + 1]
    def repeat(value):
        return jnp.concatenate([value] * n_basis, axis=1)
    terms = [w_scalar * repeat(final[:width]) - w_vector * repeat(along)]
    for x in range(3):
        terms.append(w_vector * repeat(final[(x + 1) * width : (x + 2) * width]))
    sums = dot(jnp.concatenate(terms, axis=0).astype(BF16), probe_basis[...])
    charges = sums[:width]
    for x in range(3):
        charges = charges + grid[x] * sums[(x + 1) * width : (x + 2) * width]
    mixed = dot_tn(w_mix[...], charges.astype(BF16)) + columns[:, layers : layers + 1]
    density[...] = jnp.sum(silu(mixed) * columns[:, layers + 1 : layers + 2], axis=0, keepdims=True)


def few_groups(
    atom_s, atom_pos, edge_vec, edge_nbr, border_index, send_index, probe_list, probe_count,
    w_in, b_in, w_msg, w_rad, w_probe, w_mix, b_mix, w_out,
):
    atoms, half = atom_s.shape
    groups = lax.axis_size("brick") * lax.axis_size("probe")
    fan = edge_nbr.shape[0] // atoms
    rim = border_index.shape[0] // 2
    n_basis = w_rad.shape[1]
    cap = send_index.shape[1] // groups
    width = 2 * half
    every = groups * LANES
    data = pack(groups, atom_s, atom_pos, edge_vec, edge_nbr, border_index, send_index)
    weights, small = pack_weights(
        half, w_msg, w_rad, w_probe, b_in, b_mix, w_out, probe_list, probe_count
    )
    swap = [(0, 1), (1, 0)]
    weights_other = lax.ppermute(weights, "chan", swap)
    mine = lax.all_to_all(data, ("brick", "probe"), split_axis=0, concat_axis=0, tiled=True)
    anywhere = pl.BlockSpec(memory_space=pl.ANY)
    mine = pl.pallas_call(
        after_kernel,
        out_shape=jax.ShapeDtypeStruct(mine.shape, BF16),
        in_specs=[anywhere] * 2,
        out_specs=anywhere,
        input_output_aliases={0: 0},
        compiler_params=pltpu.CompilerParams(vmem_limit_bytes=16 * 1024 * 1024),
        name="after",
    )(mine, weights_other)
    other = lax.ppermute(mine, "chan", swap)
    n_probes = probe_list.shape[0] * PB
    sizes = (groups, fan, rim, half, n_basis, cap, probe_list.shape[0])
    facts, slots, probe_basis = pl.pallas_call(
        functools.partial(index_kernel, sizes, w_in.shape[0] + 2),
        out_shape=(
            jax.ShapeDtypeStruct((16, groups * cap * fan), F32),
            jax.ShapeDtypeStruct((LANES, LANES), F32),
            jax.ShapeDtypeStruct((n_basis * groups * cap, n_probes), BF16),
        ),
        compiler_params=pltpu.CompilerParams(vmem_limit_bytes=24 * 1024 * 1024),
        name="index",
    )(mine, small)
    density = pl.pallas_call(
        functools.partial(density_kernel, sizes),
        out_shape=jax.ShapeDtypeStruct((1, n_probes), F32),
        scratch_shapes=[
            pltpu.VMEM((width, every), BF16),
            pltpu.VMEM((groups, 2 * width, LANES), BF16),
            pltpu.VMEM((groups, 2 * width, LANES), BF16),
            pltpu.VMEM((4 * width, every), BF16),
            pltpu.VMEM((2,) + weights.shape, BF16),
        ],
        compiler_params=pltpu.CompilerParams(vmem_limit_bytes=40 * 1024 * 1024),
        name="density",
    )(mine, other, weights, weights_other, small, w_in, w_mix, facts, slots, probe_basis)
    return density.reshape(n_probes)


def per_device(*args):
    if lax.axis_size("brick") * lax.axis_size("probe") == FEW_GROUPS:
        return few_groups(*args)
    return many_groups(*args)


def extended(block, sides, width):
    for axis, dim in sides:
        count = lax.axis_size(axis)
        forward = [(i, i + 1) for i in range(count - 1)]
        forward.append((count - 1, 0))
        backward = [(target, source) for source, target in forward]
        low = lax.ppermute(
            lax.slice_in_dim(block, block.shape[dim] - width, None, axis=dim), axis, forward
        )
        high = lax.ppermute(lax.slice_in_dim(block, 0, width, axis=dim), axis, backward)
        block = jnp.concatenate([low, block, high], axis=dim)
    return block


def radial(distance, count, top):
    centers = jnp.arange(count).astype(jnp.float32) * (top / (count - 1))
    return jnp.exp(-2.0 * (distance[..., None] - centers) ** 2)


def make_block(
    recv_rows, recv_pos, w_scalar, w_vector, feat_width, group_no, n_blocks, list_len, n_basis
):

    def probe_block(block_in):
        block_no, listed, live_count = block_in
        index_row = (group_no * n_blocks + block_no) * PB + jnp.arange(PB, dtype=jnp.int32)
        grid_xyz = (
            jnp.stack([index_row % 16, index_row // 16 % 16, index_row // 256 % 16], axis=1).astype(
                jnp.float32
            )
            * 0.25
        )
        atom_xyz = recv_pos[:, listed]
        disp = grid_xyz[:, :, None] - atom_xyz[None]
        dist_sq = jnp.sum(disp * disp, axis=1)
        live = (jnp.arange(list_len, dtype=jnp.int32) < live_count).astype(jnp.float32)
        envelope = (1.0 - dist_sq / 64.0) ** 2 * live[None, :]
        basis = radial(jnp.sqrt(dist_sq), n_basis, 7.0) * envelope[:, :, None]
        scalar_w = basis.astype(jnp.bfloat16).reshape(PB, list_len * n_basis)
        vector_w = (
            (disp[:, :, :, None] * basis[:, None])
            .astype(jnp.bfloat16)
            .reshape(PB, 3 * list_len * n_basis)
        )
        atom_rows = recv_rows[listed]
        atom_terms = (atom_rows[:, None, :feat_width] * w_scalar[None]).reshape(
            list_len * n_basis, feat_width
        )
        vec_rows = jnp.transpose(
            atom_rows[:, feat_width:].reshape(list_len, 3, feat_width), (1, 0, 2)
        )
        vector_terms = (vec_rows[:, :, None, :] * w_vector[None, None]).reshape(
            3 * list_len * n_basis, feat_width
        )
        charge = jnp.dot(scalar_w, atom_terms, preferred_element_type=jnp.float32) + jnp.dot(
            vector_w, vector_terms, preferred_element_type=jnp.float32
        )
        return charge.astype(jnp.bfloat16)

    return probe_block


def many_groups(
    atom_s,
    atom_pos,
    edge_vec,
    edge_nbr,
    border_index,
    send_index,
    probe_list,
    probe_count,
    w_in,
    b_in,
    w_msg,
    w_rad,
    w_probe,
    w_mix,
    b_mix,
    w_out,
):
    atom_count, half_width = atom_s.shape
    n_layers = w_in.shape[0]
    width = w_in.shape[1]
    n_basis = w_rad.shape[1]
    fan_out = edge_nbr.shape[0] // atom_count
    root_fan = fan_out**0.5
    rim_rows = border_index.shape[0] // 2
    length = jnp.sqrt(jnp.sum(edge_vec * edge_vec, axis=0))
    edge_env = (1.0 - length * length / 36.0) ** 2
    edge_basis = (radial(length, n_basis, 6.0) * edge_env[:, None]).astype(jnp.bfloat16)
    edge_cols = jnp.transpose(edge_vec)
    scalars = atom_s
    vectors = jnp.zeros((atom_count, 3 * half_width), jnp.bfloat16)
    for layer_no in range(n_layers):
        full_rows = lax.all_gather(scalars, "chan", axis=1, tiled=True)
        in_weight = w_in[layer_no]
        in_bias = b_in[layer_no]
        msg_weight = w_msg[layer_no].reshape(width, 3 * half_width)
        rad_weight = w_rad[layer_no].reshape(n_basis, 3 * half_width)
        hidden_act = jax.nn.silu(
            jnp.dot(full_rows, in_weight, preferred_element_type=jnp.float32) + in_bias
        ).astype(jnp.bfloat16)
        inner_tab = jnp.concatenate(
            [
                jnp.dot(hidden_act, msg_weight, preferred_element_type=jnp.float32).astype(
                    jnp.bfloat16
                ),
                vectors,
            ],
            axis=1,
        )
        padded = extended(inner_tab[border_index], ((("brick", "probe"), 0),), rim_rows)
        lookup = jnp.concatenate([inner_tab, padded[:rim_rows], padded[3 * rim_rows :]], axis=0)
        neighbour_rows = lookup[edge_nbr]
        filters = jnp.dot(edge_basis, rad_weight, preferred_element_type=jnp.float32)
        weighted = neighbour_rows[:, : 3 * half_width] * filters
        neighbour_vec = neighbour_rows[:, 3 * half_width :].reshape(-1, 3, half_width)
        vector_gate = weighted[:, None, half_width : 2 * half_width]
        along_edge = weighted[:, None, 2 * half_width :]
        delta_vec = neighbour_vec * vector_gate + along_edge * edge_cols[:, :, None]
        delta_scalar = (
            weighted[:, :half_width].reshape(atom_count, fan_out, half_width).sum(axis=1) / root_fan
        )
        delta_vec = delta_vec.reshape(atom_count, fan_out, 3 * half_width).sum(axis=1) / root_fan
        scalars = (scalars + delta_scalar).astype(jnp.bfloat16)
        vectors = (vectors + delta_vec).astype(jnp.bfloat16)
    features = jnp.concatenate([scalars, vectors], axis=1)
    picks = send_index[0]
    n_brick = lax.axis_size("brick")
    n_probe = lax.axis_size("probe")
    n_groups = n_brick * n_probe
    slot_cap = picks.shape[0] // n_groups
    out_rows = features[picks]
    out_pos = jnp.transpose(atom_pos)[picks].astype(jnp.bfloat16)
    received = (
        lax.all_to_all(
            out_rows.reshape(n_groups, slot_cap, 4 * half_width),
            ("brick", "probe"),
            split_axis=0,
            concat_axis=0,
            tiled=True,
        ),
        lax.all_to_all(
            out_pos.reshape(n_groups, slot_cap, 3),
            ("brick", "probe"),
            split_axis=0,
            concat_axis=0,
            tiled=True,
        ),
    )
    recv_count = n_groups * slot_cap
    recv_rows = received[0].reshape(recv_count, 4 * half_width)
    recv_pos = jnp.transpose(received[1].reshape(recv_count, 3)).astype(jnp.float32)
    group_no = lax.axis_index("brick") * n_probe + lax.axis_index("probe")
    n_blocks, list_len = probe_list.shape
    probe_block = make_block(
        recv_rows,
        recv_pos,
        w_probe[:, 0, :],
        w_probe[:, 1, :],
        half_width,
        group_no,
        n_blocks,
        list_len,
        n_basis,
    )
    charges = lax.map(
        probe_block, (jnp.arange(n_blocks, dtype=jnp.int32), probe_list, probe_count)
    ).reshape(n_blocks * PB, half_width)
    mix_rows = lax.dynamic_slice_in_dim(w_mix, lax.axis_index("chan") * half_width, half_width, 0)
    mixed = lax.psum(jnp.dot(charges, mix_rows, preferred_element_type=jnp.float32), "chan")
    return jnp.sum(jax.nn.silu(mixed + b_mix) * w_out, axis=1)


def solution(mesh):
    in_specs = (
        P(("image", "brick", "probe"), "chan"),
        P(None, ("image", "brick", "probe")),
        P(None, ("image", "brick", "probe")),
        P(("image", "brick", "probe")),
        P(("image", "brick", "probe")),
        P(("image", "brick", "probe"), None),
        P(("image", "brick", "probe"), None),
        P(("image", "brick", "probe")),
        P(),
        P(),
        P(None, None, None, "chan"),
        P(None, None, None, "chan"),
        P(None, None, "chan"),
        P(),
        P(),
        P(),
    )
    out_specs = P(("image", "brick", "probe"))
    return jax.shard_map(
        per_device, mesh=mesh, in_specs=in_specs, out_specs=out_specs, check_vma=False
    )
```

```python
import functools
import itertools
import math

import jax
import jax.numpy as jnp
from jax import lax
from jax.experimental import pallas as pl
from jax.experimental.pallas import tpu as pltpu
from jax.sharding import PartitionSpec as P

PB = 128
LANES = 128
FEW_GROUPS = 8
SMALL = 16
TOGETHER = 2
ROOT = (2.0 * math.log2(math.e)) ** 0.5
F32 = jnp.float32
BF16 = jnp.bfloat16


def iota(shape, dim):
    return lax.broadcasted_iota(jnp.int32, shape, dim)


def dot(a, b):
    return jnp.dot(a, b, preferred_element_type=F32)


def dot_tn(a, b):
    return lax.dot_general(a, b, (((0,), (0,)), ((), ())), preferred_element_type=F32)


def one_hot(mask):
    return jnp.where(mask, 1.0, 0.0).astype(BF16)


def same(names, row):
    return jnp.where(names == row, jnp.ones_like(names), jnp.zeros_like(names))


def silu(x):
    half_x = 0.5 * x
    return half_x * jnp.tanh(half_x) + half_x


def bell(scaled, center):
    away = scaled - center
    return jnp.exp2(-(away * away))


def lane_atom(lane, fan, tiles):
    return (lane % tiles) * (LANES // fan) + lane // tiles


def length_keeping_round(exact):
    choices = []
    for value in exact:
        near = value.astype(BF16).astype(F32)
        step = jnp.where(value > near, 1.01 / 256.0, -1.01 / 256.0) * jnp.abs(near)
        choices.append((near, (near + step).astype(BF16).astype(F32)))
    target = sum(value * value for value in exact)
    best, best_error = None, None
    for picked in itertools.product(*choices):
        error = jnp.abs(sum(value * value for value in picked) - target)
        if best is None:
            best, best_error = picked, error
            continue
        better = error < best_error
        best = tuple(jnp.where(better, new, old) for new, old in zip(picked, best))
        best_error = jnp.where(better, error, best_error)
    return best


def pack_kernel(
    fan, atom_s, atom_pos, edge_vec, edge_nbr, border, send, data_out, natural
):
    half, atoms = atom_s.shape
    tiles = atoms * fan // LANES
    per_tile = LANES // fan
    part = lax.axis_index("chan")
    perm = one_hot(lane_atom(iota((atoms, LANES), 1), fan, tiles) == iota((atoms, LANES), 0))
    scalars = dot(atom_s[...], perm).astype(BF16)
    for tile in range(tiles):
        for comp in range(3):
            natural[comp * tiles + tile : comp * tiles + tile + 1, :] = edge_vec[
                comp : comp + 1, tile * LANES : (tile + 1) * LANES
            ]
    exact = [natural[comp * tiles : (comp + 1) * tiles, :] for comp in range(3)]
    for comp, value in enumerate(length_keeping_round(exact)):
        natural[comp * tiles : (comp + 1) * tiles, :] = value
    natural[3 * tiles : 4 * tiles, :] = edge_nbr[...].astype(F32)
    natural[4 * tiles :, :] = jnp.zeros((LANES - 4 * tiles, LANES), F32)
    turned = natural[...].T
    lane = iota((fan, LANES), 1)
    sorted_rows = []
    for comp in range(4):
        rows = jnp.zeros((fan, LANES), F32)
        for a in range(per_tile):
            piece = turned[a * fan : (a + 1) * fan, :]
            shift = (a * tiles - comp * tiles) % LANES
            piece = pltpu.roll(piece, shift, 1) if shift else piece
            rows = jnp.where(lane // tiles == a, piece, rows)
        sorted_rows.append(rows)
    blank = jnp.zeros((1, LANES), F32)
    every_edge = jnp.concatenate(sorted_rows, axis=0).astype(BF16)
    sorted_rows = [jnp.where(part == 0, rows[: fan // 2], rows[fan // 2 :]) for rows in sorted_rows]
    border_row = jnp.concatenate(
        [border[...].astype(F32), jnp.zeros((1, LANES - border.shape[1]), F32)], axis=1
    )
    picks = send.shape[1]
    groups = data_out.shape[0]
    cap = picks // groups
    block = fan * cap
    lane = iota((picks, groups * block), 1)
    place = (lane // block) * cap + lane % cap
    send_row = jnp.broadcast_to(send[...].astype(F32), (8, picks)).astype(BF16)
    wanted = dot(send_row, one_hot(iota((picks, groups * block), 0) == place))[0:1]
    atom_col = lane_atom(iota((LANES, groups * block), 0), fan, tiles).astype(F32)
    spread = dot(every_edge, one_hot(atom_col == wanted))
    edge_k = iota(spread.shape, 0) % fan
    spread = jnp.where(edge_k == (iota(spread.shape, 1) % block) // cap, spread, 0.0)
    picked = jnp.sum(spread.reshape(4, fan, groups * block), axis=1)
    pick_atom = one_hot(iota((atoms, picks), 0).astype(F32) == send[...].astype(F32))
    facts = [send[...].astype(F32)]
    pos = dot(atom_pos[...].astype(BF16), pick_atom)
    facts += [pos[x : x + 1] for x in range(3)]
    owner = iota((groups, picks), 1) // cap == iota((groups, picks), 0)
    facts = jnp.concatenate([jnp.where(owner, fact, 0.0) for fact in facts], axis=1)
    row = iota((4 * picks, LANES), 0)
    place = (row // picks) * cap + row % cap
    facts = dot(facts.astype(BF16), one_hot(place == iota((4 * picks, LANES), 1)))
    edge_part = jnp.concatenate(sorted_rows, axis=0).astype(BF16)
    for group in range(groups):
        mine = slice(group * block, (group + 1) * block)
        rest = [facts[group : group + 1], border_row]
        for comp in (0, 2):
            rest.append(
                jnp.concatenate([picked[comp : comp + 1, mine], picked[comp + 1 : comp + 2, mine]], axis=1)
            )
        rest = jnp.concatenate(rest + [blank] * 4, axis=0)
        data_out[group, 0:half, :] = scalars
        data_out[group, half : half + 2 * fan, :] = edge_part
        data_out[group, half + 2 * fan :, :] = rest.astype(BF16)


def weight_kernel(
    w_msg, w_rad, w_probe, b_in, b_mix, w_out, probe_list, probe_count, weight_out, small_out
):
    at = 0
    for piece in (b_in, b_mix, w_out, probe_list, probe_count):
        rows, cols = piece.shape
        small_out[at : at + rows, 0:cols] = piece[...].astype(F32)
        at += rows
    probe_rows = [w_probe[r].astype(F32) for r in range(w_probe.shape[0])]
    radial = jnp.concatenate([w_rad[...].astype(F32)] + probe_rows, axis=0).T.astype(BF16)
    weight_out[: w_msg.shape[0], :] = w_msg[...]
    weight_out[w_msg.shape[0] :, :] = radial


def pack(copies, atom_s, atom_pos, edge_vec, edge_nbr, border_index, send_index):
    atoms, half = atom_s.shape
    fan = edge_nbr.shape[0] // atoms
    return pl.pallas_call(
        functools.partial(pack_kernel, fan),
        out_shape=jax.ShapeDtypeStruct((copies, half + 4 * fan // 2 + 8, LANES), BF16),
        scratch_shapes=[pltpu.VMEM((LANES, LANES), F32)],
        name="pack",
    )(
        atom_s.T,
        atom_pos,
        edge_vec,
        edge_nbr.reshape(-1, LANES),
        border_index.reshape(1, -1),
        send_index,
    )


def pack_weights(half, w_msg, w_rad, w_probe, b_in, b_mix, w_out, probe_list, probe_count):
    return pl.pallas_call(
        weight_kernel,
        out_shape=(
            jax.ShapeDtypeStruct((w_msg.size // LANES + half, LANES), BF16),
            jax.ShapeDtypeStruct((SMALL, LANES), F32),
        ),
        name="pack_weights",
    )(
        jnp.transpose(w_msg, (0, 2, 3, 1)).reshape(-1, LANES),
        jnp.transpose(w_rad, (0, 2, 1, 3)).reshape(-1, half),
        w_probe,
        b_in,
        b_mix.reshape(1, -1),
        w_out.reshape(1, -1),
        probe_list,
        probe_count.reshape(1, -1),
    )


def after_kernel(block, there, same_block):
    pass


def probe_grid(me, probes):
    number = me * probes + iota((1, probes), 1)
    return [(n % 16).astype(F32) * 0.25 - 1.875 for n in (number, number // 16, number // 256)]


def index_kernel(sizes, list_at, data_mine, small, facts_out, slots, probe_basis):
    groups, fan, rim, half, n_basis, cap, n_blocks = sizes
    tiles = fan
    received = groups * cap
    per_group = fan * cap
    edges = received * fan
    rest_at = half + 2 * fan
    me = lax.axis_index("brick") * lax.axis_size("probe") + lax.axis_index("probe")
    small_rows = small[...]
    rest = [data_mine[g, rest_at : rest_at + 8, :].astype(F32) for g in range(groups)]
    facts = jnp.concatenate([rows[0:1] for rows in rest], axis=0).astype(BF16)
    lane = iota((LANES, 4 * received), 1)
    wanted = (lane // received) * cap + lane % cap
    facts = dot(facts, one_hot(iota((LANES, 4 * received), 0) == wanted))
    source = (iota(facts.shape, 1) % received) // cap
    facts = jnp.sum(jnp.where(source == iota(facts.shape, 0), facts, 0.0), axis=0, keepdims=True)
    pick_atoms = facts[:, 0:received]
    for comp in range(3):
        rows = [r[2 + comp // 2 : 3 + comp // 2, (comp % 2) * per_group :][:, :per_group] for r in rest]
        facts_out[comp : comp + 1, :] = jnp.concatenate(rows, axis=1)
    nbr = jnp.concatenate([r[3:4, per_group : 2 * per_group] for r in rest], axis=1).astype(jnp.int32)

    home = iota((1, edges), 1) // per_group
    is_low = (nbr >= LANES) & (nbr < LANES + rim)
    is_up = nbr >= LANES + rim
    owner = jnp.where(
        is_low, (home + groups - 1) % groups, jnp.where(is_up, (home + 1) % groups, home)
    )
    entry = owner * 2 * rim + jnp.where(is_low, nbr - (LANES - rim), nbr - (LANES + rim))
    entry = jnp.where(is_low | is_up, entry, -1)
    border_all = jnp.concatenate([r[1:2, 0 : 2 * rim] for r in rest], axis=1)
    border_all = jnp.broadcast_to(border_all, (16, groups * 2 * rim)).astype(BF16)
    seen = dot(border_all, one_hot(iota((groups * 2 * rim, edges), 0) == entry))[0:1]
    target = jnp.where(entry < 0, nbr, seen.astype(jnp.int32))

    column = iota((groups * LANES, 1), 0)
    column_name = (column // LANES) * LANES + lane_atom(column % LANES, fan, tiles)
    home = iota((1, received), 1) // cap
    self_hot = one_hot(column_name == home * LANES + pick_atoms.astype(jnp.int32))
    uses = dot(self_hot, jnp.ones((received, LANES), BF16))
    uses = [uses[g * LANES : (g + 1) * LANES] for g in range(groups)]
    quad = groups // 2
    window_hot, near_groups = [], []
    for h in range(2):
        lanes = slice(h * edges // 2, (h + 1) * edges // 2)
        near = lax.rem(owner[:, lanes] + 2 * groups - (h * quad + groups - 1), groups)
        hot = one_hot(column_name[: (quad + 2) * LANES] == near * LANES + target[:, lanes])
        window_hot.append(hot)
        near_groups.append(near)
        used = dot(hot, jnp.ones((edges // 2, LANES), BF16))
        for i in range(quad + 2):
            g = (h * quad + groups - 1 + i) % groups
            uses[g] = uses[g] + used[i * LANES : (i + 1) * LANES]
    lane = iota((LANES, LANES), 1)
    needed = jnp.zeros((LANES, LANES), F32)
    for g in range(groups):
        needed = jnp.where((lane == g) & (uses[g] > 0.0), 1.0, needed)
    order = dot(one_hot(lane <= iota((LANES, LANES), 0)), needed.astype(BF16))
    slot = jnp.where(needed > 0.0, order - 1.0, -1.0)
    slots[...] = slot
    slot_rows = slot.T
    facts_out[8:9, 0:LANES] = order[LANES - 1 : LANES, :]

    for h in range(2):
        lanes = slice(h * edges // 2, (h + 1) * edges // 2)
        in_window = [(h * quad + groups - 1 + i) % groups for i in range(quad + 2)]
        row = jnp.concatenate([slot_rows[g : g + 1] for g in in_window], axis=1)
        row = jnp.broadcast_to(row, (16, (quad + 2) * LANES)).astype(BF16)
        place = dot(row, window_hot[h])[0:1]
        facts_out[3:4, lanes] = near_groups[h].astype(F32) * LANES + place
    row = jnp.concatenate([slot_rows[g : g + 1] for g in range(groups)], axis=1)
    row = jnp.broadcast_to(row, (16, groups * LANES)).astype(BF16)
    facts_out[7:8, 0:received] = home.astype(F32) * LANES + dot(row, self_hot)[0:1]

    shifted = facts - 1.875
    for x in range(3):
        facts_out[4 + x : 5 + x, 0:received] = shifted[:, (1 + x) * received : (2 + x) * received]
    pos_cols = jnp.broadcast_to(shifted, (LANES, 4 * received)).T
    list_len = LANES
    counts = []
    for block in range(n_blocks):
        limit = small_rows[list_at + n_blocks : list_at + n_blocks + 1, block : block + 1]
        live = iota((1, list_len), 1).astype(F32) < limit
        named = jnp.where(live, small_rows[list_at + block : list_at + block + 1], -1.0)
        hits = jnp.where(iota((received, list_len), 0).astype(F32) == named, 1.0, 0.0)
        counts.append(jnp.broadcast_to(jnp.sum(hits, axis=1, keepdims=True), (received, PB)))
    counts = jnp.concatenate(counts, axis=1)
    probes = n_blocks * PB
    grid = probe_grid(me, probes)
    dist_sq = jnp.zeros((received, probes), F32)
    for x in range(3):
        dist_sq = dist_sq + (grid[x] - pos_cols[(1 + x) * received : (2 + x) * received, 0:1]) ** 2
    dist = jnp.sqrt(dist_sq) * ROOT
    envelope = (1.0 - dist_sq / 64.0) ** 2 * counts
    probe_basis[...] = jnp.concatenate(
        [
            (bell(dist, r * (ROOT * 7.0 / (n_basis - 1))) * envelope).astype(BF16)
            for r in range(n_basis)
        ],
        axis=0,
    )


def density_kernel(
    sizes,
    data_mine,
    data_other,
    weights_mine,
    weights_other,
    small,
    w_in,
    w_mix,
    facts,
    slots,
    probe_basis,
    density,
    state0,
    own0,
    faces0,
    state1,
    weights,
):
    groups, fan, rim, half, n_basis, cap, n_blocks = sizes
    layers = w_in.shape[0]
    width = 2 * half
    tiles = LANES * fan // LANES
    root_fan = fan**0.5
    me = lax.axis_index("brick") * lax.axis_size("probe") + lax.axis_index("probe")
    part = lax.axis_index("chan")
    weights[part] = weights_mine[...]
    weights[1 - part] = weights_other[...]
    every = groups * LANES
    edge_at = half
    n_edge = 4 * fan // 2
    rest_at = half + n_edge

    def data(group, c, rows):
        return (data_mine, data_other)[c][group, rows, :]

    def weight(layer, p):
        at = (layer * 3 + p) * half
        return jnp.concatenate([weights[c, at : at + half, :] for c in range(2)], axis=0)

    def radial_weight(layer, p):
        at = (layer * 3 + p) * n_basis
        return radial_all[:, at : at + n_basis]

    def edge_rows(group):
        return [data(group, c, slice(edge_at, rest_at)).astype(F32) for c in range(2)]

    def border_of(group):
        return data(group, 0, slice(rest_at, rest_at + 8)).astype(F32)[1:2, 0 : 2 * rim]

    centers = iota((n_basis, 1), 0).astype(F32) * (ROOT * 6.0 / (n_basis - 1))

    def basis_of(length, env):
        return (bell(length * ROOT, centers) * env).astype(BF16)

    small_rows = small[...]
    columns = small_rows.T
    radial_at = weights.shape[1] - half
    radial_all = jnp.concatenate([weights[c, radial_at:, :] for c in range(2)], axis=0)

    some = LANES // 2
    crowded = jnp.max(facts[8:9, 0:groups]) > some

    received = groups * cap
    edges = received * fan
    per_group = fan * cap
    pick_vec = [facts[x : x + 1, :] for x in range(3)]
    pos = facts[4:7, 0:received]
    length = jnp.sqrt(sum(x * x for x in pick_vec))
    basis1 = basis_of(length, (1.0 - length * length / 36.0) ** 2)
    quad = groups // 2
    window = [[(h * quad + groups - 1 + i) % groups for i in range(quad + 2)] for h in range(2)]
    near_row = iota(((quad + 2) * LANES, edges // 2), 0).astype(F32)
    window_pick = [
        one_hot(near_row == facts[3:4, h * edges // 2 : (h + 1) * edges // 2]) for h in range(2)
    ]
    chosen_atoms = one_hot(iota((every, received), 0).astype(F32) == facts[7:8, 0:received])

    terms_shape = (2 * n_basis, n_basis * received)
    probe_weight = radial_all[:, 3 * layers * n_basis :]
    w_scalar, w_vector = (
        dot(probe_weight, one_hot(iota(terms_shape, 1) // received * 2 + p == iota(terms_shape, 0)))
        for p in range(2)
    )

    probes = density.shape[1]
    grid = probe_grid(me, probes)

    for group in range(groups):
        for c in range(2):
            place = part if c == 0 else 1 - part
            rows = pl.ds(pl.multiple_of(place * half, half), half)
            state0[rows, group * LANES : (group + 1) * LANES] = data(group, c, slice(0, half))
    hidden = silu(dot_tn(w_in[0], state0[...]) + columns[:, 0:1]).astype(BF16)
    weight_ac = jnp.concatenate([weight(0, 0), weight(0, 2)], axis=0)
    messages = dot(weight_ac, hidden).astype(BF16)
    atom_col = lane_atom(iota((LANES, 2 * rim), 0), fan, tiles).astype(F32)
    for group in range(groups):
        own = messages[:, group * LANES : (group + 1) * LANES]
        own0[group] = own
        border_row = border_of(group)
        faces0[group, :, 0 : 2 * rim] = dot(own, one_hot(atom_col == border_row)).astype(BF16)

    row = iota((LANES + 2 * rim, 1), 0)
    names = jnp.where(
        row < LANES,
        lane_atom(row, fan, tiles),
        jnp.where(row < LANES + rim, row + rim, row - rim),
    ).astype(F32)
    names = jnp.broadcast_to(names, (LANES + 2 * rim, LANES)).astype(BF16)
    upper_lane = iota((2 * width, 2 * rim), 1) < rim
    radial_ac = jnp.concatenate([radial_weight(0, 0), radial_weight(0, 2)], axis=0)
    radial_rows = jnp.concatenate([jnp.zeros((2 * width, LANES + 2 * rim), BF16), radial_ac], axis=1)
    blank = jnp.zeros((2 * width, n_basis), BF16)

    step = fan // 2

    def update(group, first_slot):
        up = (group + 1) % groups
        low = (group + groups - 1) % groups
        ghosts = jnp.where(
            upper_lane,
            faces0[up, :, 0 : 2 * rim].astype(F32),
            faces0[low, :, 0 : 2 * rim].astype(F32),
        ).astype(BF16)
        table = jnp.concatenate([own0[group], ghosts, blank], axis=1)
        left = jnp.concatenate(
            [
                block[at : at + 16]
                for at in range(0, 2 * width, 16)
                for block in (table, radial_rows)
            ],
            axis=0,
        )
        lanes = slice(group * LANES, (group + 1) * LANES)
        slot_lane = (iota((LANES, some), 1) + first_slot).astype(F32)
        in_slot = one_hot(slots[:, group : group + 1] == slot_lane)
        source = jnp.concatenate(
            [data(group, c, slice(edge_at, rest_at)) for c in range(2)] + [state0[:, lanes]], axis=0
        )
        source = dot(source, in_slot)
        rows = jnp.concatenate([source[:n_edge], source[n_edge : 2 * n_edge]], axis=1)
        own_scalars = source[2 * n_edge :]
        vec = [rows[x * step : (x + 1) * step] for x in range(3)]
        nbr = rows[3 * step : 4 * step]
        length = jnp.sqrt(vec[0] * vec[0] + vec[1] * vec[1] + vec[2] * vec[2])
        env = (1.0 - length * length / 36.0) ** 2
        acc = jnp.zeros((width, LANES), F32)
        acc_vec = [jnp.zeros((width, LANES), F32) for _ in range(3)]
        for first in range(0, step, TOGETHER):
            ks = range(first, first + TOGETHER)
            picked = jnp.concatenate([same(names, nbr[k : k + 1].astype(BF16)) for k in ks], axis=1)
            basis = jnp.concatenate(
                [basis_of(length[k : k + 1], env[k : k + 1]) for k in ks], axis=1
            )
            both = dot(left, jnp.concatenate([picked, basis], axis=0))
            prod = jnp.concatenate(
                [both[at : at + 16] * both[at + 16 : at + 32] for at in range(0, 4 * width, 32)],
                axis=0,
            )
            for i, k in enumerate(ks):
                block = prod[:, i * LANES : (i + 1) * LANES]
                acc = acc + block[:width]
                for x in range(3):
                    acc_vec[x] = acc_vec[x] + block[width:] * vec[x][k : k + 1]
        acc, *acc_vec = [(a[:, :some] + a[:, some:]) * (1.0 / root_fan) for a in [acc] + acc_vec]
        return jnp.concatenate([own_scalars + acc] + acc_vec, axis=0)

    for group in range(groups):
        state = update(group, 0)
        state = jnp.concatenate([state, jnp.zeros_like(state)], axis=1)
        state1[:, group * LANES : (group + 1) * LANES] = state.astype(BF16)

    @pl.when(crowded)
    def _():
        for group in range(groups):

            @pl.when(jnp.max(facts[8:9, group : group + 1]) > some)
            def _():
                lanes = slice(group * LANES + some, (group + 1) * LANES)
                state1[:, lanes] = update(group, some).astype(BF16)

    rows = []
    for h in range(2):
        near_states = jnp.concatenate(
            [state1[:, g * LANES : (g + 1) * LANES] for g in window[h]], axis=1
        )
        rows.append(dot(near_states, window_pick[h]))
    rows = jnp.concatenate(rows, axis=1)
    hidden = silu(dot_tn(w_in[1], rows[:width].astype(BF16)) + columns[:, 1:2]).astype(BF16)
    weight_abc = jnp.concatenate([weight(1, p) for p in range(3)], axis=0)
    messages = dot(weight_abc, hidden).astype(BF16).astype(F32)
    radial_abc = jnp.concatenate([radial_weight(1, p) for p in range(3)], axis=0)
    filters = dot(radial_abc, basis1)
    weighted = messages * filters
    gate = weighted[width : 2 * width]
    along = weighted[2 * width :]
    parts = [weighted[:width]]
    for x in range(3):
        parts.append(rows[(1 + x) * width : (2 + x) * width] * gate + along * pick_vec[x])
    parts = jnp.concatenate(parts, axis=0).astype(BF16)
    edge = iota((edges, received), 0)
    slot = (edge // per_group) * cap + edge % cap
    delta = dot(parts, one_hot(slot == iota((edges, received), 1)))
    final = (dot(state1[...], chosen_atoms) + delta / root_fan).astype(BF16).astype(F32)

    along = final[width : 2 * width] * pos[0:1]
    for x in range(1, 3):
        along = along + final[(x + 1) * width : (x + 2) * width] * pos[x : x + 1]
    def repeat(value):
        return jnp.concatenate([value] * n_basis, axis=1)
    terms = [w_scalar * repeat(final[:width]) - w_vector * repeat(along)]
    for x in range(3):
        terms.append(w_vector * repeat(final[(x + 1) * width : (x + 2) * width]))
    sums = dot(jnp.concatenate(terms, axis=0).astype(BF16), probe_basis[...])
    charges = sums[:width]
    for x in range(3):
        charges = charges + grid[x] * sums[(x + 1) * width : (x + 2) * width]
    mixed = dot_tn(w_mix[...], charges.astype(BF16)) + columns[:, layers : layers + 1]
    density[...] = jnp.sum(silu(mixed) * columns[:, layers + 1 : layers + 2], axis=0, keepdims=True)


def few_groups(
    atom_s, atom_pos, edge_vec, edge_nbr, border_index, send_index, probe_list, probe_count,
    w_in, b_in, w_msg, w_rad, w_probe, w_mix, b_mix, w_out,
):
    atoms, half = atom_s.shape
    groups = lax.axis_size("brick") * lax.axis_size("probe")
    fan = edge_nbr.shape[0] // atoms
    rim = border_index.shape[0] // 2
    n_basis = w_rad.shape[1]
    cap = send_index.shape[1] // groups
    width = 2 * half
    every = groups * LANES
    data = pack(groups, atom_s, atom_pos, edge_vec, edge_nbr, border_index, send_index)
    weights, small = pack_weights(
        half, w_msg, w_rad, w_probe, b_in, b_mix, w_out, probe_list, probe_count
    )
    swap = [(0, 1), (1, 0)]
    weights_other = lax.ppermute(weights, "chan", swap)
    mine = lax.all_to_all(data, ("brick", "probe"), split_axis=0, concat_axis=0, tiled=True)
    anywhere = pl.BlockSpec(memory_space=pl.ANY)
    mine = pl.pallas_call(
        after_kernel,
        out_shape=jax.ShapeDtypeStruct(mine.shape, BF16),
        in_specs=[anywhere] * 2,
        out_specs=anywhere,
        input_output_aliases={0: 0},
        compiler_params=pltpu.CompilerParams(vmem_limit_bytes=16 * 1024 * 1024),
        name="after",
    )(mine, weights_other)
    other = lax.ppermute(mine, "chan", swap)
    n_probes = probe_list.shape[0] * PB
    sizes = (groups, fan, rim, half, n_basis, cap, probe_list.shape[0])
    facts, slots, probe_basis = pl.pallas_call(
        functools.partial(index_kernel, sizes, w_in.shape[0] + 2),
        out_shape=(
            jax.ShapeDtypeStruct((16, groups * cap * fan), F32),
            jax.ShapeDtypeStruct((LANES, LANES), F32),
            jax.ShapeDtypeStruct((n_basis * groups * cap, n_probes), BF16),
        ),
        compiler_params=pltpu.CompilerParams(vmem_limit_bytes=24 * 1024 * 1024),
        name="index",
    )(mine, small)
    density = pl.pallas_call(
        functools.partial(density_kernel, sizes),
        out_shape=jax.ShapeDtypeStruct((1, n_probes), F32),
        scratch_shapes=[
            pltpu.VMEM((width, every), BF16),
            pltpu.VMEM((groups, 2 * width, LANES), BF16),
            pltpu.VMEM((groups, 2 * width, LANES), BF16),
            pltpu.VMEM((4 * width, every), BF16),
            pltpu.VMEM((2,) + weights.shape, BF16),
        ],
        compiler_params=pltpu.CompilerParams(vmem_limit_bytes=40 * 1024 * 1024),
        name="density",
    )(mine, other, weights, weights_other, small, w_in, w_mix, facts, slots, probe_basis)
    return density.reshape(n_probes)


def per_device(*args):
    if lax.axis_size("brick") * lax.axis_size("probe") == FEW_GROUPS:
        return few_groups(*args)
    return many_groups(*args)


def extended(block, sides, width):
    for axis, dim in sides:
        count = lax.axis_size(axis)
        forward = [(i, i + 1) for i in range(count - 1)]
        forward.append((count - 1, 0))
        backward = [(target, source) for source, target in forward]
        low = lax.ppermute(
            lax.slice_in_dim(block, block.shape[dim] - width, None, axis=dim), axis, forward
        )
        high = lax.ppermute(lax.slice_in_dim(block, 0, width, axis=dim), axis, backward)
        block = jnp.concatenate([low, block, high], axis=dim)
    return block


def radial(distance, count, top):
    centers = jnp.arange(count).astype(jnp.float32) * (top / (count - 1))
    return jnp.exp(-2.0 * (distance[..., None] - centers) ** 2)


def make_block(
    recv_rows, recv_pos, w_scalar, w_vector, feat_width, group_no, n_blocks, list_len, n_basis
):

    def probe_block(block_in):
        block_no, listed, live_count = block_in
        index_row = (group_no * n_blocks + block_no) * PB + jnp.arange(PB, dtype=jnp.int32)
        grid_xyz = (
            jnp.stack([index_row % 16, index_row // 16 % 16, index_row // 256 % 16], axis=1).astype(
                jnp.float32
            )
            * 0.25
        )
        atom_xyz = recv_pos[:, listed]
        disp = grid_xyz[:, :, None] - atom_xyz[None]
        dist_sq = jnp.sum(disp * disp, axis=1)
        live = (jnp.arange(list_len, dtype=jnp.int32) < live_count).astype(jnp.float32)
        envelope = (1.0 - dist_sq / 64.0) ** 2 * live[None, :]
        basis = radial(jnp.sqrt(dist_sq), n_basis, 7.0) * envelope[:, :, None]
        scalar_w = basis.astype(jnp.bfloat16).reshape(PB, list_len * n_basis)
        vector_w = (
            (disp[:, :, :, None] * basis[:, None])
            .astype(jnp.bfloat16)
            .reshape(PB, 3 * list_len * n_basis)
        )
        atom_rows = recv_rows[listed]
        atom_terms = (atom_rows[:, None, :feat_width] * w_scalar[None]).reshape(
            list_len * n_basis, feat_width
        )
        vec_rows = jnp.transpose(
            atom_rows[:, feat_width:].reshape(list_len, 3, feat_width), (1, 0, 2)
        )
        vector_terms = (vec_rows[:, :, None, :] * w_vector[None, None]).reshape(
            3 * list_len * n_basis, feat_width
        )
        charge = jnp.dot(scalar_w, atom_terms, preferred_element_type=jnp.float32) + jnp.dot(
            vector_w, vector_terms, preferred_element_type=jnp.float32
        )
        return charge.astype(jnp.bfloat16)

    return probe_block


def many_groups(
    atom_s,
    atom_pos,
    edge_vec,
    edge_nbr,
    border_index,
    send_index,
    probe_list,
    probe_count,
    w_in,
    b_in,
    w_msg,
    w_rad,
    w_probe,
    w_mix,
    b_mix,
    w_out,
):
    atom_count, half_width = atom_s.shape
    n_layers = w_in.shape[0]
    width = w_in.shape[1]
    n_basis = w_rad.shape[1]
    fan_out = edge_nbr.shape[0] // atom_count
    root_fan = fan_out**0.5
    rim_rows = border_index.shape[0] // 2
    length = jnp.sqrt(jnp.sum(edge_vec * edge_vec, axis=0))
    edge_env = (1.0 - length * length / 36.0) ** 2
    edge_basis = (radial(length, n_basis, 6.0) * edge_env[:, None]).astype(jnp.bfloat16)
    edge_cols = jnp.transpose(edge_vec)
    scalars = atom_s
    vectors = jnp.zeros((atom_count, 3 * half_width), jnp.bfloat16)
    for layer_no in range(n_layers):
        full_rows = lax.all_gather(scalars, "chan", axis=1, tiled=True)
        in_weight = w_in[layer_no]
        in_bias = b_in[layer_no]
        msg_weight = w_msg[layer_no].reshape(width, 3 * half_width)
        rad_weight = w_rad[layer_no].reshape(n_basis, 3 * half_width)
        hidden_act = jax.nn.silu(
            jnp.dot(full_rows, in_weight, preferred_element_type=jnp.float32) + in_bias
        ).astype(jnp.bfloat16)
        inner_tab = jnp.concatenate(
            [
                jnp.dot(hidden_act, msg_weight, preferred_element_type=jnp.float32).astype(
                    jnp.bfloat16
                ),
                vectors,
            ],
            axis=1,
        )
        padded = extended(inner_tab[border_index], ((("brick", "probe"), 0),), rim_rows)
        lookup = jnp.concatenate([inner_tab, padded[:rim_rows], padded[3 * rim_rows :]], axis=0)
        neighbour_rows = lookup[edge_nbr]
        filters = jnp.dot(edge_basis, rad_weight, preferred_element_type=jnp.float32)
        weighted = neighbour_rows[:, : 3 * half_width] * filters
        neighbour_vec = neighbour_rows[:, 3 * half_width :].reshape(-1, 3, half_width)
        vector_gate = weighted[:, None, half_width : 2 * half_width]
        along_edge = weighted[:, None, 2 * half_width :]
        delta_vec = neighbour_vec * vector_gate + along_edge * edge_cols[:, :, None]
        delta_scalar = (
            weighted[:, :half_width].reshape(atom_count, fan_out, half_width).sum(axis=1) / root_fan
        )
        delta_vec = delta_vec.reshape(atom_count, fan_out, 3 * half_width).sum(axis=1) / root_fan
        scalars = (scalars + delta_scalar).astype(jnp.bfloat16)
        vectors = (vectors + delta_vec).astype(jnp.bfloat16)
    features = jnp.concatenate([scalars, vectors], axis=1)
    picks = send_index[0]
    n_brick = lax.axis_size("brick")
    n_probe = lax.axis_size("probe")
    n_groups = n_brick * n_probe
    slot_cap = picks.shape[0] // n_groups
    out_rows = features[picks]
    out_pos = jnp.transpose(atom_pos)[picks].astype(jnp.bfloat16)
    received = (
        lax.all_to_all(
            out_rows.reshape(n_groups, slot_cap, 4 * half_width),
            ("brick", "probe"),
            split_axis=0,
            concat_axis=0,
            tiled=True,
        ),
        lax.all_to_all(
            out_pos.reshape(n_groups, slot_cap, 3),
            ("brick", "probe"),
            split_axis=0,
            concat_axis=0,
            tiled=True,
        ),
    )
    recv_count = n_groups * slot_cap
    recv_rows = received[0].reshape(recv_count, 4 * half_width)
    recv_pos = jnp.transpose(received[1].reshape(recv_count, 3)).astype(jnp.float32)
    group_no = lax.axis_index("brick") * n_probe + lax.axis_index("probe")
    n_blocks, list_len = probe_list.shape
    probe_block = make_block(
        recv_rows,
        recv_pos,
        w_probe[:, 0, :],
        w_probe[:, 1, :],
        half_width,
        group_no,
        n_blocks,
        list_len,
        n_basis,
    )
    charges = lax.map(
        probe_block, (jnp.arange(n_blocks, dtype=jnp.int32), probe_list, probe_count)
    ).reshape(n_blocks * PB, half_width)
    mix_rows = lax.dynamic_slice_in_dim(w_mix, lax.axis_index("chan") * half_width, half_width, 0)
    mixed = lax.psum(jnp.dot(charges, mix_rows, preferred_element_type=jnp.float32), "chan")
    return jnp.sum(jax.nn.silu(mixed + b_mix) * w_out, axis=1)


def solution(mesh):
    in_specs = (
        P(("image", "brick", "probe"), "chan"),
        P(None, ("image", "brick", "probe")),
        P(None, ("image", "brick", "probe")),
        P(("image", "brick", "probe")),
        P(("image", "brick", "probe")),
        P(("image", "brick", "probe"), None),
        P(("image", "brick", "probe"), None),
        P(("image", "brick", "probe")),
        P(),
        P(),
        P(None, None, None, "chan"),
        P(None, None, None, "chan"),
        P(None, None, "chan"),
        P(),
        P(),
        P(),
    )
    out_specs = P(("image", "brick", "probe"))
    return jax.shard_map(
        per_device, mesh=mesh, in_specs=in_specs, out_specs=out_specs, check_vma=False
    )
```

```python
import functools
import itertools
import math

import jax
import jax.numpy as jnp
from jax import lax
from jax.experimental import pallas as pl
from jax.experimental.pallas import tpu as pltpu
from jax.sharding import PartitionSpec as P

PB = 128
LANES = 128
FEW_GROUPS = 8
SMALL = 16
TOGETHER = 4
ROOT = (2.0 * math.log2(math.e)) ** 0.5
F32 = jnp.float32
BF16 = jnp.bfloat16


def iota(shape, dim):
    return lax.broadcasted_iota(jnp.int32, shape, dim)


def dot(a, b):
    return jnp.dot(a, b, preferred_element_type=F32)


def dot_tn(a, b):
    return lax.dot_general(a, b, (((0,), (0,)), ((), ())), preferred_element_type=F32)


def one_hot(mask):
    return jnp.where(mask, 1.0, 0.0).astype(BF16)


def same(names, row):
    return jnp.where(names == row, jnp.ones_like(names), jnp.zeros_like(names))


def silu(x):
    half_x = 0.5 * x
    return half_x * jnp.tanh(half_x) + half_x


def bell(scaled, center):
    away = scaled - center
    return jnp.exp2(-(away * away))


def lane_atom(lane, fan, tiles):
    return (lane % tiles) * (LANES // fan) + lane // tiles


def length_keeping_round(exact):
    choices = []
    for value in exact:
        near = value.astype(BF16).astype(F32)
        step = jnp.where(value > near, 1.01 / 256.0, -1.01 / 256.0) * jnp.abs(near)
        choices.append((near, (near + step).astype(BF16).astype(F32)))
    target = sum(value * value for value in exact)
    best, best_error = None, None
    for picked in itertools.product(*choices):
        error = jnp.abs(sum(value * value for value in picked) - target)
        if best is None:
            best, best_error = picked, error
            continue
        better = error < best_error
        best = tuple(jnp.where(better, new, old) for new, old in zip(picked, best))
        best_error = jnp.where(better, error, best_error)
    return best


def pack_kernel(
    fan, atom_s, atom_pos, edge_vec, edge_nbr, border, send, data_out, natural
):
    half, atoms = atom_s.shape
    tiles = atoms * fan // LANES
    per_tile = LANES // fan
    part = lax.axis_index("chan")
    perm = one_hot(lane_atom(iota((atoms, LANES), 1), fan, tiles) == iota((atoms, LANES), 0))
    scalars = dot(atom_s[...], perm).astype(BF16)
    for tile in range(tiles):
        for comp in range(3):
            natural[comp * tiles + tile : comp * tiles + tile + 1, :] = edge_vec[
                comp : comp + 1, tile * LANES : (tile + 1) * LANES
            ]
    exact = [natural[comp * tiles : (comp + 1) * tiles, :] for comp in range(3)]
    for comp, value in enumerate(length_keeping_round(exact)):
        natural[comp * tiles : (comp + 1) * tiles, :] = value
    natural[3 * tiles : 4 * tiles, :] = edge_nbr[...].astype(F32)
    natural[4 * tiles :, :] = jnp.zeros((LANES - 4 * tiles, LANES), F32)
    turned = natural[...].T
    lane = iota((fan, LANES), 1)
    sorted_rows = []
    for comp in range(4):
        rows = jnp.zeros((fan, LANES), F32)
        for a in range(per_tile):
            piece = turned[a * fan : (a + 1) * fan, :]
            shift = (a * tiles - comp * tiles) % LANES
            piece = pltpu.roll(piece, shift, 1) if shift else piece
            rows = jnp.where(lane // tiles == a, piece, rows)
        sorted_rows.append(rows)
    blank = jnp.zeros((1, LANES), F32)
    every_edge = jnp.concatenate(sorted_rows, axis=0).astype(BF16)
    sorted_rows = [jnp.where(part == 0, rows[: fan // 2], rows[fan // 2 :]) for rows in sorted_rows]
    border_row = jnp.concatenate(
        [border[...].astype(F32), jnp.zeros((1, LANES - border.shape[1]), F32)], axis=1
    )
    picks = send.shape[1]
    groups = data_out.shape[0]
    cap = picks // groups
    block = fan * cap
    lane = iota((picks, groups * block), 1)
    place = (lane // block) * cap + lane % cap
    send_row = jnp.broadcast_to(send[...].astype(F32), (8, picks)).astype(BF16)
    wanted = dot(send_row, one_hot(iota((picks, groups * block), 0) == place))[0:1]
    atom_col = lane_atom(iota((LANES, groups * block), 0), fan, tiles).astype(F32)
    spread = dot(every_edge, one_hot(atom_col == wanted))
    edge_k = iota(spread.shape, 0) % fan
    spread = jnp.where(edge_k == (iota(spread.shape, 1) % block) // cap, spread, 0.0)
    picked = jnp.sum(spread.reshape(4, fan, groups * block), axis=1)
    pick_atom = one_hot(iota((atoms, picks), 0).astype(F32) == send[...].astype(F32))
    facts = [send[...].astype(F32)]
    pos = dot(atom_pos[...].astype(BF16), pick_atom)
    facts += [pos[x : x + 1] for x in range(3)]
    owner = iota((groups, picks), 1) // cap == iota((groups, picks), 0)
    facts = jnp.concatenate([jnp.where(owner, fact, 0.0) for fact in facts], axis=1)
    row = iota((4 * picks, LANES), 0)
    place = (row // picks) * cap + row % cap
    facts = dot(facts.astype(BF16), one_hot(place == iota((4 * picks, LANES), 1)))
    edge_part = jnp.concatenate(sorted_rows, axis=0).astype(BF16)
    for group in range(groups):
        mine = slice(group * block, (group + 1) * block)
        rest = [facts[group : group + 1], border_row]
        for comp in (0, 2):
            rest.append(
                jnp.concatenate([picked[comp : comp + 1, mine], picked[comp + 1 : comp + 2, mine]], axis=1)
            )
        rest = jnp.concatenate(rest + [blank] * 4, axis=0)
        data_out[group, 0:half, :] = scalars
        data_out[group, half : half + 2 * fan, :] = edge_part
        data_out[group, half + 2 * fan :, :] = rest.astype(BF16)


def weight_kernel(
    w_msg, w_rad, w_probe, b_in, b_mix, w_out, probe_list, probe_count, weight_out, small_out
):
    at = 0
    for piece in (b_in, b_mix, w_out, probe_list, probe_count):
        rows, cols = piece.shape
        small_out[at : at + rows, 0:cols] = piece[...].astype(F32)
        at += rows
    probe_rows = [w_probe[r].astype(F32) for r in range(w_probe.shape[0])]
    radial = jnp.concatenate([w_rad[...].astype(F32)] + probe_rows, axis=0).T.astype(BF16)
    weight_out[: w_msg.shape[0], :] = w_msg[...]
    weight_out[w_msg.shape[0] :, :] = radial


def pack(copies, atom_s, atom_pos, edge_vec, edge_nbr, border_index, send_index):
    atoms, half = atom_s.shape
    fan = edge_nbr.shape[0] // atoms
    return pl.pallas_call(
        functools.partial(pack_kernel, fan),
        out_shape=jax.ShapeDtypeStruct((copies, half + 4 * fan // 2 + 8, LANES), BF16),
        scratch_shapes=[pltpu.VMEM((LANES, LANES), F32)],
        name="pack",
    )(
        atom_s.T,
        atom_pos,
        edge_vec,
        edge_nbr.reshape(-1, LANES),
        border_index.reshape(1, -1),
        send_index,
    )


def pack_weights(half, w_msg, w_rad, w_probe, b_in, b_mix, w_out, probe_list, probe_count):
    return pl.pallas_call(
        weight_kernel,
        out_shape=(
            jax.ShapeDtypeStruct((w_msg.size // LANES + half, LANES), BF16),
            jax.ShapeDtypeStruct((SMALL, LANES), F32),
        ),
        name="pack_weights",
    )(
        jnp.transpose(w_msg, (0, 2, 3, 1)).reshape(-1, LANES),
        jnp.transpose(w_rad, (0, 2, 1, 3)).reshape(-1, half),
        w_probe,
        b_in,
        b_mix.reshape(1, -1),
        w_out.reshape(1, -1),
        probe_list,
        probe_count.reshape(1, -1),
    )


def after_kernel(block, there, same_block):
    pass


def probe_grid(me, probes):
    number = me * probes + iota((1, probes), 1)
    return [(n % 16).astype(F32) * 0.25 - 1.875 for n in (number, number // 16, number // 256)]


def index_kernel(sizes, list_at, data_mine, small, facts_out, slots, probe_basis):
    groups, fan, rim, half, n_basis, cap, n_blocks = sizes
    tiles = fan
    received = groups * cap
    per_group = fan * cap
    edges = received * fan
    rest_at = half + 2 * fan
    me = lax.axis_index("brick") * lax.axis_size("probe") + lax.axis_index("probe")
    small_rows = small[...]
    rest = [data_mine[g, rest_at : rest_at + 8, :].astype(F32) for g in range(groups)]
    facts = jnp.concatenate([rows[0:1] for rows in rest], axis=0).astype(BF16)
    lane = iota((LANES, 4 * received), 1)
    wanted = (lane // received) * cap + lane % cap
    facts = dot(facts, one_hot(iota((LANES, 4 * received), 0) == wanted))
    source = (iota(facts.shape, 1) % received) // cap
    facts = jnp.sum(jnp.where(source == iota(facts.shape, 0), facts, 0.0), axis=0, keepdims=True)
    pick_atoms = facts[:, 0:received]
    for comp in range(3):
        rows = [r[2 + comp // 2 : 3 + comp // 2, (comp % 2) * per_group :][:, :per_group] for r in rest]
        facts_out[comp : comp + 1, :] = jnp.concatenate(rows, axis=1)
    nbr = jnp.concatenate([r[3:4, per_group : 2 * per_group] for r in rest], axis=1).astype(jnp.int32)

    home = iota((1, edges), 1) // per_group
    is_low = (nbr >= LANES) & (nbr < LANES + rim)
    is_up = nbr >= LANES + rim
    owner = jnp.where(
        is_low, (home + groups - 1) % groups, jnp.where(is_up, (home + 1) % groups, home)
    )
    entry = owner * 2 * rim + jnp.where(is_low, nbr - (LANES - rim), nbr - (LANES + rim))
    entry = jnp.where(is_low | is_up, entry, -1)
    border_all = jnp.concatenate([r[1:2, 0 : 2 * rim] for r in rest], axis=1)
    border_all = jnp.broadcast_to(border_all, (16, groups * 2 * rim)).astype(BF16)
    seen = dot(border_all, one_hot(iota((groups * 2 * rim, edges), 0) == entry))[0:1]
    target = jnp.where(entry < 0, nbr, seen.astype(jnp.int32))

    column = iota((groups * LANES, 1), 0)
    column_name = (column // LANES) * LANES + lane_atom(column % LANES, fan, tiles)
    home = iota((1, received), 1) // cap
    self_hot = one_hot(column_name == home * LANES + pick_atoms.astype(jnp.int32))
    uses = dot(self_hot, jnp.ones((received, LANES), BF16))
    uses = [uses[g * LANES : (g + 1) * LANES] for g in range(groups)]
    quad = groups // 2
    window_hot, near_groups = [], []
    for h in range(2):
        lanes = slice(h * edges // 2, (h + 1) * edges // 2)
        near = lax.rem(owner[:, lanes] + 2 * groups - (h * quad + groups - 1), groups)
        hot = one_hot(column_name[: (quad + 2) * LANES] == near * LANES + target[:, lanes])
        window_hot.append(hot)
        near_groups.append(near)
        used = dot(hot, jnp.ones((edges // 2, LANES), BF16))
        for i in range(quad + 2):
            g = (h * quad + groups - 1 + i) % groups
            uses[g] = uses[g] + used[i * LANES : (i + 1) * LANES]
    lane = iota((LANES, LANES), 1)
    needed = jnp.zeros((LANES, LANES), F32)
    for g in range(groups):
        needed = jnp.where((lane == g) & (uses[g] > 0.0), 1.0, needed)
    order = dot(one_hot(lane <= iota((LANES, LANES), 0)), needed.astype(BF16))
    slot = jnp.where(needed > 0.0, order - 1.0, -1.0)
    slots[...] = slot
    slot_rows = slot.T
    facts_out[8:9, 0:LANES] = order[LANES - 1 : LANES, :]

    for h in range(2):
        lanes = slice(h * edges // 2, (h + 1) * edges // 2)
        in_window = [(h * quad + groups - 1 + i) % groups for i in range(quad + 2)]
        row = jnp.concatenate([slot_rows[g : g + 1] for g in in_window], axis=1)
        row = jnp.broadcast_to(row, (16, (quad + 2) * LANES)).astype(BF16)
        place = dot(row, window_hot[h])[0:1]
        facts_out[3:4, lanes] = near_groups[h].astype(F32) * LANES + place
    row = jnp.concatenate([slot_rows[g : g + 1] for g in range(groups)], axis=1)
    row = jnp.broadcast_to(row, (16, groups * LANES)).astype(BF16)
    facts_out[7:8, 0:received] = home.astype(F32) * LANES + dot(row, self_hot)[0:1]

    shifted = facts - 1.875
    for x in range(3):
        facts_out[4 + x : 5 + x, 0:received] = shifted[:, (1 + x) * received : (2 + x) * received]
    pos_cols = jnp.broadcast_to(shifted, (LANES, 4 * received)).T
    list_len = LANES
    counts = []
    for block in range(n_blocks):
        limit = small_rows[list_at + n_blocks : list_at + n_blocks + 1, block : block + 1]
        live = iota((1, list_len), 1).astype(F32) < limit
        named = jnp.where(live, small_rows[list_at + block : list_at + block + 1], -1.0)
        hits = jnp.where(iota((received, list_len), 0).astype(F32) == named, 1.0, 0.0)
        counts.append(jnp.broadcast_to(jnp.sum(hits, axis=1, keepdims=True), (received, PB)))
    counts = jnp.concatenate(counts, axis=1)
    probes = n_blocks * PB
    grid = probe_grid(me, probes)
    dist_sq = jnp.zeros((received, probes), F32)
    for x in range(3):
        dist_sq = dist_sq + (grid[x] - pos_cols[(1 + x) * received : (2 + x) * received, 0:1]) ** 2
    dist = jnp.sqrt(dist_sq) * ROOT
    envelope = (1.0 - dist_sq / 64.0) ** 2 * counts
    probe_basis[...] = jnp.concatenate(
        [
            (bell(dist, r * (ROOT * 7.0 / (n_basis - 1))) * envelope).astype(BF16)
            for r in range(n_basis)
        ],
        axis=0,
    )


def density_kernel(
    sizes,
    data_mine,
    data_other,
    weights_mine,
    weights_other,
    small,
    w_in,
    w_mix,
    facts,
    slots,
    probe_basis,
    density,
    state0,
    own0,
    faces0,
    state1,
    weights,
):
    groups, fan, rim, half, n_basis, cap, n_blocks = sizes
    layers = w_in.shape[0]
    width = 2 * half
    tiles = LANES * fan // LANES
    root_fan = fan**0.5
    me = lax.axis_index("brick") * lax.axis_size("probe") + lax.axis_index("probe")
    part = lax.axis_index("chan")
    weights[part] = weights_mine[...]
    weights[1 - part] = weights_other[...]
    every = groups * LANES
    edge_at = half
    n_edge = 4 * fan // 2
    rest_at = half + n_edge

    def data(group, c, rows):
        return (data_mine, data_other)[c][group, rows, :]

    def weight(layer, p):
        at = (layer * 3 + p) * half
        return jnp.concatenate([weights[c, at : at + half, :] for c in range(2)], axis=0)

    def radial_weight(layer, p):
        at = (layer * 3 + p) * n_basis
        return radial_all[:, at : at + n_basis]

    def edge_rows(group):
        return [data(group, c, slice(edge_at, rest_at)).astype(F32) for c in range(2)]

    def border_of(group):
        return data(group, 0, slice(rest_at, rest_at + 8)).astype(F32)[1:2, 0 : 2 * rim]

    centers = iota((n_basis, 1), 0).astype(F32) * (ROOT * 6.0 / (n_basis - 1))

    def basis_of(length, env):
        return (bell(length * ROOT, centers) * env).astype(BF16)

    small_rows = small[...]
    columns = small_rows.T
    radial_at = weights.shape[1] - half
    radial_all = jnp.concatenate([weights[c, radial_at:, :] for c in range(2)], axis=0)

    received = groups * cap
    edges = received * fan
    per_group = fan * cap
    pick_vec = [facts[x : x + 1, :] for x in range(3)]
    pos = facts[4:7, 0:received]
    length = jnp.sqrt(sum(x * x for x in pick_vec))
    basis1 = basis_of(length, (1.0 - length * length / 36.0) ** 2)
    quad = groups // 2
    window = [[(h * quad + groups - 1 + i) % groups for i in range(quad + 2)] for h in range(2)]
    near_row = iota(((quad + 2) * LANES, edges // 2), 0).astype(F32)
    window_pick = [
        one_hot(near_row == facts[3:4, h * edges // 2 : (h + 1) * edges // 2]) for h in range(2)
    ]
    chosen_atoms = one_hot(iota((every, received), 0).astype(F32) == facts[7:8, 0:received])

    terms_shape = (2 * n_basis, n_basis * received)
    probe_weight = radial_all[:, 3 * layers * n_basis :]
    w_scalar, w_vector = (
        dot(probe_weight, one_hot(iota(terms_shape, 1) // received * 2 + p == iota(terms_shape, 0)))
        for p in range(2)
    )

    probes = density.shape[1]
    grid = probe_grid(me, probes)

    for group in range(groups):
        for c in range(2):
            place = part if c == 0 else 1 - part
            rows = pl.ds(pl.multiple_of(place * half, half), half)
            state0[rows, group * LANES : (group + 1) * LANES] = data(group, c, slice(0, half))
    hidden = silu(dot_tn(w_in[0], state0[...]) + columns[:, 0:1]).astype(BF16)
    weight_ac = jnp.concatenate([weight(0, 0), weight(0, 2)], axis=0)
    messages = dot(weight_ac, hidden).astype(BF16)
    atom_col = lane_atom(iota((LANES, 2 * rim), 0), fan, tiles).astype(F32)
    for group in range(groups):
        own = messages[:, group * LANES : (group + 1) * LANES]
        own0[group] = own
        border_row = border_of(group)
        faces0[group, :, 0 : 2 * rim] = dot(own, one_hot(atom_col == border_row)).astype(BF16)

    row = iota((LANES + 2 * rim, 1), 0)
    names = jnp.where(
        row < LANES,
        lane_atom(row, fan, tiles),
        jnp.where(row < LANES + rim, row + rim, row - rim),
    ).astype(F32)
    names = jnp.broadcast_to(names, (LANES + 2 * rim, LANES)).astype(BF16)
    upper_lane = iota((2 * width, 2 * rim), 1) < rim
    radial_ac = jnp.concatenate([radial_weight(0, 0), radial_weight(0, 2)], axis=0)
    radial_rows = jnp.concatenate([jnp.zeros((2 * width, LANES + 2 * rim), BF16), radial_ac], axis=1)
    blank = jnp.zeros((2 * width, n_basis), BF16)

    some = LANES // 2
    step = fan // 2

    def update(group, first_slot):
        up = (group + 1) % groups
        low = (group + groups - 1) % groups
        ghosts = jnp.where(
            upper_lane,
            faces0[up, :, 0 : 2 * rim].astype(F32),
            faces0[low, :, 0 : 2 * rim].astype(F32),
        ).astype(BF16)
        table = jnp.concatenate([own0[group], ghosts, blank], axis=1)
        left = jnp.concatenate(
            [
                block[at : at + 16]
                for at in range(0, 2 * width, 16)
                for block in (table, radial_rows)
            ],
            axis=0,
        )
        lanes = slice(group * LANES, (group + 1) * LANES)
        slot_lane = (iota((LANES, some), 1) + first_slot).astype(F32)
        in_slot = one_hot(slots[:, group : group + 1] == slot_lane)
        source = jnp.concatenate(
            [data(group, c, slice(edge_at, rest_at)) for c in range(2)] + [state0[:, lanes]], axis=0
        )
        source = dot(source, in_slot)
        rows = jnp.concatenate([source[:n_edge], source[n_edge : 2 * n_edge]], axis=1)
        own_scalars = source[2 * n_edge :]
        vec = [rows[x * step : (x + 1) * step] for x in range(3)]
        nbr = rows[3 * step : 4 * step]
        length = jnp.sqrt(vec[0] * vec[0] + vec[1] * vec[1] + vec[2] * vec[2])
        env = (1.0 - length * length / 36.0) ** 2
        acc = jnp.zeros((width, LANES), F32)
        acc_vec = [jnp.zeros((width, LANES), F32) for _ in range(3)]
        for first in range(0, step, TOGETHER):
            ks = range(first, first + TOGETHER)
            picked = jnp.concatenate([same(names, nbr[k : k + 1].astype(BF16)) for k in ks], axis=1)
            basis = jnp.concatenate(
                [basis_of(length[k : k + 1], env[k : k + 1]) for k in ks], axis=1
            )
            both = dot(left, jnp.concatenate([picked, basis], axis=0))
            prod = jnp.concatenate(
                [both[at : at + 16] * both[at + 16 : at + 32] for at in range(0, 4 * width, 32)],
                axis=0,
            )
            for i, k in enumerate(ks):
                block = prod[:, i * LANES : (i + 1) * LANES]
                acc = acc + block[:width]
                for x in range(3):
                    acc_vec[x] = acc_vec[x] + block[width:] * vec[x][k : k + 1]
        acc, *acc_vec = [(a[:, :some] + a[:, some:]) / root_fan for a in [acc] + acc_vec]
        return jnp.concatenate([own_scalars + acc] + acc_vec, axis=0)

    for group in range(groups):
        state = update(group, 0)
        state = jnp.concatenate([state, jnp.zeros_like(state)], axis=1)
        state1[:, group * LANES : (group + 1) * LANES] = state.astype(BF16)

    @pl.when(jnp.max(facts[8:9, 0:groups]) > some)
    def _():
        for group in range(groups):

            @pl.when(jnp.max(facts[8:9, group : group + 1]) > some)
            def _():
                lanes = slice(group * LANES + some, (group + 1) * LANES)
                state1[:, lanes] = update(group, some).astype(BF16)

    rows = []
    for h in range(2):
        near_states = jnp.concatenate(
            [state1[:, g * LANES : (g + 1) * LANES] for g in window[h]], axis=1
        )
        rows.append(dot(near_states, window_pick[h]))
    rows = jnp.concatenate(rows, axis=1)
    hidden = silu(dot_tn(w_in[1], rows[:width].astype(BF16)) + columns[:, 1:2]).astype(BF16)
    weight_abc = jnp.concatenate([weight(1, p) for p in range(3)], axis=0)
    messages = dot(weight_abc, hidden).astype(BF16).astype(F32)
    radial_abc = jnp.concatenate([radial_weight(1, p) for p in range(3)], axis=0)
    filters = dot(radial_abc, basis1)
    weighted = messages * filters
    gate = weighted[width : 2 * width]
    along = weighted[2 * width :]
    parts = [weighted[:width]]
    for x in range(3):
        parts.append(rows[(1 + x) * width : (2 + x) * width] * gate + along * pick_vec[x])
    parts = jnp.concatenate(parts, axis=0).astype(BF16)
    edge = iota((edges, received), 0)
    slot = (edge // per_group) * cap + edge % cap
    delta = dot(parts, one_hot(slot == iota((edges, received), 1)))
    final = (dot(state1[...], chosen_atoms) + delta / root_fan).astype(BF16).astype(F32)

    along = final[width : 2 * width] * pos[0:1]
    for x in range(1, 3):
        along = along + final[(x + 1) * width : (x + 2) * width] * pos[x : x + 1]
    def repeat(value):
        return jnp.concatenate([value] * n_basis, axis=1)
    terms = [w_scalar * repeat(final[:width]) - w_vector * repeat(along)]
    for x in range(3):
        terms.append(w_vector * repeat(final[(x + 1) * width : (x + 2) * width]))
    sums = dot(jnp.concatenate(terms, axis=0).astype(BF16), probe_basis[...])
    charges = sums[:width]
    for x in range(3):
        charges = charges + grid[x] * sums[(x + 1) * width : (x + 2) * width]
    mixed = dot_tn(w_mix[...], charges.astype(BF16)) + columns[:, layers : layers + 1]
    density[...] = jnp.sum(silu(mixed) * columns[:, layers + 1 : layers + 2], axis=0, keepdims=True)


def few_groups(
    atom_s, atom_pos, edge_vec, edge_nbr, border_index, send_index, probe_list, probe_count,
    w_in, b_in, w_msg, w_rad, w_probe, w_mix, b_mix, w_out,
):
    atoms, half = atom_s.shape
    groups = lax.axis_size("brick") * lax.axis_size("probe")
    fan = edge_nbr.shape[0] // atoms
    rim = border_index.shape[0] // 2
    n_basis = w_rad.shape[1]
    cap = send_index.shape[1] // groups
    width = 2 * half
    every = groups * LANES
    data = pack(groups, atom_s, atom_pos, edge_vec, edge_nbr, border_index, send_index)
    weights, small = pack_weights(
        half, w_msg, w_rad, w_probe, b_in, b_mix, w_out, probe_list, probe_count
    )
    swap = [(0, 1), (1, 0)]
    weights_other = lax.ppermute(weights, "chan", swap)
    mine = lax.all_to_all(data, ("brick", "probe"), split_axis=0, concat_axis=0, tiled=True)
    anywhere = pl.BlockSpec(memory_space=pl.ANY)
    mine = pl.pallas_call(
        after_kernel,
        out_shape=jax.ShapeDtypeStruct(mine.shape, BF16),
        in_specs=[anywhere] * 2,
        out_specs=anywhere,
        input_output_aliases={0: 0},
        compiler_params=pltpu.CompilerParams(vmem_limit_bytes=16 * 1024 * 1024),
        name="after",
    )(mine, weights_other)
    other = lax.ppermute(mine, "chan", swap)
    n_probes = probe_list.shape[0] * PB
    sizes = (groups, fan, rim, half, n_basis, cap, probe_list.shape[0])
    facts, slots, probe_basis = pl.pallas_call(
        functools.partial(index_kernel, sizes, w_in.shape[0] + 2),
        out_shape=(
            jax.ShapeDtypeStruct((16, groups * cap * fan), F32),
            jax.ShapeDtypeStruct((LANES, LANES), F32),
            jax.ShapeDtypeStruct((n_basis * groups * cap, n_probes), BF16),
        ),
        compiler_params=pltpu.CompilerParams(vmem_limit_bytes=24 * 1024 * 1024),
        name="index",
    )(mine, small)
    density = pl.pallas_call(
        functools.partial(density_kernel, sizes),
        out_shape=jax.ShapeDtypeStruct((1, n_probes), F32),
        scratch_shapes=[
            pltpu.VMEM((width, every), BF16),
            pltpu.VMEM((groups, 2 * width, LANES), BF16),
            pltpu.VMEM((groups, 2 * width, LANES), BF16),
            pltpu.VMEM((4 * width, every), BF16),
            pltpu.VMEM((2,) + weights.shape, BF16),
        ],
        compiler_params=pltpu.CompilerParams(vmem_limit_bytes=40 * 1024 * 1024),
        name="density",
    )(mine, other, weights, weights_other, small, w_in, w_mix, facts, slots, probe_basis)
    return density.reshape(n_probes)


def per_device(*args):
    if lax.axis_size("brick") * lax.axis_size("probe") == FEW_GROUPS:
        return few_groups(*args)
    return many_groups(*args)


def extended(block, sides, width):
    for axis, dim in sides:
        count = lax.axis_size(axis)
        forward = [(i, i + 1) for i in range(count - 1)]
        forward.append((count - 1, 0))
        backward = [(target, source) for source, target in forward]
        low = lax.ppermute(
            lax.slice_in_dim(block, block.shape[dim] - width, None, axis=dim), axis, forward
        )
        high = lax.ppermute(lax.slice_in_dim(block, 0, width, axis=dim), axis, backward)
        block = jnp.concatenate([low, block, high], axis=dim)
    return block


def radial(distance, count, top):
    centers = jnp.arange(count).astype(jnp.float32) * (top / (count - 1))
    return jnp.exp(-2.0 * (distance[..., None] - centers) ** 2)


def make_block(
    recv_rows, recv_pos, w_scalar, w_vector, feat_width, group_no, n_blocks, list_len, n_basis
):

    def probe_block(block_in):
        block_no, listed, live_count = block_in
        index_row = (group_no * n_blocks + block_no) * PB + jnp.arange(PB, dtype=jnp.int32)
        grid_xyz = (
            jnp.stack([index_row % 16, index_row // 16 % 16, index_row // 256 % 16], axis=1).astype(
                jnp.float32
            )
            * 0.25
        )
        atom_xyz = recv_pos[:, listed]
        disp = grid_xyz[:, :, None] - atom_xyz[None]
        dist_sq = jnp.sum(disp * disp, axis=1)
        live = (jnp.arange(list_len, dtype=jnp.int32) < live_count).astype(jnp.float32)
        envelope = (1.0 - dist_sq / 64.0) ** 2 * live[None, :]
        basis = radial(jnp.sqrt(dist_sq), n_basis, 7.0) * envelope[:, :, None]
        scalar_w = basis.astype(jnp.bfloat16).reshape(PB, list_len * n_basis)
        vector_w = (
            (disp[:, :, :, None] * basis[:, None])
            .astype(jnp.bfloat16)
            .reshape(PB, 3 * list_len * n_basis)
        )
        atom_rows = recv_rows[listed]
        atom_terms = (atom_rows[:, None, :feat_width] * w_scalar[None]).reshape(
            list_len * n_basis, feat_width
        )
        vec_rows = jnp.transpose(
            atom_rows[:, feat_width:].reshape(list_len, 3, feat_width), (1, 0, 2)
        )
        vector_terms = (vec_rows[:, :, None, :] * w_vector[None, None]).reshape(
            3 * list_len * n_basis, feat_width
        )
        charge = jnp.dot(scalar_w, atom_terms, preferred_element_type=jnp.float32) + jnp.dot(
            vector_w, vector_terms, preferred_element_type=jnp.float32
        )
        return charge.astype(jnp.bfloat16)

    return probe_block


def many_groups(
    atom_s,
    atom_pos,
    edge_vec,
    edge_nbr,
    border_index,
    send_index,
    probe_list,
    probe_count,
    w_in,
    b_in,
    w_msg,
    w_rad,
    w_probe,
    w_mix,
    b_mix,
    w_out,
):
    atom_count, half_width = atom_s.shape
    n_layers = w_in.shape[0]
    width = w_in.shape[1]
    n_basis = w_rad.shape[1]
    fan_out = edge_nbr.shape[0] // atom_count
    root_fan = fan_out**0.5
    rim_rows = border_index.shape[0] // 2
    length = jnp.sqrt(jnp.sum(edge_vec * edge_vec, axis=0))
    edge_env = (1.0 - length * length / 36.0) ** 2
    edge_basis = (radial(length, n_basis, 6.0) * edge_env[:, None]).astype(jnp.bfloat16)
    edge_cols = jnp.transpose(edge_vec)
    scalars = atom_s
    vectors = jnp.zeros((atom_count, 3 * half_width), jnp.bfloat16)
    for layer_no in range(n_layers):
        full_rows = lax.all_gather(scalars, "chan", axis=1, tiled=True)
        in_weight = w_in[layer_no]
        in_bias = b_in[layer_no]
        msg_weight = w_msg[layer_no].reshape(width, 3 * half_width)
        rad_weight = w_rad[layer_no].reshape(n_basis, 3 * half_width)
        hidden_act = jax.nn.silu(
            jnp.dot(full_rows, in_weight, preferred_element_type=jnp.float32) + in_bias
        ).astype(jnp.bfloat16)
        inner_tab = jnp.concatenate(
            [
                jnp.dot(hidden_act, msg_weight, preferred_element_type=jnp.float32).astype(
                    jnp.bfloat16
                ),
                vectors,
            ],
            axis=1,
        )
        padded = extended(inner_tab[border_index], ((("brick", "probe"), 0),), rim_rows)
        lookup = jnp.concatenate([inner_tab, padded[:rim_rows], padded[3 * rim_rows :]], axis=0)
        neighbour_rows = lookup[edge_nbr]
        filters = jnp.dot(edge_basis, rad_weight, preferred_element_type=jnp.float32)
        weighted = neighbour_rows[:, : 3 * half_width] * filters
        neighbour_vec = neighbour_rows[:, 3 * half_width :].reshape(-1, 3, half_width)
        vector_gate = weighted[:, None, half_width : 2 * half_width]
        along_edge = weighted[:, None, 2 * half_width :]
        delta_vec = neighbour_vec * vector_gate + along_edge * edge_cols[:, :, None]
        delta_scalar = (
            weighted[:, :half_width].reshape(atom_count, fan_out, half_width).sum(axis=1) / root_fan
        )
        delta_vec = delta_vec.reshape(atom_count, fan_out, 3 * half_width).sum(axis=1) / root_fan
        scalars = (scalars + delta_scalar).astype(jnp.bfloat16)
        vectors = (vectors + delta_vec).astype(jnp.bfloat16)
    features = jnp.concatenate([scalars, vectors], axis=1)
    picks = send_index[0]
    n_brick = lax.axis_size("brick")
    n_probe = lax.axis_size("probe")
    n_groups = n_brick * n_probe
    slot_cap = picks.shape[0] // n_groups
    out_rows = features[picks]
    out_pos = jnp.transpose(atom_pos)[picks].astype(jnp.bfloat16)
    received = (
        lax.all_to_all(
            out_rows.reshape(n_groups, slot_cap, 4 * half_width),
            ("brick", "probe"),
            split_axis=0,
            concat_axis=0,
            tiled=True,
        ),
        lax.all_to_all(
            out_pos.reshape(n_groups, slot_cap, 3),
            ("brick", "probe"),
            split_axis=0,
            concat_axis=0,
            tiled=True,
        ),
    )
    recv_count = n_groups * slot_cap
    recv_rows = received[0].reshape(recv_count, 4 * half_width)
    recv_pos = jnp.transpose(received[1].reshape(recv_count, 3)).astype(jnp.float32)
    group_no = lax.axis_index("brick") * n_probe + lax.axis_index("probe")
    n_blocks, list_len = probe_list.shape
    probe_block = make_block(
        recv_rows,
        recv_pos,
        w_probe[:, 0, :],
        w_probe[:, 1, :],
        half_width,
        group_no,
        n_blocks,
        list_len,
        n_basis,
    )
    charges = lax.map(
        probe_block, (jnp.arange(n_blocks, dtype=jnp.int32), probe_list, probe_count)
    ).reshape(n_blocks * PB, half_width)
    mix_rows = lax.dynamic_slice_in_dim(w_mix, lax.axis_index("chan") * half_width, half_width, 0)
    mixed = lax.psum(jnp.dot(charges, mix_rows, preferred_element_type=jnp.float32), "chan")
    return jnp.sum(jax.nn.silu(mixed + b_mix) * w_out, axis=1)


def solution(mesh):
    in_specs = (
        P(("image", "brick", "probe"), "chan"),
        P(None, ("image", "brick", "probe")),
        P(None, ("image", "brick", "probe")),
        P(("image", "brick", "probe")),
        P(("image", "brick", "probe")),
        P(("image", "brick", "probe"), None),
        P(("image", "brick", "probe"), None),
        P(("image", "brick", "probe")),
        P(),
        P(),
        P(None, None, None, "chan"),
        P(None, None, None, "chan"),
        P(None, None, "chan"),
        P(),
        P(),
        P(),
    )
    out_specs = P(("image", "brick", "probe"))
    return jax.shard_map(
        per_device, mesh=mesh, in_specs=in_specs, out_specs=out_specs, check_vma=False
    )
```
